32 devices in a mesh: section: 2 (over core), mp: 2 (over x), dp: 8 (over z, y).
Axes of the slice: x: 2, y: 2, z: 4, core: 2. Of those that a mesh axis runs over, the one named last changes fastest.
Arguments:
- tokens: bfloat16 [2, 512, 8, 1024], P(None, 'mp', 'dp'), may hold values from -6 to 6
- valid_mask: int32 [2, 512, 8], P(None, None, 'dp'), may hold values from 0 to 1, as said below
- buckets: int32 [512], replicated, may hold values from 0 to 31, as said below
- state_init: bfloat16 [512, 8, 1024], P('mp', 'dp'), may hold values from -6 to 6
- norm_gain: float32 [2, 2, 1024], P('section'), may hold values from 0.5 to 1.5
- norm_shift: float32 [2, 2, 1024], P('section'), may hold values from -1.75 to 1.75
- w_qkv: bfloat16 [2, 3, 1024, 1024], P('section', None, None, 'mp'), may hold values from -0.1875 to 0.1875
- w_out: bfloat16 [2, 1024, 1024], P('section', 'mp'), may hold values from -1.5 to 1.5
- rel_bias: float32 [2, 32, 8], P('section', None, 'mp'), may hold values from -6 to 6
- w_up: bfloat16 [2, 1024, 4096], P('section', None, 'mp'), may hold values from -0.1875 to 0.1875
- up_bias: float32 [2, 4096], P('section', 'mp'), may hold values from -1.75 to 1.75
- w_down: bfloat16 [2, 4096, 1024], P('section', 'mp'), may hold values from -0.09375 to 0.09375
- down_bias: float32 [2, 1024], P('section'), may hold values from -1.75 to 1.75
- state_gain: float32 [1024], replicated, may hold values from 0.5 to 1.5
- state_shift: float32 [1024], replicated, may hold values from -1.75 to 1.75
- w_state_qkv: bfloat16 [3, 1024, 1024], P(None, None, 'mp'), may hold values from -0.1875 to 0.1875
- w_state_out: bfloat16 [1024, 1024], P('mp'), may hold values from -1.5 to 1.5
- gate_bias: float32 [1024], replicated, may hold values from -2 to 2
- cotangent: bfloat16 [2, 512, 8, 1024], P(None, 'mp', 'dp'), may hold values from -6 to 6
Outputs:
- acts: bfloat16 [2, 2, 512, 8, 1024], P('section', None, 'mp', 'dp')
- input_grads: float32 [2, 2, 512, 8, 1024], P('section', None, 'mp', 'dp')
- final_state: float32 [512, 8, 1024], P('mp', 'dp')
- grad_norm_gain: float32 [2, 2, 1024], P('section')
- grad_norm_shift: float32 [2, 2, 1024], P('section')
- grad_w_qkv: float32 [2, 3, 1024, 1024], P('section', None, None, 'mp')
- grad_w_out: float32 [2, 1024, 1024], P('section', 'mp')
- grad_rel_bias: float32 [2, 32, 8], P('section', None, 'mp')
- grad_w_up: float32 [2, 1024, 4096], P('section', None, 'mp')
- grad_up_bias: float32 [2, 4096], P('section', 'mp')
- grad_w_down: float32 [2, 4096, 1024], P('section', 'mp')
- grad_down_bias: float32 [2, 1024], P('section')
- grad_state_gain: float32 [1024], replicated
- grad_state_shift: float32 [1024], replicated
- grad_w_state_qkv: float32 [3, 1024, 1024], P(None, None, 'mp')
- grad_w_state_out: float32 [1024, 1024], P('mp')
- grad_gate_bias: float32 [1024], replicated
The draws below stay inside these ranges and needn't reach their ends.
Inputs may be any that keep to these rules, and one draw needn't show every extreme that they name: `valid_mask`: in each block of 512 tokens of a document the valid tokens come first; at most 153 tokens at a block's end are invalid, and in every draw some block has exactly 153 invalid. `buckets`: never falls as the distance grows; distance 0 has bucket 0 and distance 512 - 1 has bucket 32 - 1.
All inputs are finite; a program needn't handle non-finite values.
Results may differ from the reference program's by a relative error of at most 0.03.
Values may be sent and summed in bfloat16 or wider, within the bound.
A program may use at most 320 MiB of HBM per device.

```python
from functools import partial
import jax
import jax.numpy as jnp
from jax import lax

D = 1024
H = 8
HD = 128
FF = 4096
BLK = 512
S = 512
NB = 32
M = 2
DOCS = 8
PAD = 153


def draw_valid_mask(key, part):
    key = jax.random.fold_in(key, 11)
    key_pads, key_pick = jax.random.split(key)
    pad_counts = jax.random.randint(key_pads, (M * DOCS,), 0, PAD + 1)
    chosen = jax.random.randint(key_pick, (), 0, M * DOCS)
    pad_counts = jnp.where(jnp.arange(M * DOCS) == chosen, PAD, pad_counts).reshape(M, 1, DOCS)
    places = jnp.arange(BLK).reshape(1, BLK, 1)
    return (places < BLK - pad_counts).astype(jnp.int32)


def draw_buckets(key, part):
    key = jax.random.fold_in(key, 23)
    drawn_values = jax.random.randint(key, (BLK,), 0, NB)
    ordered = jnp.sort(drawn_values)
    places = jnp.arange(BLK)
    ordered = jnp.where(places == 0, 0, ordered)
    return jnp.where(places == BLK - 1, NB - 1, ordered).astype(jnp.int32)


def shard_levels(own_key, dims, cuts, least, largest):
    level, own = 1.0, jax.random.fold_in(own_key, 6)
    for dim, parts in cuts:
        heights = jnp.exp(jax.random.uniform(jax.random.fold_in(own, dim), (parts,), jnp.float32, least / len(cuts), largest / len(cuts)))
        level = level * jnp.repeat(heights, dims[dim] // parts).reshape([-1 if axis == dim else 1 for axis in range(len(dims))])
    return level


def noise(stream_key, extent, scale, limit, cuts=(), held_as=jnp.bfloat16):
    entries = scale * jax.random.normal(stream_key, extent, jnp.float32)
    if cuts:
        entries = entries * shard_levels(stream_key, extent, cuts, -0.22, 0.18)
    return jnp.clip(entries, -limit, limit).astype(held_as)


def setup_inputs(seed: int = 0) -> dict:
    key_list = jax.random.split(jax.random.key(seed), 20)
    return {
        "tokens": noise(key_list[0], (M, BLK, DOCS, D), 1.0, 6.0, ((1, 2), (2, 8))),
        "valid_mask": draw_valid_mask(jax.random.fold_in(key_list[19], 71), 0),
        "buckets": draw_buckets(jax.random.fold_in(key_list[19], 71), 0),
        "state_init": noise(key_list[3], (S, DOCS, D), 1.0, 6.0, ((0, 2), (1, 8))),
        "norm_gain": jnp.clip(1.0 + 0.1 * jax.random.normal(key_list[4], (2, 2, D), jnp.float32), 0.5, 1.5),
        "norm_shift": noise(key_list[5], (2, 2, D), 0.3, 1.75, ((0, 2),), jnp.float32),
        "w_qkv": noise(key_list[6], (2, 3, D, D), D ** -0.5, 0.1875, ((0, 2), (3, 2))),
        "w_out": noise(key_list[7], (2, D, D), (max(D // 64, 1)) ** -0.5, 1.5, ((0, 2), (1, 2))),
        "rel_bias": noise(key_list[8], (2, NB, H), 1.0, 6.0, ((0, 2), (2, 2)), jnp.float32),
        "w_up": noise(key_list[9], (2, D, FF), D ** -0.5, 0.1875, ((0, 2), (2, 2))),
        "up_bias": noise(key_list[10], (2, FF), 0.3, 1.75, ((0, 2), (1, 2)), jnp.float32),
        "w_down": noise(key_list[11], (2, FF, D), FF ** -0.5, 0.09375, ((0, 2), (1, 2))),
        "down_bias": noise(key_list[12], (2, D), 0.3, 1.75, ((0, 2),), jnp.float32),
        "state_gain": jnp.clip(1.0 + 0.1 * jax.random.normal(key_list[13], (D,), jnp.float32), 0.5, 1.5),
        "state_shift": noise(key_list[14], (D,), 0.3, 1.75, (), jnp.float32),
        "w_state_qkv": noise(key_list[15], (3, D, D), D ** -0.5, 0.1875, ((2, 2),)),
        "w_state_out": noise(key_list[16], (D, D), (max(D // 64, 1)) ** -0.5, 1.5, ((0, 2),)),
        "gate_bias": jnp.clip(jax.random.uniform(key_list[17], (D,), jnp.float32, -2.0, 2.0), -2.0, 2.0),
        "cotangent": noise(key_list[18], (M, BLK, DOCS, D), 1.0, 6.0, ((1, 2), (2, 8))),
    }


@jax.custom_vjp
def low(v):
    return lax.optimization_barrier(v.astype(jnp.bfloat16)).astype(jnp.float32)

@jax.custom_vjp
def low_back(v):
    return v

def low_keep(v):
    return (low(v), None)

def low_pass(kept, grad):
    return (grad,)

def back_keep(v):
    return (v, None)

def back_low(kept, grad):
    return (low(grad),)
low.defvjp(low_keep, low_pass)
low_back.defvjp(back_keep, back_low)
eps = 1e-05
negative = -1000000000.0
highest = lax.Precision.HIGHEST

def layer_norm(values, gain, shift):
    average = lax.optimization_barrier(jnp.mean(values, axis=-1, keepdims=True))
    centered = values - average
    spread = lax.optimization_barrier(jnp.mean(centered * centered, axis=-1, keepdims=True))
    return centered * lax.rsqrt(spread + eps) * gain + shift

def matmul(left, right):
    return jnp.dot(left, right, precision=highest, preferred_element_type=jnp.float32)

def window_tables(buckets, rel_layer):
    query_pos = jnp.arange(BLK)[:, None]
    key_pos = jnp.arange(2 * BLK)[None, :]
    offset = key_pos - query_pos
    inside = (offset >= 1) & (offset <= BLK)
    distance = jnp.clip(BLK - offset, 0, BLK - 1).astype(jnp.int32)
    bucket_grid = jnp.take(buckets, distance)
    bias_table = jnp.take(rel_layer, bucket_grid, axis=0)
    return (inside, jnp.transpose(bias_table, (2, 0, 1)))

def block_step(params, recurrent, inside, window_bias, carry, inputs):
    key_prev, value_prev, valid_prev, state_now = carry
    rows_in, valid_cur = inputs
    scale_factor = HD ** (-0.5)
    normed = low(layer_norm(rows_in, params['gain'][0], params['shift'][0]))
    query = low(low_back(matmul(normed, params['qkv'][0]))).reshape(BLK, H, HD)
    key_cur = low(low_back(matmul(normed, params['qkv'][1]))).reshape(BLK, H, HD)
    value_cur = low(low_back(matmul(normed, params['qkv'][2]))).reshape(BLK, H, HD)
    key_win = jnp.concatenate([key_prev, key_cur], axis=0)
    value_win = jnp.concatenate([value_prev, value_cur], axis=0)
    valid_win = jnp.concatenate([valid_prev, valid_cur], axis=0) > 0.5
    window_logits = low_back(jnp.einsum('qhe,khe->hqk', query, key_win, precision=highest)) * scale_factor + window_bias
    window_logits = jnp.where(inside[None] & valid_win[None, None, :], window_logits, negative)
    if recurrent:
        state_normed = low(layer_norm(state_now, params['state_gain'], params['state_shift']))
        state_query = low(low_back(matmul(state_normed, params['state_qkv'][0]))).reshape(S, H, HD)
        state_key = low(low_back(matmul(state_normed, params['state_qkv'][1]))).reshape(S, H, HD)
        state_value = low(low_back(matmul(state_normed, params['state_qkv'][2]))).reshape(S, H, HD)
        state_logits = low_back(jnp.einsum('qhe,khe->hqk', query, state_key, precision=highest)) * scale_factor
        probs = jax.nn.softmax(jnp.concatenate([state_logits, window_logits], axis=-1), axis=-1)
        values_all = jnp.concatenate([state_value, value_win], axis=0)
    else:
        probs = jax.nn.softmax(window_logits, axis=-1)
        values_all = value_win
    attended = low(low_back(jnp.einsum('hqk,khe->qhe', low(probs), values_all, precision=highest))).reshape(BLK, D)
    hidden_rows = rows_in + low_back(matmul(attended, params['out']))
    mlp_in = low(layer_norm(hidden_rows, params['gain'][1], params['shift'][1]))
    pre_act = low_back(matmul(mlp_in, params['up'])) + params['up_bias']
    activated = low(jax.nn.gelu(pre_act, approximate=False))
    result_rows = hidden_rows + low_back(matmul(activated, params['down'])) + params['down_bias']
    if recurrent:
        recur_logits = low_back(jnp.einsum('she,khe->hsk', state_query, key_cur, precision=highest)) * scale_factor
        recur_logits = jnp.where((valid_cur > 0.5)[None, None, :], recur_logits, negative)
        recur_probs = jax.nn.softmax(recur_logits, axis=-1)
        recalled = low(low_back(jnp.einsum('hsk,khe->she', low(recur_probs), value_cur, precision=highest))).reshape(S, D)
        update = low_back(matmul(recalled, params['state_out']))
        gate = jax.nn.sigmoid(params['gate'])
        state_now = gate * state_now + (1.0 - gate) * update
    return ((key_cur, value_cur, valid_cur, state_now), result_rows)

def run_layer(params, recurrent, buckets, rows_seq, valid_seq, state_start):
    inside, window_bias = window_tables(buckets, params['rel'])
    start = (jnp.zeros((BLK, H, HD), jnp.float32), jnp.zeros((BLK, H, HD), jnp.float32), jnp.zeros((BLK,), jnp.float32), state_start)
    stepper = jax.checkpoint(partial(block_step, params, recurrent, inside, window_bias))
    final, outputs = lax.scan(stepper, start, (rows_seq, valid_seq))
    return (outputs, final[3])

def layer_params(weights, layer):
    return {'gain': weights['norm_gain'][layer], 'shift': weights['norm_shift'][layer], 'qkv': weights['w_qkv'][layer], 'out': weights['w_out'][layer], 'rel': weights['rel_bias'][layer], 'up': weights['w_up'][layer], 'up_bias': weights['up_bias'][layer], 'down': weights['w_down'][layer], 'down_bias': weights['down_bias'][layer], 'state_gain': weights['state_gain'], 'state_shift': weights['state_shift'], 'state_qkv': weights['w_state_qkv'], 'state_out': weights['w_state_out'], 'gate': weights['gate_bias']}

def document(rows_doc, probe, valid_doc, state_doc, weights, buckets):
    first_out, unused = run_layer(layer_params(weights, 0), False, buckets, rows_doc, valid_doc, state_doc)
    sent = low(low_back(first_out)) + probe
    second_out, final_state = run_layer(layer_params(weights, 1), True, buckets, sent, valid_doc, state_doc)
    return (sent, second_out, final_state)

def reference(tokens, valid_mask, buckets, state_init, norm_gain, norm_shift, w_qkv, w_out, rel_bias, w_up, up_bias, w_down, down_bias, state_gain, state_shift, w_state_qkv, w_state_out, gate_bias, cotangent):
    weights = {'norm_gain': norm_gain.astype(jnp.float32), 'norm_shift': norm_shift.astype(jnp.float32), 'w_qkv': w_qkv.astype(jnp.float32), 'w_out': w_out.astype(jnp.float32), 'rel_bias': rel_bias.astype(jnp.float32), 'w_up': w_up.astype(jnp.float32), 'up_bias': up_bias.astype(jnp.float32), 'w_down': w_down.astype(jnp.float32), 'down_bias': down_bias.astype(jnp.float32), 'state_gain': state_gain.astype(jnp.float32), 'state_shift': state_shift.astype(jnp.float32), 'w_state_qkv': w_state_qkv.astype(jnp.float32), 'w_state_out': w_state_out.astype(jnp.float32), 'gate_bias': gate_bias.astype(jnp.float32)}
    rows_docs = jnp.moveaxis(tokens, 2, 0).astype(jnp.float32)
    valid_docs = jnp.moveaxis(valid_mask, 2, 0).astype(jnp.float32)
    state_docs = jnp.moveaxis(state_init, 1, 0).astype(jnp.float32)
    cot_docs = jnp.moveaxis(cotangent, 2, 0).astype(jnp.float32)
    zero_grads = jax.tree.map(jnp.zeros_like, weights)

    def per_doc(running, inputs):
        rows_doc, valid_doc, state_doc, cot_doc = inputs
        probe = jnp.zeros_like(rows_doc)

        def forward(rows_arg, probe_arg, weight_set):
            return document(rows_arg, probe_arg, valid_doc, state_doc, weight_set, buckets)
        outputs, pullback = jax.vjp(forward, rows_doc, probe, weights)
        sent, second_out, final_state = outputs
        grad_rows, grad_probe, grad_weights = pullback((jnp.zeros_like(sent), cot_doc, jnp.zeros_like(final_state)))
        running = jax.tree.map(jnp.add, running, grad_weights)
        return (running, (sent, second_out, final_state, grad_rows, grad_probe))
    running, per_docs = lax.scan(per_doc, zero_grads, (rows_docs, valid_docs, state_docs, cot_docs))
    sent, second_out, final_state, grad_rows, grad_probe = per_docs
    acts = jnp.moveaxis(jnp.stack([sent, second_out]), 1, 3).astype(jnp.bfloat16)
    input_grads = jnp.moveaxis(jnp.stack([grad_rows, grad_probe]), 1, 3)
    final_out = jnp.moveaxis(final_state, 0, 1)
    return (acts, input_grads, final_out, running['norm_gain'], running['norm_shift'], running['w_qkv'], running['w_out'], running['rel_bias'], running['w_up'], running['up_bias'], running['w_down'], running['down_bias'], running['state_gain'], running['state_shift'], running['w_state_qkv'], running['w_state_out'], running['gate_bias'])
```

```python
from functools import partial
from types import SimpleNamespace

import jax
import jax.numpy as jnp
from jax import lax
from jax.experimental import pallas as pl
from jax.experimental.pallas import tpu as pltpu
from jax.sharding import PartitionSpec as P

MESH = pl.DeviceIdType.MESH
f32, bf16 = jnp.float32, jnp.bfloat16
eps = 1e-05
negative = -1000000000.0
VMEM_LIMIT = 60 * 1024 * 1024


def dot(left, right):
    return lax.dot_general(left, right, (((1,), (0,)), ((), ())), preferred_element_type=f32)


def dot_nt(left, right):
    return lax.dot_general(left, right, (((1,), (1,)), ((), ())), preferred_element_type=f32)


def dot_tn(left, right):
    return lax.dot_general(left, right, (((0,), (0,)), ((), ())), preferred_element_type=f32)


def norm_parts(values):
    average = jnp.mean(values, axis=-1, keepdims=True)
    centered = values - average
    spread = jnp.mean(centered * centered, axis=-1, keepdims=True)
    scale = lax.rsqrt(spread + eps)
    return centered * scale, scale


def layer_norm(values, gain, shift):
    return norm_parts(values)[0] * gain + shift


class Place:
    def __init__(self, rows):
        self.c, self.x = lax.axis_index("section"), lax.axis_index("mp")
        self.core = {"section": 1 - self.c}
        self.chip = {"mp": 1 - self.x}
        self.quarter, self.half = rows // 4, rows // 2

    def rows(self, x_other=False, c_other=False):
        x = 1 - self.x if x_other else self.x
        c = 1 - self.c if c_other else self.c
        return pl.ds(pl.multiple_of(x * self.half + c * self.quarter, self.quarter), self.quarter)

    def chip_rows(self, x_other=False):
        x = 1 - self.x if x_other else self.x
        return pl.ds(pl.multiple_of(x * self.half, self.half), self.half)

    def core_rows(self, c_other=False):
        c = 1 - self.c if c_other else self.c
        return pl.ds(pl.multiple_of(c * self.quarter, self.quarter), self.quarter)

    def meet(self):
        barrier = pltpu.get_barrier_semaphore()
        for other in (self.core, self.chip):
            pl.semaphore_signal(barrier, inc=1, device_id=other, device_id_type=MESH)
        pl.semaphore_wait(barrier, 2)


class Net:
    def __init__(self, send_sems, recv_sems):
        self.send_sems, self.recv_sems, self.copies = send_sems, recv_sems, []

    def copy(self, source, target, device):
        index = len(self.copies)
        made = pltpu.make_async_remote_copy(
            src_ref=source,
            dst_ref=target,
            send_sem=self.send_sems.at[index],
            recv_sem=self.recv_sems.at[index],
            device_id=device,
            device_id_type=MESH,
        )
        made.start()
        self.copies.append(made)
        return made

    def drain(self):
        for made in self.copies:
            made.wait_send()


class Local:
    def __init__(self, sems):
        self.sems, self.copies, self.waited = sems, [], set()

    def copy(self, source, target):
        made = pltpu.make_async_copy(source, target, self.sems.at[len(self.copies)])
        made.start()
        self.copies.append(made)
        return len(self.copies) - 1

    def wait(self, *indices):
        for index in indices:
            if index not in self.waited:
                self.waited.add(index)
                self.copies[index].wait()

    def drain(self):
        self.wait(*range(len(self.copies)))


class Gather:
    def __init__(self, place, net, buffer):
        self.place, self.net, self.buffer = place, net, buffer

    def start(self):
        own = self.buffer.at[self.place.rows()]
        self.from_chip = self.net.copy(own, own, self.place.chip)
        self.from_core = self.net.copy(own, own, self.place.core)

    def forward(self):
        self.from_chip.wait_recv()
        passed = self.buffer.at[self.place.rows(x_other=True)]
        self.passed = self.net.copy(passed, passed, self.place.core)

    def finish(self):
        self.from_core.wait_recv()
        self.passed.wait_recv()


class Scatter:
    def __init__(self, place, net, part, near, out, far):
        self.place, self.net, self.part = place, net, part
        self.near, self.out, self.far = near, out, far

    def send(self, x_other):
        slot = 0 if x_other else 1
        rows = self.place.rows(x_other=x_other, c_other=True)
        made = self.net.copy(self.part.at[rows], self.near.at[slot], self.place.core)
        if x_other:
            self.first = made
        else:
            self.second = made

    def middle(self):
        self.first.wait_recv()
        mine = self.part[self.place.rows(x_other=True), :].astype(f32)
        self.out[...] = (mine + self.near[0].astype(f32)).astype(bf16)
        self.across = self.net.copy(self.out, self.far, self.place.chip)

    def finish(self):
        self.second.wait_recv()
        total = self.part[self.place.rows(), :].astype(f32) + self.near[1].astype(f32)
        self.across.wait_recv()
        return total + self.far[...].astype(f32)


def share_kernel(place_rows, qkv, out, up, down, sqkv, sout, small, *rest):
    targets, staged, (local_sems, send_sems, recv_sems) = rest[:7], rest[7:14], rest[14:]
    place = Place(place_rows)
    net, local = Net(send_sems, recv_sems), Local(local_sems)
    layer = place.c

    def half(array, axis, c):
        width = array.shape[axis] // 2
        index = [slice(None)] * len(array.shape)
        index[axis] = pl.ds(pl.multiple_of(c * width, width), width)
        return array.at[tuple(index)]

    shared = ((qkv, 2), (out, 0), (up, 1), (down, 0))
    kept = [half(array, axis, place.c) for array, axis in shared + ((sqkv, 2), (sout, 0))] + [small]
    sent = [half(array, axis, 1 - place.c) for array, axis in shared] + [small]
    finals = [target.at[layer] for target in targets[:4]] + [targets[4], targets[5], targets[6].at[layer]]
    place.meet()
    for source, target in zip(sent, finals[:4] + finals[6:]):
        net.copy(source, target, place.core)
    inward = [local.copy(source, stage) for source, stage in zip(kept, staged)]
    for index, stage, target in zip(inward, staged, finals):
        local.wait(index)
        local.copy(stage, target)
    for made in net.copies:
        made.wait_recv()
    local.drain()
    net.drain()


def share_weights(block_len, qkv, out, up, down, sqkv, sout, small):
    def halved(shape, axis, stacked=True):
        shape = list(shape)
        shape[axis] //= 2
        return jax.ShapeDtypeStruct(([2] if stacked else []) + shape, bf16)

    anywhere = pl.BlockSpec(memory_space=pl.ANY)
    return pl.pallas_call(
        partial(share_kernel, block_len),
        out_shape=(
            halved(qkv.shape, 2),
            halved(out.shape, 0),
            halved(up.shape, 1),
            halved(down.shape, 0),
            halved(sqkv.shape, 2, False),
            halved(sout.shape, 0, False),
            jax.ShapeDtypeStruct((2,) + small.shape, f32),
        ),
        in_specs=[anywhere] * 7,
        out_specs=[anywhere] * 7,
        scratch_shapes=[
            pltpu.VMEM(halved(array.shape, axis, False).shape, bf16)
            for array, axis in ((qkv, 2), (out, 0), (up, 1), (down, 0), (sqkv, 2), (sout, 0))
        ]
        + [
            pltpu.VMEM(small.shape, f32),
            pltpu.SemaphoreType.DMA((14,)),
            pltpu.SemaphoreType.DMA((5,)),
            pltpu.SemaphoreType.DMA((5,)),
        ],
        compiler_params=pltpu.CompilerParams(
            collective_id=0, has_side_effects=True, vmem_limit_bytes=VMEM_LIMIT
        ),
        name="share_weights",
    )(qkv, out, up, down, sqkv, sout, small)


def fill_bias(bias, row0):
    head_count, length = row0.shape
    for head in range(head_count):
        start = jnp.broadcast_to(row0[head : head + 1, :], (bias.shape[1], length))
        rolled = pltpu.roll(start, 0, axis=1, stride=1, stride_axis=0)
        bias[head, :, :length] = rolled
        bias[head, :, length:] = rolled


def bias_columns(index, chunk, length):
    return pl.ds(pl.multiple_of(length - index * chunk, chunk), length)


def window_logits(query, key_cur, key_prev, bias, valid, block, first_row, scale):
    logits = dot_nt(query, key_cur)
    rows = first_row + lax.broadcasted_iota(jnp.int32, logits.shape, 0)
    here = lax.broadcasted_iota(jnp.int32, logits.shape, 1) <= rows
    usable = valid[block : block + 1, :] > 0.5
    if key_prev is None:
        keep = here & usable
    else:
        logits = jnp.where(here, logits, dot_nt(query, key_prev))
        keep = jnp.where(here, valid[block : block + 1, :], valid[block - 1 : block, :]) > 0.5
    return jnp.where(keep, logits * scale + bias, negative), here


def forward_kernel(layer, names, *refs):
    r = SimpleNamespace(**dict(zip(names, refs)))
    rec = layer == 1
    length = r.u_v.shape[1]
    heads = r.row0.shape[0]
    head_size = r.att_v.shape[2] // heads
    width = heads * head_size
    scale = head_size ** (-0.5)
    place = Place(length)
    net, local = Net(r.send_sems, r.recv_sems), Local(r.local_sems)
    chunk = min(128, length)

    place.meet()
    load = [local.copy(r.wqkv.at[layer], r.wqkv_v), local.copy(r.wout.at[layer], r.wout_v)]
    load_mlp = [local.copy(r.wup.at[layer], r.wup_v), local.copy(r.wdown.at[layer], r.wdown_v)]
    load_state = []
    if rec:
        load_state = [local.copy(r.wsqkv, r.wsqkv_v), local.copy(r.wsout, r.wsout_v)]

    gain = lambda index: r.gain[index : index + 1, :]
    shift = lambda index: r.shift[index : index + 1, :]

    def gather(buffer):
        return Gather(place, net, buffer)

    scatter_count = [0]

    def scatter():
        index = scatter_count[0]
        scatter_count[0] += 1
        return Scatter(
            place, net, r.part.at[index], r.near.at[index], r.out.at[index], r.far.at[index]
        )

    def norm_state(rows, index):
        r.sn_v[index, place.rows(), :] = layer_norm(rows, r.sgain[...], r.sshift[...]).astype(bf16)

    def norm_first(block):
        rows = r.x[block, place.core_rows(), :].astype(f32)
        r.u_v[block, place.rows(), :] = layer_norm(rows, gain(0), shift(0)).astype(bf16)

    def project(source, weights, target):
        for part in range(3):
            target[:, part * width : (part + 1) * width] = dot(source[...], weights[part]).astype(bf16)

    def reduce_from(values, weights, to):
        columns = weights.shape[1]
        step = min(512, columns)
        for x_other in (True, False):
            rows = place.chip_rows(x_other)

            @pl.loop(0, columns // step)
            def _(index):
                at = pl.ds(pl.multiple_of(index * step, step), step)
                to.part[rows, at] = dot(values[rows, :], weights[:, at]).astype(bf16)

            to.send(x_other)

    def attend(block):
        qkv = r.qkv_v.at[block]
        prev = r.qkv_v.at[block - 1] if block > 0 else None

        @pl.loop(0, length // chunk)
        def _(index):
            at = pl.ds(pl.multiple_of(index * chunk, chunk), chunk)
            lses = []
            for head in range(heads):
                q_at = slice(head * head_size, (head + 1) * head_size)
                k_at = slice(width + head * head_size, width + (head + 1) * head_size)
                v_at = slice(2 * width + head * head_size, 2 * width + (head + 1) * head_size)
                query = qkv[at, q_at]
                logits, here = window_logits(
                    query,
                    qkv[:, k_at],
                    None if prev is None else prev[:, k_at],
                    r.bias[head, :, bias_columns(index, chunk, length)],
                    r.valid,
                    block,
                    index * chunk,
                    scale,
                )
                peak = jnp.max(logits, axis=-1, keepdims=True)
                if rec:
                    state = r.sqkv_v.at[block]
                    state_logits = dot_nt(query, state[:, k_at]) * scale
                    peak = jnp.maximum(peak, jnp.max(state_logits, axis=-1, keepdims=True))
                probs = jnp.exp(logits - peak)
                total = jnp.sum(probs, axis=-1, keepdims=True)
                if prev is None:
                    result = dot(probs.astype(bf16), qkv[:, v_at])
                else:
                    result = dot(jnp.where(here, probs, 0.0).astype(bf16), qkv[:, v_at])
                    result += dot(jnp.where(here, 0.0, probs).astype(bf16), prev[:, v_at])
                if rec:
                    state_probs = jnp.exp(state_logits - peak)
                    total += jnp.sum(state_probs, axis=-1, keepdims=True)
                    result += dot(state_probs.astype(bf16), state[:, v_at])
                r.att_v[block, at, q_at] = (result / total).astype(bf16)
                lses.append(peak + jnp.log(total))
            lane = lax.broadcasted_iota(jnp.int32, (chunk, 128), 1)
            packed = jnp.zeros((chunk, 128), f32)
            for head in range(heads):
                packed = jnp.where(lane == head, lses[head], packed)
            r.lse_v[block, at, :] = packed

    def recur(block):
        qkv, state = r.qkv_v.at[block], r.sqkv_v.at[block]

        @pl.loop(0, length // chunk)
        def _(index):
            at = pl.ds(pl.multiple_of(index * chunk, chunk), chunk)
            lses = []
            for head in range(heads):
                q_at = slice(head * head_size, (head + 1) * head_size)
                k_at = slice(width + head * head_size, width + (head + 1) * head_size)
                v_at = slice(2 * width + head * head_size, 2 * width + (head + 1) * head_size)
                logits = dot_nt(state[at, q_at], qkv[:, k_at]) * scale
                logits = jnp.where(r.valid[block : block + 1, :] > 0.5, logits, negative)
                peak = jnp.max(logits, axis=-1, keepdims=True)
                probs = jnp.exp(logits - peak)
                total = jnp.sum(probs, axis=-1, keepdims=True)
                r.sout_v[block, at, q_at] = (dot(probs.astype(bf16), qkv[:, v_at]) / total).astype(bf16)
                lses.append(peak + jnp.log(total))
            if block == 0:
                lane = lax.broadcasted_iota(jnp.int32, (chunk, 128), 1)
                packed = jnp.zeros((chunk, 128), f32)
                for head in range(heads):
                    packed = jnp.where(lane == head, lses[head], packed)
                r.rlse_v[at, :] = packed

    def take_branch(block, from_out):
        rows = r.x[block, place.core_rows(), :].astype(f32) + from_out.finish()
        r.h_v[block] = rows
        r.wn_v[block, place.rows(), :] = layer_norm(rows, gain(1), shift(1)).astype(bf16)

    def feed_up(block):
        columns = r.wup_v.shape[1]
        step = 256

        @pl.loop(0, columns // step)
        def _(index):
            at = pl.ds(pl.multiple_of(index * step, step), step)
            pre = dot(r.wn_v[block], r.wup_v[:, at]) + r.up_bias[:, at]
            r.pre_v[block, :, at] = pre.astype(bf16)
            r.act[block, :, at] = (0.5 * pre * (1.0 + lax.erf(pre * (0.5**0.5)))).astype(bf16)

    def take_result(block, from_down):
        rows = r.h_v[block] + from_down.finish() + r.down_bias[...]
        own = r.acts_v.at[block, place.core_rows()]
        own[...] = rows.astype(bf16)
        return net.copy(own, own, place.core)

    branch = [scatter(), scatter()]
    result = [scatter(), scatter()]
    first = [gather(r.u_v.at[block]) for block in range(2)]
    second = [gather(r.wn_v.at[block]) for block in range(2)]
    if rec:
        update = [scatter(), scatter()]
        state = [gather(r.sn_v.at[block]) for block in range(2)]
        gate = r.gate[...]
        norm_state(r.state[place.core_rows(), :].astype(f32), 0)
        state[0].start()
    norm_first(0)
    first[0].start()
    norm_first(1)
    first[1].start()
    fill_bias(r.bias, r.row0)
    if rec:
        state[0].forward()
    first[0].forward()
    if rec:
        state[0].finish()
        local.wait(*load_state)
        project(r.sn_v.at[0], r.wsqkv_v, r.sqkv_v.at[0])
    first[0].finish()
    local.wait(*load)
    project(r.u_v.at[0], r.wqkv_v, r.qkv_v.at[0])
    if rec:
        recur(0)
        reduce_from(r.sout_v.at[0], r.wsout_v, update[0])
    first[1].forward()
    if rec:
        update[0].middle()
    attend(0)
    reduce_from(r.att_v.at[0], r.wout_v, branch[0])
    first[1].finish()
    project(r.u_v.at[1], r.wqkv_v, r.qkv_v.at[1])
    local.copy(r.u_v, r.u)
    local.copy(r.qkv_v, r.qkv)
    branch[0].middle()
    if rec:
        update_rows = update[0].finish()
        r.z_v[...] = update_rows
        state_rows = gate * r.state[place.core_rows(), :].astype(f32) + (1.0 - gate) * update_rows
        r.s1_v[...] = state_rows
        norm_state(state_rows, 1)
        state[1].start()
        local.copy(r.z_v, r.z)
        local.copy(r.s1_v, r.s1)
    else:
        attend(1)
        reduce_from(r.att_v.at[1], r.wout_v, branch[1])
    take_branch(0, branch[0])
    second[0].start()
    if rec:
        state[1].forward()
        state[1].finish()
        project(r.sn_v.at[1], r.wsqkv_v, r.sqkv_v.at[1])
        local.copy(r.sn_v, r.sn)
        local.copy(r.sqkv_v, r.sqkv)
        attend(1)
        reduce_from(r.att_v.at[1], r.wout_v, branch[1])
    local.copy(r.att_v, r.att)
    local.copy(r.lse_v, r.lse)
    second[0].forward()
    branch[1].middle()
    second[0].finish()
    local.wait(*load_mlp)
    feed_up(0)
    reduce_from(r.act.at[0], r.wdown_v, result[0])
    take_branch(1, branch[1])
    second[1].start()
    local.copy(r.h_v, r.h)
    result[0].middle()
    if rec:
        recur(1)
        reduce_from(r.sout_v.at[1], r.wsout_v, update[1])
        local.copy(r.sout_v, r.sout)
        local.copy(r.rlse_v, r.rlse)
    second[1].forward()
    second[1].finish()
    local.copy(r.wn_v, r.wn)
    feed_up(1)
    local.copy(r.pre_v, r.pre)
    reduce_from(r.act.at[1], r.wdown_v, result[1])
    sent = [take_result(0, result[0])]
    result[1].middle()
    if rec:
        update[1].middle()
    sent.append(take_result(1, result[1]))
    if rec:
        own = r.final_v.at[place.core_rows()]
        own[...] = gate * r.s1_v[...] + (1.0 - gate) * update[1].finish()
        sent.append(net.copy(own, own, place.core))
    for made in sent:
        made.wait_recv()
    local.copy(r.acts_v, r.acts)
    if rec:
        local.copy(r.final_v, r.final)
    local.drain()
    net.drain()


def forward_layer(layer, block_len, small, row0, valid, weights, rows, state):
    rec = layer == 1
    wqkv, wout, wup, wdown = weights[:4]
    model = rows.shape[2]
    width, hidden = wqkv.shape[3], wup.shape[2]
    quarter = block_len // 4
    heads = row0.shape[0]

    def held(shape, dtype):
        return jax.ShapeDtypeStruct(shape, dtype)

    outs = dict(
        u=held((2, block_len, model), bf16),
        qkv=held((2, block_len, 3 * width), bf16),
        lse=held((2, block_len, 128), f32),
        att=held((2, block_len, width), bf16),
        wn=held((2, block_len, model), bf16),
        pre=held((2, block_len, hidden), bf16),
        h=held((2, quarter, model), f32),
        acts=held((2, 2 * quarter, model), bf16),
    )
    ins = dict(
        x=rows,
        gain=small.gain[layer],
        shift=small.shift[layer],
        up_bias=small.up_bias[layer],
        down_bias=small.down_bias[layer],
        row0=row0,
        valid=valid,
    )
    far_ins = dict(wqkv=wqkv, wout=wout, wup=wup, wdown=wdown)
    if rec:
        outs.update(
            sn=held((2, block_len, model), bf16),
            sqkv=held((2, block_len, 3 * width), bf16),
            rlse=held((block_len, 128), f32),
            sout=held((2, block_len, width), bf16),
            s1=held((quarter, model), f32),
            z=held((quarter, model), f32),
            final=held((2 * quarter, model), f32),
        )
        ins.update(state=state, sgain=small.sgain, sshift=small.sshift, gate=small.gate)
        far_ins.update(wsqkv=weights[4], wsout=weights[5])
    scatters = 6 if rec else 4
    copies = (3 * 6 + 3 * 6 + 3) if rec else (3 * 4 + 3 * 4 + 2)
    scratch = {name + "_v": pltpu.VMEM(kind.shape, kind.dtype) for name, kind in outs.items()}
    scratch.update(
        wqkv_v=pltpu.VMEM(wqkv.shape[1:], bf16),
        wout_v=pltpu.VMEM(wout.shape[1:], bf16),
        wup_v=pltpu.VMEM(wup.shape[1:], bf16),
        wdown_v=pltpu.VMEM(wdown.shape[1:], bf16),
        act=pltpu.VMEM((2, block_len, hidden), bf16),
        bias=pltpu.VMEM((heads, min(128, block_len), 2 * block_len), f32),
        part=pltpu.VMEM((scatters, block_len, model), bf16),
        near=pltpu.VMEM((scatters, 2, quarter, model), bf16),
        out=pltpu.VMEM((scatters, quarter, model), bf16),
        far=pltpu.VMEM((scatters, quarter, model), bf16),
        send_sems=pltpu.SemaphoreType.DMA((copies,)),
        recv_sems=pltpu.SemaphoreType.DMA((copies,)),
        local_sems=pltpu.SemaphoreType.DMA((6 + len(outs),)),
    )
    if rec:
        scratch.update(
            wsqkv_v=pltpu.VMEM(weights[4].shape, bf16),
            wsout_v=pltpu.VMEM(weights[5].shape, bf16),
        )
    anywhere = pl.BlockSpec(memory_space=pl.ANY)
    inside = pl.BlockSpec(memory_space=pltpu.VMEM)
    results = pl.pallas_call(
        partial(forward_kernel, layer, [*ins, *far_ins, *outs, *scratch]),
        out_shape=tuple(outs.values()),
        in_specs=[inside] * len(ins) + [anywhere] * len(far_ins),
        out_specs=[anywhere] * len(outs),
        scratch_shapes=list(scratch.values()),
        compiler_params=pltpu.CompilerParams(
            collective_id=1 + layer, has_side_effects=True, vmem_limit_bytes=VMEM_LIMIT
        ),
        name="forward_recurrent" if rec else "forward_local",
    )(*ins.values(), *far_ins.values())
    return SimpleNamespace(**dict(zip(outs, results)))


def norm_back(rows, gain, grad):
    normed, scale = norm_parts(rows)
    inner = grad * gain
    means = jnp.mean(inner, axis=-1, keepdims=True), jnp.mean(inner * normed, axis=-1, keepdims=True)
    by_rows = scale * (inner - means[0] - normed * means[1])
    return by_rows, jnp.sum(grad * normed, axis=0, keepdims=True), jnp.sum(grad, axis=0, keepdims=True)


GAIN0, GAIN1, SHIFT0, SHIFT1, DOWN_BIAS, SGAIN, SSHIFT, GATE, UP_BIAS, BY_DISTANCE = range(10)
SMALL_ROWS = 16


def backward_kernel(layer, names, *refs):
    r = SimpleNamespace(**dict(zip(names, refs)))
    rec = layer == 1
    heads, length = r.row0.shape
    head_size = r.att_v.shape[1] // heads
    width = heads * head_size
    hidden = r.wup_v.shape[1]
    model = r.wup_v.shape[0]
    scale = head_size ** (-0.5)
    place = Place(length)
    net, local = Net(r.send_sems, r.recv_sems), Local(r.local_sems)
    chunk = min(128, length)

    place.meet()
    wdown = local.copy(r.wdown.at[layer], r.wdown_v)
    pre = local.copy(r.pre, r.pre_v)
    wup = local.copy(r.wup.at[layer], r.wup_v)
    hidden_rows = local.copy(r.h, r.h_v)
    wn = local.copy(r.wn, r.wn_v)
    attention = [
        local.copy(r.wout.at[layer], r.wout_v),
        local.copy(r.qkv, r.qkv_v),
        local.copy(r.att, r.att_v),
        local.copy(r.lse, r.lse_v),
    ]
    if rec:
        attention += [local.copy(r.sqkv, r.sqkv_v), local.copy(r.wsqkv, r.wsqkv_v)]
        chain = [
            local.copy(r.s1, r.s1_v),
            local.copy(r.z, r.z_v),
            local.copy(r.wsout, r.wsout_v),
            local.copy(r.sout, r.sout_v),
            local.copy(r.rlse, r.rlse_v),
        ]
    wqkv = local.copy(r.wqkv.at[layer], r.wqkv_v)

    gain = lambda index: r.gain[index : index + 1, :]
    small = r.small_v
    small[...] = jnp.zeros(small.shape, f32)
    r.dkv[...] = jnp.zeros(r.dkv.shape, f32)
    r.dbias[...] = jnp.zeros(r.dbias.shape, f32)
    if rec:
        r.dskv[...] = jnp.zeros(r.dskv.shape, f32)

    def add_small(index, value):
        small[index : index + 1, :] += value

    def gather(buffer):
        return Gather(place, net, buffer)

    scatter_count = [0]

    def scatter():
        index = scatter_count[0]
        scatter_count[0] += 1
        return Scatter(
            place, net, r.part.at[index], r.near.at[index], r.out.at[index], r.far.at[index]
        )

    def block_rows(block):
        return slice(block * length, (block + 1) * length)

    def own_grad(block):
        return r.gy[block, place.core_rows(), :].astype(bf16).astype(f32)

    def feed_back(block):
        step = 256
        rows = block_rows(block)

        @pl.loop(0, hidden // step)
        def _(index):
            at = pl.ds(pl.multiple_of(index * step, step), step)
            pre = r.pre_v[rows, at].astype(f32)
            by_act = dot_nt(r.g[rows, :], r.wdown_v[at, :])
            below = 0.5 * (1.0 + lax.erf(pre * (0.5**0.5)))
            r.act[rows, at] = (pre * below).astype(bf16)
            by_pre = by_act * (below + pre * jnp.exp(-0.5 * pre * pre) * 0.3989422804014327)
            small[UP_BIAS : UP_BIAS + 1, at] += jnp.sum(by_pre, axis=0, keepdims=True)
            r.dpre[rows, at] = by_pre.astype(bf16)

    def reduce_back(terms, to):
        step = min(512, model)
        for x_other in (True, False):
            rows = place.chip_rows(x_other)

            @pl.loop(0, model // step)
            def _(index):
                at = pl.ds(pl.multiple_of(index * step, step), step)
                total = None
                for values, weights in terms:
                    term = dot_nt(values[rows, :], weights[at, :])
                    total = term if total is None else total + term
                to.part[rows, at] = total.astype(bf16)

            to.send(x_other)

    def take_feed(block, from_feed):
        by_norm = from_feed.finish()
        grad = own_grad(block)
        by_rows, by_gain, by_shift = norm_back(r.h_v[block], gain(1), by_norm)
        add_small(GAIN1, by_gain)
        add_small(SHIFT1, by_shift)
        add_small(DOWN_BIAS, jnp.sum(grad, axis=0, keepdims=True))
        total = grad + by_rows
        r.dh[block] = total
        r.hg[pl.ds(place_row(block), place.quarter), :] = total.astype(bf16)

    def place_row(block):
        return pl.multiple_of(block * length + place.x * place.half + place.c * place.quarter, place.quarter)

    def weight_grad(left, right, target, at_row=0):
        step = 256

        @pl.loop(0, left.shape[1] // step)
        def _(index):
            at = pl.ds(pl.multiple_of(index * step, step), step)
            to = pl.ds(pl.multiple_of(at_row + index * step, step), step)
            target[to, :] = dot_tn(left[:, at], right[...]).astype(bf16)

    def projection_grad(normed, grads, target):
        for part in range(3):
            to = slice(part * width, (part + 1) * width)

            @pl.loop(0, model // width)
            def _(index):
                at = pl.ds(pl.multiple_of(index * width, width), width)
                target[to, at] = dot_tn(normed[:, at], grads[:, to]).astype(bf16)

    def branch_back(block):
        r.datt[block] = dot_nt(r.hg[block_rows(block), :], r.wout_v[...]).astype(bf16)

    def columns(head, part):
        return slice(part * width + head * head_size, part * width + (head + 1) * head_size)

    def attend_back(block):
        qkv = r.qkv_v.at[block]
        prev = r.qkv_v.at[block - 1] if block > 0 else None
        state = r.sqkv_v.at[block] if rec else None

        @pl.loop(0, length // chunk)
        def _(index):
            at = pl.ds(pl.multiple_of(index * chunk, chunk), chunk)
            block_at = pl.ds(pl.multiple_of(block * length + index * chunk, chunk), chunk)
            for head in range(heads):
                q_at, k_at, v_at = (columns(head, part) for part in range(3))
                query, key, value = qkv[at, q_at], qkv[:, k_at], qkv[:, v_at]
                logits, here = window_logits(
                    query,
                    key,
                    None if prev is None else prev[:, k_at],
                    r.bias[head, :, bias_columns(index, chunk, length)],
                    r.valid,
                    block,
                    index * chunk,
                    scale,
                )
                lse = r.lse_v[block, at, head : head + 1]
                probs = jnp.exp(logits - lse)
                grad = r.datt[block, at, q_at]
                delta = jnp.sum(
                    grad.astype(f32) * r.att_v[block_at, q_at].astype(f32), axis=-1, keepdims=True
                )
                by_probs = dot_nt(grad, value)
                if prev is not None:
                    by_probs = jnp.where(here, by_probs, dot_nt(grad, prev[:, v_at]))
                by_logits = probs * (by_probs - delta)
                r.dbias[head, :, bias_columns(index, chunk, length)] += by_logits
                by_logits = by_logits * scale
                if prev is None:
                    low = by_logits.astype(bf16)
                    low_probs = probs.astype(bf16)
                    by_query = dot(low, key)
                else:
                    low = jnp.where(here, by_logits, 0.0).astype(bf16)
                    low_probs = jnp.where(here, probs, 0.0).astype(bf16)
                    low_prev = jnp.where(here, 0.0, by_logits).astype(bf16)
                    low_probs_prev = jnp.where(here, 0.0, probs).astype(bf16)
                    by_query = dot(low, key) + dot(low_prev, prev[:, k_at])
                    r.dkv[block - 1, :, q_at] += dot_tn(low_prev, query)
                    r.dkv[block - 1, :, k_at] += dot_tn(low_probs_prev, grad)
                r.dkv[block, :, q_at] += dot_tn(low, query)
                r.dkv[block, :, k_at] += dot_tn(low_probs, grad)
                if rec:
                    state_probs = jnp.exp(dot_nt(query, state[:, k_at]) * scale - lse)
                    by_state = state_probs * (dot_nt(grad, state[:, v_at]) - delta) * scale
                    low_state = by_state.astype(bf16)
                    by_query += dot(low_state, state[:, k_at])
                    r.dskv[:, q_at] += dot_tn(low_state, query)
                    r.dskv[:, k_at] += dot_tn(state_probs.astype(bf16), grad)
                r.dqkv[block_at, q_at] = by_query.astype(bf16)

    def recur_back():
        qkv, state = r.qkv_v.at[0], r.sqkv_v.at[0]

        @pl.loop(0, length // chunk)
        def _(index):
            at = pl.ds(pl.multiple_of(index * chunk, chunk), chunk)
            for head in range(heads):
                q_at, k_at, v_at = (columns(head, part) for part in range(3))
                query, key, value = state[at, q_at], qkv[:, k_at], qkv[:, v_at]
                logits = dot_nt(query, key) * scale
                logits = jnp.where(r.valid[0:1, :] > 0.5, logits, negative)
                probs = jnp.exp(logits - r.rlse_v[at, head : head + 1])
                grad = r.dsout[at, q_at]
                delta = jnp.sum(
                    grad.astype(f32) * r.sout_v[0, at, q_at].astype(f32), axis=-1, keepdims=True
                )
                low = (probs * (dot_nt(grad, value) - delta) * scale).astype(bf16)
                r.dsqkv[at, q_at] = dot(low, key).astype(bf16)
                r.dkv[0, :, q_at] += dot_tn(low, query)
                r.dkv[0, :, k_at] += dot_tn(probs.astype(bf16), grad)

    def close_keys(block):
        r.dqkv[block_rows(block), width:] = r.dkv[block].astype(bf16)

    def close_state(block):
        r.dsqkv[block_rows(block), width:] = r.dskv[...].astype(bf16)
        if block == 1:
            r.dskv[...] = jnp.zeros(r.dskv.shape, f32)

    def input_back(block, to):
        rows = block_rows(block)
        reduce_back(
            [
                (r.dqkv.at[rows, part * width : (part + 1) * width], r.wqkv_v.at[part])
                for part in range(3)
            ],
            to,
        )

    def state_back(block, to):
        rows = block_rows(block)
        reduce_back(
            [
                (r.dsqkv.at[rows, part * width : (part + 1) * width], r.wsqkv_v.at[part])
                for part in ((0, 1, 2) if block == 0 else (1, 2))
            ],
            to,
        )

    def take_input(block, from_input):
        by_norm = from_input.finish()
        rows = r.x[block, place.core_rows(), :].astype(f32)
        by_rows, by_gain, by_shift = norm_back(rows, gain(0), by_norm)
        add_small(GAIN0, by_gain)
        add_small(SHIFT0, by_shift)
        own = r.ig_v.at[block, place.core_rows()]
        own[...] = r.dh[block] + by_rows
        return net.copy(own, own, place.core)

    def take_state(rows, from_state):
        by_rows, by_gain, by_shift = norm_back(rows, r.sgain[...], from_state.finish())
        add_small(SGAIN, by_gain)
        add_small(SSHIFT, by_shift)
        return by_rows

    def close_bias():
        tile = r.dbias.shape[1]
        for head in range(heads):
            folded = r.dbias[head, :, :length] + r.dbias[head, :, length:]
            row = lax.broadcasted_iota(jnp.int32, folded.shape, 0)
            bit = 1
            while bit < tile:
                moved = pltpu.roll(folded, length - bit, axis=1)
                folded = jnp.where((row & bit) != 0, moved, folded)
                bit *= 2
            small[BY_DISTANCE : BY_DISTANCE + 1, head * length : (head + 1) * length] = jnp.sum(
                folded, axis=0, keepdims=True
            )

    at_qkv, at_out, at_up = 0, 3 * width, 4 * width
    at_down = at_up + model
    at_sqkv = at_down + hidden
    at_sout = at_sqkv + 3 * width

    feed = [scatter(), scatter()]
    inputs = [scatter(), scatter()]
    grads = [gather(r.g.at[block_rows(block)]) for block in range(2)]
    hiddens = [gather(r.hg.at[block_rows(block)]) for block in range(2)]
    if rec:
        states = [scatter(), scatter()]
        updates = gather(r.ug)
    for block in (1, 0):
        r.g[pl.ds(place_row(block), place.quarter), :] = own_grad(block).astype(bf16)
        grads[block].start()
    fill_bias(r.bias, r.row0)
    grads[1].forward()
    local.wait(wdown, pre, wup)
    grads[1].finish()
    feed_back(1)
    reduce_back([(r.dpre.at[block_rows(1)], r.wup_v)], feed[1])
    grads[0].forward()
    grads[0].finish()
    feed_back(0)
    feed[1].middle()
    reduce_back([(r.dpre.at[block_rows(0)], r.wup_v)], feed[0])
    local.wait(hidden_rows)
    take_feed(1, feed[1])
    hiddens[1].start()
    feed[0].middle()
    weight_grad(r.act, r.g, r.pre_v)
    down_out = local.copy(r.pre_v, r.dw.at[at_down:at_sqkv])
    hiddens[1].forward()
    take_feed(0, feed[0])
    hiddens[0].start()
    hiddens[1].finish()
    local.wait(*attention)
    branch_back(1)
    attend_back(1)
    close_keys(1)
    if rec:
        close_state(1)
        state_back(1, states[1])
    hiddens[0].forward()
    local.wait(wqkv)
    input_back(1, inputs[1])
    if rec:
        states[1].middle()
    hiddens[0].finish()
    branch_back(0)
    inputs[1].middle()
    if rec:
        local.wait(*chain)
        gate = r.gate[...]
        by_state = take_state(r.s1_v[...], states[1])
        before = r.state[place.core_rows(), :].astype(f32)
        add_small(
            GATE,
            jnp.sum(by_state * (before - r.z_v[...]) * gate * (1.0 - gate), axis=0, keepdims=True),
        )
        r.ug[place.rows(), :] = ((1.0 - gate) * by_state).astype(bf16)
        updates.start()
    attend_back(0)
    if rec:
        updates.forward()
        updates.finish()
        r.dsout[...] = dot_nt(r.ug[...], r.wsout_v[...]).astype(bf16)
        recur_back()
    close_keys(0)
    input_back(0, inputs[0])
    if rec:
        close_state(0)
        state_back(0, states[0])
    sent = [take_input(1, inputs[1])]
    inputs[0].middle()
    if rec:
        states[0].middle()
    local.wait(wn)
    weight_grad(r.wn_v, r.dpre, r.act)
    up_out = local.copy(r.act, r.dw.at[at_up:at_down])
    u_in = local.copy(r.u, r.wn_v)
    weight_grad(r.att_v, r.hg, r.dpre, at_out)
    if rec:
        local.wait(down_out)
        sn_in = local.copy(r.sn, r.pre_v)
    close_bias()
    local.wait(u_in)
    projection_grad(r.wn_v, r.dqkv, r.dpre)
    local.copy(r.dpre, r.dw.at[at_qkv:at_up])
    if rec:
        local.wait(sn_in, up_out)
        r.dsqkv[block_rows(1), 0:width] = jnp.zeros((length, width), bf16)
        projection_grad(r.pre_v, r.dsqkv, r.act)
        weight_grad(r.sout_v.at[0], r.ug, r.act, at_sout - at_sqkv)
        local.copy(r.act, r.dw.at[at_sqkv:])
    sent.append(take_input(0, inputs[0]))
    if rec:
        take_state(r.state[place.core_rows(), :].astype(f32), states[0])
    local.copy(small, r.small)
    for made in sent:
        made.wait_recv()
    local.copy(r.ig_v, r.ig)
    local.drain()
    net.drain()


def backward_layer(layer, block_len, small, row0, valid, weights, grad_rows, rows, state, kept):
    rec = layer == 1
    wqkv, wout, wup, wdown = weights[:4]
    model = rows.shape[2]
    width, hidden = wqkv.shape[3], wup.shape[2]
    quarter = block_len // 4
    heads = row0.shape[0]

    def held(shape, dtype):
        return jax.ShapeDtypeStruct(shape, dtype)

    dw_rows = 4 * width + model + hidden + (4 * width if rec else 0)
    outs = dict(
        dw=held((dw_rows, model), bf16),
        small=held((SMALL_ROWS, model), f32),
        ig=held((2, 2 * quarter, model), f32),
    )
    ins = dict(
        gy=grad_rows, x=rows, gain=small.gain[layer], shift=small.shift[layer], row0=row0, valid=valid
    )

    def flat(array):
        return array.reshape((-1,) + array.shape[2:])

    stacked = dict(wqkv=wqkv, wout=wout, wup=wup, wdown=wdown)
    copied = dict(
        qkv=kept.qkv, lse=kept.lse, att=flat(kept.att), wn=flat(kept.wn), pre=flat(kept.pre), h=kept.h
    )
    late = dict(u=flat(kept.u))
    if rec:
        ins.update(state=state, sgain=small.sgain, sshift=small.sshift, gate=small.gate)
        copied.update(wsqkv=weights[4], wsout=weights[5])
        copied.update(sqkv=kept.sqkv, rlse=kept.rlse, sout=kept.sout, s1=kept.s1, z=kept.z)
        late.update(sn=flat(kept.sn))
    far_ins = {**stacked, **copied, **late}
    scatters = 6 if rec else 4
    copies = (3 * 6 + 3 * 5 + 2) if rec else (3 * 4 + 3 * 4 + 2)
    scratch = dict(small_v=pltpu.VMEM(outs["small"].shape, f32), ig_v=pltpu.VMEM(outs["ig"].shape, f32))
    for name, array in stacked.items():
        scratch[name + "_v"] = pltpu.VMEM(array.shape[1:], array.dtype)
    for name, array in copied.items():
        scratch[name + "_v"] = pltpu.VMEM(array.shape, array.dtype)
    scratch.update(
        g=pltpu.VMEM((2 * block_len, model), bf16),
        hg=pltpu.VMEM((2 * block_len, model), bf16),
        act=pltpu.VMEM((2 * block_len, hidden), bf16),
        dpre=pltpu.VMEM((2 * block_len, hidden), bf16),
        dh=pltpu.VMEM((2, quarter, model), f32),
        datt=pltpu.VMEM((2, block_len, width), bf16),
        dkv=pltpu.VMEM((2, block_len, 2 * width), f32),
        dqkv=pltpu.VMEM((2 * block_len, 3 * width), bf16),
        dbias=pltpu.VMEM((heads, min(128, block_len), 2 * block_len), f32),
        bias=pltpu.VMEM((heads, min(128, block_len), 2 * block_len), f32),
        part=pltpu.VMEM((scatters, block_len, model), bf16),
        near=pltpu.VMEM((scatters, 2, quarter, model), bf16),
        out=pltpu.VMEM((scatters, quarter, model), bf16),
        far=pltpu.VMEM((scatters, quarter, model), bf16),
        send_sems=pltpu.SemaphoreType.DMA((copies,)),
        recv_sems=pltpu.SemaphoreType.DMA((copies,)),
        local_sems=pltpu.SemaphoreType.DMA((len(far_ins) + 6,)),
    )
    if rec:
        scratch.update(
            ug=pltpu.VMEM((block_len, model), bf16),
            dsout=pltpu.VMEM((block_len, width), bf16),
            dskv=pltpu.VMEM((block_len, 2 * width), f32),
            dsqkv=pltpu.VMEM((2 * block_len, 3 * width), bf16),
        )
    anywhere = pl.BlockSpec(memory_space=pl.ANY)
    inside = pl.BlockSpec(memory_space=pltpu.VMEM)
    results = pl.pallas_call(
        partial(backward_kernel, layer, [*ins, *far_ins, *outs, *scratch]),
        out_shape=tuple(outs.values()),
        in_specs=[inside] * len(ins) + [anywhere] * len(far_ins),
        out_specs=[anywhere] * len(outs),
        scratch_shapes=list(scratch.values()),
        compiler_params=pltpu.CompilerParams(
            collective_id=3 + layer, has_side_effects=True, vmem_limit_bytes=VMEM_LIMIT
        ),
        name="backward_recurrent" if rec else "backward_local",
    )(*ins.values(), *far_ins.values())
    return SimpleNamespace(**dict(zip(outs, results)))


def ring_place(n, c, d):
    if n % 2:
        at = d

        def index_at(p):
            return p

    else:
        a, b = d // 2, d % 2
        at = a + b * (n - 1 - 2 * a)

        def index_at(p):
            b = p // (n // 2)
            return 2 * (p + b * (n - 1 - 2 * p)) + b

    def flip(p):
        return p + c * (n - 1 - 2 * p)

    return flip(at), lambda p: index_at(flip(p))


def sum_kernel(
    n, subs, parts_1, parts_0, small, full, small_out, mine, held, small_held, small_sum, small_far,
    rs_send, rs_recv, ag_send, ag_recv, core_send, core_recv, small_send, small_recv, local_sems,
):
    c, x, d = lax.axis_index("section"), lax.axis_index("mp"), lax.axis_index("dp")
    q, index_at = ring_place(n, c, d)
    after, before = {"dp": index_at((q + 1) % n)}, {"dp": index_at((q + n - 1) % n)}
    core, chip = {"section": 1 - c}, {"mp": 1 - x}
    chunk = mine.shape[0] // n
    sub = chunk // subs

    def rows(owner, k):
        return pl.ds(pl.multiple_of(owner * chunk + k * sub, sub), sub)

    def piece(k):
        return slice(k * sub, (k + 1) * sub)

    def remote(source, target, send, recv, to):
        return pltpu.make_async_remote_copy(
            src_ref=source, dst_ref=target, send_sem=send, recv_sem=recv, device_id=to, device_id_type=MESH
        )

    def reduce_first(k):
        return remote(mine.at[rows(q, k)], held.at[0, piece(k)], rs_send.at[0, k], rs_recv.at[0, k], after)

    def reduce_next(s, k):
        return remote(held.at[s - 1, piece(k)], held.at[s, piece(k)], rs_send.at[s, k], rs_recv.at[s, k], after)

    def gathered(s, k):
        return full.at[c, rows((q + 1 - s + n) % n, k)]

    def gather(s, k, source=None):
        target = gathered(s, k)
        source = target if source is None else source
        return remote(source, target, ag_send.at[s, k], ag_recv.at[s, k], after)

    def to_core(s, k, source=None):
        target = gathered(s, k)
        source = target if source is None else source
        return remote(source, target, core_send.at[s, k], core_recv.at[s, k], core)

    def from_core(s, k):
        target = full.at[1 - c, rows((n - q - s + n) % n, k)]
        return remote(target, target, core_send.at[s, k], core_recv.at[s, k], core)

    def small_step(s, first):
        source = small if first else small_held.at[s - 1]
        return remote(source, small_held.at[s], small_send.at[s], small_recv.at[s], after)

    barrier = pltpu.get_barrier_semaphore()
    for other in (after, before, core, chip):
        pl.semaphore_signal(barrier, inc=1, device_id=other, device_id_type=MESH)
    size_1 = parts_1.shape[0]
    loads = [
        pltpu.make_async_copy(parts_1, mine.at[:size_1], local_sems.at[0]),
        pltpu.make_async_copy(parts_0, mine.at[size_1:], local_sems.at[1]),
    ]
    for made in loads:
        made.start()
    pl.semaphore_wait(barrier, 4)
    small_step(0, True).start()
    for made in loads:
        made.wait()
    for k in range(subs):
        reduce_first(k).start()

    def add_own(s, k):
        held[s, piece(k), :] = (
            held[s, piece(k), :].astype(f32) + mine[rows((q + n - 1 - s) % n, k), :].astype(f32)
        ).astype(bf16)

    @pl.loop(0, n - 2)
    def _(s):
        for k in range(subs):
            remote(held.at[s, piece(k)], held.at[s, piece(k)], rs_send.at[s, k], rs_recv.at[s, k], after).wait_recv()
            add_own(s, k)
            reduce_next(s + 1, k).start()
        small_step(s, True).wait_recv()
        small_step(s + 1, False).start()

    last = n - 2
    finals = []
    for k in range(subs):
        summed = held.at[last, piece(k)]
        remote(summed, summed, rs_send.at[last, k], rs_recv.at[last, k], after).wait_recv()
        add_own(last, k)
        gather(0, k, summed).start()
        to_core(0, k, summed).start()
        made = pltpu.make_async_copy(summed, gathered(0, k), local_sems.at[k])
        made.start()
        finals.append(made)

    small_step(last, True).wait_recv()
    small_out[0] = small[...]

    @pl.loop(0, n - 1)
    def _(s):
        small_out[0] += small_held[s]

    between = remote(small_out.at[0], small_out.at[1], small_send.at[n - 1], small_recv.at[n - 1], core)
    between.start()
    between.wait_recv()
    small_sum[...] = small_out[0] + small_out[1]
    across = remote(small_sum, small_far, small_send.at[n], small_recv.at[n], chip)
    across.start()
    across.wait_recv()
    small_out[2] = small_sum[...] + small_far[...]

    @pl.loop(0, n - 2)
    def _(s):
        for k in range(subs):
            gather(s, k, gathered(s + 1, k)).wait_recv()
            gather(s + 1, k).start()
            to_core(s + 1, k).start()

    for k in range(subs):
        gather(last, k, gathered(last + 1, k)).wait_recv()
        to_core(last + 1, k).start()

    @pl.loop(0, n)
    def _(s):
        for k in range(subs):
            from_core(s, k).wait_recv()
            to_core(s, k).wait_send()

    @pl.loop(0, n - 1)
    def _(s):
        for k in range(subs):
            remote(held.at[s, piece(k)], held.at[s, piece(k)], rs_send.at[s, k], rs_recv.at[s, k], after).wait_send()
            gather(s, k).wait_send()
        small_step(s, True).wait_send()

    between.wait_send()
    across.wait_send()
    for made in finals:
        made.wait()


def sum_gradients(n, parts_1, parts_0, small):
    total, model = parts_1.shape[0] + parts_0.shape[0], parts_1.shape[1]
    chunk = total // n
    subs = max(k for k in range(1, 9) if chunk % (16 * k) == 0)
    anywhere = pl.BlockSpec(memory_space=pl.ANY)
    inside = pl.BlockSpec(memory_space=pltpu.VMEM)
    sems = pltpu.SemaphoreType.DMA
    return pl.pallas_call(
        partial(sum_kernel, n, subs),
        out_shape=(
            jax.ShapeDtypeStruct((2, total, model), bf16),
            jax.ShapeDtypeStruct((3,) + small.shape, f32),
        ),
        in_specs=[anywhere, anywhere, inside],
        out_specs=[anywhere, inside],
        scratch_shapes=[
            pltpu.VMEM((total, model), bf16),
            pltpu.VMEM((n - 1, chunk, model), bf16),
            pltpu.VMEM((n - 1,) + small.shape, f32),
            pltpu.VMEM(small.shape, f32),
            pltpu.VMEM(small.shape, f32),
            sems((n - 1, subs)),
            sems((n - 1, subs)),
            sems((n - 1, subs)),
            sems((n - 1, subs)),
            sems((n, subs)),
            sems((n, subs)),
            sems((n + 1,)),
            sems((n + 1,)),
            sems((max(2, subs),)),
        ],
        compiler_params=pltpu.CompilerParams(
            collective_id=5, has_side_effects=True, vmem_limit_bytes=VMEM_LIMIT
        ),
        name="sum_gradients",
    )(parts_1, parts_0, small)


def place_kernel(width, hidden, size_1, full, qkv, out, up, down, sqkv, sout, inward, outward, in_sems, out_sems):
    model = full.shape[2]
    base = (1 - lax.axis_index("section")) * size_1
    slots = inward.shape[0]
    at_out, at_up = 3 * width, 4 * width
    at_down = at_up + model
    at_sqkv = at_down + hidden
    at_sout = at_sqkv + 3 * width
    jobs = []
    for half in range(2):
        columns = slice(half * width, (half + 1) * width)

        def projection(target, row):
            return [target.at[index : index + width, columns] for index in range(0, model, width)]

        for part in range(3):
            jobs.append((half, base + part * width, projection(qkv.at[0, part], part)))
            jobs.append((half, at_sqkv + part * width, projection(sqkv.at[part], part)))
        jobs.append((half, base + at_out, [out.at[0, columns]]))
        jobs.append((half, at_sout, [sout.at[columns]]))
        for row in range(0, model, width):
            wide = slice(half * hidden, (half + 1) * hidden)
            jobs.append((half, base + at_up + row, [up.at[0, row : row + width, wide]]))
        for row in range(0, hidden, width):
            at = half * hidden + row
            jobs.append((half, base + at_down + row, [down.at[0, at : at + width]]))

    def load(index):
        half, row, _ = jobs[index]
        at = row if isinstance(row, int) else pl.multiple_of(row, width)
        slot = index % slots
        return pltpu.make_async_copy(full.at[half, pl.ds(at, width)], inward.at[slot], in_sems.at[slot])

    def stores(index):
        targets, slot = jobs[index][2], index % slots
        step = model // len(targets)
        return [
            pltpu.make_async_copy(
                outward.at[slot, :, k * step : (k + 1) * step], target, out_sems.at[slot, k]
            )
            for k, target in enumerate(targets)
        ]

    for index in range(slots):
        load(index).start()
    for index in range(len(jobs)):
        slot = index % slots
        load(index).wait()
        if index >= slots:
            for made in stores(index - slots):
                made.wait()
        outward[slot] = inward[slot].astype(f32)
        for made in stores(index):
            made.start()
        if index + slots < len(jobs):
            load(index + slots).start()
    for index in range(len(jobs) - slots, len(jobs)):
        for made in stores(index):
            made.wait()


def place_gradients(full, width, hidden, size_1):
    model = full.shape[2]
    anywhere = pl.BlockSpec(memory_space=pl.ANY)
    slots = 4
    shapes = (
        (1, 3, model, 2 * width),
        (1, 2 * width, model),
        (1, model, 2 * hidden),
        (1, 2 * hidden, model),
        (3, model, 2 * width),
        (2 * width, model),
    )
    return pl.pallas_call(
        partial(place_kernel, width, hidden, size_1),
        out_shape=[jax.ShapeDtypeStruct(shape, f32) for shape in shapes],
        in_specs=[anywhere],
        out_specs=[anywhere] * 6,
        scratch_shapes=[
            pltpu.VMEM((slots, width, model), bf16),
            pltpu.VMEM((slots, width, model), f32),
            pltpu.SemaphoreType.DMA((slots,)),
            pltpu.SemaphoreType.DMA((slots, model // width)),
        ],
        compiler_params=pltpu.CompilerParams(vmem_limit_bytes=VMEM_LIMIT),
        name="place_gradients",
    )(full)


def pack_small(arrays, width):
    flat = jnp.concatenate([array.astype(f32).reshape(-1) for array in arrays])
    return jnp.pad(flat, (0, -flat.size % (8 * width))).reshape(-1, width)


def unpack_small(packed, shapes):
    flat = packed.reshape(packed.shape[0], -1)
    found, at = [], 0
    for shape in shapes:
        size = 1
        for extent in shape:
            size *= extent
        found.append(flat[:, at : at + size].reshape((packed.shape[0],) + tuple(shape)))
        at += size
    return found


def local_part(
    tokens, valid_mask, buckets, state_init, norm_gain, norm_shift, w_qkv, w_out, rel_bias, w_up, up_bias,
    w_down, down_bias, state_gain, state_shift, w_state_qkv, w_state_out, gate_bias, cotangent,
):
    block_len = valid_mask.shape[1]
    model = tokens.shape[3]
    core = lax.axis_index("section")
    bucket_count, chip_heads = rel_bias.shape[1:]
    heads = chip_heads // 2
    hidden = w_up.shape[2] // 2
    valid = valid_mask[:, :, 0].astype(f32)
    packed = pack_small([norm_gain[0], norm_shift[0], down_bias[0], up_bias[0], rel_bias[0]], model)
    *weights, small_all = share_weights(
        block_len, w_qkv[0], w_out[0], w_up[0], w_down[0], w_state_qkv, w_state_out, packed
    )
    gains, shifts, down_biases, up_biases, rels = unpack_small(
        small_all, [(2, model), (2, model), (1, model), (1, 2 * hidden), (bucket_count, chip_heads)]
    )
    small = SimpleNamespace(
        gain=gains,
        shift=shifts,
        down_bias=down_biases,
        up_bias=lax.dynamic_slice_in_dim(up_biases, core * hidden, hidden, 2),
        sgain=state_gain[None],
        sshift=state_shift[None],
        gate=jax.nn.sigmoid(gate_bias)[None],
    )
    rels = lax.dynamic_slice_in_dim(rels, core * heads, heads, 2)
    back = jnp.concatenate([buckets[:1], buckets[:0:-1]])
    back_hot = back[:, None] == jnp.arange(bucket_count)[None, :]
    row0 = jnp.sum(jnp.where(back_hot[None, None], jnp.swapaxes(rels, 1, 2)[:, :, None, :], 0.0), axis=-1)
    rows = tokens[:, :, 0, :]
    state = state_init[:, 0, :]
    kept0 = forward_layer(0, block_len, small, row0[0], valid, weights, rows, state)
    kept1 = forward_layer(1, block_len, small, row0[1], valid, weights, kept0.acts, state)
    acts = jnp.where(core == 0, kept0.acts, kept1.acts)[None, :, :, None, :]
    final_state = kept1.final[:, None, :]
    grad1 = backward_layer(
        1, block_len, small, row0[1], valid, weights, cotangent[:, :, 0, :], kept0.acts, state, kept1
    )
    grad0 = backward_layer(0, block_len, small, row0[0], valid, weights, grad1.ig, rows, state, kept0)
    input_grads = jnp.where(core == 0, grad0.ig, grad1.ig)[None, :, :, None, :]
    full, sums = sum_gradients(
        lax.axis_size("dp"), grad1.dw, grad0.dw, jnp.concatenate([grad0.small, grad1.small])
    )
    width = heads * (w_qkv.shape[3] // chip_heads)
    sums = sums.reshape(3, 2, SMALL_ROWS, model)
    everywhere = sums[2]
    own = lax.dynamic_index_in_dim(everywhere, core, 0, keepdims=False)
    by_core = jnp.where(core == 0, sums[:2], sums[1::-1])
    by_core = lax.dynamic_index_in_dim(by_core, core, 1, keepdims=False)
    qkv_grad, out_grad, up_grad, down_grad, state_qkv_grad, state_out_grad = place_gradients(
        full, width, hidden, grad1.dw.shape[0]
    )
    by_distance = by_core[:, BY_DISTANCE, : heads * block_len].reshape(chip_heads, block_len)
    by_bucket = jnp.sum(jnp.where(back_hot[:, :, None], by_distance.T[:, None, :], 0.0), axis=0)
    return (
        acts,
        input_grads,
        final_state,
        own[GAIN0 : GAIN1 + 1][None],
        own[SHIFT0 : SHIFT1 + 1][None],
        qkv_grad,
        out_grad,
        by_bucket[None],
        up_grad,
        by_core[:, UP_BIAS, :hidden].reshape(1, 2 * hidden),
        down_grad,
        own[DOWN_BIAS][None],
        everywhere[1, SGAIN],
        everywhere[1, SSHIFT],
        state_qkv_grad,
        state_out_grad,
        everywhere[1, GATE],
    )


def solution(mesh):
    in_specs = (
        P(None, "mp", "dp", None),
        P(None, None, "dp"),
        P(),
        P("mp", "dp", None),
        P("section", None, None),
        P("section", None, None),
        P("section", None, None, "mp"),
        P("section", "mp", None),
        P("section", None, "mp"),
        P("section", None, "mp"),
        P("section", "mp"),
        P("section", "mp", None),
        P("section", None),
        P(),
        P(),
        P(None, None, "mp"),
        P("mp", None),
        P(),
        P(None, "mp", "dp", None),
    )
    out_specs = (
        P("section", None, "mp", "dp", None),
        P("section", None, "mp", "dp", None),
        P("mp", "dp", None),
        P("section", None, None),
        P("section", None, None),
        P("section", None, None, "mp"),
        P("section", "mp", None),
        P("section", None, "mp"),
        P("section", None, "mp"),
        P("section", "mp"),
        P("section", "mp", None),
        P("section", None),
        P(),
        P(),
        P(None, None, "mp"),
        P("mp", None),
        P(),
    )
    return jax.shard_map(local_part, mesh=mesh, in_specs=in_specs, out_specs=out_specs, check_vma=False)
```

```python
from functools import partial
from types import SimpleNamespace

import jax
import jax.numpy as jnp
from jax import lax
from jax.experimental import pallas as pl
from jax.experimental.pallas import tpu as pltpu
from jax.sharding import PartitionSpec as P

MESH = pl.DeviceIdType.MESH
f32, bf16 = jnp.float32, jnp.bfloat16
eps = 1e-05
negative = -1000000000.0
VMEM_LIMIT = 60 * 1024 * 1024


def dot(left, right):
    return lax.dot_general(left, right, (((1,), (0,)), ((), ())), preferred_element_type=f32)


def dot_nt(left, right):
    return lax.dot_general(left, right, (((1,), (1,)), ((), ())), preferred_element_type=f32)


def dot_tn(left, right):
    return lax.dot_general(left, right, (((0,), (0,)), ((), ())), preferred_element_type=f32)


def norm_parts(values):
    average = jnp.mean(values, axis=-1, keepdims=True)
    centered = values - average
    spread = jnp.mean(centered * centered, axis=-1, keepdims=True)
    scale = lax.rsqrt(spread + eps)
    return centered * scale, scale


def layer_norm(values, gain, shift):
    return norm_parts(values)[0] * gain + shift


class Place:
    def __init__(self, rows):
        self.c, self.x = lax.axis_index("section"), lax.axis_index("mp")
        self.core = {"section": 1 - self.c}
        self.chip = {"mp": 1 - self.x}
        self.quarter, self.half = rows // 4, rows // 2

    def rows(self, x_other=False, c_other=False):
        x = 1 - self.x if x_other else self.x
        c = 1 - self.c if c_other else self.c
        return pl.ds(pl.multiple_of(x * self.half + c * self.quarter, self.quarter), self.quarter)

    def chip_rows(self, x_other=False):
        x = 1 - self.x if x_other else self.x
        return pl.ds(pl.multiple_of(x * self.half, self.half), self.half)

    def core_rows(self, c_other=False):
        c = 1 - self.c if c_other else self.c
        return pl.ds(pl.multiple_of(c * self.quarter, self.quarter), self.quarter)

    def meet(self):
        barrier = pltpu.get_barrier_semaphore()
        for other in (self.core, self.chip):
            pl.semaphore_signal(barrier, inc=1, device_id=other, device_id_type=MESH)
        pl.semaphore_wait(barrier, 2)


class Net:
    def __init__(self, send_sems, recv_sems):
        self.send_sems, self.recv_sems, self.copies = send_sems, recv_sems, []

    def copy(self, source, target, device):
        index = len(self.copies)
        made = pltpu.make_async_remote_copy(
            src_ref=source,
            dst_ref=target,
            send_sem=self.send_sems.at[index],
            recv_sem=self.recv_sems.at[index],
            device_id=device,
            device_id_type=MESH,
        )
        made.start()
        self.copies.append(made)
        return made

    def sent(self, *copies):
        for made in copies:
            made.wait_send()
        self.copies = [None if any(held is made for made in copies) else held for held in self.copies]

    def drain(self):
        for made in self.copies:
            if made is not None:
                made.wait_send()


class Local:
    def __init__(self, sems):
        self.sems, self.copies, self.waited = sems, [], set()

    def copy(self, source, target):
        made = pltpu.make_async_copy(source, target, self.sems.at[len(self.copies)])
        made.start()
        self.copies.append(made)
        return len(self.copies) - 1

    def wait(self, *indices):
        for index in indices:
            if index not in self.waited:
                self.waited.add(index)
                self.copies[index].wait()

    def drain(self):
        self.wait(*range(len(self.copies)))


class Gather:
    def __init__(self, place, net, buffer):
        self.place, self.net, self.buffer = place, net, buffer

    def start(self):
        own = self.buffer.at[self.place.rows()]
        self.from_chip = self.net.copy(own, own, self.place.chip)
        self.from_core = self.net.copy(own, own, self.place.core)

    def forward(self):
        self.from_chip.wait_recv()
        passed = self.buffer.at[self.place.rows(x_other=True)]
        self.passed = self.net.copy(passed, passed, self.place.core)

    def finish(self):
        self.from_core.wait_recv()
        self.passed.wait_recv()


class Scatter:
    def __init__(self, place, net, part, near, out, far):
        self.place, self.net, self.part = place, net, part
        self.near, self.out, self.far = near, out, far

    def send(self, x_other):
        slot = 0 if x_other else 1
        rows = self.place.rows(x_other=x_other, c_other=True)
        made = self.net.copy(self.part.at[rows], self.near.at[slot], self.place.core)
        if x_other:
            self.first = made
        else:
            self.second = made

    def middle(self):
        self.first.wait_recv()
        mine = self.part[self.place.rows(x_other=True), :].astype(f32)
        self.out[...] = (mine + self.near[0].astype(f32)).astype(bf16)
        self.across = self.net.copy(self.out, self.far, self.place.chip)

    def finish(self):
        self.second.wait_recv()
        total = self.part[self.place.rows(), :].astype(f32) + self.near[1].astype(f32)
        self.across.wait_recv()
        return total + self.far[...].astype(f32)

    def release(self):
        self.net.sent(self.first, self.second, self.across)


def share_kernel(place_rows, qkv, out, up, down, sqkv, sout, small, *rest):
    targets, staged, (local_sems, send_sems, recv_sems) = rest[:7], rest[7:14], rest[14:]
    place = Place(place_rows)
    net, local = Net(send_sems, recv_sems), Local(local_sems)
    layer = place.c

    def half(array, axis, c):
        width = array.shape[axis] // 2
        index = [slice(None)] * len(array.shape)
        index[axis] = pl.ds(pl.multiple_of(c * width, width), width)
        return array.at[tuple(index)]

    shared = ((qkv, 2), (out, 0), (up, 1), (down, 0))
    kept = [half(array, axis, place.c) for array, axis in shared + ((sqkv, 2), (sout, 0))] + [small]
    sent = [half(array, axis, 1 - place.c) for array, axis in shared] + [small]
    finals = [target.at[layer] for target in targets[:4]] + [targets[4], targets[5], targets[6].at[layer]]
    place.meet()
    for source, target in zip(sent, finals[:4] + finals[6:]):
        net.copy(source, target, place.core)
    inward = [local.copy(source, stage) for source, stage in zip(kept, staged)]
    for index, stage, target in zip(inward, staged, finals):
        local.wait(index)
        local.copy(stage, target)
    for made in net.copies:
        made.wait_recv()
    local.drain()
    net.drain()


def share_weights(block_len, qkv, out, up, down, sqkv, sout, small):
    def halved(shape, axis, stacked=True):
        shape = list(shape)
        shape[axis] //= 2
        return jax.ShapeDtypeStruct(([2] if stacked else []) + shape, bf16)

    anywhere = pl.BlockSpec(memory_space=pl.ANY)
    return pl.pallas_call(
        partial(share_kernel, block_len),
        out_shape=(
            halved(qkv.shape, 2),
            halved(out.shape, 0),
            halved(up.shape, 1),
            halved(down.shape, 0),
            halved(sqkv.shape, 2, False),
            halved(sout.shape, 0, False),
            jax.ShapeDtypeStruct((2,) + small.shape, f32),
        ),
        in_specs=[anywhere] * 7,
        out_specs=[anywhere] * 7,
        scratch_shapes=[
            pltpu.VMEM(halved(array.shape, axis, False).shape, bf16)
            for array, axis in ((qkv, 2), (out, 0), (up, 1), (down, 0), (sqkv, 2), (sout, 0))
        ]
        + [
            pltpu.VMEM(small.shape, f32),
            pltpu.SemaphoreType.DMA((14,)),
            pltpu.SemaphoreType.DMA((5,)),
            pltpu.SemaphoreType.DMA((5,)),
        ],
        compiler_params=pltpu.CompilerParams(
            collective_id=0, has_side_effects=True, vmem_limit_bytes=VMEM_LIMIT
        ),
        name="share_weights",
    )(qkv, out, up, down, sqkv, sout, small)


def fill_bias(bias, row0):
    head_count, length = row0.shape
    for head in range(head_count):
        start = jnp.broadcast_to(row0[head : head + 1, :], (bias.shape[1], length))
        rolled = pltpu.roll(start, 0, axis=1, stride=1, stride_axis=0)
        bias[head, :, :length] = rolled
        bias[head, :, length:] = rolled


def bias_columns(index, chunk, length):
    return pl.ds(pl.multiple_of(length - index * chunk, chunk), length)


def window_logits(query, key_cur, key_prev, bias, valid, block, first_row, scale):
    logits = dot_nt(query, key_cur)
    rows = first_row + lax.broadcasted_iota(jnp.int32, logits.shape, 0)
    here = lax.broadcasted_iota(jnp.int32, logits.shape, 1) <= rows
    usable = valid[block : block + 1, :] > 0.5
    if key_prev is None:
        keep = here & usable
    else:
        logits = jnp.where(here, logits, dot_nt(query, key_prev))
        keep = jnp.where(here, valid[block : block + 1, :], valid[block - 1 : block, :]) > 0.5
    return jnp.where(keep, logits * scale + bias, negative), here


def forward_kernel(layer, names, *refs):
    r = SimpleNamespace(**dict(zip(names, refs)))
    rec = layer == 1
    length = r.u_v.shape[1]
    heads = r.row0.shape[0]
    head_size = r.att_v.shape[2] // heads
    width = heads * head_size
    scale = head_size ** (-0.5)
    place = Place(length)
    net, local = Net(r.send_sems, r.recv_sems), Local(r.local_sems)
    chunk = min(128, length)

    place.meet()
    load = [local.copy(r.wqkv.at[layer], r.wqkv_v), local.copy(r.wout.at[layer], r.wout_v)]
    load_mlp = [local.copy(r.wup.at[layer], r.wup_v), local.copy(r.wdown.at[layer], r.wdown_v)]
    load_state = []
    if rec:
        load_state = [local.copy(r.wsqkv, r.wsqkv_v), local.copy(r.wsout, r.wsout_v)]

    gain = lambda index: r.gain[index : index + 1, :]
    shift = lambda index: r.shift[index : index + 1, :]

    def gather(buffer):
        return Gather(place, net, buffer)

    scatter_count = [0]

    def scatter():
        index = scatter_count[0]
        scatter_count[0] += 1
        return Scatter(
            place, net, r.part.at[index], r.near.at[index], r.out.at[index], r.far.at[index]
        )

    def norm_state(rows, index):
        r.sn_v[index, place.rows(), :] = layer_norm(rows, r.sgain[...], r.sshift[...]).astype(bf16)

    def norm_first(block):
        rows = r.x[block, place.core_rows(), :].astype(f32)
        r.u_v[block, place.rows(), :] = layer_norm(rows, gain(0), shift(0)).astype(bf16)

    def project(source, weights, target):
        for part in range(3):
            target[:, part * width : (part + 1) * width] = dot(source[...], weights[part]).astype(bf16)

    def reduce_from(values, weights, to):
        columns = weights.shape[1]
        step = min(512, columns)
        for x_other in (True, False):
            rows = place.chip_rows(x_other)

            @pl.loop(0, columns // step)
            def _(index):
                at = pl.ds(pl.multiple_of(index * step, step), step)
                to.part[rows, at] = dot(values[rows, :], weights[:, at]).astype(bf16)

            to.send(x_other)

    def attend(block):
        qkv = r.qkv_v.at[block]
        prev = r.qkv_v.at[block - 1] if block > 0 else None

        @pl.loop(0, length // chunk)
        def _(index):
            at = pl.ds(pl.multiple_of(index * chunk, chunk), chunk)
            lses = []
            for head in range(heads):
                q_at = slice(head * head_size, (head + 1) * head_size)
                k_at = slice(width + head * head_size, width + (head + 1) * head_size)
                v_at = slice(2 * width + head * head_size, 2 * width + (head + 1) * head_size)
                query = qkv[at, q_at]
                logits, here = window_logits(
                    query,
                    qkv[:, k_at],
                    None if prev is None else prev[:, k_at],
                    r.bias[head, :, bias_columns(index, chunk, length)],
                    r.valid,
                    block,
                    index * chunk,
                    scale,
                )
                peak = jnp.max(logits, axis=-1, keepdims=True)
                if rec:
                    state = r.sqkv_v.at[block]
                    state_logits = dot_nt(query, state[:, k_at]) * scale
                    peak = jnp.maximum(peak, jnp.max(state_logits, axis=-1, keepdims=True))
                probs = jnp.exp(logits - peak)
                total = jnp.sum(probs, axis=-1, keepdims=True)
                if prev is None:
                    result = dot(probs.astype(bf16), qkv[:, v_at])
                else:
                    result = dot(jnp.where(here, probs, 0.0).astype(bf16), qkv[:, v_at])
                    result += dot(jnp.where(here, 0.0, probs).astype(bf16), prev[:, v_at])
                if rec:
                    state_probs = jnp.exp(state_logits - peak)
                    total += jnp.sum(state_probs, axis=-1, keepdims=True)
                    result += dot(state_probs.astype(bf16), state[:, v_at])
                r.att_v[block, at, q_at] = (result / total).astype(bf16)
                lses.append(peak + jnp.log(total))
            lane = lax.broadcasted_iota(jnp.int32, (chunk, 128), 1)
            packed = jnp.zeros((chunk, 128), f32)
            for head in range(heads):
                packed = jnp.where(lane == head, lses[head], packed)
            r.lse_v[block, at, :] = packed

    def recur(block):
        qkv, state = r.qkv_v.at[block], r.sqkv_v.at[block]

        @pl.loop(0, length // chunk)
        def _(index):
            at = pl.ds(pl.multiple_of(index * chunk, chunk), chunk)
            lses = []
            for head in range(heads):
                q_at = slice(head * head_size, (head + 1) * head_size)
                k_at = slice(width + head * head_size, width + (head + 1) * head_size)
                v_at = slice(2 * width + head * head_size, 2 * width + (head + 1) * head_size)
                logits = dot_nt(state[at, q_at], qkv[:, k_at]) * scale
                logits = jnp.where(r.valid[block : block + 1, :] > 0.5, logits, negative)
                peak = jnp.max(logits, axis=-1, keepdims=True)
                probs = jnp.exp(logits - peak)
                total = jnp.sum(probs, axis=-1, keepdims=True)
                r.sout_v[block, at, q_at] = (dot(probs.astype(bf16), qkv[:, v_at]) / total).astype(bf16)
                lses.append(peak + jnp.log(total))
            if block == 0:
                lane = lax.broadcasted_iota(jnp.int32, (chunk, 128), 1)
                packed = jnp.zeros((chunk, 128), f32)
                for head in range(heads):
                    packed = jnp.where(lane == head, lses[head], packed)
                r.rlse_v[at, :] = packed

    def take_branch(block, from_out):
        rows = r.x[block, place.core_rows(), :].astype(f32) + from_out.finish()
        r.h_v[block] = rows
        r.wn_v[block, place.rows(), :] = layer_norm(rows, gain(1), shift(1)).astype(bf16)

    def feed_up(block):
        columns = r.wup_v.shape[1]
        step = 256

        @pl.loop(0, columns // step)
        def _(index):
            at = pl.ds(pl.multiple_of(index * step, step), step)
            pre = dot(r.wn_v[block], r.wup_v[:, at]) + r.up_bias[:, at]
            r.pre_v[block, :, at] = pre.astype(bf16)
            r.act[block, :, at] = (0.5 * pre * (1.0 + lax.erf(pre * (0.5**0.5)))).astype(bf16)

    def take_result(block, from_down):
        rows = r.h_v[block] + from_down.finish() + r.down_bias[...]
        own = r.acts_v.at[block, place.core_rows()]
        own[...] = rows.astype(bf16)
        return net.copy(own, own, place.core)

    branch = [scatter(), scatter()]
    result = [scatter(), scatter()]
    first = [gather(r.u_v.at[block]) for block in range(2)]
    second = [gather(r.wn_v.at[block]) for block in range(2)]
    if rec:
        update = [scatter(), scatter()]
        state = [gather(r.sn_v.at[block]) for block in range(2)]
        gate = r.gate[...]
        norm_state(r.state[place.core_rows(), :].astype(f32), 0)
        state[0].start()
    norm_first(0)
    first[0].start()
    norm_first(1)
    first[1].start()
    fill_bias(r.bias, r.row0)
    if rec:
        state[0].forward()
    first[0].forward()
    if rec:
        state[0].finish()
        local.wait(*load_state)
        project(r.sn_v.at[0], r.wsqkv_v, r.sqkv_v.at[0])
    first[0].finish()
    local.wait(*load)
    project(r.u_v.at[0], r.wqkv_v, r.qkv_v.at[0])
    if rec:
        recur(0)
        reduce_from(r.sout_v.at[0], r.wsout_v, update[0])
    first[1].forward()
    if rec:
        update[0].middle()
    attend(0)
    reduce_from(r.att_v.at[0], r.wout_v, branch[0])
    first[1].finish()
    project(r.u_v.at[1], r.wqkv_v, r.qkv_v.at[1])
    local.copy(r.u_v, r.u)
    local.copy(r.qkv_v, r.qkv)
    branch[0].middle()
    if rec:
        update_rows = update[0].finish()
        r.z_v[...] = update_rows
        state_rows = gate * r.state[place.core_rows(), :].astype(f32) + (1.0 - gate) * update_rows
        r.s1_v[...] = state_rows
        norm_state(state_rows, 1)
        state[1].start()
        local.copy(r.z_v, r.z)
        local.copy(r.s1_v, r.s1)
    else:
        attend(1)
        reduce_from(r.att_v.at[1], r.wout_v, branch[1])
    take_branch(0, branch[0])
    second[0].start()
    if rec:
        state[1].forward()
        state[1].finish()
        project(r.sn_v.at[1], r.wsqkv_v, r.sqkv_v.at[1])
        local.copy(r.sn_v, r.sn)
        local.copy(r.sqkv_v, r.sqkv)
        attend(1)
        reduce_from(r.att_v.at[1], r.wout_v, branch[1])
    local.copy(r.att_v, r.att)
    local.copy(r.lse_v, r.lse)
    second[0].forward()
    branch[1].middle()
    second[0].finish()
    local.wait(*load_mlp)
    feed_up(0)
    reduce_from(r.act.at[0], r.wdown_v, result[0])
    take_branch(1, branch[1])
    second[1].start()
    local.copy(r.h_v, r.h)
    result[0].middle()
    if rec:
        recur(1)
        reduce_from(r.sout_v.at[1], r.wsout_v, update[1])
        local.copy(r.sout_v, r.sout)
        local.copy(r.rlse_v, r.rlse)
    second[1].forward()
    second[1].finish()
    local.copy(r.wn_v, r.wn)
    feed_up(1)
    local.copy(r.pre_v, r.pre)
    reduce_from(r.act.at[1], r.wdown_v, result[1])
    sent = [take_result(0, result[0])]
    result[1].middle()
    if rec:
        update[1].middle()
    sent.append(take_result(1, result[1]))
    if rec:
        own = r.final_v.at[place.core_rows()]
        own[...] = gate * r.s1_v[...] + (1.0 - gate) * update[1].finish()
        sent.append(net.copy(own, own, place.core))
    for made in sent:
        made.wait_recv()
    local.copy(r.acts_v, r.acts)
    if rec:
        local.copy(r.final_v, r.final)
    local.drain()
    net.drain()


def forward_layer(layer, block_len, small, row0, valid, weights, rows, state):
    rec = layer == 1
    wqkv, wout, wup, wdown = weights[:4]
    model = rows.shape[2]
    width, hidden = wqkv.shape[3], wup.shape[2]
    quarter = block_len // 4
    heads = row0.shape[0]

    def held(shape, dtype):
        return jax.ShapeDtypeStruct(shape, dtype)

    outs = dict(
        u=held((2, block_len, model), bf16),
        qkv=held((2, block_len, 3 * width), bf16),
        lse=held((2, block_len, 128), f32),
        att=held((2, block_len, width), bf16),
        wn=held((2, block_len, model), bf16),
        pre=held((2, block_len, hidden), bf16),
        h=held((2, quarter, model), f32),
        acts=held((2, 2 * quarter, model), bf16),
    )
    ins = dict(
        x=rows,
        gain=small.gain[layer],
        shift=small.shift[layer],
        up_bias=small.up_bias[layer],
        down_bias=small.down_bias[layer],
        row0=row0,
        valid=valid,
    )
    far_ins = dict(wqkv=wqkv, wout=wout, wup=wup, wdown=wdown)
    if rec:
        outs.update(
            sn=held((2, block_len, model), bf16),
            sqkv=held((2, block_len, 3 * width), bf16),
            rlse=held((block_len, 128), f32),
            sout=held((2, block_len, width), bf16),
            s1=held((quarter, model), f32),
            z=held((quarter, model), f32),
            final=held((2 * quarter, model), f32),
        )
        ins.update(state=state, sgain=small.sgain, sshift=small.sshift, gate=small.gate)
        far_ins.update(wsqkv=weights[4], wsout=weights[5])
    scatters = 6 if rec else 4
    copies = (3 * 6 + 3 * 6 + 3) if rec else (3 * 4 + 3 * 4 + 2)
    scratch = {name + "_v": pltpu.VMEM(kind.shape, kind.dtype) for name, kind in outs.items()}
    scratch.update(
        wqkv_v=pltpu.VMEM(wqkv.shape[1:], bf16),
        wout_v=pltpu.VMEM(wout.shape[1:], bf16),
        wup_v=pltpu.VMEM(wup.shape[1:], bf16),
        wdown_v=pltpu.VMEM(wdown.shape[1:], bf16),
        act=pltpu.VMEM((2, block_len, hidden), bf16),
        bias=pltpu.VMEM((heads, min(128, block_len), 2 * block_len), f32),
        part=pltpu.VMEM((scatters, block_len, model), bf16),
        near=pltpu.VMEM((scatters, 2, quarter, model), bf16),
        out=pltpu.VMEM((scatters, quarter, model), bf16),
        far=pltpu.VMEM((scatters, quarter, model), bf16),
        send_sems=pltpu.SemaphoreType.DMA((copies,)),
        recv_sems=pltpu.SemaphoreType.DMA((copies,)),
        local_sems=pltpu.SemaphoreType.DMA((6 + len(outs),)),
    )
    if rec:
        scratch.update(
            wsqkv_v=pltpu.VMEM(weights[4].shape, bf16),
            wsout_v=pltpu.VMEM(weights[5].shape, bf16),
        )
    anywhere = pl.BlockSpec(memory_space=pl.ANY)
    inside = pl.BlockSpec(memory_space=pltpu.VMEM)
    results = pl.pallas_call(
        partial(forward_kernel, layer, [*ins, *far_ins, *outs, *scratch]),
        out_shape=tuple(outs.values()),
        in_specs=[inside] * len(ins) + [anywhere] * len(far_ins),
        out_specs=[anywhere] * len(outs),
        scratch_shapes=list(scratch.values()),
        compiler_params=pltpu.CompilerParams(
            collective_id=1 + layer, has_side_effects=True, vmem_limit_bytes=VMEM_LIMIT
        ),
        name="forward_recurrent" if rec else "forward_local",
    )(*ins.values(), *far_ins.values())
    return SimpleNamespace(**dict(zip(outs, results)))


def ring_place(n, c, d):
    if n % 2:
        at = d

        def index_at(p):
            return p

    else:
        a, b = d // 2, d % 2
        at = a + b * (n - 1 - 2 * a)

        def index_at(p):
            b = p // (n // 2)
            return 2 * (p + b * (n - 1 - 2 * p)) + b

    def flip(p):
        return p + c * (n - 1 - 2 * p)

    return flip(at), lambda p: index_at(flip(p))


class Ring:
    def __init__(self, n):
        self.n, self.c = n, lax.axis_index("section")
        self.q, index_at = ring_place(n, self.c, lax.axis_index("dp"))
        self.after = {"dp": index_at((self.q + 1) % n)}
        self.before = {"dp": index_at((self.q + n - 1) % n)}
        self.core, self.chip = {"section": 1 - self.c}, {"mp": 1 - lax.axis_index("mp")}

    def meet(self):
        barrier = pltpu.get_barrier_semaphore()
        for other in (self.after, self.before, self.core, self.chip):
            pl.semaphore_signal(barrier, inc=1, device_id=other, device_id_type=MESH)
        pl.semaphore_wait(barrier, 4)


def remote(source, target, send, recv, to):
    return pltpu.make_async_remote_copy(
        src_ref=source, dst_ref=target, send_sem=send, recv_sem=recv, device_id=to, device_id_type=MESH
    )


def ring_subs(n, rows, most):
    return max(k for k in range(1, most + 1) if rows // n % (16 * k) == 0)


def ring_scratch(n, rows, model, most):
    subs = ring_subs(n, rows, most)
    sems = pltpu.SemaphoreType.DMA
    return dict(
        held=pltpu.VMEM((n - 1, rows // n, model), bf16),
        rs_send=sems((n - 1, subs)),
        rs_recv=sems((n - 1, subs)),
        ag_send=sems((n - 1, subs)),
        ag_recv=sems((n - 1, subs)),
        core_send=sems((n, subs)),
        core_recv=sems((n, subs)),
        own_sems=sems((subs,)),
    )


class RingSum:
    def __init__(self, ring, mine, full, held, rs_send, rs_recv, ag_send, ag_recv, core_send, core_recv, own_sems):
        self.ring, self.mine, self.full, self.held = ring, mine, full, held
        self.rs_send, self.rs_recv, self.ag_send, self.ag_recv = rs_send, rs_recv, ag_send, ag_recv
        self.core_send, self.core_recv, self.own_sems = core_send, core_recv, own_sems
        self.chunk, self.subs = held.shape[1], own_sems.shape[0]
        self.sub = self.chunk // self.subs
        self.half = (ring.n - 1) * self.subs
        self.total = 2 * self.half
        self.done = 0

    def rows(self, owner, k):
        owner = (owner + 2 * self.ring.n) % self.ring.n
        return pl.ds(pl.multiple_of(owner * self.chunk + k * self.sub, self.sub), self.sub)

    def piece(self, k):
        return slice(k * self.sub, (k + 1) * self.sub) if isinstance(k, int) else pl.ds(
            pl.multiple_of(k * self.sub, self.sub), self.sub
        )

    def summed(self, s, k):
        return self.held.at[s, self.piece(k)]

    def gathered(self, s, k):
        return self.full.at[self.ring.c, self.rows(self.ring.q + 1 - s, k)]

    def reduce(self, s, k, source):
        return remote(source, self.summed(s, k), self.rs_send.at[s, k], self.rs_recv.at[s, k], self.ring.after)

    def gather(self, s, k, source):
        return remote(source, self.gathered(s, k), self.ag_send.at[s, k], self.ag_recv.at[s, k], self.ring.after)

    def to_core(self, s, k, source):
        return remote(source, self.gathered(s, k), self.core_send.at[s, k], self.core_recv.at[s, k], self.ring.core)

    def from_core(self, s, k):
        n, q = self.ring.n, self.ring.q
        target = self.full.at[1 - self.ring.c, self.rows(n - q - s, k)]
        return remote(target, target, self.core_send.at[s, k], self.core_recv.at[s, k], self.ring.core)

    def own(self, k):
        return pltpu.make_async_copy(self.summed(self.ring.n - 2, k), self.gathered(0, k), self.own_sems.at[k])

    def start(self):
        for k in range(self.subs):
            self.reduce(0, k, self.mine.at[self.rows(self.ring.q, k)]).start()

    def add(self, s, k):
        self.reduce(s, k, self.summed(s, k)).wait_recv()
        self.held[s, self.piece(k), :] = (
            self.held[s, self.piece(k), :].astype(f32)
            + self.mine[self.rows(self.ring.q - 1 - s, k), :].astype(f32)
        ).astype(bf16)

    def add_middle(self, s, k):
        self.add(s, k)
        self.reduce(s + 1, k, self.summed(s, k)).start()

    def add_last(self, s, k):
        self.add(s, k)
        self.gather(0, k, self.summed(s, k)).start()
        self.to_core(0, k, self.summed(s, k)).start()
        self.own(k).start()

    def pass_middle(self, s, k):
        at = self.gathered(s + 1, k)
        self.gather(s, k, at).wait_recv()
        self.gather(s + 1, k, at).start()
        self.to_core(s + 1, k, at).start()

    def pass_last(self, s, k):
        at = self.gathered(s + 1, k)
        self.gather(s, k, at).wait_recv()
        self.to_core(s + 1, k, at).start()

    def pump_one(self, t):
        last = self.ring.n - 2
        s, k = t // self.subs, t % self.subs
        kinds = (
            (s < last, self.add_middle, s),
            (s == last, self.add_last, s),
            ((s > last) & (s < 2 * last + 1), self.pass_middle, s - last - 1),
            (s == 2 * last + 1, self.pass_last, s - last - 1),
        )
        for here, act, step in kinds:
            if isinstance(t, int):
                if here:
                    act(step, k)
            else:
                pl.when(here)(partial(act, step, k))

    def pump(self, count=1):
        for _ in range(min(count, self.total - self.done)):
            self.pump_one(self.done)
            self.done += 1

    def pumps_in(self, loop_steps, each):
        each = min(each, (self.total - self.done) // loop_steps)
        base = self.done
        self.done += each * loop_steps

        def pump(index):
            for piece in range(each):
                self.pump_one(base + index * each + piece)

        return pump

    def run(self, until):
        last = self.ring.n - 2
        for first, end, act in (
            (0, last, self.add_middle),
            (last, last + 1, self.add_last),
            (last + 1, 2 * last + 1, self.pass_middle),
            (2 * last + 1, 2 * last + 2, self.pass_last),
        ):
            while self.done < min(end * self.subs, until) and self.done % self.subs:
                self.pump()
            step, stop = self.done // self.subs, min(end, until // self.subs)
            if first <= step < stop:
                base = last + 1 if first > last else 0

                @pl.loop(step - base, stop - base)
                def _(s):
                    for k in range(self.subs):
                        act(s, k)

                self.done = stop * self.subs

    def release_mine(self):
        for k in range(self.subs):
            self.reduce(0, k, self.mine.at[self.rows(self.ring.q, k)]).wait_send()

    def finish(self, released=False):
        self.run(self.total)
        if not released:
            self.release_mine()
        last = self.ring.n - 2

        @pl.loop(0, last + 2)
        def _(s):
            for k in range(self.subs):
                self.from_core(s, k).wait_recv()
                self.to_core(s, k, self.gathered(s, k)).wait_send()

        @pl.loop(0, last + 1)
        def _(s):
            for k in range(self.subs):
                self.gather(s, k, self.gathered(s, k)).wait_send()

        @pl.loop(0, last)
        def _(s):
            for k in range(self.subs):
                self.reduce(s + 1, k, self.summed(s, k)).wait_send()

        for k in range(self.subs):
            self.own(k).wait()


def sum_kernel(n, parts, small, full, small_out, mine, small_held, small_sum, small_far, *rest):
    ring_refs, (small_send, small_recv, local_sems) = rest[:-3], rest[-3:]
    ring = Ring(n)
    flow = RingSum(ring, mine, full, *ring_refs)

    def small_step(s, first):
        source = small if first else small_held.at[s - 1]
        return remote(source, small_held.at[s], small_send.at[s], small_recv.at[s], ring.after)

    load = pltpu.make_async_copy(parts, mine, local_sems.at[0])
    load.start()
    ring.meet()
    small_step(0, True).start()
    load.wait()
    flow.start()

    @pl.loop(0, n - 2)
    def _(s):
        for k in range(flow.subs):
            flow.add_middle(s, k)
        small_step(s, True).wait_recv()
        small_step(s + 1, False).start()

    flow.done = (n - 2) * flow.subs
    flow.run(flow.half)
    small_step(n - 2, True).wait_recv()
    small_out[0] = small[...]

    @pl.loop(0, n - 1)
    def _(s):
        small_out[0] += small_held[s]

    between = remote(small_out.at[0], small_out.at[1], small_send.at[n - 1], small_recv.at[n - 1], ring.core)
    between.start()
    between.wait_recv()
    small_sum[...] = small_out[0] + small_out[1]
    across = remote(small_sum, small_far, small_send.at[n], small_recv.at[n], ring.chip)
    across.start()
    across.wait_recv()
    small_out[2] = small_sum[...] + small_far[...]
    flow.finish()

    @pl.loop(0, n - 1)
    def _(s):
        small_step(s, True).wait_send()

    between.wait_send()
    across.wait_send()


def sum_gradients(n, parts, small):
    rows, model = parts.shape
    anywhere = pl.BlockSpec(memory_space=pl.ANY)
    inside = pl.BlockSpec(memory_space=pltpu.VMEM)
    sems = pltpu.SemaphoreType.DMA
    return pl.pallas_call(
        partial(sum_kernel, n),
        out_shape=(
            jax.ShapeDtypeStruct((2, rows, model), bf16),
            jax.ShapeDtypeStruct((3,) + small.shape, f32),
        ),
        in_specs=[anywhere, inside],
        out_specs=[anywhere, inside],
        scratch_shapes=[
            pltpu.VMEM((rows, model), bf16),
            pltpu.VMEM((n - 1,) + small.shape, f32),
            pltpu.VMEM(small.shape, f32),
            pltpu.VMEM(small.shape, f32),
            *ring_scratch(n, rows, model, 6).values(),
            sems((n + 1,)),
            sems((n + 1,)),
            sems((1,)),
        ],
        compiler_params=pltpu.CompilerParams(
            collective_id=5, has_side_effects=True, vmem_limit_bytes=VMEM_LIMIT
        ),
        name="sum_gradients",
    )(parts, small)


def norm_back(rows, gain, grad):
    normed, scale = norm_parts(rows)
    inner = grad * gain
    means = jnp.mean(inner, axis=-1, keepdims=True), jnp.mean(inner * normed, axis=-1, keepdims=True)
    by_rows = scale * (inner - means[0] - normed * means[1])
    return by_rows, jnp.sum(grad * normed, axis=0, keepdims=True), jnp.sum(grad, axis=0, keepdims=True)


GAIN0, GAIN1, SHIFT0, SHIFT1, DOWN_BIAS, SGAIN, SSHIFT, GATE, UP_BIAS, BY_DISTANCE = range(10)
SMALL_ROWS = 16


def backward_kernel(layer, n, ring_names, names, *refs):
    r = SimpleNamespace(**dict(zip(names, refs)))
    rec = layer == 1
    heads, length = r.row0.shape
    head_size = r.att_v.shape[1] // heads
    width = heads * head_size
    hidden = r.wup_v.shape[1]
    model = r.wup_v.shape[0]
    scale = head_size ** (-0.5)
    place = Place(length)
    net, local = Net(r.send_sems, r.recv_sems), Local(r.local_sems)
    chunk = min(128, length)

    ring = Ring(n)
    r.act, r.pre_v = r.work.at[:model], r.work.at[model:]
    if not rec:
        parts = local.copy(r.parts, r.mine)
    flow = RingSum(ring, r.work if rec else r.mine, r.full, *[getattr(r, name) for name in ring_names])
    ring.meet()
    wdown = local.copy(r.wdown.at[layer], r.wdown_v)
    pre = local.copy(r.pre, r.pre_v)
    wup = local.copy(r.wup.at[layer], r.wup_v)
    hidden_rows = local.copy(r.h, r.h_v)
    wn = local.copy(r.wn, r.wn_v)
    attention = [
        local.copy(r.wout.at[layer], r.wout_v),
        local.copy(r.qkv, r.qkv_v),
        local.copy(r.att, r.att_v),
        local.copy(r.lse, r.lse_v),
    ]
    if rec:
        attention += [local.copy(r.sqkv, r.sqkv_v), local.copy(r.wsqkv, r.wsqkv_v)]
        chain = [
            local.copy(r.s1, r.s1_v),
            local.copy(r.z, r.z_v),
            local.copy(r.wsout, r.wsout_v),
            local.copy(r.sout, r.sout_v),
            local.copy(r.rlse, r.rlse_v),
        ]
    wqkv = local.copy(r.wqkv.at[layer], r.wqkv_v)

    gain = lambda index: r.gain[index : index + 1, :]
    small = r.small_v
    small[...] = jnp.zeros(small.shape, f32)
    r.dkv[...] = jnp.zeros(r.dkv.shape, f32)
    r.dbias[...] = jnp.zeros(r.dbias.shape, f32)
    if rec:
        r.dskv[...] = jnp.zeros(r.dskv.shape, f32)

    def add_small(index, value):
        small[index : index + 1, :] += value

    def gather(buffer):
        return Gather(place, net, buffer)

    scatter_count = [0]

    def scatter(slot):
        index = scatter_count[0]
        scatter_count[0] += 1
        return Scatter(place, net, r.part.at[slot], r.near.at[index], r.out.at[slot], r.far.at[index])

    def block_rows(block):
        return slice(block * length, (block + 1) * length)

    def own_grad(block):
        return r.gy[block, place.core_rows(), :].astype(bf16).astype(f32)

    def feed_back(block):
        step = 256
        rows = block_rows(block)

        @pl.loop(0, hidden // step)
        def _(index):
            at = pl.ds(pl.multiple_of(index * step, step), step)
            pre = r.pre_v[rows, at].astype(f32)
            by_act = dot_nt(r.g[rows, :], r.wdown_v[at, :])
            below = 0.5 * (1.0 + lax.erf(pre * (0.5**0.5)))
            r.act[rows, at] = (pre * below).astype(bf16)
            by_pre = by_act * (below + pre * jnp.exp(-0.5 * pre * pre) * 0.3989422804014327)
            small[UP_BIAS : UP_BIAS + 1, at] += jnp.sum(by_pre, axis=0, keepdims=True)
            r.dpre[rows, at] = by_pre.astype(bf16)

    def reduce_back(terms, to):
        step = min(512, model)
        for x_other in (True, False):
            rows = place.chip_rows(x_other)

            @pl.loop(0, model // step)
            def _(index):
                at = pl.ds(pl.multiple_of(index * step, step), step)
                total = None
                for values, weights in terms:
                    term = dot_nt(values[rows, :], weights[at, :])
                    total = term if total is None else total + term
                to.part[rows, at] = total.astype(bf16)

            to.send(x_other)

    def take_feed(block, from_feed):
        by_norm = from_feed.finish()
        grad = own_grad(block)
        by_rows, by_gain, by_shift = norm_back(r.h_v[block], gain(1), by_norm)
        add_small(GAIN1, by_gain)
        add_small(SHIFT1, by_shift)
        add_small(DOWN_BIAS, jnp.sum(grad, axis=0, keepdims=True))
        total = grad + by_rows
        r.ig_v[block, place.core_rows(), :] = total
        r.hg[pl.ds(place_row(block), place.quarter), :] = total.astype(bf16)

    def place_row(block):
        return pl.multiple_of(block * length + place.x * place.half + place.c * place.quarter, place.quarter)

    def weight_grad(left, right, target, at_row=0):
        step = 256

        @pl.loop(0, left.shape[1] // step)
        def _(index):
            at = pl.ds(pl.multiple_of(index * step, step), step)
            to = pl.ds(pl.multiple_of(at_row + index * step, step), step)
            target[to, :] = dot_tn(left[:, at], right[...]).astype(bf16)

    def projection_grad(normed, grads, target):
        for part in range(3):
            to = slice(part * width, (part + 1) * width)

            @pl.loop(0, model // width)
            def _(index):
                at = pl.ds(pl.multiple_of(index * width, width), width)
                target[to, at] = dot_tn(normed[:, at], grads[:, to]).astype(bf16)

    def branch_back(block):
        r.datt[block] = dot_nt(r.hg[block_rows(block), :], r.wout_v[...]).astype(bf16)

    def columns(head, part):
        return slice(part * width + head * head_size, part * width + (head + 1) * head_size)

    def attend_back(block):
        qkv = r.qkv_v.at[block]
        prev = r.qkv_v.at[block - 1] if block > 0 else None
        state = r.sqkv_v.at[block] if rec else None
        pump = flow.pumps_in(length // chunk, 1)

        @pl.loop(0, length // chunk)
        def _(index):
            pump(index)
            at = pl.ds(pl.multiple_of(index * chunk, chunk), chunk)
            block_at = pl.ds(pl.multiple_of(block * length + index * chunk, chunk), chunk)
            for head in range(heads):
                q_at, k_at, v_at = (columns(head, part) for part in range(3))
                query, key, value = qkv[at, q_at], qkv[:, k_at], qkv[:, v_at]
                logits, here = window_logits(
                    query,
                    key,
                    None if prev is None else prev[:, k_at],
                    r.bias[head, :, bias_columns(index, chunk, length)],
                    r.valid,
                    block,
                    index * chunk,
                    scale,
                )
                lse = r.lse_v[block, at, head : head + 1]
                probs = jnp.exp(logits - lse)
                grad = r.datt[block, at, q_at]
                delta = jnp.sum(
                    grad.astype(f32) * r.att_v[block_at, q_at].astype(f32), axis=-1, keepdims=True
                )
                by_probs = dot_nt(grad, value)
                if prev is not None:
                    by_probs = jnp.where(here, by_probs, dot_nt(grad, prev[:, v_at]))
                by_logits = probs * (by_probs - delta)
                r.dbias[head, :, bias_columns(index, chunk, length)] += by_logits
                by_logits = by_logits * scale
                if prev is None:
                    low = by_logits.astype(bf16)
                    low_probs = probs.astype(bf16)
                    by_query = dot(low, key)
                else:
                    low = jnp.where(here, by_logits, 0.0).astype(bf16)
                    low_probs = jnp.where(here, probs, 0.0).astype(bf16)
                    low_prev = jnp.where(here, 0.0, by_logits).astype(bf16)
                    low_probs_prev = jnp.where(here, 0.0, probs).astype(bf16)
                    by_query = dot(low, key) + dot(low_prev, prev[:, k_at])
                    r.dkv[block - 1, :, q_at] += dot_tn(low_prev, query)
                    r.dkv[block - 1, :, k_at] += dot_tn(low_probs_prev, grad)
                r.dkv[block, :, q_at] += dot_tn(low, query)
                r.dkv[block, :, k_at] += dot_tn(low_probs, grad)
                if rec:
                    state_probs = jnp.exp(dot_nt(query, state[:, k_at]) * scale - lse)
                    by_state = state_probs * (dot_nt(grad, state[:, v_at]) - delta) * scale
                    low_state = by_state.astype(bf16)
                    by_query += dot(low_state, state[:, k_at])
                    r.dskv[:, q_at] += dot_tn(low_state, query)
                    r.dskv[:, k_at] += dot_tn(state_probs.astype(bf16), grad)
                r.dqkv[block_at, q_at] = by_query.astype(bf16)

    def recur_back():
        qkv, state = r.qkv_v.at[0], r.sqkv_v.at[0]
        pump = flow.pumps_in(length // chunk, 1)

        @pl.loop(0, length // chunk)
        def _(index):
            pump(index)
            at = pl.ds(pl.multiple_of(index * chunk, chunk), chunk)
            for head in range(heads):
                q_at, k_at, v_at = (columns(head, part) for part in range(3))
                query, key, value = state[at, q_at], qkv[:, k_at], qkv[:, v_at]
                logits = dot_nt(query, key) * scale
                logits = jnp.where(r.valid[0:1, :] > 0.5, logits, negative)
                probs = jnp.exp(logits - r.rlse_v[at, head : head + 1])
                grad = r.dsout[at, q_at]
                delta = jnp.sum(
                    grad.astype(f32) * r.sout_v[0, at, q_at].astype(f32), axis=-1, keepdims=True
                )
                low = (probs * (dot_nt(grad, value) - delta) * scale).astype(bf16)
                r.dsqkv[at, q_at] = dot(low, key).astype(bf16)
                r.dkv[0, :, q_at] += dot_tn(low, query)
                r.dkv[0, :, k_at] += dot_tn(probs.astype(bf16), grad)

    def close_keys(block):
        r.dqkv[block_rows(block), width:] = r.dkv[block].astype(bf16)

    def close_state(block):
        r.dsqkv[block_rows(block), width:] = r.dskv[...].astype(bf16)
        if block == 1:
            r.dskv[...] = jnp.zeros(r.dskv.shape, f32)

    def input_back(block, to):
        rows = block_rows(block)
        reduce_back(
            [
                (r.dqkv.at[rows, part * width : (part + 1) * width], r.wqkv_v.at[part])
                for part in range(3)
            ],
            to,
        )

    def state_back(block, to):
        rows = block_rows(block)
        reduce_back(
            [
                (r.dsqkv.at[rows, part * width : (part + 1) * width], r.wsqkv_v.at[part])
                for part in ((0, 1, 2) if block == 0 else (1, 2))
            ],
            to,
        )

    def take_input(block, from_input):
        by_norm = from_input.finish()
        rows = r.x[block, place.core_rows(), :].astype(f32)
        by_rows, by_gain, by_shift = norm_back(rows, gain(0), by_norm)
        add_small(GAIN0, by_gain)
        add_small(SHIFT0, by_shift)
        own = r.ig_v.at[block, place.core_rows()]
        own[...] += by_rows
        return net.copy(own, own, place.core)

    def take_state(rows, from_state):
        by_rows, by_gain, by_shift = norm_back(rows, r.sgain[...], from_state.finish())
        add_small(SGAIN, by_gain)
        add_small(SSHIFT, by_shift)
        return by_rows

    def close_bias():
        tile = r.dbias.shape[1]
        for head in range(heads):
            folded = r.dbias[head, :, :length] + r.dbias[head, :, length:]
            row = lax.broadcasted_iota(jnp.int32, folded.shape, 0)
            bit = 1
            while bit < tile:
                moved = pltpu.roll(folded, length - bit, axis=1)
                folded = jnp.where((row & bit) != 0, moved, folded)
                bit *= 2
            small[BY_DISTANCE : BY_DISTANCE + 1, head * length : (head + 1) * length] = jnp.sum(
                folded, axis=0, keepdims=True
            )

    if rec:
        at_qkv, at_sqkv = 0, 4 * width
    else:
        at_up, at_down, at_qkv = 0, model, model + hidden
    at_out = 3 * width

    feed = [scatter(0), scatter(1)]
    inputs = [scatter(2 if rec else 0), scatter(1)]
    grads = [gather(r.g.at[block_rows(block)]) for block in range(2)]
    hiddens = [gather(r.hg.at[block_rows(block)]) for block in range(2)]
    if rec:
        states = [scatter(0), scatter(0)]
        updates = gather(r.ug)
    for block in (1, 0):
        r.g[pl.ds(place_row(block), place.quarter), :] = own_grad(block).astype(bf16)
        grads[block].start()
    fill_bias(r.bias, r.row0)
    if not rec:
        local.wait(parts)
        flow.start()
    grads[1].forward()
    local.wait(wdown, pre, wup)
    grads[1].finish()
    if not rec:
        flow.pump(2)
    feed_back(1)
    reduce_back([(r.dpre.at[block_rows(1)], r.wup_v)], feed[1])
    grads[0].forward()
    if not rec:
        flow.pump(2)
    grads[0].finish()
    feed_back(0)
    feed[1].middle()
    if not rec:
        flow.pump(2)
    reduce_back([(r.dpre.at[block_rows(0)], r.wup_v)], feed[0])
    local.wait(hidden_rows)
    take_feed(1, feed[1])
    hiddens[1].start()
    feed[0].middle()
    weight_grad(r.act, r.g, r.pre_v)
    hiddens[1].forward()
    local.wait(wn)
    weight_grad(r.wn_v, r.dpre, r.act)
    if rec:
        flow.start()
    else:
        flow.pump(2)
        feed_out = [local.copy(r.act, r.dw.at[at_up:at_down]), local.copy(r.pre_v, r.dw.at[at_down:at_qkv])]
    take_feed(0, feed[0])
    hiddens[0].start()
    u_in = local.copy(r.u, r.wn_v)
    hiddens[1].finish()
    local.wait(*attention)
    branch_back(1)
    flow.pump(1)
    attend_back(1)
    close_keys(1)
    feed[0].release()
    feed[1].release()
    if rec:
        close_state(1)
        state_back(1, states[1])
    hiddens[0].forward()
    flow.pump(1)
    local.wait(wqkv)
    input_back(1, inputs[1])
    if rec:
        states[1].middle()
    hiddens[0].finish()
    branch_back(0)
    flow.pump(1)
    inputs[1].middle()
    if rec:
        local.wait(*chain)
        gate = r.gate[...]
        by_state = take_state(r.s1_v[...], states[1])
        states[1].release()
        before = r.state[place.core_rows(), :].astype(f32)
        add_small(
            GATE,
            jnp.sum(by_state * (before - r.z_v[...]) * gate * (1.0 - gate), axis=0, keepdims=True),
        )
        r.ug[place.rows(), :] = ((1.0 - gate) * by_state).astype(bf16)
        updates.start()
    attend_back(0)
    if rec:
        updates.forward()
        flow.pump(1)
        updates.finish()
        r.dsout[...] = dot_nt(r.ug[...], r.wsout_v[...]).astype(bf16)
        recur_back()
    close_keys(0)
    flow.pump(1)
    input_back(0, inputs[0])
    flow.pump(1)
    if rec:
        close_state(0)
        state_back(0, states[0])
        flow.pump(1)
    sent = [take_input(1, inputs[1])]
    inputs[0].middle()
    if rec:
        states[0].middle()
    weight_grad(r.att_v, r.hg, r.dpre, at_out)
    flow.pump(1)
    close_bias()
    local.wait(u_in)
    projection_grad(r.wn_v, r.dqkv, r.dpre)
    local.copy(r.dpre, r.dw.at[at_qkv : at_qkv + 4 * width])
    flow.pump(1)
    if rec:
        r.dsqkv[block_rows(1), 0:width] = jnp.zeros((length, width), bf16)
        sn_in = local.copy(r.sn, r.wn_v)
        flow.run(flow.half)
        flow.release_mine()
        local.wait(sn_in)
        projection_grad(r.wn_v, r.dsqkv, r.act)
        flow.pump(1)
        weight_grad(r.sout_v.at[0], r.ug, r.act, at_out)
        local.copy(r.act, r.dw.at[at_sqkv:])
        flow.pump(1)
    sent.append(take_input(0, inputs[0]))
    if rec:
        take_state(r.state[place.core_rows(), :].astype(f32), states[0])
    flow.pump(1)
    local.copy(small, r.small)
    for made in sent:
        made.wait_recv()
    local.copy(r.ig_v, r.ig)
    flow.finish(released=rec)
    local.drain()
    net.drain()


def backward_layer(layer, n, block_len, small, row0, valid, weights, grad_rows, rows, state, kept, parts=None):
    rec = layer == 1
    wqkv, wout, wup, wdown = weights[:4]
    model = rows.shape[2]
    width, hidden = wqkv.shape[3], wup.shape[2]
    quarter = block_len // 4
    heads = row0.shape[0]

    def held(shape, dtype):
        return jax.ShapeDtypeStruct(shape, dtype)

    dw_rows = 8 * width if rec else model + hidden + 4 * width
    ring_rows = model + hidden if rec else parts.shape[0]
    outs = dict(
        full=held((2, ring_rows, model), bf16),
        dw=held((dw_rows, model), bf16),
        small=held((SMALL_ROWS, model), f32),
        ig=held((2, 2 * quarter, model), f32),
    )
    ins = dict(
        gy=grad_rows, x=rows, gain=small.gain[layer], shift=small.shift[layer], row0=row0, valid=valid
    )

    def flat(array):
        return array.reshape((-1,) + array.shape[2:])

    stacked = dict(wqkv=wqkv, wout=wout, wup=wup, wdown=wdown)
    copied = dict(
        qkv=kept.qkv, lse=kept.lse, att=flat(kept.att), wn=flat(kept.wn), h=kept.h
    )
    late = dict(pre=flat(kept.pre), u=flat(kept.u))
    if rec:
        ins.update(state=state, sgain=small.sgain, sshift=small.sshift, gate=small.gate)
        copied.update(wsqkv=weights[4], wsout=weights[5])
        copied.update(sqkv=kept.sqkv, rlse=kept.rlse, sout=kept.sout, s1=kept.s1, z=kept.z)
        late.update(sn=flat(kept.sn))
    else:
        late.update(parts=parts)
    far_ins = {**stacked, **copied, **late}
    scatters = 6 if rec else 4
    copies = (3 * 6 + 3 * 5 + 2) if rec else (3 * 4 + 3 * 4 + 2)
    scratch = dict(small_v=pltpu.VMEM(outs["small"].shape, f32), ig_v=pltpu.VMEM(outs["ig"].shape, f32))
    for name, array in stacked.items():
        scratch[name + "_v"] = pltpu.VMEM(array.shape[1:], array.dtype)
    for name, array in copied.items():
        scratch[name + "_v"] = pltpu.VMEM(array.shape, array.dtype)
    scratch.update(
        g=pltpu.VMEM((2 * block_len, model), bf16),
        hg=pltpu.VMEM((2 * block_len, model), bf16),
        work=pltpu.VMEM((model + hidden, model), bf16),
        dpre=pltpu.VMEM((2 * block_len, hidden), bf16),
        datt=pltpu.VMEM((2, block_len, width), bf16),
        dkv=pltpu.VMEM((2, block_len, 2 * width), f32),
        dqkv=pltpu.VMEM((2 * block_len, 3 * width), bf16),
        dbias=pltpu.VMEM((heads, min(128, block_len), 2 * block_len), f32),
        bias=pltpu.VMEM((heads, min(128, block_len), 2 * block_len), f32),
        part=pltpu.VMEM((scatters // 2, block_len, model), bf16),
        near=pltpu.VMEM((scatters, 2, quarter, model), bf16),
        out=pltpu.VMEM((scatters // 2, quarter, model), bf16),
        far=pltpu.VMEM((scatters, quarter, model), bf16),
        send_sems=pltpu.SemaphoreType.DMA((copies,)),
        recv_sems=pltpu.SemaphoreType.DMA((copies,)),
        local_sems=pltpu.SemaphoreType.DMA((len(far_ins) + 6,)),
    )
    if rec:
        scratch.update(
            ug=pltpu.VMEM((block_len, model), bf16),
            dsout=pltpu.VMEM((block_len, width), bf16),
            dskv=pltpu.VMEM((block_len, 2 * width), f32),
            dsqkv=pltpu.VMEM((2 * block_len, 3 * width), bf16),
        )
    else:
        scratch.update(mine=pltpu.VMEM((ring_rows, model), bf16))
    ring_refs = ring_scratch(n, ring_rows, model, 2)
    scratch.update(ring_refs)
    anywhere = pl.BlockSpec(memory_space=pl.ANY)
    inside = pl.BlockSpec(memory_space=pltpu.VMEM)
    results = pl.pallas_call(
        partial(backward_kernel, layer, n, list(ring_refs), [*ins, *far_ins, *outs, *scratch]),
        out_shape=tuple(outs.values()),
        in_specs=[inside] * len(ins) + [anywhere] * len(far_ins),
        out_specs=[anywhere] * len(outs),
        scratch_shapes=list(scratch.values()),
        compiler_params=pltpu.CompilerParams(
            collective_id=3 + layer, has_side_effects=True, vmem_limit_bytes=VMEM_LIMIT
        ),
        name="backward_recurrent" if rec else "backward_local",
    )(*ins.values(), *far_ins.values())
    return SimpleNamespace(**dict(zip(outs, results)))


def place_kernel(
    width, hidden, feed_1, rest_1, full_0, qkv, out, up, down, sqkv, sout, inward, outward, in_sems, out_sems
):
    model = full_0.shape[2]
    layer = lax.axis_index("section")
    slots = inward.shape[0]
    at_rest = model + hidden
    jobs = []
    for half in range(2):
        columns = slice(half * width, (half + 1) * width)

        def projection(target):
            return [target.at[index : index + width, columns] for index in range(0, model, width)]

        for row in range(0, model, width):
            wide = slice(half * hidden, (half + 1) * hidden)
            jobs.append((half, (feed_1, row), row, [up.at[0, row : row + width, wide]]))
        for row in range(0, hidden, width):
            at = half * hidden + row
            jobs.append((half, (feed_1, model + row), model + row, [down.at[0, at : at + width]]))
        for part in range(3):
            row = part * width
            jobs.append((half, (rest_1, row), at_rest + row, projection(qkv.at[0, part])))
            jobs.append((half, (rest_1, 4 * width + row), None, projection(sqkv.at[part])))
        jobs.append((half, (rest_1, 3 * width), at_rest + 3 * width, [out.at[0, columns]]))
        jobs.append((half, (rest_1, 7 * width), None, [sout.at[columns]]))

    def load(index, start):
        half, (array, row), row_0, _ = jobs[index]
        slot = index % slots

        def made(source, at):
            return pltpu.make_async_copy(source.at[half, at : at + width], inward.at[slot], in_sems.at[slot])

        if not start:
            made(array, row).wait()
        elif row_0 is None:
            made(array, row).start()
        else:
            pl.when(layer == 1)(lambda: made(array, row).start())
            pl.when(layer == 0)(lambda: made(full_0, row_0).start())

    def stores(index):
        targets, slot = jobs[index][3], index % slots
        step = model // len(targets)
        return [
            pltpu.make_async_copy(
                outward.at[slot, :, k * step : (k + 1) * step], target, out_sems.at[slot, k]
            )
            for k, target in enumerate(targets)
        ]

    for index in range(slots):
        load(index, True)
    for index in range(len(jobs)):
        slot = index % slots
        load(index, False)
        if index >= slots:
            for made in stores(index - slots):
                made.wait()
        outward[slot] = inward[slot].astype(f32)
        for made in stores(index):
            made.start()
        if index + slots < len(jobs):
            load(index + slots, True)
    for index in range(len(jobs) - slots, len(jobs)):
        for made in stores(index):
            made.wait()


def place_gradients(feed_1, rest_1, full_0, width, hidden):
    model = full_0.shape[2]
    anywhere = pl.BlockSpec(memory_space=pl.ANY)
    slots = 4
    shapes = (
        (1, 3, model, 2 * width),
        (1, 2 * width, model),
        (1, model, 2 * hidden),
        (1, 2 * hidden, model),
        (3, model, 2 * width),
        (2 * width, model),
    )
    return pl.pallas_call(
        partial(place_kernel, width, hidden),
        out_shape=[jax.ShapeDtypeStruct(shape, f32) for shape in shapes],
        in_specs=[anywhere] * 3,
        out_specs=[anywhere] * 6,
        scratch_shapes=[
            pltpu.VMEM((slots, width, model), bf16),
            pltpu.VMEM((slots, width, model), f32),
            pltpu.SemaphoreType.DMA((slots,)),
            pltpu.SemaphoreType.DMA((slots, model // width)),
        ],
        compiler_params=pltpu.CompilerParams(vmem_limit_bytes=VMEM_LIMIT),
        name="place_gradients",
    )(feed_1, rest_1, full_0)


def pack_small(arrays, width):
    flat = jnp.concatenate([array.astype(f32).reshape(-1) for array in arrays])
    return jnp.pad(flat, (0, -flat.size % (8 * width))).reshape(-1, width)


def unpack_small(packed, shapes):
    flat = packed.reshape(packed.shape[0], -1)
    found, at = [], 0
    for shape in shapes:
        size = 1
        for extent in shape:
            size *= extent
        found.append(flat[:, at : at + size].reshape((packed.shape[0],) + tuple(shape)))
        at += size
    return found


def local_part(
    tokens, valid_mask, buckets, state_init, norm_gain, norm_shift, w_qkv, w_out, rel_bias, w_up, up_bias,
    w_down, down_bias, state_gain, state_shift, w_state_qkv, w_state_out, gate_bias, cotangent,
):
    block_len = valid_mask.shape[1]
    model = tokens.shape[3]
    core = lax.axis_index("section")
    bucket_count, chip_heads = rel_bias.shape[1:]
    heads = chip_heads // 2
    hidden = w_up.shape[2] // 2
    valid = valid_mask[:, :, 0].astype(f32)
    packed = pack_small([norm_gain[0], norm_shift[0], down_bias[0], up_bias[0], rel_bias[0]], model)
    *weights, small_all = share_weights(
        block_len, w_qkv[0], w_out[0], w_up[0], w_down[0], w_state_qkv, w_state_out, packed
    )
    gains, shifts, down_biases, up_biases, rels = unpack_small(
        small_all, [(2, model), (2, model), (1, model), (1, 2 * hidden), (bucket_count, chip_heads)]
    )
    small = SimpleNamespace(
        gain=gains,
        shift=shifts,
        down_bias=down_biases,
        up_bias=lax.dynamic_slice_in_dim(up_biases, core * hidden, hidden, 2),
        sgain=state_gain[None],
        sshift=state_shift[None],
        gate=jax.nn.sigmoid(gate_bias)[None],
    )
    rels = lax.dynamic_slice_in_dim(rels, core * heads, heads, 2)
    back = jnp.concatenate([buckets[:1], buckets[:0:-1]])
    back_hot = back[:, None] == jnp.arange(bucket_count)[None, :]
    row0 = jnp.sum(jnp.where(back_hot[None, None], jnp.swapaxes(rels, 1, 2)[:, :, None, :], 0.0), axis=-1)
    rows = tokens[:, :, 0, :]
    state = state_init[:, 0, :]
    kept0 = forward_layer(0, block_len, small, row0[0], valid, weights, rows, state)
    kept1 = forward_layer(1, block_len, small, row0[1], valid, weights, kept0.acts, state)
    acts = jnp.where(core == 0, kept0.acts, kept1.acts)[None, :, :, None, :]
    final_state = kept1.final[:, None, :]
    docs = lax.axis_size("dp")
    grad1 = backward_layer(
        1, docs, block_len, small, row0[1], valid, weights, cotangent[:, :, 0, :], kept0.acts, state, kept1
    )
    grad0 = backward_layer(
        0, docs, block_len, small, row0[0], valid, weights, grad1.ig, rows, state, kept0, grad1.dw
    )
    input_grads = jnp.where(core == 0, grad0.ig, grad1.ig)[None, :, :, None, :]
    full, sums = sum_gradients(docs, grad0.dw, jnp.concatenate([grad0.small, grad1.small]))
    width = heads * (w_qkv.shape[3] // chip_heads)
    sums = sums.reshape(3, 2, SMALL_ROWS, model)
    everywhere = sums[2]
    own = lax.dynamic_index_in_dim(everywhere, core, 0, keepdims=False)
    by_core = jnp.where(core == 0, sums[:2], sums[1::-1])
    by_core = lax.dynamic_index_in_dim(by_core, core, 1, keepdims=False)
    qkv_grad, out_grad, up_grad, down_grad, state_qkv_grad, state_out_grad = place_gradients(
        grad1.full, grad0.full, full, width, hidden
    )
    by_distance = by_core[:, BY_DISTANCE, : heads * block_len].reshape(chip_heads, block_len)
    by_bucket = jnp.sum(jnp.where(back_hot[:, :, None], by_distance.T[:, None, :], 0.0), axis=0)
    return (
        acts,
        input_grads,
        final_state,
        own[GAIN0 : GAIN1 + 1][None],
        own[SHIFT0 : SHIFT1 + 1][None],
        qkv_grad,
        out_grad,
        by_bucket[None],
        up_grad,
        by_core[:, UP_BIAS, :hidden].reshape(1, 2 * hidden),
        down_grad,
        own[DOWN_BIAS][None],
        everywhere[1, SGAIN],
        everywhere[1, SSHIFT],
        state_qkv_grad,
        state_out_grad,
        everywhere[1, GATE],
    )


def solution(mesh):
    in_specs = (
        P(None, "mp", "dp", None),
        P(None, None, "dp"),
        P(),
        P("mp", "dp", None),
        P("section", None, None),
        P("section", None, None),
        P("section", None, None, "mp"),
        P("section", "mp", None),
        P("section", None, "mp"),
        P("section", None, "mp"),
        P("section", "mp"),
        P("section", "mp", None),
        P("section", None),
        P(),
        P(),
        P(None, None, "mp"),
        P("mp", None),
        P(),
        P(None, "mp", "dp", None),
    )
    out_specs = (
        P("section", None, "mp", "dp", None),
        P("section", None, "mp", "dp", None),
        P("mp", "dp", None),
        P("section", None, None),
        P("section", None, None),
        P("section", None, None, "mp"),
        P("section", "mp", None),
        P("section", None, "mp"),
        P("section", None, "mp"),
        P("section", "mp"),
        P("section", "mp", None),
        P("section", None),
        P(),
        P(),
        P(None, None, "mp"),
        P("mp", None),
        P(),
    )
    return jax.shard_map(local_part, mesh=mesh, in_specs=in_specs, out_specs=out_specs, check_vma=False)
```

```python
from functools import partial
from types import SimpleNamespace

import jax
import jax.numpy as jnp
from jax import lax
from jax.experimental import pallas as pl
from jax.experimental.pallas import tpu as pltpu
from jax.sharding import PartitionSpec as P

MESH = pl.DeviceIdType.MESH
f32, bf16 = jnp.float32, jnp.bfloat16
eps = 1e-05
negative = -1000000000.0
VMEM_LIMIT = 60 * 1024 * 1024


def dot(left, right):
    return lax.dot_general(left, right, (((1,), (0,)), ((), ())), preferred_element_type=f32)


def dot_nt(left, right):
    return lax.dot_general(left, right, (((1,), (1,)), ((), ())), preferred_element_type=f32)


def dot_tn(left, right):
    return lax.dot_general(left, right, (((0,), (0,)), ((), ())), preferred_element_type=f32)


def norm_parts(values):
    average = jnp.mean(values, axis=-1, keepdims=True)
    centered = values - average
    spread = jnp.mean(centered * centered, axis=-1, keepdims=True)
    scale = lax.rsqrt(spread + eps)
    return centered * scale, scale


def layer_norm(values, gain, shift):
    return norm_parts(values)[0] * gain + shift


class Place:
    def __init__(self, rows):
        self.c, self.x = lax.axis_index("section"), lax.axis_index("mp")
        self.core = {"section": 1 - self.c}
        self.chip = {"mp": 1 - self.x}
        self.quarter, self.half = rows // 4, rows // 2

    def rows(self, x_other=False, c_other=False):
        x = 1 - self.x if x_other else self.x
        c = 1 - self.c if c_other else self.c
        return pl.ds(pl.multiple_of(x * self.half + c * self.quarter, self.quarter), self.quarter)

    def chip_rows(self, x_other=False):
        x = 1 - self.x if x_other else self.x
        return pl.ds(pl.multiple_of(x * self.half, self.half), self.half)

    def core_rows(self, c_other=False):
        c = 1 - self.c if c_other else self.c
        return pl.ds(pl.multiple_of(c * self.quarter, self.quarter), self.quarter)

    def meet(self):
        barrier = pltpu.get_barrier_semaphore()
        for other in (self.core, self.chip):
            pl.semaphore_signal(barrier, inc=1, device_id=other, device_id_type=MESH)
        pl.semaphore_wait(barrier, 2)


class Net:
    def __init__(self, send_sems, recv_sems):
        self.send_sems, self.recv_sems, self.copies = send_sems, recv_sems, []

    def copy(self, source, target, device):
        index = len(self.copies)
        made = pltpu.make_async_remote_copy(
            src_ref=source,
            dst_ref=target,
            send_sem=self.send_sems.at[index],
            recv_sem=self.recv_sems.at[index],
            device_id=device,
            device_id_type=MESH,
        )
        made.start()
        self.copies.append(made)
        return made

    def sent(self, *copies):
        for made in copies:
            made.wait_send()
        self.copies = [None if any(held is made for made in copies) else held for held in self.copies]

    def drain(self):
        for made in self.copies:
            if made is not None:
                made.wait_send()


class Local:
    def __init__(self, sems):
        self.sems, self.copies, self.waited = sems, [], set()

    def copy(self, source, target):
        made = pltpu.make_async_copy(source, target, self.sems.at[len(self.copies)])
        made.start()
        self.copies.append(made)
        return len(self.copies) - 1

    def wait(self, *indices):
        for index in indices:
            if index not in self.waited:
                self.waited.add(index)
                self.copies[index].wait()

    def drain(self):
        self.wait(*range(len(self.copies)))


class Gather:
    def __init__(self, place, net, buffer):
        self.place, self.net, self.buffer = place, net, buffer

    def start(self):
        own = self.buffer.at[self.place.rows()]
        self.from_chip = self.net.copy(own, own, self.place.chip)
        self.from_core = self.net.copy(own, own, self.place.core)

    def forward(self):
        self.from_chip.wait_recv()
        passed = self.buffer.at[self.place.rows(x_other=True)]
        self.passed = self.net.copy(passed, passed, self.place.core)

    def finish(self):
        self.from_core.wait_recv()
        self.passed.wait_recv()


class Scatter:
    def __init__(self, place, net, part, near, out, far):
        self.place, self.net, self.part = place, net, part
        self.near, self.out, self.far = near, out, far

    def send(self, x_other):
        slot = 0 if x_other else 1
        rows = self.place.rows(x_other=x_other, c_other=True)
        made = self.net.copy(self.part.at[rows], self.near.at[slot], self.place.core)
        if x_other:
            self.first = made
        else:
            self.second = made

    def middle(self):
        self.first.wait_recv()
        mine = self.part[self.place.rows(x_other=True), :].astype(f32)
        self.out[...] = (mine + self.near[0].astype(f32)).astype(bf16)
        self.across = self.net.copy(self.out, self.far, self.place.chip)

    def finish(self):
        self.second.wait_recv()
        total = self.part[self.place.rows(), :].astype(f32) + self.near[1].astype(f32)
        self.across.wait_recv()
        return total + self.far[...].astype(f32)

    def release(self):
        self.net.sent(self.first, self.second, self.across)


def share_kernel(block_len, qkv, out, up, down, sqkv, sout, small, cot, *rest):
    targets, cot_all = rest[:7], rest[7]
    staged, cot_staged, (local_sems, send_sems, recv_sems) = rest[8:15], rest[15], rest[16:]
    place = Place(block_len)
    net, local = Net(send_sems, recv_sems), Local(local_sems)
    layer = place.c

    def half(array, axis, c):
        width = array.shape[axis] // 2
        index = [slice(None)] * len(array.shape)
        index[axis] = pl.ds(pl.multiple_of(c * width, width), width)
        return array.at[tuple(index)]

    shared = ((qkv, 2), (out, 0), (up, 1), (down, 0))
    kept = [half(array, axis, place.c) for array, axis in shared + ((sqkv, 2), (sout, 0))] + [small]
    sent = [half(array, axis, 1 - place.c) for array, axis in shared] + [small]
    finals = [target.at[layer] for target in targets[:4]] + [targets[4], targets[5], targets[6].at[layer]]
    place.meet()
    across, near = [], []
    for block in range(2):
        own, target = cot.at[block, place.core_rows()], cot_all.at[block, place.rows()]
        across.append(net.copy(own, target, place.chip))
        near.append(net.copy(own, target, place.core))
    for source, target in zip(sent, finals[:4] + finals[6:]):
        near.append(net.copy(source, target, place.core))
    cot_in = [local.copy(cot.at[block, place.core_rows()], cot_staged.at[block]) for block in range(2)]
    inward = [local.copy(source, stage) for source, stage in zip(kept, staged)]
    for block in range(2):
        local.wait(cot_in[block])
        local.copy(cot_staged.at[block], cot_all.at[block, place.rows()])
    for index, stage, target in zip(inward, staged, finals):
        local.wait(index)
        local.copy(stage, target)
    for block in range(2):
        across[block].wait_recv()
        passed = cot_all.at[block, place.rows(x_other=True)]
        near.append(net.copy(passed, passed, place.core))
    for made in near:
        made.wait_recv()
    local.drain()
    net.drain()


def share_weights(block_len, qkv, out, up, down, sqkv, sout, small, cot):
    def halved(shape, axis, stacked=True):
        shape = list(shape)
        shape[axis] //= 2
        return jax.ShapeDtypeStruct(([2] if stacked else []) + shape, bf16)

    anywhere = pl.BlockSpec(memory_space=pl.ANY)
    return pl.pallas_call(
        partial(share_kernel, block_len),
        out_shape=(
            halved(qkv.shape, 2),
            halved(out.shape, 0),
            halved(up.shape, 1),
            halved(down.shape, 0),
            halved(sqkv.shape, 2, False),
            halved(sout.shape, 0, False),
            jax.ShapeDtypeStruct((2,) + small.shape, f32),
            jax.ShapeDtypeStruct((2, block_len, cot.shape[2]), bf16),
        ),
        in_specs=[anywhere] * 8,
        out_specs=[anywhere] * 8,
        scratch_shapes=[
            pltpu.VMEM(halved(array.shape, axis, False).shape, bf16)
            for array, axis in ((qkv, 2), (out, 0), (up, 1), (down, 0), (sqkv, 2), (sout, 0))
        ]
        + [
            pltpu.VMEM(small.shape, f32),
            pltpu.VMEM((2, block_len // 4, cot.shape[2]), bf16),
            pltpu.SemaphoreType.DMA((18,)),
            pltpu.SemaphoreType.DMA((11,)),
            pltpu.SemaphoreType.DMA((11,)),
        ],
        compiler_params=pltpu.CompilerParams(
            collective_id=0, has_side_effects=True, vmem_limit_bytes=VMEM_LIMIT
        ),
        name="share_weights",
    )(qkv, out, up, down, sqkv, sout, small, cot)


def fill_bias(bias, row0):
    head_count, length = row0.shape
    for head in range(head_count):
        start = jnp.broadcast_to(row0[head : head + 1, :], (bias.shape[1], length))
        rolled = pltpu.roll(start, 0, axis=1, stride=1, stride_axis=0)
        bias[head, :, :length] = rolled
        bias[head, :, length:] = rolled


def bias_columns(index, chunk, length):
    return pl.ds(pl.multiple_of(length - index * chunk, chunk), length)


def window_logits(query, key_cur, key_prev, bias, valid, block, first_row, scale):
    logits = dot_nt(query, key_cur)
    rows = first_row + lax.broadcasted_iota(jnp.int32, logits.shape, 0)
    here = lax.broadcasted_iota(jnp.int32, logits.shape, 1) <= rows
    usable = valid[block : block + 1, :] > 0.5
    if key_prev is None:
        keep = here & usable
    else:
        logits = jnp.where(here, logits, dot_nt(query, key_prev))
        keep = jnp.where(here, valid[block : block + 1, :], valid[block - 1 : block, :]) > 0.5
    return jnp.where(keep, logits * scale + bias, negative), here


def forward_kernel(layer, names, *refs):
    r = SimpleNamespace(**dict(zip(names, refs)))
    rec = layer == 1
    length = r.u_v.shape[1]
    heads = r.row0.shape[0]
    head_size = r.att_v.shape[2] // heads
    width = heads * head_size
    scale = head_size ** (-0.5)
    place = Place(length)
    net, local = Net(r.send_sems, r.recv_sems), Local(r.local_sems)
    chunk = min(128, length)

    place.meet()
    load = [local.copy(r.wqkv.at[layer], r.wqkv_v), local.copy(r.wout.at[layer], r.wout_v)]
    load_mlp = [local.copy(r.wup.at[layer], r.wup_v), local.copy(r.wdown.at[layer], r.wdown_v)]
    load_state = []
    if rec:
        load_state = [local.copy(r.wsqkv, r.wsqkv_v), local.copy(r.wsout, r.wsout_v)]

    gain = lambda index: r.gain[index : index + 1, :]
    shift = lambda index: r.shift[index : index + 1, :]

    def gather(buffer):
        return Gather(place, net, buffer)

    scatter_count = [0]

    def scatter():
        index = scatter_count[0]
        scatter_count[0] += 1
        return Scatter(
            place, net, r.part.at[index], r.near.at[index], r.out.at[index], r.far.at[index]
        )

    def norm_state(rows, index):
        r.sn_v[index, place.rows(), :] = layer_norm(rows, r.sgain[...], r.sshift[...]).astype(bf16)

    def norm_first(block):
        rows = r.x[block, place.core_rows(), :].astype(f32)
        r.u_v[block, place.rows(), :] = layer_norm(rows, gain(0), shift(0)).astype(bf16)

    def project(source, weights, target):
        for part in range(3):
            target[:, part * width : (part + 1) * width] = dot(source[...], weights[part]).astype(bf16)

    def reduce_from(values, weights, to):
        columns = weights.shape[1]
        step = min(512, columns)
        for x_other in (True, False):
            rows = place.chip_rows(x_other)

            @pl.loop(0, columns // step)
            def _(index):
                at = pl.ds(pl.multiple_of(index * step, step), step)
                to.part[rows, at] = dot(values[rows, :], weights[:, at]).astype(bf16)

            to.send(x_other)

    def attend(block):
        qkv = r.qkv_v.at[block]
        prev = r.qkv_v.at[block - 1] if block > 0 else None

        @pl.loop(0, length // chunk)
        def _(index):
            at = pl.ds(pl.multiple_of(index * chunk, chunk), chunk)
            lses = []
            for head in range(heads):
                q_at = slice(head * head_size, (head + 1) * head_size)
                k_at = slice(width + head * head_size, width + (head + 1) * head_size)
                v_at = slice(2 * width + head * head_size, 2 * width + (head + 1) * head_size)
                query = qkv[at, q_at]
                logits, here = window_logits(
                    query,
                    qkv[:, k_at],
                    None if prev is None else prev[:, k_at],
                    r.bias[head, :, bias_columns(index, chunk, length)],
                    r.valid,
                    block,
                    index * chunk,
                    scale,
                )
                peak = jnp.max(logits, axis=-1, keepdims=True)
                if rec:
                    state = r.sqkv_v.at[block]
                    state_logits = dot_nt(query, state[:, k_at]) * scale
                    peak = jnp.maximum(peak, jnp.max(state_logits, axis=-1, keepdims=True))
                probs = jnp.exp(logits - peak)
                total = jnp.sum(probs, axis=-1, keepdims=True)
                if prev is None:
                    result = dot(probs.astype(bf16), qkv[:, v_at])
                else:
                    result = dot(jnp.where(here, probs, 0.0).astype(bf16), qkv[:, v_at])
                    result += dot(jnp.where(here, 0.0, probs).astype(bf16), prev[:, v_at])
                if rec:
                    state_probs = jnp.exp(state_logits - peak)
                    total += jnp.sum(state_probs, axis=-1, keepdims=True)
                    result += dot(state_probs.astype(bf16), state[:, v_at])
                r.att_v[block, at, q_at] = (result / total).astype(bf16)
                lses.append(peak + jnp.log(total))
            lane = lax.broadcasted_iota(jnp.int32, (chunk, 128), 1)
            packed = jnp.zeros((chunk, 128), f32)
            for head in range(heads):
                packed = jnp.where(lane == head, lses[head], packed)
            r.lse_v[block, at, :] = packed

    def recur(block):
        qkv, state = r.qkv_v.at[block], r.sqkv_v.at[block]

        @pl.loop(0, length // chunk)
        def _(index):
            at = pl.ds(pl.multiple_of(index * chunk, chunk), chunk)
            lses = []
            for head in range(heads):
                q_at = slice(head * head_size, (head + 1) * head_size)
                k_at = slice(width + head * head_size, width + (head + 1) * head_size)
                v_at = slice(2 * width + head * head_size, 2 * width + (head + 1) * head_size)
                logits = dot_nt(state[at, q_at], qkv[:, k_at]) * scale
                logits = jnp.where(r.valid[block : block + 1, :] > 0.5, logits, negative)
                peak = jnp.max(logits, axis=-1, keepdims=True)
                probs = jnp.exp(logits - peak)
                total = jnp.sum(probs, axis=-1, keepdims=True)
                r.sout_v[block, at, q_at] = (dot(probs.astype(bf16), qkv[:, v_at]) / total).astype(bf16)
                lses.append(peak + jnp.log(total))
            if block == 0:
                lane = lax.broadcasted_iota(jnp.int32, (chunk, 128), 1)
                packed = jnp.zeros((chunk, 128), f32)
                for head in range(heads):
                    packed = jnp.where(lane == head, lses[head], packed)
                r.rlse_v[at, :] = packed

    def take_branch(block, from_out):
        rows = r.x[block, place.core_rows(), :].astype(f32) + from_out.finish()
        r.h_v[block] = rows
        r.wn_v[block, place.rows(), :] = layer_norm(rows, gain(1), shift(1)).astype(bf16)

    def feed_up(block):
        columns = r.wup_v.shape[1]
        step = 256

        @pl.loop(0, columns // step)
        def _(index):
            at = pl.ds(pl.multiple_of(index * step, step), step)
            pre = dot(r.wn_v[block], r.wup_v[:, at]) + r.up_bias[:, at]
            r.pre_v[block, :, at] = pre.astype(bf16)
            r.act_v[block, :, at] = (0.5 * pre * (1.0 + lax.erf(pre * (0.5**0.5)))).astype(bf16)

    def take_result(block, from_down):
        rows = r.h_v[block] + from_down.finish() + r.down_bias[...]
        own = r.acts_v.at[block, place.core_rows()]
        own[...] = rows.astype(bf16)
        return net.copy(own, own, place.core)

    branch = [scatter(), scatter()]
    result = [scatter(), scatter()]
    first = [gather(r.u_v.at[block]) for block in range(2)]
    second = [gather(r.wn_v.at[block]) for block in range(2)]
    if rec:
        update = [scatter(), scatter()]
        state = [gather(r.sn_v.at[block]) for block in range(2)]
        gate = r.gate[...]
        norm_state(r.state[place.core_rows(), :].astype(f32), 0)
        state[0].start()
    norm_first(0)
    first[0].start()
    norm_first(1)
    first[1].start()
    fill_bias(r.bias, r.row0)
    if rec:
        state[0].forward()
    first[0].forward()
    if rec:
        state[0].finish()
        local.wait(*load_state)
        project(r.sn_v.at[0], r.wsqkv_v, r.sqkv_v.at[0])
    first[0].finish()
    local.wait(*load)
    project(r.u_v.at[0], r.wqkv_v, r.qkv_v.at[0])
    if rec:
        recur(0)
        reduce_from(r.sout_v.at[0], r.wsout_v, update[0])
    else:
        attend(0)
    first[1].forward()
    if rec:
        update[0].middle()
        attend(0)
    reduce_from(r.att_v.at[0], r.wout_v, branch[0])
    if not rec:
        branch[0].middle()
    first[1].finish()
    project(r.u_v.at[1], r.wqkv_v, r.qkv_v.at[1])
    local.copy(r.u_v, r.u)
    local.copy(r.qkv_v, r.qkv)
    if rec:
        branch[0].middle()
        update_rows = update[0].finish()
        r.z_v[...] = update_rows
        state_rows = gate * r.state[place.core_rows(), :].astype(f32) + (1.0 - gate) * update_rows
        r.s1_v[...] = state_rows
        norm_state(state_rows, 1)
        state[1].start()
        local.copy(r.z_v, r.z)
        local.copy(r.s1_v, r.s1)
    else:
        attend(1)
        reduce_from(r.att_v.at[1], r.wout_v, branch[1])
    take_branch(0, branch[0])
    second[0].start()
    if rec:
        state[1].forward()
        state[1].finish()
        project(r.sn_v.at[1], r.wsqkv_v, r.sqkv_v.at[1])
        local.copy(r.sn_v, r.sn)
        local.copy(r.sqkv_v, r.sqkv)
        recur(1)
        reduce_from(r.sout_v.at[1], r.wsout_v, update[1])
        local.copy(r.sout_v, r.sout)
        local.copy(r.rlse_v, r.rlse)
        attend(1)
        update[1].middle()
        reduce_from(r.att_v.at[1], r.wout_v, branch[1])
    local.copy(r.att_v, r.att)
    local.copy(r.lse_v, r.lse)
    second[0].forward()
    branch[1].middle()
    second[0].finish()
    local.wait(*load_mlp)
    feed_up(0)
    reduce_from(r.act_v.at[0], r.wdown_v, result[0])
    take_branch(1, branch[1])
    second[1].start()
    local.copy(r.h_v, r.h)
    result[0].middle()
    second[1].forward()
    second[1].finish()
    local.copy(r.wn_v, r.wn)
    feed_up(1)
    local.copy(r.pre_v, r.pre)
    local.copy(r.act_v, r.act)
    reduce_from(r.act_v.at[1], r.wdown_v, result[1])
    sent = [take_result(0, result[0])]
    result[1].middle()
    if rec:
        own = r.final_v.at[place.core_rows()]
        own[...] = gate * r.s1_v[...] + (1.0 - gate) * update[1].finish()
        sent.append(net.copy(own, own, place.core))
    sent.append(take_result(1, result[1]))
    for made in sent:
        made.wait_recv()
    local.copy(r.acts_v, r.acts)
    if rec:
        local.copy(r.final_v, r.final)
    local.drain()
    net.drain()


def forward_layer(layer, block_len, small, row0, valid, weights, rows, state):
    rec = layer == 1
    wqkv, wout, wup, wdown = weights[:4]
    model = rows.shape[2]
    width, hidden = wqkv.shape[3], wup.shape[2]
    quarter = block_len // 4
    heads = row0.shape[0]

    def held(shape, dtype):
        return jax.ShapeDtypeStruct(shape, dtype)

    outs = dict(
        u=held((2, block_len, model), bf16),
        qkv=held((2, block_len, 3 * width), bf16),
        lse=held((2, block_len, 128), f32),
        att=held((2, block_len, width), bf16),
        wn=held((2, block_len, model), bf16),
        pre=held((2, block_len, hidden), bf16),
        act=held((2, block_len, hidden), bf16),
        h=held((2, quarter, model), f32),
        acts=held((2, 2 * quarter, model), bf16),
    )
    ins = dict(
        x=rows,
        gain=small.gain[layer],
        shift=small.shift[layer],
        up_bias=small.up_bias[layer],
        down_bias=small.down_bias[layer],
        row0=row0,
        valid=valid,
    )
    far_ins = dict(wqkv=wqkv, wout=wout, wup=wup, wdown=wdown)
    if rec:
        outs.update(
            sn=held((2, block_len, model), bf16),
            sqkv=held((2, block_len, 3 * width), bf16),
            rlse=held((block_len, 128), f32),
            sout=held((2, block_len, width), bf16),
            s1=held((quarter, model), f32),
            z=held((quarter, model), f32),
            final=held((2 * quarter, model), f32),
        )
        ins.update(state=state, sgain=small.sgain, sshift=small.sshift, gate=small.gate)
        far_ins.update(wsqkv=weights[4], wsout=weights[5])
    scatters = 6 if rec else 4
    copies = (3 * 6 + 3 * 6 + 3) if rec else (3 * 4 + 3 * 4 + 2)
    scratch = {name + "_v": pltpu.VMEM(kind.shape, kind.dtype) for name, kind in outs.items()}
    scratch.update(
        wqkv_v=pltpu.VMEM(wqkv.shape[1:], bf16),
        wout_v=pltpu.VMEM(wout.shape[1:], bf16),
        wup_v=pltpu.VMEM(wup.shape[1:], bf16),
        wdown_v=pltpu.VMEM(wdown.shape[1:], bf16),
        bias=pltpu.VMEM((heads, min(128, block_len), 2 * block_len), f32),
        part=pltpu.VMEM((scatters, block_len, model), bf16),
        near=pltpu.VMEM((scatters, 2, quarter, model), bf16),
        out=pltpu.VMEM((scatters, quarter, model), bf16),
        far=pltpu.VMEM((scatters, quarter, model), bf16),
        send_sems=pltpu.SemaphoreType.DMA((copies,)),
        recv_sems=pltpu.SemaphoreType.DMA((copies,)),
        local_sems=pltpu.SemaphoreType.DMA((6 + len(outs),)),
    )
    if rec:
        scratch.update(
            wsqkv_v=pltpu.VMEM(weights[4].shape, bf16),
            wsout_v=pltpu.VMEM(weights[5].shape, bf16),
        )
    anywhere = pl.BlockSpec(memory_space=pl.ANY)
    inside = pl.BlockSpec(memory_space=pltpu.VMEM)
    results = pl.pallas_call(
        partial(forward_kernel, layer, [*ins, *far_ins, *outs, *scratch]),
        out_shape=tuple(outs.values()),
        in_specs=[inside] * len(ins) + [anywhere] * len(far_ins),
        out_specs=[anywhere] * len(outs),
        scratch_shapes=list(scratch.values()),
        compiler_params=pltpu.CompilerParams(
            collective_id=1 + layer, has_side_effects=True, vmem_limit_bytes=VMEM_LIMIT
        ),
        name="forward_recurrent" if rec else "forward_local",
    )(*ins.values(), *far_ins.values())
    return SimpleNamespace(**dict(zip(outs, results)))


def ring_place(n, c, d):
    if n % 2:
        at = d

        def index_at(p):
            return p

    else:
        a, b = d // 2, d % 2
        at = a + b * (n - 1 - 2 * a)

        def index_at(p):
            b = p // (n // 2)
            return 2 * (p + b * (n - 1 - 2 * p)) + b

    def flip(p):
        return p + c * (n - 1 - 2 * p)

    return flip(at), lambda p: index_at(flip(p))


class Ring:
    def __init__(self, n):
        self.n, self.c = n, lax.axis_index("section")
        self.q, index_at = ring_place(n, self.c, lax.axis_index("dp"))
        self.after = {"dp": index_at((self.q + 1) % n)}
        self.before = {"dp": index_at((self.q + n - 1) % n)}
        self.core, self.chip = {"section": 1 - self.c}, {"mp": 1 - lax.axis_index("mp")}

    def meet(self):
        barrier = pltpu.get_barrier_semaphore()
        for other in (self.after, self.before, self.core, self.chip):
            pl.semaphore_signal(barrier, inc=1, device_id=other, device_id_type=MESH)
        pl.semaphore_wait(barrier, 4)


def remote(source, target, send, recv, to):
    return pltpu.make_async_remote_copy(
        src_ref=source, dst_ref=target, send_sem=send, recv_sem=recv, device_id=to, device_id_type=MESH
    )


def ring_subs(n, rows, most):
    return max(k for k in range(1, most + 1) if rows // n % (16 * k) == 0)


def ring_scratch(n, rows, model, most):
    subs = ring_subs(n, rows, most)
    sems = pltpu.SemaphoreType.DMA
    return dict(
        held=pltpu.VMEM((n - 1, rows // n, model), bf16),
        rs_send=sems((n - 1, subs)),
        rs_recv=sems((n - 1, subs)),
        ag_send=sems((n - 1, subs)),
        ag_recv=sems((n - 1, subs)),
        core_send=sems((n, subs)),
        core_recv=sems((n, subs)),
        own_sems=sems((subs,)),
    )


class RingSum:
    def __init__(self, ring, mine, full, held, rs_send, rs_recv, ag_send, ag_recv, core_send, core_recv, own_sems):
        self.ring, self.mine, self.full, self.held = ring, mine, full, held
        self.rs_send, self.rs_recv, self.ag_send, self.ag_recv = rs_send, rs_recv, ag_send, ag_recv
        self.core_send, self.core_recv, self.own_sems = core_send, core_recv, own_sems
        self.chunk, self.subs = held.shape[1], own_sems.shape[0]
        self.sub = self.chunk // self.subs
        self.half = (ring.n - 1) * self.subs
        self.total = 2 * self.half
        self.done = 0

    def rows(self, owner, k):
        owner = (owner + 2 * self.ring.n) % self.ring.n
        return pl.ds(pl.multiple_of(owner * self.chunk + k * self.sub, self.sub), self.sub)

    def piece(self, k):
        return slice(k * self.sub, (k + 1) * self.sub) if isinstance(k, int) else pl.ds(
            pl.multiple_of(k * self.sub, self.sub), self.sub
        )

    def summed(self, s, k):
        return self.held.at[s, self.piece(k)]

    def gathered(self, s, k):
        return self.full.at[self.ring.c, self.rows(self.ring.q + 1 - s, k)]

    def reduce(self, s, k, source):
        return remote(source, self.summed(s, k), self.rs_send.at[s, k], self.rs_recv.at[s, k], self.ring.after)

    def gather(self, s, k, source):
        return remote(source, self.gathered(s, k), self.ag_send.at[s, k], self.ag_recv.at[s, k], self.ring.after)

    def to_core(self, s, k, source):
        return remote(source, self.gathered(s, k), self.core_send.at[s, k], self.core_recv.at[s, k], self.ring.core)

    def from_core(self, s, k):
        n, q = self.ring.n, self.ring.q
        target = self.full.at[1 - self.ring.c, self.rows(n - q - s, k)]
        return remote(target, target, self.core_send.at[s, k], self.core_recv.at[s, k], self.ring.core)

    def own(self, k):
        return pltpu.make_async_copy(self.summed(self.ring.n - 2, k), self.gathered(0, k), self.own_sems.at[k])

    def start(self):
        for k in range(self.subs):
            self.reduce(0, k, self.mine.at[self.rows(self.ring.q, k)]).start()

    def add(self, s, k):
        self.reduce(s, k, self.summed(s, k)).wait_recv()
        self.held[s, self.piece(k), :] = (
            self.held[s, self.piece(k), :].astype(f32)
            + self.mine[self.rows(self.ring.q - 1 - s, k), :].astype(f32)
        ).astype(bf16)

    def add_middle(self, s, k):
        self.add(s, k)
        self.reduce(s + 1, k, self.summed(s, k)).start()

    def add_last(self, s, k):
        self.add(s, k)
        self.gather(0, k, self.summed(s, k)).start()
        self.to_core(0, k, self.summed(s, k)).start()
        self.own(k).start()

    def pass_middle(self, s, k):
        at = self.gathered(s + 1, k)
        self.gather(s, k, at).wait_recv()
        self.gather(s + 1, k, at).start()
        self.to_core(s + 1, k, at).start()

    def pass_last(self, s, k):
        at = self.gathered(s + 1, k)
        self.gather(s, k, at).wait_recv()
        self.to_core(s + 1, k, at).start()

    def pump_one(self, t):
        last = self.ring.n - 2
        s, k = t // self.subs, t % self.subs
        kinds = (
            (s < last, self.add_middle, s),
            (s == last, self.add_last, s),
            ((s > last) & (s < 2 * last + 1), self.pass_middle, s - last - 1),
            (s == 2 * last + 1, self.pass_last, s - last - 1),
        )
        for here, act, step in kinds:
            if isinstance(t, int):
                if here:
                    act(step, k)
            else:
                pl.when(here)(partial(act, step, k))

    def pump(self, count=1):
        for _ in range(min(count, self.total - self.done)):
            self.pump_one(self.done)
            self.done += 1

    def pumps_in(self, loop_steps, each):
        each = min(each, (self.total - self.done) // loop_steps)
        base = self.done
        self.done += each * loop_steps

        def pump(index):
            for piece in range(each):
                self.pump_one(base + index * each + piece)

        return pump

    def run(self, until):
        last = self.ring.n - 2
        for first, end, act in (
            (0, last, self.add_middle),
            (last, last + 1, self.add_last),
            (last + 1, 2 * last + 1, self.pass_middle),
            (2 * last + 1, 2 * last + 2, self.pass_last),
        ):
            while self.done < min(end * self.subs, until) and self.done % self.subs:
                self.pump()
            step, stop = self.done // self.subs, min(end, until // self.subs)
            if first <= step < stop:
                base = last + 1 if first > last else 0

                @pl.loop(step - base, stop - base)
                def _(s):
                    for k in range(self.subs):
                        act(s, k)

                self.done = stop * self.subs

    def release_mine(self):
        for k in range(self.subs):
            self.reduce(0, k, self.mine.at[self.rows(self.ring.q, k)]).wait_send()

    def finish(self, released=False):
        self.run(self.total)
        if not released:
            self.release_mine()
        last = self.ring.n - 2

        @pl.loop(0, last + 2)
        def _(s):
            for k in range(self.subs):
                self.from_core(s, k).wait_recv()
                self.to_core(s, k, self.gathered(s, k)).wait_send()

        @pl.loop(0, last + 1)
        def _(s):
            for k in range(self.subs):
                self.gather(s, k, self.gathered(s, k)).wait_send()

        @pl.loop(0, last)
        def _(s):
            for k in range(self.subs):
                self.reduce(s + 1, k, self.summed(s, k)).wait_send()

        for k in range(self.subs):
            self.own(k).wait()


def sum_kernel(n, parts, small, full, small_out, mine, small_held, small_sum, small_far, *rest):
    ring_refs, (small_send, small_recv, local_sems) = rest[:-3], rest[-3:]
    ring = Ring(n)
    flow = RingSum(ring, mine, full, *ring_refs)

    def small_step(s, first):
        source = small if first else small_held.at[s - 1]
        return remote(source, small_held.at[s], small_send.at[s], small_recv.at[s], ring.after)

    load = pltpu.make_async_copy(parts, mine, local_sems.at[0])
    load.start()
    ring.meet()
    small_step(0, True).start()
    load.wait()
    flow.start()

    @pl.loop(0, n - 2)
    def _(s):
        for k in range(flow.subs):
            flow.add_middle(s, k)
        small_step(s, True).wait_recv()
        small_step(s + 1, False).start()

    flow.done = (n - 2) * flow.subs
    flow.run(flow.half)
    small_step(n - 2, True).wait_recv()
    small_out[0] = small[...]

    @pl.loop(0, n - 1)
    def _(s):
        small_out[0] += small_held[s]

    between = remote(small_out.at[0], small_out.at[1], small_send.at[n - 1], small_recv.at[n - 1], ring.core)
    between.start()
    between.wait_recv()
    small_sum[...] = small_out[0] + small_out[1]
    across = remote(small_sum, small_far, small_send.at[n], small_recv.at[n], ring.chip)
    across.start()
    across.wait_recv()
    small_out[2] = small_sum[...] + small_far[...]
    flow.finish()

    @pl.loop(0, n - 1)
    def _(s):
        small_step(s, True).wait_send()

    between.wait_send()
    across.wait_send()


def sum_gradients(n, parts, small):
    rows, model = parts.shape
    anywhere = pl.BlockSpec(memory_space=pl.ANY)
    inside = pl.BlockSpec(memory_space=pltpu.VMEM)
    sems = pltpu.SemaphoreType.DMA
    return pl.pallas_call(
        partial(sum_kernel, n),
        out_shape=(
            jax.ShapeDtypeStruct((2, rows, model), bf16),
            jax.ShapeDtypeStruct((3,) + small.shape, f32),
        ),
        in_specs=[anywhere, inside],
        out_specs=[anywhere, inside],
        scratch_shapes=[
            pltpu.VMEM((rows, model), bf16),
            pltpu.VMEM((n - 1,) + small.shape, f32),
            pltpu.VMEM(small.shape, f32),
            pltpu.VMEM(small.shape, f32),
            *ring_scratch(n, rows, model, 6).values(),
            sems((n + 1,)),
            sems((n + 1,)),
            sems((1,)),
        ],
        compiler_params=pltpu.CompilerParams(
            collective_id=5, has_side_effects=True, vmem_limit_bytes=VMEM_LIMIT
        ),
        name="sum_gradients",
    )(parts, small)


def norm_back(rows, gain, grad):
    normed, scale = norm_parts(rows)
    inner = grad * gain
    means = jnp.mean(inner, axis=-1, keepdims=True), jnp.mean(inner * normed, axis=-1, keepdims=True)
    by_rows = scale * (inner - means[0] - normed * means[1])
    return by_rows, jnp.sum(grad * normed, axis=0, keepdims=True), jnp.sum(grad, axis=0, keepdims=True)


GAIN0, GAIN1, SHIFT0, SHIFT1, DOWN_BIAS, SGAIN, SSHIFT, GATE, UP_BIAS, BY_DISTANCE = range(10)
SMALL_ROWS = 16


def backward_kernel(layer, n, ring_names, names, *refs):
    r = SimpleNamespace(**dict(zip(names, refs)))
    rec = layer == 1
    heads, length = r.row0.shape
    head_size = r.att_v.shape[1] // heads
    width = heads * head_size
    hidden = r.wup_v.shape[1]
    model = r.wup_v.shape[0]
    scale = head_size ** (-0.5)
    place = Place(length)
    net, local = Net(r.send_sems, r.recv_sems), Local(r.local_sems)
    chunk = min(128, length)

    ring = Ring(n)
    r.act, r.by_down = r.work.at[:hidden], r.work.at[hidden:]
    ring_refs = [[getattr(r, name) for name in flow_names] for flow_names in ring_names]
    if rec:
        up_flow = RingSum(ring, r.act, r.full.at[:, :model], *ring_refs[0])
        down_flow = RingSum(ring, r.by_down, r.full.at[:, model:], *ring_refs[1])
        act = [local.copy(r.act_in, r.act), local.copy(r.g_in, r.g)]
    else:
        rest_flow = RingSum(ring, r.mine, r.full, *ring_refs[0])
        parts = local.copy(r.parts, r.mine)
        act = [local.copy(r.act_in, r.act)]
    flows = []

    def launch(flow):
        flow.start()
        flows.append(flow)

    def tick(count=1):
        for _ in range(count):
            for flow in flows:
                flow.pump()

    def tick_at(index, *steps):
        for step in steps:

            @pl.when(index == step)
            def _():
                tick()

    ring.meet()
    wdown = local.copy(r.wdown.at[layer], r.wdown_v)
    pre = local.copy(r.pre, r.pre_v)
    wup = local.copy(r.wup.at[layer], r.wup_v)
    hidden_rows = local.copy(r.h, r.h_v)
    wn = local.copy(r.wn, r.wn_v)
    attention = [
        local.copy(r.wout.at[layer], r.wout_v),
        local.copy(r.qkv, r.qkv_v),
        local.copy(r.att, r.att_v),
        local.copy(r.lse, r.lse_v),
    ]
    if rec:
        attention += [local.copy(r.sqkv, r.sqkv_v), local.copy(r.wsqkv, r.wsqkv_v)]
        chain = [
            local.copy(r.s1, r.s1_v),
            local.copy(r.z, r.z_v),
            local.copy(r.wsout, r.wsout_v),
            local.copy(r.sout, r.sout_v),
            local.copy(r.rlse, r.rlse_v),
        ]
    wqkv = local.copy(r.wqkv.at[layer], r.wqkv_v)

    gain = lambda index: r.gain[index : index + 1, :]
    small = r.small_v
    small[...] = jnp.zeros(small.shape, f32)
    r.dkv[...] = jnp.zeros(r.dkv.shape, f32)
    r.dbias[...] = jnp.zeros(r.dbias.shape, f32)
    if rec:
        r.dskv[...] = jnp.zeros(r.dskv.shape, f32)

    def add_small(index, value):
        small[index : index + 1, :] += value

    def gather(buffer):
        return Gather(place, net, buffer)

    scatter_count = [0]

    def scatter(slot):
        index = scatter_count[0]
        scatter_count[0] += 1
        return Scatter(place, net, r.part.at[slot], r.near.at[index], r.out.at[slot], r.far.at[index])

    def block_rows(block):
        return slice(block * length, (block + 1) * length)

    def own_grad(block):
        return r.gy[block, place.core_rows(), :].astype(bf16).astype(f32)

    def feed_back(block):
        step = 256
        rows = block_rows(block)

        @pl.loop(0, hidden // step)
        def _(index):
            at = pl.ds(pl.multiple_of(index * step, step), step)
            pre = r.pre_v[rows, at].astype(f32)
            by_act = dot_nt(r.g[rows, :], r.wdown_v[at, :])
            below = 0.5 * (1.0 + lax.erf(pre * (0.5**0.5)))
            by_pre = by_act * (below + pre * jnp.exp(-0.5 * pre * pre) * 0.3989422804014327)
            small[UP_BIAS : UP_BIAS + 1, at] += jnp.sum(by_pre, axis=0, keepdims=True)
            r.dpre[rows, at] = by_pre.astype(bf16)

    def reduce_back(terms, to):
        step = min(512, model)
        for x_other in (True, False):
            rows = place.chip_rows(x_other)

            @pl.loop(0, model // step)
            def _(index):
                at = pl.ds(pl.multiple_of(index * step, step), step)
                total = None
                for values, weights in terms:
                    term = dot_nt(values[rows, :], weights[at, :])
                    total = term if total is None else total + term
                to.part[rows, at] = total.astype(bf16)

            to.send(x_other)

    def take_feed(block, from_feed):
        by_norm = from_feed.finish()
        grad = own_grad(block)
        by_rows, by_gain, by_shift = norm_back(r.h_v[block], gain(1), by_norm)
        add_small(GAIN1, by_gain)
        add_small(SHIFT1, by_shift)
        add_small(DOWN_BIAS, jnp.sum(grad, axis=0, keepdims=True))
        total = grad + by_rows
        r.ig_v[block, place.core_rows(), :] = total
        r.hg[pl.ds(place_row(block), place.quarter), :] = total.astype(bf16)

    def place_row(block):
        return pl.multiple_of(block * length + place.x * place.half + place.c * place.quarter, place.quarter)

    def weight_grad(left, right, target, at_row=0):
        step = 256

        @pl.loop(0, left.shape[1] // step)
        def _(index):
            at = pl.ds(pl.multiple_of(index * step, step), step)
            to = pl.ds(pl.multiple_of(at_row + index * step, step), step)
            target[to, :] = dot_tn(left[:, at], right[...]).astype(bf16)

    def projection_grad(normed, grads, target):
        for part in range(3):
            tick()
            to = slice(part * width, (part + 1) * width)

            @pl.loop(0, model // width)
            def _(index):
                at = pl.ds(pl.multiple_of(index * width, width), width)
                target[to, at] = dot_tn(normed[:, at], grads[:, to]).astype(bf16)

    def branch_back(block):
        r.datt[block] = dot_nt(r.hg[block_rows(block), :], r.wout_v[...]).astype(bf16)

    def columns(head, part):
        return slice(part * width + head * head_size, part * width + (head + 1) * head_size)

    def attend_back(block):
        qkv = r.qkv_v.at[block]
        prev = r.qkv_v.at[block - 1] if block > 0 else None
        state = r.sqkv_v.at[block] if rec else None

        @pl.loop(0, length // chunk)
        def _(index):
            tick_at(index, *((1, 2, 3) if rec and block else (1, 3)))
            at = pl.ds(pl.multiple_of(index * chunk, chunk), chunk)
            block_at = pl.ds(pl.multiple_of(block * length + index * chunk, chunk), chunk)
            for head in range(heads):
                q_at, k_at, v_at = (columns(head, part) for part in range(3))
                query, key, value = qkv[at, q_at], qkv[:, k_at], qkv[:, v_at]
                logits, here = window_logits(
                    query,
                    key,
                    None if prev is None else prev[:, k_at],
                    r.bias[head, :, bias_columns(index, chunk, length)],
                    r.valid,
                    block,
                    index * chunk,
                    scale,
                )
                lse = r.lse_v[block, at, head : head + 1]
                probs = jnp.exp(logits - lse)
                grad = r.datt[block, at, q_at]
                delta = jnp.sum(
                    grad.astype(f32) * r.att_v[block_at, q_at].astype(f32), axis=-1, keepdims=True
                )
                by_probs = dot_nt(grad, value)
                if prev is not None:
                    by_probs = jnp.where(here, by_probs, dot_nt(grad, prev[:, v_at]))
                by_logits = probs * (by_probs - delta)
                r.dbias[head, :, bias_columns(index, chunk, length)] += by_logits
                by_logits = by_logits * scale
                if prev is None:
                    low = by_logits.astype(bf16)
                    low_probs = probs.astype(bf16)
                    by_query = dot(low, key)
                else:
                    low = jnp.where(here, by_logits, 0.0).astype(bf16)
                    low_probs = jnp.where(here, probs, 0.0).astype(bf16)
                    low_prev = jnp.where(here, 0.0, by_logits).astype(bf16)
                    low_probs_prev = jnp.where(here, 0.0, probs).astype(bf16)
                    by_query = dot(low, key) + dot(low_prev, prev[:, k_at])
                    r.dkv[block - 1, :, q_at] += dot_tn(low_prev, query)
                    r.dkv[block - 1, :, k_at] += dot_tn(low_probs_prev, grad)
                r.dkv[block, :, q_at] += dot_tn(low, query)
                r.dkv[block, :, k_at] += dot_tn(low_probs, grad)
                if rec:
                    state_probs = jnp.exp(dot_nt(query, state[:, k_at]) * scale - lse)
                    by_state = state_probs * (dot_nt(grad, state[:, v_at]) - delta) * scale
                    low_state = by_state.astype(bf16)
                    by_query += dot(low_state, state[:, k_at])
                    r.dskv[:, q_at] += dot_tn(low_state, query)
                    r.dskv[:, k_at] += dot_tn(state_probs.astype(bf16), grad)
                r.dqkv[block_at, q_at] = by_query.astype(bf16)

    def recur_back():
        qkv, state = r.qkv_v.at[0], r.sqkv_v.at[0]

        @pl.loop(0, length // chunk)
        def _(index):
            tick_at(index, 2)
            at = pl.ds(pl.multiple_of(index * chunk, chunk), chunk)
            for head in range(heads):
                q_at, k_at, v_at = (columns(head, part) for part in range(3))
                query, key, value = state[at, q_at], qkv[:, k_at], qkv[:, v_at]
                logits = dot_nt(query, key) * scale
                logits = jnp.where(r.valid[0:1, :] > 0.5, logits, negative)
                probs = jnp.exp(logits - r.rlse_v[at, head : head + 1])
                grad = r.dsout[at, q_at]
                delta = jnp.sum(
                    grad.astype(f32) * r.sout_v[0, at, q_at].astype(f32), axis=-1, keepdims=True
                )
                low = (probs * (dot_nt(grad, value) - delta) * scale).astype(bf16)
                r.dsqkv[at, q_at] = dot(low, key).astype(bf16)
                r.dkv[0, :, q_at] += dot_tn(low, query)
                r.dkv[0, :, k_at] += dot_tn(probs.astype(bf16), grad)

    def close_keys(block):
        r.dqkv[block_rows(block), width:] = r.dkv[block].astype(bf16)

    def close_state(block):
        r.dsqkv[block_rows(block), width:] = r.dskv[...].astype(bf16)
        if block == 1:
            r.dskv[...] = jnp.zeros(r.dskv.shape, f32)

    def input_back(block, to):
        rows = block_rows(block)
        reduce_back(
            [
                (r.dqkv.at[rows, part * width : (part + 1) * width], r.wqkv_v.at[part])
                for part in range(3)
            ],
            to,
        )

    def state_back(block, to):
        rows = block_rows(block)
        reduce_back(
            [
                (r.dsqkv.at[rows, part * width : (part + 1) * width], r.wsqkv_v.at[part])
                for part in ((0, 1, 2) if block == 0 else (1, 2))
            ],
            to,
        )

    def take_input(block, from_input):
        by_norm = from_input.finish()
        rows = r.x[block, place.core_rows(), :].astype(f32)
        by_rows, by_gain, by_shift = norm_back(rows, gain(0), by_norm)
        add_small(GAIN0, by_gain)
        add_small(SHIFT0, by_shift)
        own = r.ig_v.at[block, place.core_rows()]
        own[...] += by_rows
        return net.copy(own, own, place.core)

    def take_state(rows, from_state):
        by_rows, by_gain, by_shift = norm_back(rows, r.sgain[...], from_state.finish())
        add_small(SGAIN, by_gain)
        add_small(SSHIFT, by_shift)
        return by_rows

    def close_bias():
        tile = r.dbias.shape[1]
        for head in range(heads):
            folded = r.dbias[head, :, :length] + r.dbias[head, :, length:]
            row = lax.broadcasted_iota(jnp.int32, folded.shape, 0)
            bit = 1
            while bit < tile:
                moved = pltpu.roll(folded, length - bit, axis=1)
                folded = jnp.where((row & bit) != 0, moved, folded)
                bit *= 2
            small[BY_DISTANCE : BY_DISTANCE + 1, head * length : (head + 1) * length] = jnp.sum(
                folded, axis=0, keepdims=True
            )

    if rec:
        at_qkv, at_sqkv = 0, 4 * width
    else:
        at_up, at_down, at_qkv = 0, model, model + hidden
    at_out = 3 * width

    feed = [scatter(0), scatter(1)]
    inputs = [scatter(2 if rec else 0), scatter(1)]
    if not rec:
        grads = [gather(r.g.at[block_rows(block)]) for block in range(2)]
    hiddens = [gather(r.hg.at[block_rows(block)]) for block in range(2)]
    if rec:
        states = [scatter(0), scatter(0)]
        updates = gather(r.ug)
    if not rec:
        for block in (1, 0):
            r.g[pl.ds(place_row(block), place.quarter), :] = own_grad(block).astype(bf16)
            grads[block].start()
        local.wait(parts)
        launch(rest_flow)
    fill_bias(r.bias, r.row0)
    local.wait(*act)
    if rec:
        weight_grad(r.act, r.g, r.by_down)
        launch(down_flow)
    else:
        tick()
        grads[1].forward()
        tick()
        grads[1].finish()
    local.wait(wdown, pre, wup)
    feed_back(1)
    tick()
    reduce_back([(r.dpre.at[block_rows(1)], r.wup_v)], feed[1])
    if rec:
        tick()
    else:
        grads[0].forward()
        tick()
        grads[0].finish()
    feed_back(0)
    feed[1].middle()
    tick()
    reduce_back([(r.dpre.at[block_rows(0)], r.wup_v)], feed[0])
    tick()
    feed[0].middle()
    if not rec:
        weight_grad(r.act, r.g, r.by_down)
        down_out = local.copy(r.by_down, r.dw.at[at_down:at_qkv])
    tick()
    local.wait(wn)
    weight_grad(r.wn_v, r.dpre, r.act)
    if rec:
        launch(up_flow)
        sn_in = local.copy(r.sn, r.pre_v)
    else:
        local.copy(r.act, r.dw.at[at_up:at_down])
    tick()
    u_in = local.copy(r.u, r.wn_v)
    local.wait(hidden_rows)
    take_feed(1, feed[1])
    hiddens[1].start()
    tick(2)
    take_feed(0, feed[0])
    hiddens[0].start()
    tick(2)
    hiddens[1].forward()
    tick()
    hiddens[1].finish()
    local.wait(*attention)
    branch_back(1)
    tick()
    attend_back(1)
    close_keys(1)
    feed[0].release()
    feed[1].release()
    if rec:
        close_state(1)
        state_back(1, states[1])
        tick()
    hiddens[0].forward()
    local.wait(wqkv)
    input_back(1, inputs[1])
    if rec:
        states[1].middle()
    tick()
    hiddens[0].finish()
    branch_back(0)
    if rec:
        tick(2)
        local.wait(*chain)
        gate = r.gate[...]
        by_state = take_state(r.s1_v[...], states[1])
        states[1].release()
        before = r.state[place.core_rows(), :].astype(f32)
        add_small(
            GATE,
            jnp.sum(by_state * (before - r.z_v[...]) * gate * (1.0 - gate), axis=0, keepdims=True),
        )
        r.ug[place.rows(), :] = ((1.0 - gate) * by_state).astype(bf16)
        updates.start()
    inputs[1].middle()
    tick()
    attend_back(0)
    tick()
    if rec:
        updates.forward()
        tick()
        updates.finish()
        r.dsout[...] = dot_nt(r.ug[...], r.wsout_v[...]).astype(bf16)
        recur_back()
        tick()
    close_keys(0)
    input_back(0, inputs[0])
    tick()
    if rec:
        close_state(0)
        state_back(0, states[0])
        tick()
    sent = [take_input(1, inputs[1])]
    inputs[0].middle()
    tick()
    if rec:
        states[0].middle()
    weight_grad(r.att_v, r.hg, r.dpre, at_out)
    close_bias()
    local.wait(u_in)
    projection_grad(r.wn_v, r.dqkv, r.dpre)
    local.copy(r.dpre, r.dw.at[at_qkv : at_qkv + 4 * width])
    tick()
    if rec:
        r.dsqkv[block_rows(1), 0:width] = jnp.zeros((length, width), bf16)
        local.wait(sn_in)
        projection_grad(r.pre_v, r.dsqkv, r.g)
        tick()
        weight_grad(r.sout_v.at[0], r.ug, r.g, at_out)
        local.copy(r.g, r.dw.at[at_sqkv:])
    sent.append(take_input(0, inputs[0]))
    if rec:
        take_state(r.state[place.core_rows(), :].astype(f32), states[0])
    local.copy(small, r.small)
    for made in sent:
        made.wait_recv()
    local.copy(r.ig_v, r.ig)
    while any(flow.done < flow.total for flow in flows):
        tick()
    for flow in flows:
        flow.finish()
    local.drain()
    net.drain()


def backward_layer(layer, n, block_len, small, row0, valid, weights, grad_rows, rows, state, kept, parts=None):
    rec = layer == 1
    wqkv, wout, wup, wdown = weights[:4]
    model = rows.shape[2]
    width, hidden = wqkv.shape[3], wup.shape[2]
    quarter = block_len // 4
    heads = row0.shape[0]

    def held(shape, dtype):
        return jax.ShapeDtypeStruct(shape, dtype)

    dw_rows = 8 * width if rec else model + hidden + 4 * width
    ring_rows = model + hidden if rec else parts.shape[0]
    outs = dict(
        full=held((2, ring_rows, model), bf16),
        dw=held((dw_rows, model), bf16),
        small=held((SMALL_ROWS, model), f32),
        ig=held((2, 2 * quarter, model), f32),
    )
    ins = dict(
        gy=grad_rows, x=rows, gain=small.gain[layer], shift=small.shift[layer], row0=row0, valid=valid
    )

    def flat(array):
        return array.reshape((-1,) + array.shape[2:])

    stacked = dict(wqkv=wqkv, wout=wout, wup=wup, wdown=wdown)
    copied = dict(
        qkv=kept.qkv, lse=kept.lse, att=flat(kept.att), wn=flat(kept.wn), pre=flat(kept.pre), h=kept.h
    )
    late = dict(act_in=flat(kept.act), u=flat(kept.u))
    if rec:
        ins.update(state=state, sgain=small.sgain, sshift=small.sshift, gate=small.gate)
        copied.update(wsqkv=weights[4], wsout=weights[5])
        copied.update(sqkv=kept.sqkv, rlse=kept.rlse, sout=kept.sout, s1=kept.s1, z=kept.z)
        late.update(sn=flat(kept.sn), g_in=flat(parts))
    else:
        late.update(parts=parts)
    far_ins = {**stacked, **copied, **late}
    scatters = 6 if rec else 4
    copies = (3 * 6 + 3 * 3 + 2) if rec else (3 * 4 + 3 * 4 + 2)
    scratch = dict(small_v=pltpu.VMEM(outs["small"].shape, f32), ig_v=pltpu.VMEM(outs["ig"].shape, f32))
    for name, array in stacked.items():
        scratch[name + "_v"] = pltpu.VMEM(array.shape[1:], array.dtype)
    for name, array in copied.items():
        scratch[name + "_v"] = pltpu.VMEM(array.shape, array.dtype)
    scratch.update(
        g=pltpu.VMEM((2 * block_len, model), bf16),
        hg=pltpu.VMEM((2 * block_len, model), bf16),
        work=pltpu.VMEM((2 * hidden, model), bf16),
        dpre=pltpu.VMEM((2 * block_len, hidden), bf16),
        datt=pltpu.VMEM((2, block_len, width), bf16),
        dkv=pltpu.VMEM((2, block_len, 2 * width), f32),
        dqkv=pltpu.VMEM((2 * block_len, 3 * width), bf16),
        dbias=pltpu.VMEM((heads, min(128, block_len), 2 * block_len), f32),
        bias=pltpu.VMEM((heads, min(128, block_len), 2 * block_len), f32),
        part=pltpu.VMEM((scatters // 2, block_len, model), bf16),
        near=pltpu.VMEM((scatters, 2, quarter, model), bf16),
        out=pltpu.VMEM((scatters // 2, quarter, model), bf16),
        far=pltpu.VMEM((scatters, quarter, model), bf16),
        send_sems=pltpu.SemaphoreType.DMA((copies,)),
        recv_sems=pltpu.SemaphoreType.DMA((copies,)),
        local_sems=pltpu.SemaphoreType.DMA((len(far_ins) + 6,)),
    )
    if rec:
        scratch.update(
            ug=pltpu.VMEM((block_len, model), bf16),
            dsout=pltpu.VMEM((block_len, width), bf16),
            dskv=pltpu.VMEM((block_len, 2 * width), f32),
            dsqkv=pltpu.VMEM((2 * block_len, 3 * width), bf16),
        )
    else:
        scratch.update(mine=pltpu.VMEM((ring_rows, model), bf16))
    ring_names = []
    for flow_rows in (model, hidden) if rec else (ring_rows,):
        flow_scratch = ring_scratch(n, flow_rows, model, 2)
        flow_scratch = {name + str(len(ring_names)): kind for name, kind in flow_scratch.items()}
        scratch.update(flow_scratch)
        ring_names.append(list(flow_scratch))
    anywhere = pl.BlockSpec(memory_space=pl.ANY)
    inside = pl.BlockSpec(memory_space=pltpu.VMEM)
    results = pl.pallas_call(
        partial(backward_kernel, layer, n, ring_names, [*ins, *far_ins, *outs, *scratch]),
        out_shape=tuple(outs.values()),
        in_specs=[inside] * len(ins) + [anywhere] * len(far_ins),
        out_specs=[anywhere] * len(outs),
        scratch_shapes=list(scratch.values()),
        compiler_params=pltpu.CompilerParams(
            collective_id=3 + layer, has_side_effects=True, vmem_limit_bytes=VMEM_LIMIT
        ),
        name="backward_recurrent" if rec else "backward_local",
    )(*ins.values(), *far_ins.values())
    return SimpleNamespace(**dict(zip(outs, results)))


def place_kernel(
    width, hidden, feed_1, rest_1, full_0, qkv, out, up, down, sqkv, sout, inward, outward, in_sems, out_sems
):
    model = full_0.shape[2]
    layer = lax.axis_index("section")
    slots = inward.shape[0]
    at_rest = model + hidden
    jobs = []
    for half in range(2):
        columns = slice(half * width, (half + 1) * width)

        def projection(target):
            return [target.at[index : index + width, columns] for index in range(0, model, width)]

        for row in range(0, model, width):
            wide = slice(half * hidden, (half + 1) * hidden)
            jobs.append((half, (feed_1, row), row, [up.at[0, row : row + width, wide]]))
        for row in range(0, hidden, width):
            at = half * hidden + row
            jobs.append((half, (feed_1, model + row), model + row, [down.at[0, at : at + width]]))
        for part in range(3):
            row = part * width
            jobs.append((half, (rest_1, row), at_rest + row, projection(qkv.at[0, part])))
            jobs.append((half, (rest_1, 4 * width + row), None, projection(sqkv.at[part])))
        jobs.append((half, (rest_1, 3 * width), at_rest + 3 * width, [out.at[0, columns]]))
        jobs.append((half, (rest_1, 7 * width), None, [sout.at[columns]]))

    def load(index, start):
        half, (array, row), row_0, _ = jobs[index]
        slot = index % slots

        def made(source, at):
            return pltpu.make_async_copy(source.at[half, at : at + width], inward.at[slot], in_sems.at[slot])

        if not start:
            made(array, row).wait()
        elif row_0 is None:
            made(array, row).start()
        else:
            pl.when(layer == 1)(lambda: made(array, row).start())
            pl.when(layer == 0)(lambda: made(full_0, row_0).start())

    def stores(index):
        targets, slot = jobs[index][3], index % slots
        step = model // len(targets)
        return [
            pltpu.make_async_copy(
                outward.at[slot, :, k * step : (k + 1) * step], target, out_sems.at[slot, k]
            )
            for k, target in enumerate(targets)
        ]

    for index in range(slots):
        load(index, True)
    for index in range(len(jobs)):
        slot = index % slots
        load(index, False)
        if index >= slots:
            for made in stores(index - slots):
                made.wait()
        outward[slot] = inward[slot].astype(f32)
        for made in stores(index):
            made.start()
        if index + slots < len(jobs):
            load(index + slots, True)
    for index in range(len(jobs) - slots, len(jobs)):
        for made in stores(index):
            made.wait()


def place_gradients(feed_1, rest_1, full_0, width, hidden):
    model = full_0.shape[2]
    anywhere = pl.BlockSpec(memory_space=pl.ANY)
    slots = 4
    shapes = (
        (1, 3, model, 2 * width),
        (1, 2 * width, model),
        (1, model, 2 * hidden),
        (1, 2 * hidden, model),
        (3, model, 2 * width),
        (2 * width, model),
    )
    return pl.pallas_call(
        partial(place_kernel, width, hidden),
        out_shape=[jax.ShapeDtypeStruct(shape, f32) for shape in shapes],
        in_specs=[anywhere] * 3,
        out_specs=[anywhere] * 6,
        scratch_shapes=[
            pltpu.VMEM((slots, width, model), bf16),
            pltpu.VMEM((slots, width, model), f32),
            pltpu.SemaphoreType.DMA((slots,)),
            pltpu.SemaphoreType.DMA((slots, model // width)),
        ],
        compiler_params=pltpu.CompilerParams(vmem_limit_bytes=VMEM_LIMIT),
        name="place_gradients",
    )(feed_1, rest_1, full_0)


def pack_small(arrays, width):
    flat = jnp.concatenate([array.astype(f32).reshape(-1) for array in arrays])
    return jnp.pad(flat, (0, -flat.size % (8 * width))).reshape(-1, width)


def unpack_small(packed, shapes):
    flat = packed.reshape(packed.shape[0], -1)
    found, at = [], 0
    for shape in shapes:
        size = 1
        for extent in shape:
            size *= extent
        found.append(flat[:, at : at + size].reshape((packed.shape[0],) + tuple(shape)))
        at += size
    return found


def local_part(
    tokens, valid_mask, buckets, state_init, norm_gain, norm_shift, w_qkv, w_out, rel_bias, w_up, up_bias,
    w_down, down_bias, state_gain, state_shift, w_state_qkv, w_state_out, gate_bias, cotangent,
):
    block_len = valid_mask.shape[1]
    model = tokens.shape[3]
    core = lax.axis_index("section")
    bucket_count, chip_heads = rel_bias.shape[1:]
    heads = chip_heads // 2
    hidden = w_up.shape[2] // 2
    valid = valid_mask[:, :, 0].astype(f32)
    packed = pack_small([norm_gain[0], norm_shift[0], down_bias[0], up_bias[0], rel_bias[0]], model)
    cot_rows = cotangent[:, :, 0, :]
    *weights, small_all, cot_all = share_weights(
        block_len, w_qkv[0], w_out[0], w_up[0], w_down[0], w_state_qkv, w_state_out, packed, cot_rows
    )
    gains, shifts, down_biases, up_biases, rels = unpack_small(
        small_all, [(2, model), (2, model), (1, model), (1, 2 * hidden), (bucket_count, chip_heads)]
    )
    small = SimpleNamespace(
        gain=gains,
        shift=shifts,
        down_bias=down_biases,
        up_bias=lax.dynamic_slice_in_dim(up_biases, core * hidden, hidden, 2),
        sgain=state_gain[None],
        sshift=state_shift[None],
        gate=jax.nn.sigmoid(gate_bias)[None],
    )
    rels = lax.dynamic_slice_in_dim(rels, core * heads, heads, 2)
    back = jnp.concatenate([buckets[:1], buckets[:0:-1]])
    back_hot = back[:, None] == jnp.arange(bucket_count)[None, :]
    row0 = jnp.sum(jnp.where(back_hot[None, None], jnp.swapaxes(rels, 1, 2)[:, :, None, :], 0.0), axis=-1)
    rows = tokens[:, :, 0, :]
    state = state_init[:, 0, :]
    kept0 = forward_layer(0, block_len, small, row0[0], valid, weights, rows, state)
    kept1 = forward_layer(1, block_len, small, row0[1], valid, weights, kept0.acts, state)
    acts = jnp.where(core == 0, kept0.acts, kept1.acts)[None, :, :, None, :]
    final_state = kept1.final[:, None, :]
    docs = lax.axis_size("dp")
    grad1 = backward_layer(
        1, docs, block_len, small, row0[1], valid, weights, cot_rows, kept0.acts, state, kept1, cot_all
    )
    grad0 = backward_layer(
        0, docs, block_len, small, row0[0], valid, weights, grad1.ig, rows, state, kept0, grad1.dw
    )
    input_grads = jnp.where(core == 0, grad0.ig, grad1.ig)[None, :, :, None, :]
    full, sums = sum_gradients(docs, grad0.dw, jnp.concatenate([grad0.small, grad1.small]))
    width = heads * (w_qkv.shape[3] // chip_heads)
    sums = sums.reshape(3, 2, SMALL_ROWS, model)
    everywhere = sums[2]
    own = lax.dynamic_index_in_dim(everywhere, core, 0, keepdims=False)
    by_core = jnp.where(core == 0, sums[:2], sums[1::-1])
    by_core = lax.dynamic_index_in_dim(by_core, core, 1, keepdims=False)
    qkv_grad, out_grad, up_grad, down_grad, state_qkv_grad, state_out_grad = place_gradients(
        grad1.full, grad0.full, full, width, hidden
    )
    by_distance = by_core[:, BY_DISTANCE, : heads * block_len].reshape(chip_heads, block_len)
    by_bucket = jnp.sum(jnp.where(back_hot[:, :, None], by_distance.T[:, None, :], 0.0), axis=0)
    return (
        acts,
        input_grads,
        final_state,
        own[GAIN0 : GAIN1 + 1][None],
        own[SHIFT0 : SHIFT1 + 1][None],
        qkv_grad,
        out_grad,
        by_bucket[None],
        up_grad,
        by_core[:, UP_BIAS, :hidden].reshape(1, 2 * hidden),
        down_grad,
        own[DOWN_BIAS][None],
        everywhere[1, SGAIN],
        everywhere[1, SSHIFT],
        state_qkv_grad,
        state_out_grad,
        everywhere[1, GATE],
    )


def solution(mesh):
    in_specs = (
        P(None, "mp", "dp", None),
        P(None, None, "dp"),
        P(),
        P("mp", "dp", None),
        P("section", None, None),
        P("section", None, None),
        P("section", None, None, "mp"),
        P("section", "mp", None),
        P("section", None, "mp"),
        P("section", None, "mp"),
        P("section", "mp"),
        P("section", "mp", None),
        P("section", None),
        P(),
        P(),
        P(None, None, "mp"),
        P("mp", None),
        P(),
        P(None, "mp", "dp", None),
    )
    out_specs = (
        P("section", None, "mp", "dp", None),
        P("section", None, "mp", "dp", None),
        P("mp", "dp", None),
        P("section", None, None),
        P("section", None, None),
        P("section", None, None, "mp"),
        P("section", "mp", None),
        P("section", None, "mp"),
        P("section", None, "mp"),
        P("section", "mp"),
        P("section", "mp", None),
        P("section", None),
        P(),
        P(),
        P(None, None, "mp"),
        P("mp", None),
        P(),
    )
    return jax.shard_map(local_part, mesh=mesh, in_specs=in_specs, out_specs=out_specs, check_vma=False)
```

```python
from functools import partial
from types import SimpleNamespace

import jax
import jax.numpy as jnp
from jax import lax
from jax.experimental import pallas as pl
from jax.experimental.pallas import tpu as pltpu
from jax.sharding import PartitionSpec as P

MESH = pl.DeviceIdType.MESH
f32, bf16 = jnp.float32, jnp.bfloat16
eps = 1e-05
negative = -1000000000.0
VMEM_LIMIT = 60 * 1024 * 1024


def dot(left, right):
    return lax.dot_general(left, right, (((1,), (0,)), ((), ())), preferred_element_type=f32)


def dot_nt(left, right):
    return lax.dot_general(left, right, (((1,), (1,)), ((), ())), preferred_element_type=f32)


def dot_tn(left, right):
    return lax.dot_general(left, right, (((0,), (0,)), ((), ())), preferred_element_type=f32)


def norm_parts(values):
    average = jnp.mean(values, axis=-1, keepdims=True)
    centered = values - average
    spread = jnp.mean(centered * centered, axis=-1, keepdims=True)
    scale = lax.rsqrt(spread + eps)
    return centered * scale, scale


def layer_norm(values, gain, shift):
    return norm_parts(values)[0] * gain + shift


class Place:
    def __init__(self, rows):
        self.c, self.x = lax.axis_index("section"), lax.axis_index("mp")
        self.core = {"section": 1 - self.c}
        self.chip = {"mp": 1 - self.x}
        self.quarter, self.half = rows // 4, rows // 2

    def rows(self, x_other=False, c_other=False):
        x = 1 - self.x if x_other else self.x
        c = 1 - self.c if c_other else self.c
        return pl.ds(pl.multiple_of(x * self.half + c * self.quarter, self.quarter), self.quarter)

    def chip_rows(self, x_other=False):
        x = 1 - self.x if x_other else self.x
        return pl.ds(pl.multiple_of(x * self.half, self.half), self.half)

    def core_rows(self, c_other=False):
        c = 1 - self.c if c_other else self.c
        return pl.ds(pl.multiple_of(c * self.quarter, self.quarter), self.quarter)

    def meet(self):
        barrier = pltpu.get_barrier_semaphore()
        for other in (self.core, self.chip):
            pl.semaphore_signal(barrier, inc=1, device_id=other, device_id_type=MESH)
        pl.semaphore_wait(barrier, 2)


class Net:
    def __init__(self, send_sems, recv_sems):
        self.send_sems, self.recv_sems, self.copies = send_sems, recv_sems, []

    def copy(self, source, target, device):
        index = len(self.copies)
        made = pltpu.make_async_remote_copy(
            src_ref=source,
            dst_ref=target,
            send_sem=self.send_sems.at[index],
            recv_sem=self.recv_sems.at[index],
            device_id=device,
            device_id_type=MESH,
        )
        made.start()
        self.copies.append(made)
        return made

    def sent(self, *copies):
        for made in copies:
            made.wait_send()
        self.copies = [None if any(held is made for made in copies) else held for held in self.copies]

    def drain(self):
        for made in self.copies:
            if made is not None:
                made.wait_send()


class Local:
    def __init__(self, sems):
        self.sems, self.copies, self.waited = sems, [], set()

    def copy(self, source, target):
        made = pltpu.make_async_copy(source, target, self.sems.at[len(self.copies)])
        made.start()
        self.copies.append(made)
        return len(self.copies) - 1

    def wait(self, *indices):
        for index in indices:
            if index not in self.waited:
                self.waited.add(index)
                self.copies[index].wait()

    def drain(self):
        self.wait(*range(len(self.copies)))


class Gather:
    def __init__(self, place, net, buffer):
        self.place, self.net, self.buffer = place, net, buffer

    def start(self):
        own = self.buffer.at[self.place.rows()]
        self.from_chip = self.net.copy(own, own, self.place.chip)
        self.from_core = self.net.copy(own, own, self.place.core)

    def forward(self):
        self.from_chip.wait_recv()
        passed = self.buffer.at[self.place.rows(x_other=True)]
        self.passed = self.net.copy(passed, passed, self.place.core)

    def finish(self):
        self.from_core.wait_recv()
        self.passed.wait_recv()


class Scatter:
    def __init__(self, place, net, part, near, out, far):
        self.place, self.net, self.part = place, net, part
        self.near, self.out, self.far = near, out, far

    def send(self, x_other):
        slot = 0 if x_other else 1
        rows = self.place.rows(x_other=x_other, c_other=True)
        made = self.net.copy(self.part.at[rows], self.near.at[slot], self.place.core)
        if x_other:
            self.first = made
        else:
            self.second = made

    def middle(self):
        self.first.wait_recv()
        mine = self.part[self.place.rows(x_other=True), :].astype(f32)
        self.out[...] = (mine + self.near[0].astype(f32)).astype(bf16)
        self.across = self.net.copy(self.out, self.far, self.place.chip)

    def finish(self):
        self.second.wait_recv()
        total = self.part[self.place.rows(), :].astype(f32) + self.near[1].astype(f32)
        self.across.wait_recv()
        return total + self.far[...].astype(f32)

    def release(self):
        self.net.sent(self.first, self.second, self.across)


def share_kernel(block_len, qkv, out, up, down, sqkv, sout, cot, *rest):
    smalls, targets, cot_all, small_all = rest[:5], rest[5:11], rest[11], rest[12:17]
    staged, cot_staged, small_staged = rest[17:23], rest[23], rest[24:29]
    local_sems, send_sems, recv_sems = rest[29:]
    place = Place(block_len)
    net, local = Net(send_sems, recv_sems), Local(local_sems)
    layer = place.c

    def half(array, axis, c):
        width = array.shape[axis] // 2
        index = [slice(None)] * len(array.shape)
        index[axis] = pl.ds(pl.multiple_of(c * width, width), width)
        return array.at[tuple(index)]

    shared = ((qkv, 2), (out, 0), (up, 1), (down, 0))
    kept = [small.at[0] for small in smalls]
    kept += [half(array, axis, place.c) for array, axis in shared + ((sqkv, 2), (sout, 0))]
    sent = [small.at[0] for small in smalls] + [half(array, axis, 1 - place.c) for array, axis in shared]
    finals = [target.at[layer] for target in (*small_all, *targets[:4])] + [targets[4], targets[5]]
    place.meet()
    across, near = [], []
    for block in range(2):
        own, target = cot.at[block, place.core_rows()], cot_all.at[block, place.rows()]
        across.append(net.copy(own, target, place.chip))
        near.append(net.copy(own, target, place.core))
    for source, target in zip(sent, finals):
        near.append(net.copy(source, target, place.core))
    cot_in = [local.copy(cot.at[block, place.core_rows()], cot_staged.at[block]) for block in range(2)]
    inward = [local.copy(source, stage) for source, stage in zip(kept, (*small_staged, *staged))]
    for block in range(2):
        local.wait(cot_in[block])
        local.copy(cot_staged.at[block], cot_all.at[block, place.rows()])
    for index, stage, target in zip(inward, (*small_staged, *staged), finals):
        local.wait(index)
        local.copy(stage, target)
    for block in range(2):
        across[block].wait_recv()
        passed = cot_all.at[block, place.rows(x_other=True)]
        near.append(net.copy(passed, passed, place.core))
    for made in near:
        made.wait_recv()
    local.drain()
    net.drain()


def share_weights(block_len, qkv, out, up, down, sqkv, sout, cot, *smalls):
    def halved(shape, axis, stacked=True):
        shape = list(shape)
        shape[axis] //= 2
        return jax.ShapeDtypeStruct(([2] if stacked else []) + shape, bf16)

    anywhere = pl.BlockSpec(memory_space=pl.ANY)
    count = 7 + len(smalls)
    return pl.pallas_call(
        partial(share_kernel, block_len),
        out_shape=(
            halved(qkv.shape, 2),
            halved(out.shape, 0),
            halved(up.shape, 1),
            halved(down.shape, 0),
            halved(sqkv.shape, 2, False),
            halved(sout.shape, 0, False),
            jax.ShapeDtypeStruct((2, block_len, cot.shape[2]), bf16),
            *(jax.ShapeDtypeStruct((2,) + small.shape[1:], f32) for small in smalls),
        ),
        in_specs=[anywhere] * count,
        out_specs=[anywhere] * count,
        scratch_shapes=[
            pltpu.VMEM(halved(array.shape, axis, False).shape, bf16)
            for array, axis in ((qkv, 2), (out, 0), (up, 1), (down, 0), (sqkv, 2), (sout, 0))
        ]
        + [pltpu.VMEM((2, block_len // 4, cot.shape[2]), bf16)]
        + [pltpu.VMEM(small.shape[1:], f32) for small in smalls]
        + [
            pltpu.SemaphoreType.DMA((2 * count + 2,)),
            pltpu.SemaphoreType.DMA((count + 4,)),
            pltpu.SemaphoreType.DMA((count + 4,)),
        ],
        compiler_params=pltpu.CompilerParams(
            collective_id=0, has_side_effects=True, vmem_limit_bytes=VMEM_LIMIT
        ),
        name="share_weights",
    )(qkv, out, up, down, sqkv, sout, cot, *smalls)


def back_hot(buckets, count):
    length = buckets.shape[1]
    hot = lax.broadcasted_iota(jnp.int32, (count, length), 0) == buckets
    both = lax.broadcasted_iota(jnp.int32, (length, length), 0) + lax.broadcasted_iota(
        jnp.int32, (length, length), 1
    )
    turn = (both == 0) | (both == length)
    return dot(jnp.where(hot, 1.0, 0.0).astype(bf16), jnp.where(turn, 1.0, 0.0).astype(bf16)).astype(bf16)


def in_parts(values):
    high = values.astype(bf16)
    rest = values - high.astype(f32)
    middle = rest.astype(bf16)
    return high, middle, (rest - middle.astype(f32)).astype(bf16)


def bias_rows(rel, buckets, c):
    hot = back_hot(buckets, rel.shape[1])
    rows = sum(dot(part, hot) for part in in_parts(rel))
    heads = rel.shape[0] // 2
    return jnp.where(c == 0, rows[:heads], rows[heads:])


def fill_bias(bias, row0):
    head_count, length = row0.shape
    for head in range(head_count):
        start = jnp.broadcast_to(row0[head : head + 1], (bias.shape[1], length))
        rolled = pltpu.roll(start, 0, axis=1, stride=1, stride_axis=0)
        bias[head, :, :length] = rolled
        bias[head, :, length:] = rolled


def bias_columns(index, chunk, length):
    return pl.ds(pl.multiple_of(length - index * chunk, chunk), length)


def window_logits(query, key_cur, key_prev, bias, valid, block, first_row, scale):
    logits = dot_nt(query, key_cur)
    rows = first_row + lax.broadcasted_iota(jnp.int32, logits.shape, 0)
    here = lax.broadcasted_iota(jnp.int32, logits.shape, 1) <= rows
    usable = valid[block : block + 1, :] > 0.5
    if key_prev is None:
        keep = here & usable
    else:
        logits = jnp.where(here, logits, dot_nt(query, key_prev))
        keep = jnp.where(here, valid[block : block + 1, :], valid[block - 1 : block, :]) > 0.5
    return jnp.where(keep, logits * scale + bias, negative), here


def forward_kernel(layer, names, *refs):
    r = SimpleNamespace(**dict(zip(names, refs)))
    rec = layer == 1
    length = r.u_v.shape[1]
    heads = r.rel.shape[1] // 2
    head_size = r.att_v.shape[2] // heads
    width = heads * head_size
    scale = head_size ** (-0.5)
    place = Place(length)
    net, local = Net(r.send_sems, r.recv_sems), Local(r.local_sems)
    chunk = min(128, length)

    place.meet()
    load = [local.copy(r.wqkv.at[layer], r.wqkv_v), local.copy(r.wout.at[layer], r.wout_v)]
    load_mlp = [local.copy(r.wup.at[layer], r.wup_v), local.copy(r.wdown.at[layer], r.wdown_v)]
    load_state = []
    if rec:
        load_state = [local.copy(r.wsqkv, r.wsqkv_v), local.copy(r.wsout, r.wsout_v)]

    gain = lambda index: r.gain[layer, index : index + 1, :]
    shift = lambda index: r.shift[layer, index : index + 1, :]

    def gather(buffer):
        return Gather(place, net, buffer)

    scatter_count = [0]

    def scatter():
        index = scatter_count[0]
        scatter_count[0] += 1
        return Scatter(
            place, net, r.part.at[index], r.near.at[index], r.out.at[index], r.far.at[index]
        )

    def norm_state(rows, index):
        r.sn_v[index, place.rows(), :] = layer_norm(rows, r.sgain[...], r.sshift[...]).astype(bf16)

    def norm_first(block):
        rows = r.x[block, place.core_rows(), :].astype(f32)
        r.u_v[block, place.rows(), :] = layer_norm(rows, gain(0), shift(0)).astype(bf16)

    def project(source, weights, target):
        for part in range(3):
            target[:, part * width : (part + 1) * width] = dot(source[...], weights[part]).astype(bf16)

    def reduce_from(values, weights, to):
        columns = weights.shape[1]
        step = min(512, columns)
        for x_other in (True, False):
            rows = place.chip_rows(x_other)

            @pl.loop(0, columns // step)
            def _(index):
                at = pl.ds(pl.multiple_of(index * step, step), step)
                to.part[rows, at] = dot(values[rows, :], weights[:, at]).astype(bf16)

            to.send(x_other)

    def attend(block):
        qkv = r.qkv_v.at[block]
        prev = r.qkv_v.at[block - 1] if block > 0 else None

        @pl.loop(0, length // chunk)
        def _(index):
            at = pl.ds(pl.multiple_of(index * chunk, chunk), chunk)
            lses = []
            for head in range(heads):
                q_at = slice(head * head_size, (head + 1) * head_size)
                k_at = slice(width + head * head_size, width + (head + 1) * head_size)
                v_at = slice(2 * width + head * head_size, 2 * width + (head + 1) * head_size)
                query = qkv[at, q_at]
                logits, here = window_logits(
                    query,
                    qkv[:, k_at],
                    None if prev is None else prev[:, k_at],
                    r.bias[head, :, bias_columns(index, chunk, length)],
                    r.valid,
                    block,
                    index * chunk,
                    scale,
                )
                peak = jnp.max(logits, axis=-1, keepdims=True)
                if rec:
                    state = r.sqkv_v.at[block]
                    state_logits = dot_nt(query, state[:, k_at]) * scale
                    peak = jnp.maximum(peak, jnp.max(state_logits, axis=-1, keepdims=True))
                probs = jnp.exp(logits - peak)
                total = jnp.sum(probs, axis=-1, keepdims=True)
                if prev is None:
                    result = dot(probs.astype(bf16), qkv[:, v_at])
                else:
                    result = dot(jnp.where(here, probs, 0.0).astype(bf16), qkv[:, v_at])
                    result += dot(jnp.where(here, 0.0, probs).astype(bf16), prev[:, v_at])
                if rec:
                    state_probs = jnp.exp(state_logits - peak)
                    total += jnp.sum(state_probs, axis=-1, keepdims=True)
                    result += dot(state_probs.astype(bf16), state[:, v_at])
                r.att_v[block, at, q_at] = (result / total).astype(bf16)
                lses.append(peak + jnp.log(total))
            lane = lax.broadcasted_iota(jnp.int32, (chunk, 128), 1)
            packed = jnp.zeros((chunk, 128), f32)
            for head in range(heads):
                packed = jnp.where(lane == head, lses[head], packed)
            r.lse_v[block, at, :] = packed

    def recur(block):
        qkv, state = r.qkv_v.at[block], r.sqkv_v.at[block]

        @pl.loop(0, length // chunk)
        def _(index):
            at = pl.ds(pl.multiple_of(index * chunk, chunk), chunk)
            lses = []
            for head in range(heads):
                q_at = slice(head * head_size, (head + 1) * head_size)
                k_at = slice(width + head * head_size, width + (head + 1) * head_size)
                v_at = slice(2 * width + head * head_size, 2 * width + (head + 1) * head_size)
                logits = dot_nt(state[at, q_at], qkv[:, k_at]) * scale
                logits = jnp.where(r.valid[block : block + 1, :] > 0.5, logits, negative)
                peak = jnp.max(logits, axis=-1, keepdims=True)
                probs = jnp.exp(logits - peak)
                total = jnp.sum(probs, axis=-1, keepdims=True)
                r.sout_v[block, at, q_at] = (dot(probs.astype(bf16), qkv[:, v_at]) / total).astype(bf16)
                lses.append(peak + jnp.log(total))
            if block == 0:
                lane = lax.broadcasted_iota(jnp.int32, (chunk, 128), 1)
                packed = jnp.zeros((chunk, 128), f32)
                for head in range(heads):
                    packed = jnp.where(lane == head, lses[head], packed)
                r.rlse_v[at, :] = packed

    def take_branch(block, from_out):
        rows = r.x[block, place.core_rows(), :].astype(f32) + from_out.finish()
        r.h_v[block] = rows
        r.wn_v[block, place.rows(), :] = layer_norm(rows, gain(1), shift(1)).astype(bf16)

    def feed_up(block):
        columns = r.wup_v.shape[1]
        step = 256

        @pl.loop(0, columns // step)
        def _(index):
            at = pl.ds(pl.multiple_of(index * step, step), step)
            bias_at = pl.ds(pl.multiple_of(place.c * columns + index * step, step), step)
            pre = dot(r.wn_v[block], r.wup_v[:, at]) + r.up_bias[layer, :, bias_at]
            r.pre_v[block, :, at] = pre.astype(bf16)
            r.act_v[block, :, at] = (0.5 * pre * (1.0 + lax.erf(pre * (0.5**0.5)))).astype(bf16)

    def take_result(block, from_down):
        rows = r.h_v[block] + from_down.finish() + r.down_bias[layer]
        own = r.acts_v.at[block, place.core_rows()]
        own[...] = rows.astype(bf16)
        return net.copy(own, own, place.core)

    branch = [scatter(), scatter()]
    result = [scatter(), scatter()]
    first = [gather(r.u_v.at[block]) for block in range(2)]
    second = [gather(r.wn_v.at[block]) for block in range(2)]
    if rec:
        update = [scatter(), scatter()]
        state = [gather(r.sn_v.at[block]) for block in range(2)]
        gate = jax.nn.sigmoid(r.gate[...])
        norm_state(r.state[place.core_rows(), :].astype(f32), 0)
        state[0].start()
    norm_first(0)
    first[0].start()
    norm_first(1)
    first[1].start()
    fill_bias(r.bias, bias_rows(r.rel[layer], r.buckets[...], place.c))
    if rec:
        state[0].forward()
    first[0].forward()
    if rec:
        state[0].finish()
        local.wait(*load_state)
        project(r.sn_v.at[0], r.wsqkv_v, r.sqkv_v.at[0])
    first[0].finish()
    local.wait(*load)
    project(r.u_v.at[0], r.wqkv_v, r.qkv_v.at[0])
    if rec:
        recur(0)
        reduce_from(r.sout_v.at[0], r.wsout_v, update[0])
    else:
        attend(0)
    first[1].forward()
    if rec:
        update[0].middle()
        attend(0)
    reduce_from(r.att_v.at[0], r.wout_v, branch[0])
    if not rec:
        branch[0].middle()
    first[1].finish()
    project(r.u_v.at[1], r.wqkv_v, r.qkv_v.at[1])
    local.copy(r.u_v, r.u)
    local.copy(r.qkv_v, r.qkv)
    if rec:
        branch[0].middle()
        update_rows = update[0].finish()
        r.z_v[...] = update_rows
        state_rows = gate * r.state[place.core_rows(), :].astype(f32) + (1.0 - gate) * update_rows
        r.s1_v[...] = state_rows
        norm_state(state_rows, 1)
        state[1].start()
        local.copy(r.z_v, r.z)
        local.copy(r.s1_v, r.s1)
    else:
        attend(1)
        reduce_from(r.att_v.at[1], r.wout_v, branch[1])
    take_branch(0, branch[0])
    second[0].start()
    if rec:
        state[1].forward()
        state[1].finish()
        project(r.sn_v.at[1], r.wsqkv_v, r.sqkv_v.at[1])
        local.copy(r.sn_v, r.sn)
        local.copy(r.sqkv_v, r.sqkv)
        recur(1)
        reduce_from(r.sout_v.at[1], r.wsout_v, update[1])
        local.copy(r.sout_v, r.sout)
        local.copy(r.rlse_v, r.rlse)
        attend(1)
        update[1].middle()
        reduce_from(r.att_v.at[1], r.wout_v, branch[1])
    local.copy(r.att_v, r.att)
    local.copy(r.lse_v, r.lse)
    second[0].forward()
    branch[1].middle()
    second[0].finish()
    local.wait(*load_mlp)
    feed_up(0)
    reduce_from(r.act_v.at[0], r.wdown_v, result[0])
    take_branch(1, branch[1])
    second[1].start()
    local.copy(r.h_v, r.h)
    result[0].middle()
    second[1].forward()
    second[1].finish()
    local.copy(r.wn_v, r.wn)
    feed_up(1)
    local.copy(r.pre_v, r.pre)
    local.copy(r.act_v, r.act)
    reduce_from(r.act_v.at[1], r.wdown_v, result[1])
    sent = [take_result(0, result[0])]
    result[1].middle()
    if rec:
        own = r.final_v.at[place.core_rows()]
        own[...] = gate * r.s1_v[...] + (1.0 - gate) * update[1].finish()
        sent.append(net.copy(own, own, place.core))
    sent.append(take_result(1, result[1]))
    for made in sent:
        made.wait_recv()
    local.copy(r.acts_v, r.acts)
    if rec:
        local.copy(r.final_v, r.final)
    local.drain()
    net.drain()


def forward_layer(layer, block_len, small, valid, weights, rows, state):
    rec = layer == 1
    wqkv, wout, wup, wdown = weights[:4]
    model = rows.shape[2]
    width, hidden = wqkv.shape[3], wup.shape[2]
    quarter = block_len // 4
    heads = small.rel.shape[1] // 2

    def held(shape, dtype):
        return jax.ShapeDtypeStruct(shape, dtype)

    outs = dict(
        u=held((2, block_len, model), bf16),
        qkv=held((2, block_len, 3 * width), bf16),
        lse=held((2, block_len, 128), f32),
        att=held((2, block_len, width), bf16),
        wn=held((2, block_len, model), bf16),
        pre=held((2, block_len, hidden), bf16),
        act=held((2, block_len, hidden), bf16),
        h=held((2, quarter, model), f32),
        acts=held((2, 2 * quarter, model), bf16),
    )
    ins = dict(
        x=rows,
        gain=small.gain,
        shift=small.shift,
        up_bias=small.up_bias,
        down_bias=small.down_bias,
        rel=small.rel,
        buckets=small.buckets,
        valid=valid,
    )
    far_ins = dict(wqkv=wqkv, wout=wout, wup=wup, wdown=wdown)
    if rec:
        outs.update(
            sn=held((2, block_len, model), bf16),
            sqkv=held((2, block_len, 3 * width), bf16),
            rlse=held((block_len, 128), f32),
            sout=held((2, block_len, width), bf16),
            s1=held((quarter, model), f32),
            z=held((quarter, model), f32),
            final=held((2 * quarter, model), f32),
        )
        ins.update(state=state, sgain=small.sgain, sshift=small.sshift, gate=small.gate)
        far_ins.update(wsqkv=weights[4], wsout=weights[5])
    scatters = 6 if rec else 4
    copies = (3 * 6 + 3 * 6 + 3) if rec else (3 * 4 + 3 * 4 + 2)
    scratch = {name + "_v": pltpu.VMEM(kind.shape, kind.dtype) for name, kind in outs.items()}
    scratch.update(
        wqkv_v=pltpu.VMEM(wqkv.shape[1:], bf16),
        wout_v=pltpu.VMEM(wout.shape[1:], bf16),
        wup_v=pltpu.VMEM(wup.shape[1:], bf16),
        wdown_v=pltpu.VMEM(wdown.shape[1:], bf16),
        bias=pltpu.VMEM((heads, min(128, block_len), 2 * block_len), f32),
        part=pltpu.VMEM((scatters, block_len, model), bf16),
        near=pltpu.VMEM((scatters, 2, quarter, model), bf16),
        out=pltpu.VMEM((scatters, quarter, model), bf16),
        far=pltpu.VMEM((scatters, quarter, model), bf16),
        send_sems=pltpu.SemaphoreType.DMA((copies,)),
        recv_sems=pltpu.SemaphoreType.DMA((copies,)),
        local_sems=pltpu.SemaphoreType.DMA((6 + len(outs),)),
    )
    if rec:
        scratch.update(
            wsqkv_v=pltpu.VMEM(weights[4].shape, bf16),
            wsout_v=pltpu.VMEM(weights[5].shape, bf16),
        )
    anywhere = pl.BlockSpec(memory_space=pl.ANY)
    inside = pl.BlockSpec(memory_space=pltpu.VMEM)
    results = pl.pallas_call(
        partial(forward_kernel, layer, [*ins, *far_ins, *outs, *scratch]),
        out_shape=tuple(outs.values()),
        in_specs=[inside] * len(ins) + [anywhere] * len(far_ins),
        out_specs=[anywhere] * len(outs),
        scratch_shapes=list(scratch.values()),
        compiler_params=pltpu.CompilerParams(
            collective_id=1 + layer, has_side_effects=True, vmem_limit_bytes=VMEM_LIMIT
        ),
        name="forward_recurrent" if rec else "forward_local",
    )(*ins.values(), *far_ins.values())
    return SimpleNamespace(**dict(zip(outs, results)))


def ring_place(n, c, d):
    if n % 2:
        at = d

        def index_at(p):
            return p

    else:
        a, b = d // 2, d % 2
        at = a + b * (n - 1 - 2 * a)

        def index_at(p):
            b = p // (n // 2)
            return 2 * (p + b * (n - 1 - 2 * p)) + b

    def flip(p):
        return p + c * (n - 1 - 2 * p)

    return flip(at), lambda p: index_at(flip(p))


class Ring:
    def __init__(self, n):
        self.n, self.c = n, lax.axis_index("section")
        self.q, index_at = ring_place(n, self.c, lax.axis_index("dp"))
        self.after = {"dp": index_at((self.q + 1) % n)}
        self.before = {"dp": index_at((self.q + n - 1) % n)}
        self.core, self.chip = {"section": 1 - self.c}, {"mp": 1 - lax.axis_index("mp")}

    def meet(self):
        barrier = pltpu.get_barrier_semaphore()
        for other in (self.after, self.before, self.core, self.chip):
            pl.semaphore_signal(barrier, inc=1, device_id=other, device_id_type=MESH)
        pl.semaphore_wait(barrier, 4)


def remote(source, target, send, recv, to):
    return pltpu.make_async_remote_copy(
        src_ref=source, dst_ref=target, send_sem=send, recv_sem=recv, device_id=to, device_id_type=MESH
    )


def ring_subs(n, rows, most):
    return max(k for k in range(1, most + 1) if rows // n % (16 * k) == 0)


def ring_scratch(n, rows, model, most):
    subs = ring_subs(n, rows, most)
    sems = pltpu.SemaphoreType.DMA
    return dict(
        held=pltpu.VMEM((n - 1, rows // n, model), bf16),
        rs_send=sems((n - 1, subs)),
        rs_recv=sems((n - 1, subs)),
        ag_send=sems((n - 1, subs)),
        ag_recv=sems((n - 1, subs)),
        core_send=sems((n, subs)),
        core_recv=sems((n, subs)),
        own_sems=sems((subs,)),
    )


class RingSum:
    def __init__(self, ring, mine, full, held, rs_send, rs_recv, ag_send, ag_recv, core_send, core_recv, own_sems):
        self.ring, self.mine, self.full, self.held = ring, mine, full, held
        self.rs_send, self.rs_recv, self.ag_send, self.ag_recv = rs_send, rs_recv, ag_send, ag_recv
        self.core_send, self.core_recv, self.own_sems = core_send, core_recv, own_sems
        self.chunk, self.subs = held.shape[1], own_sems.shape[0]
        self.sub = self.chunk // self.subs
        self.half = (ring.n - 1) * self.subs
        self.total = 2 * self.half
        self.done = 0

    def rows(self, owner, k):
        owner = (owner + 2 * self.ring.n) % self.ring.n
        return pl.ds(pl.multiple_of(owner * self.chunk + k * self.sub, self.sub), self.sub)

    def piece(self, k):
        return slice(k * self.sub, (k + 1) * self.sub) if isinstance(k, int) else pl.ds(
            pl.multiple_of(k * self.sub, self.sub), self.sub
        )

    def summed(self, s, k):
        return self.held.at[s, self.piece(k)]

    def gathered(self, s, k):
        return self.full.at[self.ring.c, self.rows(self.ring.q + 1 - s, k)]

    def reduce(self, s, k, source):
        return remote(source, self.summed(s, k), self.rs_send.at[s, k], self.rs_recv.at[s, k], self.ring.after)

    def gather(self, s, k, source):
        return remote(source, self.gathered(s, k), self.ag_send.at[s, k], self.ag_recv.at[s, k], self.ring.after)

    def to_core(self, s, k, source):
        return remote(source, self.gathered(s, k), self.core_send.at[s, k], self.core_recv.at[s, k], self.ring.core)

    def from_core(self, s, k):
        n, q = self.ring.n, self.ring.q
        target = self.full.at[1 - self.ring.c, self.rows(n - q - s, k)]
        return remote(target, target, self.core_send.at[s, k], self.core_recv.at[s, k], self.ring.core)

    def own(self, k):
        return pltpu.make_async_copy(self.summed(self.ring.n - 2, k), self.gathered(0, k), self.own_sems.at[k])

    def start(self):
        for k in range(self.subs):
            self.reduce(0, k, self.mine.at[self.rows(self.ring.q, k)]).start()

    def add(self, s, k):
        self.reduce(s, k, self.summed(s, k)).wait_recv()
        self.held[s, self.piece(k), :] = (
            self.held[s, self.piece(k), :].astype(f32)
            + self.mine[self.rows(self.ring.q - 1 - s, k), :].astype(f32)
        ).astype(bf16)

    def add_middle(self, s, k):
        self.add(s, k)
        self.reduce(s + 1, k, self.summed(s, k)).start()

    def add_last(self, s, k):
        self.add(s, k)
        self.gather(0, k, self.summed(s, k)).start()
        self.to_core(0, k, self.summed(s, k)).start()
        self.own(k).start()

    def pass_middle(self, s, k):
        at = self.gathered(s + 1, k)
        self.gather(s, k, at).wait_recv()
        self.gather(s + 1, k, at).start()
        self.to_core(s + 1, k, at).start()

    def pass_last(self, s, k):
        at = self.gathered(s + 1, k)
        self.gather(s, k, at).wait_recv()
        self.to_core(s + 1, k, at).start()

    def pump_one(self, t):
        last = self.ring.n - 2
        s, k = t // self.subs, t % self.subs
        kinds = (
            (s < last, self.add_middle, s),
            (s == last, self.add_last, s),
            ((s > last) & (s < 2 * last + 1), self.pass_middle, s - last - 1),
            (s == 2 * last + 1, self.pass_last, s - last - 1),
        )
        for here, act, step in kinds:
            if isinstance(t, int):
                if here:
                    act(step, k)
            else:
                pl.when(here)(partial(act, step, k))

    def pump(self, count=1):
        for _ in range(min(count, self.total - self.done)):
            self.pump_one(self.done)
            self.done += 1

    def pumps_in(self, loop_steps, each):
        each = min(each, (self.total - self.done) // loop_steps)
        base = self.done
        self.done += each * loop_steps

        def pump(index):
            for piece in range(each):
                self.pump_one(base + index * each + piece)

        return pump

    def run(self, until):
        last = self.ring.n - 2
        for first, end, act in (
            (0, last, self.add_middle),
            (last, last + 1, self.add_last),
            (last + 1, 2 * last + 1, self.pass_middle),
            (2 * last + 1, 2 * last + 2, self.pass_last),
        ):
            while self.done < min(end * self.subs, until) and self.done % self.subs:
                self.pump()
            step, stop = self.done // self.subs, min(end, until // self.subs)
            if first <= step < stop:
                base = last + 1 if first > last else 0

                @pl.loop(step - base, stop - base)
                def _(s):
                    for k in range(self.subs):
                        act(s, k)

                self.done = stop * self.subs

    def release_mine(self):
        for k in range(self.subs):
            self.reduce(0, k, self.mine.at[self.rows(self.ring.q, k)]).wait_send()

    def finish(self, released=False):
        self.run(self.total)
        if not released:
            self.release_mine()
        last = self.ring.n - 2

        @pl.loop(0, last + 2)
        def _(s):
            for k in range(self.subs):
                self.from_core(s, k).wait_recv()
                self.to_core(s, k, self.gathered(s, k)).wait_send()

        @pl.loop(0, last + 1)
        def _(s):
            for k in range(self.subs):
                self.gather(s, k, self.gathered(s, k)).wait_send()

        @pl.loop(0, last)
        def _(s):
            for k in range(self.subs):
                self.reduce(s + 1, k, self.summed(s, k)).wait_send()

        for k in range(self.subs):
            self.own(k).wait()


def sum_kernel(n, parts, small_0, small_1, full, small_out, mine, small_held, small_sum, small_far, small, *rest):
    ring_refs, (small_send, small_recv, local_sems) = rest[:-3], rest[-3:]
    ring = Ring(n)
    flow = RingSum(ring, mine, full, *ring_refs)

    def small_step(s, first):
        source = small if first else small_held.at[s - 1]
        return remote(source, small_held.at[s], small_send.at[s], small_recv.at[s], ring.after)

    load = pltpu.make_async_copy(parts, mine, local_sems.at[0])
    load.start()
    small[: small_0.shape[0]] = small_0[...]
    small[small_0.shape[0] :] = small_1[...]
    ring.meet()
    small_step(0, True).start()
    load.wait()
    flow.start()

    @pl.loop(0, n - 2)
    def _(s):
        for k in range(flow.subs):
            flow.add_middle(s, k)
        small_step(s, True).wait_recv()
        small_step(s + 1, False).start()

    flow.done = (n - 2) * flow.subs
    flow.run(flow.half)
    small_step(n - 2, True).wait_recv()
    small_out[0] = small[...]

    @pl.loop(0, n - 1)
    def _(s):
        small_out[0] += small_held[s]

    between = remote(small_out.at[0], small_out.at[1], small_send.at[n - 1], small_recv.at[n - 1], ring.core)
    between.start()
    between.wait_recv()
    small_sum[...] = small_out[0] + small_out[1]
    across = remote(small_sum, small_far, small_send.at[n], small_recv.at[n], ring.chip)
    across.start()
    across.wait_recv()
    small_out[2] = small_sum[...] + small_far[...]
    flow.finish()

    @pl.loop(0, n - 1)
    def _(s):
        small_step(s, True).wait_send()

    between.wait_send()
    across.wait_send()


def sum_gradients(n, parts, small_0, small_1):
    rows, model = parts.shape
    both = (small_0.shape[0] + small_1.shape[0], model)
    anywhere = pl.BlockSpec(memory_space=pl.ANY)
    inside = pl.BlockSpec(memory_space=pltpu.VMEM)
    sems = pltpu.SemaphoreType.DMA
    return pl.pallas_call(
        partial(sum_kernel, n),
        out_shape=(
            jax.ShapeDtypeStruct((2, rows, model), bf16),
            jax.ShapeDtypeStruct((3,) + both, f32),
        ),
        in_specs=[anywhere, inside, inside],
        out_specs=[anywhere, inside],
        scratch_shapes=[
            pltpu.VMEM((rows, model), bf16),
            pltpu.VMEM((n - 1,) + both, f32),
            pltpu.VMEM(both, f32),
            pltpu.VMEM(both, f32),
            pltpu.VMEM(both, f32),
            *ring_scratch(n, rows, model, 6).values(),
            sems((n + 1,)),
            sems((n + 1,)),
            sems((1,)),
        ],
        compiler_params=pltpu.CompilerParams(
            collective_id=5, has_side_effects=True, vmem_limit_bytes=VMEM_LIMIT
        ),
        name="sum_gradients",
    )(parts, small_0, small_1)


def norm_back(rows, gain, grad):
    normed, scale = norm_parts(rows)
    inner = grad * gain
    means = jnp.mean(inner, axis=-1, keepdims=True), jnp.mean(inner * normed, axis=-1, keepdims=True)
    by_rows = scale * (inner - means[0] - normed * means[1])
    return by_rows, jnp.sum(grad * normed, axis=0, keepdims=True), jnp.sum(grad, axis=0, keepdims=True)


GAIN0, GAIN1, SHIFT0, SHIFT1, DOWN_BIAS, SGAIN, SSHIFT, GATE, UP_BIAS, BY_DISTANCE = range(10)
SMALL_ROWS = 16


def backward_kernel(layer, n, ring_names, names, *refs):
    r = SimpleNamespace(**dict(zip(names, refs)))
    rec = layer == 1
    heads, length = r.rel.shape[1] // 2, r.valid.shape[1]
    head_size = r.att_v.shape[1] // heads
    width = heads * head_size
    hidden = r.wup_v.shape[1]
    model = r.wup_v.shape[0]
    scale = head_size ** (-0.5)
    place = Place(length)
    net, local = Net(r.send_sems, r.recv_sems), Local(r.local_sems)
    chunk = min(128, length)

    ring = Ring(n)
    r.act, r.by_down = r.work.at[:hidden], r.work.at[hidden:]
    ring_refs = [[getattr(r, name) for name in flow_names] for flow_names in ring_names]
    if rec:
        up_flow = RingSum(ring, r.act, r.full.at[:, :model], *ring_refs[0])
        down_flow = RingSum(ring, r.by_down, r.full.at[:, model:], *ring_refs[1])
        act = [local.copy(r.act_in, r.act), local.copy(r.g_in, r.g)]
    else:
        rest_flow = RingSum(ring, r.mine, r.full, *ring_refs[0])
        parts = local.copy(r.parts, r.mine)
        act = [local.copy(r.act_in, r.act)]
    flows = []

    def launch(flow):
        flow.start()
        flows.append(flow)

    def tick(count=1):
        for _ in range(count):
            for flow in flows:
                flow.pump()

    def tick_at(index, *steps):
        for step in steps:

            @pl.when(index == step)
            def _():
                tick()

    ring.meet()
    wdown = local.copy(r.wdown.at[layer], r.wdown_v)
    pre = local.copy(r.pre, r.pre_v)
    wup = local.copy(r.wup.at[layer], r.wup_v)
    hidden_rows = local.copy(r.h, r.h_v)
    wn = local.copy(r.wn, r.wn_v)
    attention = [
        local.copy(r.wout.at[layer], r.wout_v),
        local.copy(r.qkv, r.qkv_v),
        local.copy(r.att, r.att_v),
        local.copy(r.lse, r.lse_v),
    ]
    if rec:
        attention += [local.copy(r.sqkv, r.sqkv_v), local.copy(r.wsqkv, r.wsqkv_v)]
        chain = [
            local.copy(r.s1, r.s1_v),
            local.copy(r.z, r.z_v),
            local.copy(r.wsout, r.wsout_v),
            local.copy(r.sout, r.sout_v),
            local.copy(r.rlse, r.rlse_v),
        ]
    wqkv = local.copy(r.wqkv.at[layer], r.wqkv_v)

    gain = lambda index: r.gain[layer, index : index + 1, :]
    small = r.small_v
    small[...] = jnp.zeros(small.shape, f32)
    r.dkv[...] = jnp.zeros(r.dkv.shape, f32)
    r.dbias[...] = jnp.zeros(r.dbias.shape, f32)
    if rec:
        r.dskv[...] = jnp.zeros(r.dskv.shape, f32)

    def add_small(index, value):
        small[index : index + 1, :] += value

    def gather(buffer):
        return Gather(place, net, buffer)

    scatter_count = [0]

    def scatter(slot):
        index = scatter_count[0]
        scatter_count[0] += 1
        return Scatter(place, net, r.part.at[slot], r.near.at[index], r.out.at[slot], r.far.at[index])

    def block_rows(block):
        return slice(block * length, (block + 1) * length)

    def own_grad(block):
        return r.gy[block, place.core_rows(), :].astype(bf16).astype(f32)

    def feed_back(block):
        step = 256
        rows = block_rows(block)

        @pl.loop(0, hidden // step)
        def _(index):
            at = pl.ds(pl.multiple_of(index * step, step), step)
            pre = r.pre_v[rows, at].astype(f32)
            by_act = dot_nt(r.g[rows, :], r.wdown_v[at, :])
            below = 0.5 * (1.0 + lax.erf(pre * (0.5**0.5)))
            by_pre = by_act * (below + pre * jnp.exp(-0.5 * pre * pre) * 0.3989422804014327)
            small[UP_BIAS : UP_BIAS + 1, at] += jnp.sum(by_pre, axis=0, keepdims=True)
            r.dpre[rows, at] = by_pre.astype(bf16)

    def reduce_back(terms, to):
        step = min(512, model)
        for x_other in (True, False):
            rows = place.chip_rows(x_other)

            @pl.loop(0, model // step)
            def _(index):
                at = pl.ds(pl.multiple_of(index * step, step), step)
                total = None
                for values, weights in terms:
                    term = dot_nt(values[rows, :], weights[at, :])
                    total = term if total is None else total + term
                to.part[rows, at] = total.astype(bf16)

            to.send(x_other)

    def take_feed(block, from_feed):
        by_norm = from_feed.finish()
        grad = own_grad(block)
        by_rows, by_gain, by_shift = norm_back(r.h_v[block], gain(1), by_norm)
        add_small(GAIN1, by_gain)
        add_small(SHIFT1, by_shift)
        add_small(DOWN_BIAS, jnp.sum(grad, axis=0, keepdims=True))
        total = grad + by_rows
        r.ig_v[block, place.core_rows(), :] = total
        r.hg[pl.ds(place_row(block), place.quarter), :] = total.astype(bf16)

    def place_row(block):
        return pl.multiple_of(block * length + place.x * place.half + place.c * place.quarter, place.quarter)

    def weight_grad(left, right, target, at_row=0):
        step = 256

        @pl.loop(0, left.shape[1] // step)
        def _(index):
            at = pl.ds(pl.multiple_of(index * step, step), step)
            to = pl.ds(pl.multiple_of(at_row + index * step, step), step)
            target[to, :] = dot_tn(left[:, at], right[...]).astype(bf16)

    def projection_grad(normed, grads, target):
        for part in range(3):
            tick()
            to = slice(part * width, (part + 1) * width)

            @pl.loop(0, model // width)
            def _(index):
                at = pl.ds(pl.multiple_of(index * width, width), width)
                target[to, at] = dot_tn(normed[:, at], grads[:, to]).astype(bf16)

    def branch_back(block):
        r.datt[block] = dot_nt(r.hg[block_rows(block), :], r.wout_v[...]).astype(bf16)

    def columns(head, part):
        return slice(part * width + head * head_size, part * width + (head + 1) * head_size)

    def attend_back(block):
        qkv = r.qkv_v.at[block]
        prev = r.qkv_v.at[block - 1] if block > 0 else None
        state = r.sqkv_v.at[block] if rec else None

        @pl.loop(0, length // chunk)
        def _(index):
            tick_at(index, *((1, 2, 3) if rec and block else (1, 3)))
            at = pl.ds(pl.multiple_of(index * chunk, chunk), chunk)
            block_at = pl.ds(pl.multiple_of(block * length + index * chunk, chunk), chunk)
            for head in range(heads):
                q_at, k_at, v_at = (columns(head, part) for part in range(3))
                query, key, value = qkv[at, q_at], qkv[:, k_at], qkv[:, v_at]
                logits, here = window_logits(
                    query,
                    key,
                    None if prev is None else prev[:, k_at],
                    r.bias[head, :, bias_columns(index, chunk, length)],
                    r.valid,
                    block,
                    index * chunk,
                    scale,
                )
                lse = r.lse_v[block, at, head : head + 1]
                probs = jnp.exp(logits - lse)
                grad = r.datt[block, at, q_at]
                delta = jnp.sum(
                    grad.astype(f32) * r.att_v[block_at, q_at].astype(f32), axis=-1, keepdims=True
                )
                by_probs = dot_nt(grad, value)
                if prev is not None:
                    by_probs = jnp.where(here, by_probs, dot_nt(grad, prev[:, v_at]))
                by_logits = probs * (by_probs - delta)
                r.dbias[head, :, bias_columns(index, chunk, length)] += by_logits
                by_logits = by_logits * scale
                if prev is None:
                    low = by_logits.astype(bf16)
                    low_probs = probs.astype(bf16)
                    by_query = dot(low, key)
                else:
                    low = jnp.where(here, by_logits, 0.0).astype(bf16)
                    low_probs = jnp.where(here, probs, 0.0).astype(bf16)
                    low_prev = jnp.where(here, 0.0, by_logits).astype(bf16)
                    low_probs_prev = jnp.where(here, 0.0, probs).astype(bf16)
                    by_query = dot(low, key) + dot(low_prev, prev[:, k_at])
                    r.dkv[block - 1, :, q_at] += dot_tn(low_prev, query)
                    r.dkv[block - 1, :, k_at] += dot_tn(low_probs_prev, grad)
                r.dkv[block, :, q_at] += dot_tn(low, query)
                r.dkv[block, :, k_at] += dot_tn(low_probs, grad)
                if rec:
                    state_probs = jnp.exp(dot_nt(query, state[:, k_at]) * scale - lse)
                    by_state = state_probs * (dot_nt(grad, state[:, v_at]) - delta) * scale
                    low_state = by_state.astype(bf16)
                    by_query += dot(low_state, state[:, k_at])
                    r.dskv[:, q_at] += dot_tn(low_state, query)
                    r.dskv[:, k_at] += dot_tn(state_probs.astype(bf16), grad)
                r.dqkv[block_at, q_at] = by_query.astype(bf16)

    def recur_back():
        qkv, state = r.qkv_v.at[0], r.sqkv_v.at[0]

        @pl.loop(0, length // chunk)
        def _(index):
            tick_at(index, 2)
            at = pl.ds(pl.multiple_of(index * chunk, chunk), chunk)
            for head in range(heads):
                q_at, k_at, v_at = (columns(head, part) for part in range(3))
                query, key, value = state[at, q_at], qkv[:, k_at], qkv[:, v_at]
                logits = dot_nt(query, key) * scale
                logits = jnp.where(r.valid[0:1, :] > 0.5, logits, negative)
                probs = jnp.exp(logits - r.rlse_v[at, head : head + 1])
                grad = r.dsout[at, q_at]
                delta = jnp.sum(
                    grad.astype(f32) * r.sout_v[0, at, q_at].astype(f32), axis=-1, keepdims=True
                )
                low = (probs * (dot_nt(grad, value) - delta) * scale).astype(bf16)
                r.dsqkv[at, q_at] = dot(low, key).astype(bf16)
                r.dkv[0, :, q_at] += dot_tn(low, query)
                r.dkv[0, :, k_at] += dot_tn(probs.astype(bf16), grad)

    def close_keys(block):
        r.dqkv[block_rows(block), width:] = r.dkv[block].astype(bf16)

    def close_state(block):
        r.dsqkv[block_rows(block), width:] = r.dskv[...].astype(bf16)
        if block == 1:
            r.dskv[...] = jnp.zeros(r.dskv.shape, f32)

    def input_back(block, to):
        rows = block_rows(block)
        reduce_back(
            [
                (r.dqkv.at[rows, part * width : (part + 1) * width], r.wqkv_v.at[part])
                for part in range(3)
            ],
            to,
        )

    def state_back(block, to):
        rows = block_rows(block)
        reduce_back(
            [
                (r.dsqkv.at[rows, part * width : (part + 1) * width], r.wsqkv_v.at[part])
                for part in ((0, 1, 2) if block == 0 else (1, 2))
            ],
            to,
        )

    def take_input(block, from_input):
        by_norm = from_input.finish()
        rows = r.x[block, place.core_rows(), :].astype(f32)
        by_rows, by_gain, by_shift = norm_back(rows, gain(0), by_norm)
        add_small(GAIN0, by_gain)
        add_small(SHIFT0, by_shift)
        own = r.ig_v.at[block, place.core_rows()]
        own[...] += by_rows
        return net.copy(own, own, place.core)

    def take_state(rows, from_state):
        by_rows, by_gain, by_shift = norm_back(rows, r.sgain[...], from_state.finish())
        add_small(SGAIN, by_gain)
        add_small(SSHIFT, by_shift)
        return by_rows

    def close_bias():
        tile = r.dbias.shape[1]
        for head in range(heads):
            folded = r.dbias[head, :, :length] + r.dbias[head, :, length:]
            row = lax.broadcasted_iota(jnp.int32, folded.shape, 0)
            bit = 1
            while bit < tile:
                moved = pltpu.roll(folded, length - bit, axis=1)
                folded = jnp.where((row & bit) != 0, moved, folded)
                bit *= 2
            small[BY_DISTANCE : BY_DISTANCE + 1, head * length : (head + 1) * length] = jnp.sum(
                folded, axis=0, keepdims=True
            )

    if rec:
        at_qkv, at_sqkv = 0, 4 * width
    else:
        at_up, at_down, at_qkv = 0, model, model + hidden
    at_out = 3 * width

    feed = [scatter(0), scatter(1)]
    inputs = [scatter(2 if rec else 0), scatter(1)]
    if not rec:
        grads = [gather(r.g.at[block_rows(block)]) for block in range(2)]
    hiddens = [gather(r.hg.at[block_rows(block)]) for block in range(2)]
    if rec:
        states = [scatter(0), scatter(0)]
        updates = gather(r.ug)
    if not rec:
        for block in (1, 0):
            r.g[pl.ds(place_row(block), place.quarter), :] = own_grad(block).astype(bf16)
            grads[block].start()
        local.wait(parts)
        launch(rest_flow)
    fill_bias(r.bias, bias_rows(r.rel[layer], r.buckets[...], place.c))
    local.wait(*act)
    if rec:
        weight_grad(r.act, r.g, r.by_down)
        launch(down_flow)
    else:
        tick()
        grads[1].forward()
        tick()
        grads[1].finish()
    local.wait(wdown, pre, wup)
    feed_back(1)
    tick()
    reduce_back([(r.dpre.at[block_rows(1)], r.wup_v)], feed[1])
    if rec:
        tick()
    else:
        grads[0].forward()
        tick()
        grads[0].finish()
    feed_back(0)
    feed[1].middle()
    tick()
    reduce_back([(r.dpre.at[block_rows(0)], r.wup_v)], feed[0])
    tick()
    feed[0].middle()
    if not rec:
        weight_grad(r.act, r.g, r.by_down)
        down_out = local.copy(r.by_down, r.dw.at[at_down:at_qkv])
    tick()
    local.wait(wn)
    weight_grad(r.wn_v, r.dpre, r.act)
    if rec:
        launch(up_flow)
        sn_in = local.copy(r.sn, r.pre_v)
    else:
        local.copy(r.act, r.dw.at[at_up:at_down])
    tick()
    u_in = local.copy(r.u, r.wn_v)
    local.wait(hidden_rows)
    take_feed(1, feed[1])
    hiddens[1].start()
    tick(2)
    take_feed(0, feed[0])
    hiddens[0].start()
    tick(2)
    hiddens[1].forward()
    tick()
    hiddens[1].finish()
    local.wait(*attention)
    branch_back(1)
    tick()
    attend_back(1)
    close_keys(1)
    feed[0].release()
    feed[1].release()
    if rec:
        close_state(1)
        state_back(1, states[1])
        tick()
    hiddens[0].forward()
    local.wait(wqkv)
    input_back(1, inputs[1])
    if rec:
        states[1].middle()
    tick()
    hiddens[0].finish()
    branch_back(0)
    if rec:
        tick(2)
        local.wait(*chain)
        gate = jax.nn.sigmoid(r.gate[...])
        by_state = take_state(r.s1_v[...], states[1])
        states[1].release()
        before = r.state[place.core_rows(), :].astype(f32)
        add_small(
            GATE,
            jnp.sum(by_state * (before - r.z_v[...]) * gate * (1.0 - gate), axis=0, keepdims=True),
        )
        r.ug[place.rows(), :] = ((1.0 - gate) * by_state).astype(bf16)
        updates.start()
    inputs[1].middle()
    tick()
    attend_back(0)
    tick()
    if rec:
        updates.forward()
        tick()
        updates.finish()
        r.dsout[...] = dot_nt(r.ug[...], r.wsout_v[...]).astype(bf16)
        recur_back()
        tick()
    close_keys(0)
    input_back(0, inputs[0])
    tick()
    if rec:
        close_state(0)
        state_back(0, states[0])
        tick()
    sent = [take_input(1, inputs[1])]
    inputs[0].middle()
    tick()
    if rec:
        states[0].middle()
    weight_grad(r.att_v, r.hg, r.dpre, at_out)
    close_bias()
    local.wait(u_in)
    projection_grad(r.wn_v, r.dqkv, r.dpre)
    local.copy(r.dpre, r.dw.at[at_qkv : at_qkv + 4 * width])
    tick()
    if rec:
        r.dsqkv[block_rows(1), 0:width] = jnp.zeros((length, width), bf16)
        local.wait(sn_in)
        projection_grad(r.pre_v, r.dsqkv, r.g)
        tick()
        weight_grad(r.sout_v.at[0], r.ug, r.g, at_out)
        local.copy(r.g, r.dw.at[at_sqkv:])
    sent.append(take_input(0, inputs[0]))
    if rec:
        take_state(r.state[place.core_rows(), :].astype(f32), states[0])
    local.copy(small, r.small)
    for made in sent:
        made.wait_recv()
    local.copy(r.ig_v, r.ig)
    while any(flow.done < flow.total for flow in flows):
        tick()
    for flow in flows:
        flow.finish()
    local.drain()
    net.drain()


def backward_layer(layer, n, block_len, small, valid, weights, grad_rows, rows, state, kept, parts=None):
    rec = layer == 1
    wqkv, wout, wup, wdown = weights[:4]
    model = rows.shape[2]
    width, hidden = wqkv.shape[3], wup.shape[2]
    quarter = block_len // 4
    heads = small.rel.shape[1] // 2

    def held(shape, dtype):
        return jax.ShapeDtypeStruct(shape, dtype)

    dw_rows = 8 * width if rec else model + hidden + 4 * width
    ring_rows = model + hidden if rec else parts.shape[0]
    outs = dict(
        full=held((2, ring_rows, model), bf16),
        dw=held((dw_rows, model), bf16),
        small=held((SMALL_ROWS, model), f32),
        ig=held((2, 2 * quarter, model), f32),
    )
    ins = dict(
        gy=grad_rows, x=rows, gain=small.gain, rel=small.rel, buckets=small.buckets, valid=valid
    )

    def flat(array):
        return array.reshape((-1,) + array.shape[2:])

    stacked = dict(wqkv=wqkv, wout=wout, wup=wup, wdown=wdown)
    copied = dict(
        qkv=kept.qkv, lse=kept.lse, att=flat(kept.att), wn=flat(kept.wn), pre=flat(kept.pre), h=kept.h
    )
    late = dict(act_in=flat(kept.act), u=flat(kept.u))
    if rec:
        ins.update(state=state, sgain=small.sgain, sshift=small.sshift, gate=small.gate)
        copied.update(wsqkv=weights[4], wsout=weights[5])
        copied.update(sqkv=kept.sqkv, rlse=kept.rlse, sout=kept.sout, s1=kept.s1, z=kept.z)
        late.update(sn=flat(kept.sn), g_in=flat(parts))
    else:
        late.update(parts=parts)
    far_ins = {**stacked, **copied, **late}
    scatters = 6 if rec else 4
    copies = (3 * 6 + 3 * 3 + 2) if rec else (3 * 4 + 3 * 4 + 2)
    scratch = dict(small_v=pltpu.VMEM(outs["small"].shape, f32), ig_v=pltpu.VMEM(outs["ig"].shape, f32))
    for name, array in stacked.items():
        scratch[name + "_v"] = pltpu.VMEM(array.shape[1:], array.dtype)
    for name, array in copied.items():
        scratch[name + "_v"] = pltpu.VMEM(array.shape, array.dtype)
    scratch.update(
        g=pltpu.VMEM((2 * block_len, model), bf16),
        hg=pltpu.VMEM((2 * block_len, model), bf16),
        work=pltpu.VMEM((2 * hidden, model), bf16),
        dpre=pltpu.VMEM((2 * block_len, hidden), bf16),
        datt=pltpu.VMEM((2, block_len, width), bf16),
        dkv=pltpu.VMEM((2, block_len, 2 * width), f32),
        dqkv=pltpu.VMEM((2 * block_len, 3 * width), bf16),
        dbias=pltpu.VMEM((heads, min(128, block_len), 2 * block_len), f32),
        bias=pltpu.VMEM((heads, min(128, block_len), 2 * block_len), f32),
        part=pltpu.VMEM((scatters // 2, block_len, model), bf16),
        near=pltpu.VMEM((scatters, 2, quarter, model), bf16),
        out=pltpu.VMEM((scatters // 2, quarter, model), bf16),
        far=pltpu.VMEM((scatters, quarter, model), bf16),
        send_sems=pltpu.SemaphoreType.DMA((copies,)),
        recv_sems=pltpu.SemaphoreType.DMA((copies,)),
        local_sems=pltpu.SemaphoreType.DMA((len(far_ins) + 6,)),
    )
    if rec:
        scratch.update(
            ug=pltpu.VMEM((block_len, model), bf16),
            dsout=pltpu.VMEM((block_len, width), bf16),
            dskv=pltpu.VMEM((block_len, 2 * width), f32),
            dsqkv=pltpu.VMEM((2 * block_len, 3 * width), bf16),
        )
    else:
        scratch.update(mine=pltpu.VMEM((ring_rows, model), bf16))
    ring_names = []
    for flow_rows in (model, hidden) if rec else (ring_rows,):
        flow_scratch = ring_scratch(n, flow_rows, model, 2)
        flow_scratch = {name + str(len(ring_names)): kind for name, kind in flow_scratch.items()}
        scratch.update(flow_scratch)
        ring_names.append(list(flow_scratch))
    anywhere = pl.BlockSpec(memory_space=pl.ANY)
    inside = pl.BlockSpec(memory_space=pltpu.VMEM)
    results = pl.pallas_call(
        partial(backward_kernel, layer, n, ring_names, [*ins, *far_ins, *outs, *scratch]),
        out_shape=tuple(outs.values()),
        in_specs=[inside] * len(ins) + [anywhere] * len(far_ins),
        out_specs=[anywhere] * len(outs),
        scratch_shapes=list(scratch.values()),
        compiler_params=pltpu.CompilerParams(
            collective_id=3 + layer, has_side_effects=True, vmem_limit_bytes=VMEM_LIMIT
        ),
        name="backward_recurrent" if rec else "backward_local",
    )(*ins.values(), *far_ins.values())
    return SimpleNamespace(**dict(zip(outs, results)))


def place_kernel(
    width, hidden, feed_1, rest_1, full_0, acts_0, acts_1, igs_0, igs_1, state, sums, buckets,
    qkv, out, up, down, sqkv, sout, acts, igs, final, gain, shift, rel, up_bias, down_bias, sgain, sshift, gate,
    inward, outward, acts_v, igs_v, state_v, igs_tiles, state_tiles, in_sems, out_sems, row_sems,
):
    model = full_0.shape[2]
    layer = lax.axis_index("section")
    slots = inward.shape[0]

    rows_in = []
    for index, (first, second, target) in enumerate(((acts_0, acts_1, acts_v), (igs_0, igs_1, igs_v))):
        pl.when(layer == 0)(pltpu.make_async_copy(first, target, row_sems.at[index]).start)
        pl.when(layer == 1)(pltpu.make_async_copy(second, target, row_sems.at[index]).start)
        rows_in.append(pltpu.make_async_copy(first, target, row_sems.at[index]))
    rows_in.append(pltpu.make_async_copy(state, state_v, row_sems.at[2]))
    rows_in[2].start()
    at_rest = model + hidden
    jobs = []
    for half in range(2):
        columns = slice(half * width, (half + 1) * width)

        def projection(target):
            return [target.at[index : index + width, columns] for index in range(0, model, width)]

        for row in range(0, model, width):
            wide = slice(half * hidden, (half + 1) * hidden)
            jobs.append((half, (feed_1, row), row, [up.at[0, row : row + width, wide]]))
        for row in range(0, hidden, width):
            at = half * hidden + row
            jobs.append((half, (feed_1, model + row), model + row, [down.at[0, at : at + width]]))
        for part in range(3):
            row = part * width
            jobs.append((half, (rest_1, row), at_rest + row, projection(qkv.at[0, part])))
            jobs.append((half, (rest_1, 4 * width + row), None, projection(sqkv.at[part])))
        jobs.append((half, (rest_1, 3 * width), at_rest + 3 * width, [out.at[0, columns]]))
        jobs.append((half, (rest_1, 7 * width), None, [sout.at[columns]]))

    def load(index, start):
        half, (array, row), row_0, _ = jobs[index]
        slot = index % slots

        def made(source, at):
            return pltpu.make_async_copy(source.at[half, at : at + width], inward.at[slot], in_sems.at[slot])

        if not start:
            made(array, row).wait()
        elif row_0 is None:
            made(array, row).start()
        else:
            pl.when(layer == 1)(lambda: made(array, row).start())
            pl.when(layer == 0)(lambda: made(full_0, row_0).start())

    def stores(index):
        targets, slot = jobs[index][3], index % slots
        step = model // len(targets)
        return [
            pltpu.make_async_copy(
                outward.at[slot, :, k * step : (k + 1) * step], target, out_sems.at[slot, k]
            )
            for k, target in enumerate(targets)
        ]

    for index in range(slots):
        load(index, True)
    for index in range(len(jobs)):
        slot = index % slots
        load(index, False)
        if index >= slots:
            for made in stores(index - slots):
                made.wait()
        outward[slot] = inward[slot].astype(f32)
        for made in stores(index):
            made.start()
        if index + slots < len(jobs):
            load(index + slots, True)
    mine = [jnp.where(layer == 0, sums[index, :SMALL_ROWS], sums[index, SMALL_ROWS:]) for index in range(3)]
    gain[0] = mine[2][GAIN0 : GAIN1 + 1]
    shift[0] = mine[2][SHIFT0 : SHIFT1 + 1]
    down_bias[...] = mine[2][DOWN_BIAS : DOWN_BIAS + 1]
    for target, row in ((sgain, SGAIN), (sshift, SSHIFT), (gate, GATE)):
        target[...] = sums[2, SMALL_ROWS + row : SMALL_ROWS + row + 1]
    by_core = [jnp.where(layer == 0, mine[0], mine[1]), jnp.where(layer == 0, mine[1], mine[0])]
    heads, length = rel.shape[1] // 2, buckets.shape[1]
    hot = back_hot(buckets[...], rel.shape[2])
    for half in range(2):
        up_bias[:, half * hidden : (half + 1) * hidden] = by_core[half][UP_BIAS : UP_BIAS + 1, :hidden]
        for head in range(heads):
            row = by_core[half][BY_DISTANCE : BY_DISTANCE + 1, head * length : (head + 1) * length]
            at = half * heads + head
            row = jnp.broadcast_to(row, (16, length))
            rel[0, at : at + 1, :] = sum(dot_nt(part, hot) for part in in_parts(row))[:1]

    rows_out = []
    rows_in[0].wait()
    rows_out.append(pltpu.make_async_copy(acts_v, acts, row_sems.at[0]))
    rows_out[0].start()
    tiles = model // 128
    for index, source, target in ((1, igs_v, igs_tiles), (2, state_v, state_tiles)):
        rows_in[index].wait()
        for tile in range(tiles):
            target[..., tile, :] = source[..., tile * 128 : (tile + 1) * 128]
        rows_out.append(pltpu.make_async_copy(target, igs if index == 1 else final, row_sems.at[index]))
        rows_out[index].start()
    for index in range(len(jobs) - slots, len(jobs)):
        for made in stores(index):
            made.wait()
    for made in rows_out:
        made.wait()


def place_gradients(feed_1, rest_1, full_0, acts, igs, final, sums, buckets, bucket_count, chip_heads, width, hidden):
    model = full_0.shape[2]
    anywhere = pl.BlockSpec(memory_space=pl.ANY)
    inside = pl.BlockSpec(memory_space=pltpu.VMEM)
    slots, tiles = 4, model // 128
    blocks, rows = acts[0].shape[:2]
    far_shapes = (
        ((1, 3, model, 2 * width), f32),
        ((1, 2 * width, model), f32),
        ((1, model, 2 * hidden), f32),
        ((1, 2 * hidden, model), f32),
        ((3, model, 2 * width), f32),
        ((2 * width, model), f32),
        ((blocks, rows, model), bf16),
        ((blocks, rows, tiles, 128), f32),
        ((rows, tiles, 128), f32),
    )
    near_shapes = (
        (1, 2, model),
        (1, 2, model),
        (1, chip_heads, bucket_count),
        (1, 2 * hidden),
        (1, model),
        (1, model),
        (1, model),
        (1, model),
    )
    return pl.pallas_call(
        partial(place_kernel, width, hidden),
        out_shape=[jax.ShapeDtypeStruct(*kind) for kind in far_shapes]
        + [jax.ShapeDtypeStruct(shape, f32) for shape in near_shapes],
        in_specs=[anywhere] * 8 + [inside] * 2,
        out_specs=[anywhere] * len(far_shapes) + [inside] * len(near_shapes),
        scratch_shapes=[
            pltpu.VMEM((slots, width, model), bf16),
            pltpu.VMEM((slots, width, model), f32),
            pltpu.VMEM((blocks, rows, model), bf16),
            pltpu.VMEM((blocks, rows, model), f32),
            pltpu.VMEM((rows, model), f32),
            pltpu.VMEM((blocks, rows, tiles, 128), f32),
            pltpu.VMEM((rows, tiles, 128), f32),
            pltpu.SemaphoreType.DMA((slots,)),
            pltpu.SemaphoreType.DMA((slots, model // width)),
            pltpu.SemaphoreType.DMA((3,)),
        ],
        compiler_params=pltpu.CompilerParams(vmem_limit_bytes=VMEM_LIMIT),
        name="place_gradients",
    )(feed_1, rest_1, full_0, *acts, *igs, final, sums, buckets)


def local_part(
    tokens, valid_mask, buckets, state_init, norm_gain, norm_shift, w_qkv, w_out, rel_bias, w_up, up_bias,
    w_down, down_bias, state_gain, state_shift, w_state_qkv, w_state_out, gate_bias, cotangent,
):
    block_len = valid_mask.shape[1]
    model = tokens.shape[3]
    bucket_count, chip_heads = rel_bias.shape[1:]
    docs = lax.axis_size("dp")
    valid = valid_mask[:, :, 0].astype(f32)
    cot_rows = cotangent[:, :, 0, :]
    rows = tokens[:, :, 0, :]
    state = state_init[:, 0, :]
    smalls = (
        norm_gain, norm_shift, up_bias[:, None, :], down_bias[:, None, :], jnp.swapaxes(rel_bias, 1, 2)
    )
    *weights, cot_all, gains, shifts, up_biases, down_biases, rels = share_weights(
        block_len, w_qkv[0], w_out[0], w_up[0], w_down[0], w_state_qkv, w_state_out, cot_rows, *smalls
    )
    small = SimpleNamespace(
        gain=gains,
        shift=shifts,
        up_bias=up_biases,
        down_bias=down_biases,
        rel=rels,
        buckets=buckets[None],
        sgain=state_gain[None],
        sshift=state_shift[None],
        gate=gate_bias[None],
    )
    kept0 = forward_layer(0, block_len, small, valid, weights, rows, state)
    kept1 = forward_layer(1, block_len, small, valid, weights, kept0.acts, state)
    grad1 = backward_layer(1, docs, block_len, small, valid, weights, cot_rows, kept0.acts, state, kept1, cot_all)
    grad0 = backward_layer(0, docs, block_len, small, valid, weights, grad1.ig, rows, state, kept0, grad1.dw)
    full, sums = sum_gradients(docs, grad0.dw, grad0.small, grad1.small)
    (
        qkv_grad, out_grad, up_grad, down_grad, state_qkv_grad, state_out_grad, acts, input_grads, final,
        gain_grad, shift_grad, rel_grad, up_bias_grad, down_bias_grad, sgain_grad, sshift_grad, gate_grad,
    ) = place_gradients(
        grad1.full, grad0.full, full, (kept0.acts, kept1.acts), (grad0.ig, grad1.ig), kept1.final, sums,
        small.buckets, bucket_count, chip_heads, weights[0].shape[3], weights[2].shape[2],
    )
    return (
        acts[None, :, :, None, :],
        input_grads.reshape(1, 2, -1, 1, model),
        final.reshape(-1, 1, model),
        gain_grad,
        shift_grad,
        qkv_grad,
        out_grad,
        jnp.swapaxes(rel_grad, 1, 2),
        up_grad,
        up_bias_grad,
        down_grad,
        down_bias_grad,
        sgain_grad[0],
        sshift_grad[0],
        state_qkv_grad,
        state_out_grad,
        gate_grad[0],
    )


def solution(mesh):
    in_specs = (
        P(None, "mp", "dp", None),
        P(None, None, "dp"),
        P(),
        P("mp", "dp", None),
        P("section", None, None),
        P("section", None, None),
        P("section", None, None, "mp"),
        P("section", "mp", None),
        P("section", None, "mp"),
        P("section", None, "mp"),
        P("section", "mp"),
        P("section", "mp", None),
        P("section", None),
        P(),
        P(),
        P(None, None, "mp"),
        P("mp", None),
        P(),
        P(None, "mp", "dp", None),
    )
    out_specs = (
        P("section", None, "mp", "dp", None),
        P("section", None, "mp", "dp", None),
        P("mp", "dp", None),
        P("section", None, None),
        P("section", None, None),
        P("section", None, None, "mp"),
        P("section", "mp", None),
        P("section", None, "mp"),
        P("section", None, "mp"),
        P("section", "mp"),
        P("section", "mp", None),
        P("section", None),
        P(),
        P(),
        P(None, None, "mp"),
        P("mp", None),
        P(),
    )
    return jax.shard_map(local_part, mesh=mesh, in_specs=in_specs, out_specs=out_specs, check_vma=False)
```

```python
from functools import partial
from types import SimpleNamespace

import jax
import jax.numpy as jnp
from jax import lax
from jax.experimental import pallas as pl
from jax.experimental.pallas import tpu as pltpu
from jax.sharding import PartitionSpec as P

MESH = pl.DeviceIdType.MESH
f32, bf16 = jnp.float32, jnp.bfloat16
eps = 1e-05
negative = -1000000000.0
VMEM_LIMIT = 62 * 1024 * 1024


def dot(left, right):
    return lax.dot_general(left, right, (((1,), (0,)), ((), ())), preferred_element_type=f32)


def dot_nt(left, right):
    return lax.dot_general(left, right, (((1,), (1,)), ((), ())), preferred_element_type=f32)


def dot_tn(left, right):
    return lax.dot_general(left, right, (((0,), (0,)), ((), ())), preferred_element_type=f32)


def norm_parts(values):
    average = jnp.mean(values, axis=-1, keepdims=True)
    centered = values - average
    spread = jnp.mean(centered * centered, axis=-1, keepdims=True)
    scale = lax.rsqrt(spread + eps)
    return centered * scale, scale


def layer_norm(values, gain, shift):
    return norm_parts(values)[0] * gain + shift


class Place:
    def __init__(self, rows):
        self.c, self.x = lax.axis_index("section"), lax.axis_index("mp")
        self.core = {"section": 1 - self.c}
        self.chip = {"mp": 1 - self.x}
        self.quarter, self.half = rows // 4, rows // 2

    def rows(self, x_other=False, c_other=False):
        x = 1 - self.x if x_other else self.x
        c = 1 - self.c if c_other else self.c
        return pl.ds(pl.multiple_of(x * self.half + c * self.quarter, self.quarter), self.quarter)

    def chip_rows(self, x_other=False):
        x = 1 - self.x if x_other else self.x
        return pl.ds(pl.multiple_of(x * self.half, self.half), self.half)

    def core_rows(self, c_other=False):
        c = 1 - self.c if c_other else self.c
        return pl.ds(pl.multiple_of(c * self.quarter, self.quarter), self.quarter)

    def meet(self):
        barrier = pltpu.get_barrier_semaphore()
        for other in (self.core, self.chip):
            pl.semaphore_signal(barrier, inc=1, device_id=other, device_id_type=MESH)
        pl.semaphore_wait(barrier, 2)


class Net:
    def __init__(self, send_sems, recv_sems):
        self.send_sems, self.recv_sems, self.copies = send_sems, recv_sems, []

    def copy(self, source, target, device):
        index = len(self.copies)
        made = pltpu.make_async_remote_copy(
            src_ref=source,
            dst_ref=target,
            send_sem=self.send_sems.at[index],
            recv_sem=self.recv_sems.at[index],
            device_id=device,
            device_id_type=MESH,
        )
        made.start()
        self.copies.append(made)
        return made

    def sent(self, *copies):
        for made in copies:
            made.wait_send()
        self.copies = [None if any(held is made for made in copies) else held for held in self.copies]

    def drain(self):
        for made in self.copies:
            if made is not None:
                made.wait_send()


class Local:
    def __init__(self, sems):
        self.sems, self.copies, self.waited = sems, [], set()

    def copy(self, source, target):
        made = pltpu.make_async_copy(source, target, self.sems.at[len(self.copies)])
        made.start()
        self.copies.append(made)
        return len(self.copies) - 1

    def wait(self, *indices):
        for index in indices:
            if index not in self.waited:
                self.waited.add(index)
                self.copies[index].wait()

    def drain(self):
        self.wait(*range(len(self.copies)))


class Gather:
    def __init__(self, place, net, buffer):
        self.place, self.net, self.buffer = place, net, buffer

    def start(self):
        own = self.buffer.at[self.place.rows()]
        self.from_chip = self.net.copy(own, own, self.place.chip)
        self.from_core = self.net.copy(own, own, self.place.core)

    def forward(self):
        self.from_chip.wait_recv()
        passed = self.buffer.at[self.place.rows(x_other=True)]
        self.passed = self.net.copy(passed, passed, self.place.core)

    def finish(self):
        self.from_core.wait_recv()
        self.passed.wait_recv()


class Scatter:
    def __init__(self, place, net, part, near, out, far):
        self.place, self.net, self.part = place, net, part
        self.near, self.out, self.far = near, out, far

    def send(self, x_other):
        slot = 0 if x_other else 1
        rows = self.place.rows(x_other=x_other, c_other=True)
        made = self.net.copy(self.part.at[rows], self.near.at[slot], self.place.core)
        if x_other:
            self.first = made
        else:
            self.second = made

    def middle(self):
        self.first.wait_recv()
        mine = self.part[self.place.rows(x_other=True), :].astype(f32)
        self.out[...] = (mine + self.near[0].astype(f32)).astype(bf16)
        self.across = self.net.copy(self.out, self.far, self.place.chip)

    def finish(self):
        self.second.wait_recv()
        total = self.part[self.place.rows(), :].astype(f32) + self.near[1].astype(f32)
        self.across.wait_recv()
        return total + self.far[...].astype(f32)

    def release(self):
        self.net.sent(self.first, self.second, self.across)


def back_hot(buckets, count):
    length = buckets.shape[1]
    hot = lax.broadcasted_iota(jnp.int32, (count, length), 0) == buckets
    both = lax.broadcasted_iota(jnp.int32, (length, length), 0) + lax.broadcasted_iota(
        jnp.int32, (length, length), 1
    )
    turn = (both == 0) | (both == length)
    return dot(jnp.where(hot, 1.0, 0.0).astype(bf16), jnp.where(turn, 1.0, 0.0).astype(bf16)).astype(bf16)


def in_parts(values):
    high = values.astype(bf16)
    rest = values - high.astype(f32)
    middle = rest.astype(bf16)
    return high, middle, (rest - middle.astype(f32)).astype(bf16)


def bias_rows(rel, buckets, c):
    hot = back_hot(buckets, rel.shape[1])
    rows = sum(dot(part, hot) for part in in_parts(rel))
    heads = rel.shape[0] // 2
    return jnp.where(c == 0, rows[:heads], rows[heads:])


def fill_bias(bias, row0):
    head_count, length = row0.shape
    for head in range(head_count):
        start = jnp.broadcast_to(row0[head : head + 1], (bias.shape[1], length))
        rolled = pltpu.roll(start, 0, axis=1, stride=1, stride_axis=0)
        bias[head, :, :length] = rolled
        bias[head, :, length:] = rolled


def bias_columns(index, chunk, length):
    return pl.ds(pl.multiple_of(length - index * chunk, chunk), length)


def window_logits(query, key_cur, key_prev, bias, valid, block, first_row, scale):
    logits = dot_nt(query, key_cur)
    rows = first_row + lax.broadcasted_iota(jnp.int32, logits.shape, 0)
    here = lax.broadcasted_iota(jnp.int32, logits.shape, 1) <= rows
    usable = valid[block : block + 1, :] > 0.5
    if key_prev is None:
        keep = here & usable
    else:
        logits = jnp.where(here, logits, dot_nt(query, key_prev))
        keep = jnp.where(here, valid[block : block + 1, :], valid[block - 1 : block, :]) > 0.5
    return jnp.where(keep, logits * scale + bias, negative), here


def forward_kernel(layer, names, *refs):
    r = SimpleNamespace(**dict(zip(names, refs)))
    rec = layer == 1
    length = r.u_v.shape[1]
    heads = r.rel.shape[1] // 2
    head_size = r.att_v.shape[2] // heads
    width = heads * head_size
    scale = head_size ** (-0.5)
    place = Place(length)
    net, local = Net(r.send_sems, r.recv_sems), Local(r.local_sems)
    chunk = min(128, length)

    place.meet()
    if rec:
        load = [local.copy(r.wqkv.at[layer], r.wqkv_v), local.copy(r.wout.at[layer], r.wout_v)]
        load_mlp = [local.copy(r.wup.at[layer], r.wup_v), local.copy(r.wdown.at[layer], r.wdown_v)]
        load_state = [local.copy(r.wsqkv, r.wsqkv_v), local.copy(r.wsout, r.wsout_v)]
    else:
        def share(source, target, axis=None):
            def half(c):
                if axis is None:
                    return source.at[0]
                size = source.shape[axis] // 2
                index = [slice(None)] * len(source.shape)
                index[axis] = pl.ds(pl.multiple_of(c * size, size), size)
                return source.at[tuple(index)]

            target = target.at[place.c]
            return net.copy(half(1 - place.c), target, place.core), local.copy(half(place.c), target)

        def shared(*pairs):
            for far, near in pairs:
                far.wait_recv()
                local.wait(near)

        smalls = [
            share(r.gain_own, r.gain),
            share(r.shift_own, r.shift),
            share(r.up_bias_own, r.up_bias),
            share(r.down_bias_own, r.down_bias),
            share(r.rel_own, r.rel),
        ]
        first_weights = [share(r.qkv_own, r.wqkv_s, 2), share(r.out_own, r.wout_s, 0)]
        later_weights = [share(r.up_own, r.wup_s, 1), share(r.down_own, r.wdown_s, 0)]
        state_weights = []
        for source, target, axis in ((r.sqkv_own, r.wsqkv_s, 2), (r.sout_own, r.wsout_s, 0)):
            size = source.shape[axis] // 2
            at = pl.ds(pl.multiple_of(place.c * size, size), size)
            part = source.at[:, :, at] if axis == 2 else source.at[at]
            state_weights.append(local.copy(part, target))
        r.wqkv_v, r.wout_v = r.wqkv_s.at[layer], r.wout_s.at[layer]
        r.wup_v, r.wdown_v = r.wup_s.at[layer], r.wdown_s.at[layer]

    gain = lambda index: r.gain[layer, index : index + 1, :]
    shift = lambda index: r.shift[layer, index : index + 1, :]

    def gather(buffer):
        return Gather(place, net, buffer)

    scatter_count = [0]

    def scatter():
        index = scatter_count[0]
        scatter_count[0] += 1
        return Scatter(
            place, net, r.part.at[index], r.near.at[index], r.out.at[index], r.far.at[index]
        )

    def norm_state(rows, index):
        r.sn_v[index, place.rows(), :] = layer_norm(rows, r.sgain[...], r.sshift[...]).astype(bf16)

    def norm_first(block):
        rows = r.x[block, place.core_rows(), :].astype(f32)
        r.u_v[block, place.rows(), :] = layer_norm(rows, gain(0), shift(0)).astype(bf16)

    def project(source, weights, target):
        for part in range(3):
            target[:, part * width : (part + 1) * width] = dot(source[...], weights[part]).astype(bf16)

    def reduce_from(values, weights, to):
        columns = weights.shape[1]
        step = min(512, columns)
        for x_other in (True, False):
            rows = place.chip_rows(x_other)

            @pl.loop(0, columns // step)
            def _(index):
                at = pl.ds(pl.multiple_of(index * step, step), step)
                to.part[rows, at] = dot(values[rows, :], weights[:, at]).astype(bf16)

            to.send(x_other)

    def head_columns(head):
        return [slice(part * width + head * head_size, part * width + (head + 1) * head_size) for part in range(3)]

    def pack(columns):
        lane = lax.broadcasted_iota(jnp.int32, (chunk, 128), 1)
        packed = jnp.zeros((chunk, 128), f32)
        for index, column in enumerate(columns):
            packed = jnp.where(lane == index, column, packed)
        return packed

    def attend_window(index, head, block):
        qkv = r.qkv_v.at[block]
        prev = r.qkv_v.at[block - 1] if block > 0 else None
        at = pl.ds(pl.multiple_of(index * chunk, chunk), chunk)
        q_at, k_at, v_at = head_columns(head)
        logits, here = window_logits(
            qkv[at, q_at],
            qkv[:, k_at],
            None if prev is None else prev[:, k_at],
            r.bias[head, :, bias_columns(index, chunk, length)],
            r.valid,
            block,
            index * chunk,
            scale,
        )
        peak = jnp.max(logits, axis=-1, keepdims=True)
        probs = jnp.exp(logits - peak)
        total = jnp.sum(probs, axis=-1, keepdims=True)
        if prev is None:
            result = dot(probs.astype(bf16), qkv[:, v_at])
        else:
            result = dot(jnp.where(here, probs, 0.0).astype(bf16), qkv[:, v_at])
            result += dot(jnp.where(here, 0.0, probs).astype(bf16), prev[:, v_at])
        return peak, total, result

    def attend_state(index, head, block, window):
        peak_window, total_window, result_window = window
        at = pl.ds(pl.multiple_of(index * chunk, chunk), chunk)
        q_at, k_at, v_at = head_columns(head)
        state = r.sqkv_v.at[block]
        logits = dot_nt(r.qkv_v[block, at, q_at], state[:, k_at]) * scale
        peak = jnp.maximum(peak_window, jnp.max(logits, axis=-1, keepdims=True))
        less = jnp.exp(peak_window - peak)
        probs = jnp.exp(logits - peak)
        total = total_window * less + jnp.sum(probs, axis=-1, keepdims=True)
        return peak, total, result_window * less + dot(probs.astype(bf16), state[:, v_at])

    def attend(block, window=True, state=rec):
        @pl.loop(0, length // chunk)
        def _(index):
            at = pl.ds(pl.multiple_of(index * chunk, chunk), chunk)
            kept = []
            for head in range(heads):
                q_at = head_columns(head)[0]
                if window:
                    found = attend_window(index, head, block)
                else:
                    found = (
                        r.lse_v[block, at, 2 * head : 2 * head + 1],
                        r.lse_v[block, at, 2 * head + 1 : 2 * head + 2],
                        r.early[at, q_at],
                    )
                if state:
                    found = attend_state(index, head, block, found)
                if state or not rec:
                    peak, total, result = found
                    r.att_v[block, at, q_at] = (result / total).astype(bf16)
                    kept.append(peak + jnp.log(total))
                else:
                    r.early[at, q_at] = found[2]
                    kept.extend(found[:2])
            r.lse_v[block, at, :] = pack(kept)

    def recur(block):
        qkv, state = r.qkv_v.at[block], r.sqkv_v.at[block]

        @pl.loop(0, length // chunk)
        def _(index):
            at = pl.ds(pl.multiple_of(index * chunk, chunk), chunk)
            lses = []
            for head in range(heads):
                q_at = slice(head * head_size, (head + 1) * head_size)
                k_at = slice(width + head * head_size, width + (head + 1) * head_size)
                v_at = slice(2 * width + head * head_size, 2 * width + (head + 1) * head_size)
                logits = dot_nt(state[at, q_at], qkv[:, k_at]) * scale
                logits = jnp.where(r.valid[block : block + 1, :] > 0.5, logits, negative)
                peak = jnp.max(logits, axis=-1, keepdims=True)
                probs = jnp.exp(logits - peak)
                total = jnp.sum(probs, axis=-1, keepdims=True)
                r.sout_v[block, at, q_at] = (dot(probs.astype(bf16), qkv[:, v_at]) / total).astype(bf16)
                lses.append(peak + jnp.log(total))
            if block == 0:
                r.rlse_v[at, :] = pack(lses)

    def take_branch(block, from_out):
        rows = r.x[block, place.core_rows(), :].astype(f32) + from_out.finish()
        r.h_v[block] = rows
        r.wn_v[block, place.rows(), :] = layer_norm(rows, gain(1), shift(1)).astype(bf16)

    def feed_up(block):
        columns = r.wup_v.shape[1]
        step = 256

        @pl.loop(0, columns // step)
        def _(index):
            at = pl.ds(pl.multiple_of(index * step, step), step)
            bias_at = pl.ds(pl.multiple_of(place.c * columns + index * step, step), step)
            pre = dot(r.wn_v[block], r.wup_v[:, at]) + r.up_bias[layer, :, bias_at]
            r.pre_v[block, :, at] = pre.astype(bf16)
            r.act_v[block, :, at] = (0.5 * pre * (1.0 + lax.erf(pre * (0.5**0.5)))).astype(bf16)

    def take_result(block, from_down):
        rows = r.h_v[block] + from_down.finish() + r.down_bias[layer]
        own = r.acts_v.at[block, place.core_rows()]
        own[...] = rows.astype(bf16)
        return net.copy(own, own, place.core)

    def cotangent(block):
        own = r.cot_v.at[block, place.rows()]
        local.wait(local.copy(r.cot.at[block, place.core_rows()], own))
        cot[block].start()

    branch = [scatter(), scatter()]
    result = [scatter(), scatter()]
    first = [gather(r.u_v.at[block]) for block in range(2)]
    second = [gather(r.wn_v.at[block]) for block in range(2)]
    if rec:
        update = [scatter()]
        state = [gather(r.sn_v.at[block]) for block in range(2)]
        gate = jax.nn.sigmoid(r.gate[...])
        norm_state(r.state[place.core_rows(), :].astype(f32), 0)
        state[0].start()
    else:
        cot = [gather(r.cot_v.at[block]) for block in range(2)]
        cotangent(1)
        shared(*smalls)
    norm_first(0)
    first[0].start()
    norm_first(1)
    first[1].start()
    fill_bias(r.bias, bias_rows(r.rel[layer], r.buckets[...], place.c))
    if rec:
        state[0].forward()
    if not rec:
        cot[1].forward()
    first[0].forward()
    if rec:
        state[0].finish()
        local.wait(*load_state)
        project(r.sn_v.at[0], r.wsqkv_v, r.sqkv_v.at[0])
    first[0].finish()
    if rec:
        local.wait(*load)
    else:
        shared(*first_weights)
    project(r.u_v.at[0], r.wqkv_v, r.qkv_v.at[0])
    if rec:
        recur(0)
        reduce_from(r.sout_v.at[0], r.wsout_v, update[0])
    else:
        attend(0)
    first[1].forward()
    if rec:
        update[0].middle()
        attend(0)
    reduce_from(r.att_v.at[0], r.wout_v, branch[0])
    if not rec:
        branch[0].middle()
    first[1].finish()
    project(r.u_v.at[1], r.wqkv_v, r.qkv_v.at[1])
    local.copy(r.u_v, r.u)
    local.copy(r.qkv_v, r.qkv)
    if rec:
        branch[0].middle()
        update_rows = update[0].finish()
        r.z_v[...] = update_rows
        state_rows = gate * r.state[place.core_rows(), :].astype(f32) + (1.0 - gate) * update_rows
        r.s1_v[...] = state_rows
        norm_state(state_rows, 1)
        state[1].start()
        local.copy(r.z_v, r.z)
        local.copy(r.s1_v, r.s1)
        attend(1, state=False)
    else:
        attend(1)
        reduce_from(r.att_v.at[1], r.wout_v, branch[1])
    take_branch(0, branch[0])
    second[0].start()
    if rec:
        state[1].forward()
        state[1].finish()
        project(r.sn_v.at[1], r.wsqkv_v, r.sqkv_v.at[1])
        local.copy(r.sn_v, r.sn)
        local.copy(r.sqkv_v, r.sqkv)
        attend(1, window=False)
        reduce_from(r.att_v.at[1], r.wout_v, branch[1])
    local.copy(r.att_v, r.att)
    local.copy(r.lse_v, r.lse)
    second[0].forward()
    branch[1].middle()
    second[0].finish()
    if rec:
        local.wait(*load_mlp)
    else:
        shared(*later_weights)
        local.wait(*state_weights)
        for source, target in (
            (r.wqkv_s, r.wqkv),
            (r.wout_s, r.wout),
            (r.wup_s, r.wup),
            (r.wdown_s, r.wdown),
            (r.wsqkv_s, r.wsqkv),
            (r.wsout_s, r.wsout),
            (r.gain, r.gain_both),
            (r.shift, r.shift_both),
            (r.up_bias, r.up_bias_both),
            (r.down_bias, r.down_bias_both),
            (r.rel, r.rel_both),
        ):
            local.copy(source, target)
    feed_up(0)
    reduce_from(r.act_v.at[0], r.wdown_v, result[0])
    take_branch(1, branch[1])
    second[1].start()
    local.copy(r.h_v, r.h)
    result[0].middle()
    if rec:
        recur(1)
        local.copy(r.sout_v, r.sout)
        local.copy(r.rlse_v, r.rlse)
    second[1].forward()
    second[1].finish()
    local.copy(r.wn_v, r.wn)
    feed_up(1)
    local.copy(r.pre_v, r.pre)
    local.copy(r.act_v, r.act)
    reduce_from(r.act_v.at[1], r.wdown_v, result[1])
    sent = [take_result(0, result[0])]
    result[1].middle()
    if not rec:
        cotangent(0)
    sent.append(take_result(1, result[1]))
    for made in sent:
        made.wait_recv()
    local.copy(r.acts_v, r.acts)
    if not rec:
        cot[0].forward()
        cot[1].finish()
        cot[0].finish()
        local.copy(r.cot_v, r.cot_all)
    local.drain()
    net.drain()


def forward_layer(layer, block_len, small, valid, weights, rows, state, cot=None):
    rec = layer == 1
    wqkv, wout, wup, wdown = weights[:4]
    model = rows.shape[2]
    width, hidden = (wqkv.shape[3], wup.shape[2]) if rec else (wqkv.shape[2] // 2, wup.shape[1] // 2)
    quarter = block_len // 4
    heads = small.rel.shape[1] // 2

    def held(shape, dtype):
        return jax.ShapeDtypeStruct(shape, dtype)

    outs = dict(
        u=held((2, block_len, model), bf16),
        qkv=held((2, block_len, 3 * width), bf16),
        lse=held((2, block_len, 128), f32),
        att=held((2, block_len, width), bf16),
        wn=held((2, block_len, model), bf16),
        pre=held((2, block_len, hidden), bf16),
        act=held((2, block_len, hidden), bf16),
        h=held((2, quarter, model), f32),
        acts=held((2, 2 * quarter, model), bf16),
    )
    ins = dict(x=rows, buckets=small.buckets, valid=valid)
    names = ("gain", "shift", "up_bias", "down_bias", "rel")
    smalls = {name: getattr(small, name) for name in names}
    shapes = dict(
        wqkv=(3, model, width),
        wout=(width, model),
        wup=(model, hidden),
        wdown=(hidden, model),
        wsqkv=(3, model, width),
        wsout=(width, model),
    )
    scratch, given = {}, {}
    if rec:
        outs.update(
            sn=held((2, block_len, model), bf16),
            sqkv=held((2, block_len, 3 * width), bf16),
            rlse=held((block_len, 128), f32),
            sout=held((2, block_len, width), bf16),
            s1=held((quarter, model), f32),
            z=held((quarter, model), f32),
        )
        ins.update(state=state, sgain=small.sgain, sshift=small.sshift, gate=small.gate, **smalls)
        far_ins = dict(wqkv=wqkv, wout=wout, wup=wup, wdown=wdown, wsqkv=weights[4], wsout=weights[5])
        scratch.update({name + "_v": pltpu.VMEM(shape, bf16) for name, shape in shapes.items()})
        scratch.update(early=pltpu.VMEM((block_len, width), f32))
    else:
        far_ins = dict(
            qkv_own=wqkv, out_own=wout, up_own=wup, down_own=wdown, sqkv_own=weights[4], sout_own=weights[5]
        )
        far_ins.update({name + "_own": array for name, array in smalls.items()}, cot=cot)
        given = dict(cot_all=held((2, block_len, model), bf16))
        scratch.update(cot_v=pltpu.VMEM((2, block_len, model), bf16))
        for name, shape in shapes.items():
            shape = shape if name.startswith("ws") else (2, *shape)
            given[name] = held(shape, bf16)
            scratch[name + "_s"] = pltpu.VMEM(shape, bf16)
        for name, array in smalls.items():
            given[name + "_both"] = held((2, *array.shape[1:]), f32)
            scratch[name] = pltpu.VMEM((2, *array.shape[1:]), f32)
    scatters = 5 if rec else 4
    copies = (3 * 6 + 3 * 5 + 2) if rec else (3 * 6 + 3 * 4 + 2 + 9)
    scratch.update({name + "_v": pltpu.VMEM(kind.shape, kind.dtype) for name, kind in outs.items()})
    outs.update(given)
    scratch.update(
        bias=pltpu.VMEM((heads, min(128, block_len), 2 * block_len), f32),
        part=pltpu.VMEM((scatters, block_len, model), bf16),
        near=pltpu.VMEM((scatters, 2, quarter, model), bf16),
        out=pltpu.VMEM((scatters, quarter, model), bf16),
        far=pltpu.VMEM((scatters, quarter, model), bf16),
        send_sems=pltpu.SemaphoreType.DMA((copies,)),
        recv_sems=pltpu.SemaphoreType.DMA((copies,)),
        local_sems=pltpu.SemaphoreType.DMA((len(far_ins) + len(outs) + 1,)),
    )
    anywhere = pl.BlockSpec(memory_space=pl.ANY)
    inside = pl.BlockSpec(memory_space=pltpu.VMEM)
    results = pl.pallas_call(
        partial(forward_kernel, layer, [*ins, *far_ins, *outs, *scratch]),
        out_shape=tuple(outs.values()),
        in_specs=[inside] * len(ins) + [anywhere] * len(far_ins),
        out_specs=[anywhere] * len(outs),
        scratch_shapes=list(scratch.values()),
        compiler_params=pltpu.CompilerParams(
            collective_id=1 + layer, has_side_effects=True, vmem_limit_bytes=VMEM_LIMIT
        ),
        name="forward_recurrent" if rec else "forward_local",
    )(*ins.values(), *far_ins.values())
    return SimpleNamespace(**dict(zip(outs, results)))


def ring_place(n, c, d):
    if n % 2:
        at = d

        def index_at(p):
            return p

    else:
        a, b = d // 2, d % 2
        at = a + b * (n - 1 - 2 * a)

        def index_at(p):
            b = p // (n // 2)
            return 2 * (p + b * (n - 1 - 2 * p)) + b

    def flip(p):
        return p + c * (n - 1 - 2 * p)

    return flip(at), lambda p: index_at(flip(p))


class Ring:
    def __init__(self, n):
        self.n, self.c = n, lax.axis_index("section")
        self.q, index_at = ring_place(n, self.c, lax.axis_index("dp"))
        self.after = {"dp": index_at((self.q + 1) % n)}
        self.before = {"dp": index_at((self.q + n - 1) % n)}
        self.core, self.chip = {"section": 1 - self.c}, {"mp": 1 - lax.axis_index("mp")}

    def meet(self):
        barrier = pltpu.get_barrier_semaphore()
        for other in (self.after, self.before, self.core, self.chip):
            pl.semaphore_signal(barrier, inc=1, device_id=other, device_id_type=MESH)
        pl.semaphore_wait(barrier, 4)


def remote(source, target, send, recv, to):
    return pltpu.make_async_remote_copy(
        src_ref=source, dst_ref=target, send_sem=send, recv_sem=recv, device_id=to, device_id_type=MESH
    )


def ring_subs(n, rows, most):
    return max(k for k in range(1, most + 1) if rows // n % (16 * k) == 0)


def ring_scratch(n, rows, model, most):
    subs = ring_subs(n, rows, most)
    sems = pltpu.SemaphoreType.DMA
    return dict(
        held=pltpu.VMEM((n - 1, rows // n, model), bf16),
        rs_send=sems((n - 1, subs)),
        rs_recv=sems((n - 1, subs)),
        ag_send=sems((n - 1, subs)),
        ag_recv=sems((n - 1, subs)),
        core_send=sems((n, subs)),
        core_recv=sems((n, subs)),
        own_sems=sems((subs,)),
    )


class RingSum:
    def __init__(self, ring, mine, full, held, rs_send, rs_recv, ag_send, ag_recv, core_send, core_recv, own_sems):
        self.ring, self.mine, self.full, self.held = ring, mine, full, held
        self.rs_send, self.rs_recv, self.ag_send, self.ag_recv = rs_send, rs_recv, ag_send, ag_recv
        self.core_send, self.core_recv, self.own_sems = core_send, core_recv, own_sems
        self.chunk, self.subs = held.shape[1], own_sems.shape[0]
        self.sub = self.chunk // self.subs
        self.half = (ring.n - 1) * self.subs
        self.total = 2 * self.half
        self.done = 0

    def rows(self, owner, k):
        owner = (owner + 2 * self.ring.n) % self.ring.n
        return pl.ds(pl.multiple_of(owner * self.chunk + k * self.sub, self.sub), self.sub)

    def piece(self, k):
        return slice(k * self.sub, (k + 1) * self.sub) if isinstance(k, int) else pl.ds(
            pl.multiple_of(k * self.sub, self.sub), self.sub
        )

    def summed(self, s, k):
        return self.held.at[s, self.piece(k)]

    def gathered(self, s, k):
        return self.full.at[self.ring.c, self.rows(self.ring.q + 1 - s, k)]

    def reduce(self, s, k, source):
        return remote(source, self.summed(s, k), self.rs_send.at[s, k], self.rs_recv.at[s, k], self.ring.after)

    def gather(self, s, k, source):
        return remote(source, self.gathered(s, k), self.ag_send.at[s, k], self.ag_recv.at[s, k], self.ring.after)

    def to_core(self, s, k, source):
        return remote(source, self.gathered(s, k), self.core_send.at[s, k], self.core_recv.at[s, k], self.ring.core)

    def from_core(self, s, k):
        n, q = self.ring.n, self.ring.q
        target = self.full.at[1 - self.ring.c, self.rows(n - q - s, k)]
        return remote(target, target, self.core_send.at[s, k], self.core_recv.at[s, k], self.ring.core)

    def own(self, k):
        return pltpu.make_async_copy(self.summed(self.ring.n - 2, k), self.gathered(0, k), self.own_sems.at[k])

    def start(self):
        for k in range(self.subs):
            self.reduce(0, k, self.mine.at[self.rows(self.ring.q, k)]).start()

    def add(self, s, k):
        self.reduce(s, k, self.summed(s, k)).wait_recv()
        self.held[s, self.piece(k), :] = (
            self.held[s, self.piece(k), :].astype(f32)
            + self.mine[self.rows(self.ring.q - 1 - s, k), :].astype(f32)
        ).astype(bf16)

    def add_middle(self, s, k):
        self.add(s, k)
        self.reduce(s + 1, k, self.summed(s, k)).start()

    def add_last(self, s, k):
        self.add(s, k)
        self.gather(0, k, self.summed(s, k)).start()
        self.to_core(0, k, self.summed(s, k)).start()
        self.own(k).start()

    def pass_middle(self, s, k):
        at = self.gathered(s + 1, k)
        self.gather(s, k, at).wait_recv()
        self.gather(s + 1, k, at).start()
        self.to_core(s + 1, k, at).start()

    def pass_last(self, s, k):
        at = self.gathered(s + 1, k)
        self.gather(s, k, at).wait_recv()
        self.to_core(s + 1, k, at).start()

    def pump_one(self, t):
        last = self.ring.n - 2
        s, k = t // self.subs, t % self.subs
        kinds = (
            (s < last, self.add_middle, s),
            (s == last, self.add_last, s),
            ((s > last) & (s < 2 * last + 1), self.pass_middle, s - last - 1),
            (s == 2 * last + 1, self.pass_last, s - last - 1),
        )
        for here, act, step in kinds:
            if isinstance(t, int):
                if here:
                    act(step, k)
            else:
                pl.when(here)(partial(act, step, k))

    def pump(self, count=1):
        for _ in range(min(count, self.total - self.done)):
            self.pump_one(self.done)
            self.done += 1

    def pumps_in(self, loop_steps, each):
        each = min(each, (self.total - self.done) // loop_steps)
        base = self.done
        self.done += each * loop_steps

        def pump(index):
            for piece in range(each):
                self.pump_one(base + index * each + piece)

        return pump

    def run(self, until):
        last = self.ring.n - 2
        for first, end, act in (
            (0, last, self.add_middle),
            (last, last + 1, self.add_last),
            (last + 1, 2 * last + 1, self.pass_middle),
            (2 * last + 1, 2 * last + 2, self.pass_last),
        ):
            while self.done < min(end * self.subs, until) and self.done % self.subs:
                self.pump()
            step, stop = self.done // self.subs, min(end, until // self.subs)
            if first <= step < stop:
                base = last + 1 if first > last else 0

                @pl.loop(step - base, stop - base)
                def _(s):
                    for k in range(self.subs):
                        act(s, k)

                self.done = stop * self.subs

    def release_mine(self):
        for k in range(self.subs):
            self.reduce(0, k, self.mine.at[self.rows(self.ring.q, k)]).wait_send()

    def finish(self, released=False):
        self.run(self.total)
        if not released:
            self.release_mine()
        last = self.ring.n - 2

        @pl.loop(0, last + 2)
        def _(s):
            for k in range(self.subs):
                self.from_core(s, k).wait_recv()
                self.to_core(s, k, self.gathered(s, k)).wait_send()

        @pl.loop(0, last + 1)
        def _(s):
            for k in range(self.subs):
                self.gather(s, k, self.gathered(s, k)).wait_send()

        @pl.loop(0, last)
        def _(s):
            for k in range(self.subs):
                self.reduce(s + 1, k, self.summed(s, k)).wait_send()

        for k in range(self.subs):
            self.own(k).wait()


def sum_kernel(n, parts, small_0, small_1, full, small_out, mine, small_held, small_sum, small_far, small, *rest):
    ring_refs, (small_send, small_recv, local_sems) = rest[:-3], rest[-3:]
    ring = Ring(n)
    flow = RingSum(ring, mine, full, *ring_refs)

    def small_step(s, first):
        source = small if first else small_held.at[s - 1]
        return remote(source, small_held.at[s], small_send.at[s], small_recv.at[s], ring.after)

    load = pltpu.make_async_copy(parts, mine, local_sems.at[0])
    load.start()
    small[: small_0.shape[0]] = small_0[...]
    small[small_0.shape[0] :] = small_1[...]
    ring.meet()
    small_step(0, True).start()
    load.wait()
    flow.start()

    @pl.loop(0, n - 2)
    def _(s):
        for k in range(flow.subs):
            flow.add_middle(s, k)
        small_step(s, True).wait_recv()
        small_step(s + 1, False).start()

    flow.done = (n - 2) * flow.subs
    flow.run(flow.half)
    small_step(n - 2, True).wait_recv()
    small_out[0] = small[...]

    @pl.loop(0, n - 1)
    def _(s):
        small_out[0] += small_held[s]

    between = remote(small_out.at[0], small_out.at[1], small_send.at[n - 1], small_recv.at[n - 1], ring.core)
    between.start()
    between.wait_recv()
    small_sum[...] = small_out[0] + small_out[1]
    across = remote(small_sum, small_far, small_send.at[n], small_recv.at[n], ring.chip)
    across.start()
    across.wait_recv()
    small_out[2] = small_sum[...] + small_far[...]
    flow.finish()

    @pl.loop(0, n - 1)
    def _(s):
        small_step(s, True).wait_send()

    between.wait_send()
    across.wait_send()


def sum_gradients(n, parts, small_0, small_1):
    rows, model = parts.shape
    both = (small_0.shape[0] + small_1.shape[0], model)
    anywhere = pl.BlockSpec(memory_space=pl.ANY)
    inside = pl.BlockSpec(memory_space=pltpu.VMEM)
    sems = pltpu.SemaphoreType.DMA
    return pl.pallas_call(
        partial(sum_kernel, n),
        out_shape=(
            jax.ShapeDtypeStruct((2, rows, model), bf16),
            jax.ShapeDtypeStruct((3,) + both, f32),
        ),
        in_specs=[anywhere, inside, inside],
        out_specs=[anywhere, inside],
        scratch_shapes=[
            pltpu.VMEM((rows, model), bf16),
            pltpu.VMEM((n - 1,) + both, f32),
            pltpu.VMEM(both, f32),
            pltpu.VMEM(both, f32),
            pltpu.VMEM(both, f32),
            *ring_scratch(n, rows, model, 6).values(),
            sems((n + 1,)),
            sems((n + 1,)),
            sems((1,)),
        ],
        compiler_params=pltpu.CompilerParams(
            collective_id=5, has_side_effects=True, vmem_limit_bytes=VMEM_LIMIT
        ),
        name="sum_gradients",
    )(parts, small_0, small_1)


def norm_back(rows, gain, grad):
    normed, scale = norm_parts(rows)
    inner = grad * gain
    means = jnp.mean(inner, axis=-1, keepdims=True), jnp.mean(inner * normed, axis=-1, keepdims=True)
    by_rows = scale * (inner - means[0] - normed * means[1])
    return by_rows, jnp.sum(grad * normed, axis=0, keepdims=True), jnp.sum(grad, axis=0, keepdims=True)


GAIN0, GAIN1, SHIFT0, SHIFT1, DOWN_BIAS, SGAIN, SSHIFT, GATE, UP_BIAS, BY_DISTANCE = range(10)
SMALL_ROWS = 16


def backward_kernel(layer, n, ring_names, names, *refs):
    r = SimpleNamespace(**dict(zip(names, refs)))
    rec = layer == 1
    heads, length = r.rel.shape[1] // 2, r.valid.shape[1]
    head_size = r.att_v.shape[1] // heads
    width = heads * head_size
    hidden = r.wup_v.shape[1]
    model = r.wup_v.shape[0]
    scale = head_size ** (-0.5)
    place = Place(length)
    net, local = Net(r.send_sems, r.recv_sems), Local(r.local_sems)
    chunk = min(128, length)

    ring = Ring(n)
    r.act, r.by_down = r.work.at[:hidden], r.work.at[hidden:]
    ring_refs = [[getattr(r, name) for name in flow_names] for flow_names in ring_names]
    if rec:
        up_flow = RingSum(ring, r.act, r.full.at[:, :model], *ring_refs[0])
        down_flow = RingSum(ring, r.by_down, r.full.at[:, model:], *ring_refs[1])
        act = [local.copy(r.act_in, r.act), local.copy(r.g_in, r.g)]
    else:
        rest_flow = RingSum(ring, r.mine, r.full, *ring_refs[0])
        parts = local.copy(r.parts, r.mine)
        act = [local.copy(r.act_in, r.act)]
    flows = []

    def launch(flow):
        flow.start()
        flows.append(flow)

    def tick(count=1):
        for _ in range(count):
            for flow in flows:
                flow.pump()

    def tick_at(index, *steps):
        for step in steps:

            @pl.when(index == step)
            def _():
                tick()

    ring.meet()
    wdown = local.copy(r.wdown.at[layer], r.wdown_v)
    pre = local.copy(r.pre, r.pre_v)
    wup = local.copy(r.wup.at[layer], r.wup_v)
    hidden_rows = local.copy(r.h, r.h_v)
    wn = local.copy(r.wn, r.wn_v)
    attention = [
        local.copy(r.wout.at[layer], r.wout_v),
        local.copy(r.qkv, r.qkv_v),
        local.copy(r.att, r.att_v),
        local.copy(r.lse, r.lse_v),
    ]
    if rec:
        attention += [local.copy(r.sqkv, r.sqkv_v), local.copy(r.wsqkv, r.wsqkv_v)]
        chain = [
            local.copy(r.s1, r.s1_v),
            local.copy(r.z, r.z_v),
            local.copy(r.wsout, r.wsout_v),
            local.copy(r.sout, r.sout_v),
            local.copy(r.rlse, r.rlse_v),
        ]
    wqkv = [local.copy(r.wqkv.at[layer], r.wqkv_v)]
    wqkv += [local.copy(r.x.at[block, place.core_rows()], r.x_v.at[block]) for block in range(2)]
    if rec:
        chain.append(local.copy(r.state.at[place.core_rows()], r.state_v))

    gain = lambda index: r.gain[layer, index : index + 1, :]
    small = r.small_v
    small[...] = jnp.zeros(small.shape, f32)
    r.dkv[...] = jnp.zeros(r.dkv.shape, f32)
    r.dbias[...] = jnp.zeros(r.dbias.shape, f32)
    if rec:
        r.dskv[...] = jnp.zeros(r.dskv.shape, f32)

    def add_small(index, value):
        small[index : index + 1, :] += value

    def gather(buffer):
        return Gather(place, net, buffer)

    scatter_count = [0]

    def scatter(slot):
        index = scatter_count[0]
        scatter_count[0] += 1
        return Scatter(place, net, r.part.at[slot], r.near.at[index], r.out.at[slot], r.far.at[index])

    def block_rows(block):
        return slice(block * length, (block + 1) * length)

    def own_grad(block):
        if rec:
            return r.g[pl.ds(place_row(block), place.quarter), :].astype(f32)
        return r.gy[block, place.core_rows(), :].astype(bf16).astype(f32)

    def feed_back(block):
        step = 256
        rows = block_rows(block)

        @pl.loop(0, hidden // step)
        def _(index):
            at = pl.ds(pl.multiple_of(index * step, step), step)
            pre = r.pre_v[rows, at].astype(f32)
            by_act = dot_nt(r.g[rows, :], r.wdown_v[at, :])
            below = 0.5 * (1.0 + lax.erf(pre * (0.5**0.5)))
            by_pre = by_act * (below + pre * jnp.exp(-0.5 * pre * pre) * 0.3989422804014327)
            small[UP_BIAS : UP_BIAS + 1, at] += jnp.sum(by_pre, axis=0, keepdims=True)
            r.dpre[rows, at] = by_pre.astype(bf16)

    def reduce_back(terms, to):
        step = min(512, model)
        for x_other in (True, False):
            rows = place.chip_rows(x_other)

            @pl.loop(0, model // step)
            def _(index):
                at = pl.ds(pl.multiple_of(index * step, step), step)
                total = None
                for values, weights in terms:
                    term = dot_nt(values[rows, :], weights[at, :])
                    total = term if total is None else total + term
                to.part[rows, at] = total.astype(bf16)

            to.send(x_other)

    def update_last():
        step = min(512, model)
        for x_other in (True, False):
            rows = place.chip_rows(x_other)

            @pl.loop(0, model // step)
            def _(index):
                at = pl.ds(pl.multiple_of(index * step, step), step)
                last_update.part[rows, at] = dot(r.sout_v[1, rows, :], r.wsout_v[:, at]).astype(bf16)

            last_update.send(x_other)

    def take_feed(block, from_feed):
        by_norm = from_feed.finish()
        grad = own_grad(block)
        by_rows, by_gain, by_shift = norm_back(r.h_v[block], gain(1), by_norm)
        add_small(GAIN1, by_gain)
        add_small(SHIFT1, by_shift)
        add_small(DOWN_BIAS, jnp.sum(grad, axis=0, keepdims=True))
        total = grad + by_rows
        r.ig_v[block] = total
        r.hg[pl.ds(place_row(block), place.quarter), :] = total.astype(bf16)

    def place_row(block):
        return pl.multiple_of(block * length + place.x * place.half + place.c * place.quarter, place.quarter)

    def weight_grad(left, right, target, at_row=0):
        step = 256

        @pl.loop(0, left.shape[1] // step)
        def _(index):
            at = pl.ds(pl.multiple_of(index * step, step), step)
            to = pl.ds(pl.multiple_of(at_row + index * step, step), step)
            target[to, :] = dot_tn(left[:, at], right[...]).astype(bf16)

    def projection_grad(normed, grads, target):
        @pl.loop(0, model // width)
        def _(index):
            tick_at(index, 0, 1, 2)
            at = pl.ds(pl.multiple_of(index * width, width), width)
            found = dot_tn(normed[:, at], grads[...]).astype(bf16)
            for part in range(3):
                to = slice(part * width, (part + 1) * width)
                target[to, at] = found[:, to]

    def branch_back(block):
        r.datt[block] = dot_nt(r.hg[block_rows(block), :], r.wout_v[...]).astype(bf16)

    def columns(head, part):
        return slice(part * width + head * head_size, part * width + (head + 1) * head_size)

    def attend_back(block, window=True, state=rec):
        qkv = r.qkv_v.at[block]
        prev = r.qkv_v.at[block - 1] if block > 0 else None

        @pl.loop(0, length // chunk)
        def _(index):
            if window:
                tick_at(index, 1, 3)
            at = pl.ds(pl.multiple_of(index * chunk, chunk), chunk)
            block_at = pl.ds(pl.multiple_of(block * length + index * chunk, chunk), chunk)
            for head in range(heads):
                q_at, k_at, v_at = (columns(head, part) for part in range(3))
                early_at = pl.ds(pl.multiple_of(index * width + head * head_size, head_size), head_size)
                query = qkv[at, q_at]
                lse = r.lse_v[block, at, head : head + 1]
                grad = r.datt[block, at, q_at]
                delta = jnp.sum(
                    grad.astype(f32) * r.att_v[block_at, q_at].astype(f32), axis=-1, keepdims=True
                )
                by_query = None
                if state:
                    skv = r.sqkv_v.at[block]
                    state_probs = jnp.exp(dot_nt(query, skv[:, k_at]) * scale - lse)
                    by_state = state_probs * (dot_nt(grad, skv[:, v_at]) - delta) * scale
                    low_state = by_state.astype(bf16)
                    by_query = dot(low_state, skv[:, k_at])
                    r.dskv[:, q_at] += dot_tn(low_state, query)
                    r.dskv[:, k_at] += dot_tn(state_probs.astype(bf16), grad)
                    if not window:
                        r.h_v[0, :, early_at] = by_query
                elif rec:
                    by_query = r.h_v[0, :, early_at]
                if not window:
                    continue
                key, value = qkv[:, k_at], qkv[:, v_at]
                logits, here = window_logits(
                    query,
                    key,
                    None if prev is None else prev[:, k_at],
                    r.bias[head, :, bias_columns(index, chunk, length)],
                    r.valid,
                    block,
                    index * chunk,
                    scale,
                )
                probs = jnp.exp(logits - lse)
                by_probs = dot_nt(grad, value)
                if prev is not None:
                    by_probs = jnp.where(here, by_probs, dot_nt(grad, prev[:, v_at]))
                by_logits = probs * (by_probs - delta)
                r.dbias[head, :, bias_columns(index, chunk, length)] += by_logits
                by_logits = by_logits * scale
                if prev is None:
                    low = by_logits.astype(bf16)
                    low_probs = probs.astype(bf16)
                    by_window = dot(low, key)
                else:
                    low = jnp.where(here, by_logits, 0.0).astype(bf16)
                    low_probs = jnp.where(here, probs, 0.0).astype(bf16)
                    low_prev = jnp.where(here, 0.0, by_logits).astype(bf16)
                    low_probs_prev = jnp.where(here, 0.0, probs).astype(bf16)
                    by_window = dot(low, key) + dot(low_prev, prev[:, k_at])
                    r.dkv[block - 1, :, q_at] += dot_tn(low_prev, query)
                    r.dkv[block - 1, :, k_at] += dot_tn(low_probs_prev, grad)
                r.dkv[block, :, q_at] += dot_tn(low, query)
                r.dkv[block, :, k_at] += dot_tn(low_probs, grad)
                by_query = by_window if by_query is None else by_query + by_window
                r.dqkv[block_at, q_at] = by_query.astype(bf16)

    def recur_back():
        qkv, state = r.qkv_v.at[0], r.sqkv_v.at[0]

        @pl.loop(0, length // chunk)
        def _(index):
            tick_at(index, 2)
            at = pl.ds(pl.multiple_of(index * chunk, chunk), chunk)
            for head in range(heads):
                q_at, k_at, v_at = (columns(head, part) for part in range(3))
                query, key, value = state[at, q_at], qkv[:, k_at], qkv[:, v_at]
                logits = dot_nt(query, key) * scale
                logits = jnp.where(r.valid[0:1, :] > 0.5, logits, negative)
                probs = jnp.exp(logits - r.rlse_v[at, head : head + 1])
                grad = r.dsout[at, q_at]
                delta = jnp.sum(
                    grad.astype(f32) * r.sout_v[0, at, q_at].astype(f32), axis=-1, keepdims=True
                )
                low = (probs * (dot_nt(grad, value) - delta) * scale).astype(bf16)
                r.dsqkv[at, q_at] = dot(low, key).astype(bf16)
                r.dkv[0, :, q_at] += dot_tn(low, query)
                r.dkv[0, :, k_at] += dot_tn(probs.astype(bf16), grad)

    def close_keys(block):
        r.dqkv[block_rows(block), width:] = r.dkv[block].astype(bf16)

    def close_state(block):
        r.dsqkv[block_rows(block), width:] = r.dskv[...].astype(bf16)
        if block == 1:
            r.dskv[...] = jnp.zeros(r.dskv.shape, f32)

    def input_back(block, to):
        rows = block_rows(block)
        reduce_back(
            [
                (r.dqkv.at[rows, part * width : (part + 1) * width], r.wqkv_v.at[part])
                for part in range(3)
            ],
            to,
        )

    def state_back(block, to):
        rows = block_rows(block)
        reduce_back(
            [
                (r.dsqkv.at[rows, part * width : (part + 1) * width], r.wsqkv_v.at[part])
                for part in ((0, 1, 2) if block == 0 else (1, 2))
            ],
            to,
        )

    def give(rows, target):
        local.copy(rows, target)
        return net.copy(rows, target, place.core)

    def take_input(block, from_input):
        by_norm = from_input.finish()
        rows = r.x_v[block].astype(f32)
        by_rows, by_gain, by_shift = norm_back(rows, gain(0), by_norm)
        add_small(GAIN0, by_gain)
        add_small(SHIFT0, by_shift)
        r.ig_v[block] += by_rows
        return give(r.ig_v.at[block], r.ig.at[block, place.core_rows()])

    def take_state(rows, from_state):
        by_rows, by_gain, by_shift = norm_back(rows, r.sgain[...], from_state.finish())
        add_small(SGAIN, by_gain)
        add_small(SSHIFT, by_shift)
        return by_rows

    def close_bias():
        tile = r.dbias.shape[1]
        for head in range(heads):
            folded = r.dbias[head, :, :length] + r.dbias[head, :, length:]
            row = lax.broadcasted_iota(jnp.int32, folded.shape, 0)
            bit = 1
            while bit < tile:
                moved = pltpu.roll(folded, length - bit, axis=1)
                folded = jnp.where((row & bit) != 0, moved, folded)
                bit *= 2
            small[BY_DISTANCE : BY_DISTANCE + 1, head * length : (head + 1) * length] = jnp.sum(
                folded, axis=0, keepdims=True
            )

    if rec:
        at_qkv, at_sqkv = 0, 4 * width
    else:
        at_up, at_down, at_qkv = 0, model, model + hidden
    at_out = 3 * width

    feed = [scatter(0), scatter(1)]
    inputs = [scatter(2 if rec else 0), scatter(1)]
    if not rec:
        grads = [gather(r.g.at[block_rows(block)]) for block in range(2)]
    hiddens = [gather(r.hg.at[block_rows(block)]) for block in range(2)]
    if rec:
        states = [scatter(0), scatter(0)]
        last_update = scatter(2)
        updates = gather(r.ug)
    if not rec:
        for block in (1, 0):
            r.g[pl.ds(place_row(block), place.quarter), :] = own_grad(block).astype(bf16)
            grads[block].start()
        local.wait(parts)
        launch(rest_flow)
    fill_bias(r.bias, bias_rows(r.rel[layer], r.buckets[...], place.c))
    local.wait(*act)
    if rec:
        weight_grad(r.act, r.g, r.by_down)
        launch(down_flow)
    else:
        tick()
        grads[1].forward()
        tick()
        grads[1].finish()
    local.wait(wdown, pre, wup)
    feed_back(1)
    tick()
    reduce_back([(r.dpre.at[block_rows(1)], r.wup_v)], feed[1])
    if rec:
        tick()
    else:
        grads[0].forward()
        tick()
        grads[0].finish()
    feed_back(0)
    feed[1].middle()
    tick()
    reduce_back([(r.dpre.at[block_rows(0)], r.wup_v)], feed[0])
    tick()
    feed[0].middle()
    if not rec:
        weight_grad(r.act, r.g, r.by_down)
        down_out = local.copy(r.by_down, r.dw.at[at_down:at_qkv])
    tick()
    local.wait(wn)
    weight_grad(r.wn_v, r.dpre, r.act)
    if rec:
        launch(up_flow)
        sn_in = local.copy(r.sn, r.pre_v)
    else:
        local.copy(r.act, r.dw.at[at_up:at_down])
    tick()
    u_in = local.copy(r.u, r.wn_v)
    local.wait(hidden_rows)
    take_feed(1, feed[1])
    hiddens[1].start()
    tick(2)
    take_feed(0, feed[0])
    hiddens[0].start()
    tick()
    if rec:
        local.wait(*chain)
        update_last()
    tick()
    hiddens[1].forward()
    tick()
    hiddens[1].finish()
    local.wait(*attention)
    branch_back(1)
    if rec:
        last_update.middle()
    tick()
    feed[0].release()
    feed[1].release()
    if rec:
        attend_back(1, window=False)
        close_state(1)
        state_back(1, states[1])
        tick()
        hiddens[0].forward()
        states[1].middle()
        attend_back(1, state=False)
    else:
        attend_back(1)
        hiddens[0].forward()
    close_keys(1)
    local.wait(*wqkv)
    input_back(1, inputs[1])
    tick()
    hiddens[0].finish()
    branch_back(0)
    sent = []
    if rec:
        tick()
        gate = jax.nn.sigmoid(r.gate[...])
        by_state = take_state(r.s1_v[...], states[1])
        states[1].release()
        before = r.state_v[...].astype(f32)
        add_small(
            GATE,
            jnp.sum(by_state * (before - r.z_v[...]) * gate * (1.0 - gate), axis=0, keepdims=True),
        )
        r.ug[place.rows(), :] = ((1.0 - gate) * by_state).astype(bf16)
        updates.start()
        r.s1_v[...] = gate * r.s1_v[...] + (1.0 - gate) * last_update.finish()
        sent.append(give(r.s1_v, r.final.at[place.core_rows()]))
        last_update.release()
    inputs[1].middle()
    tick()
    attend_back(0)
    tick()
    if rec:
        updates.forward()
        tick()
        updates.finish()
        r.dsout[...] = dot_nt(r.ug[...], r.wsout_v[...]).astype(bf16)
        recur_back()
        tick()
    close_keys(0)
    input_back(0, inputs[0])
    tick()
    if rec:
        close_state(0)
        state_back(0, states[0])
        tick()
    sent.append(take_input(1, inputs[1]))
    inputs[0].middle()
    tick()
    if rec:
        states[0].middle()
    weight_grad(r.att_v, r.hg, r.dpre, at_out)
    close_bias()
    local.wait(u_in)
    projection_grad(r.wn_v, r.dqkv, r.dpre)
    local.copy(r.dpre, r.dw.at[at_qkv : at_qkv + 4 * width])
    tick()
    if rec:
        r.dsqkv[block_rows(1), 0:width] = jnp.zeros((length, width), bf16)
        local.wait(sn_in)
        projection_grad(r.pre_v, r.dsqkv, r.g)
        tick()
        weight_grad(r.sout_v.at[0], r.ug, r.g, at_out)
        local.copy(r.g, r.dw.at[at_sqkv:])
    sent.append(take_input(0, inputs[0]))
    if rec:
        take_state(r.state_v[...].astype(f32), states[0])
    local.copy(small, r.small)
    for made in sent:
        made.wait_recv()
    while any(flow.done < flow.total for flow in flows):
        tick()
    for flow in flows:
        flow.finish()
    local.drain()
    net.drain()


def backward_layer(layer, n, block_len, small, valid, weights, grad_rows, rows, state, kept, parts=None):
    rec = layer == 1
    wqkv, wout, wup, wdown = weights[:4]
    model = rows.shape[2]
    width, hidden = wqkv.shape[3], wup.shape[2]
    quarter = block_len // 4
    heads = small.rel.shape[1] // 2

    def held(shape, dtype):
        return jax.ShapeDtypeStruct(shape, dtype)

    dw_rows = 8 * width if rec else model + hidden + 4 * width
    ring_rows = model + hidden if rec else parts.shape[0]
    outs = dict(
        full=held((2, ring_rows, model), bf16),
        dw=held((dw_rows, model), bf16),
        small=held((SMALL_ROWS, model), f32),
        ig=held((2, 2 * quarter, model), f32),
    )
    ins = dict(
        gain=small.gain, rel=small.rel, buckets=small.buckets, valid=valid
    )

    def flat(array):
        return array.reshape((-1,) + array.shape[2:])

    stacked = dict(wqkv=wqkv, wout=wout, wup=wup, wdown=wdown)
    copied = dict(
        qkv=kept.qkv, lse=kept.lse, att=flat(kept.att), wn=flat(kept.wn), pre=flat(kept.pre), h=kept.h
    )
    late = dict(act_in=flat(kept.act), u=flat(kept.u), x=rows)
    if rec:
        late.update(state=state)
        ins.update(sgain=small.sgain, sshift=small.sshift, gate=small.gate)
        copied.update(wsqkv=weights[4], wsout=weights[5])
        copied.update(sqkv=kept.sqkv, rlse=kept.rlse, sout=kept.sout, s1=kept.s1, z=kept.z)
        late.update(sn=flat(kept.sn), g_in=flat(parts))
        outs.update(final=held((2 * quarter, model), f32))
    else:
        ins.update(gy=grad_rows)
        late.update(parts=parts)
    far_ins = {**stacked, **copied, **late}
    scatters = 7 if rec else 4
    slots = 3 if rec else 2
    copies = (3 * 7 + 3 * 3 + 3) if rec else (3 * 4 + 3 * 4 + 2)
    scratch = dict(small_v=pltpu.VMEM(outs["small"].shape, f32), ig_v=pltpu.VMEM((2, quarter, model), f32))
    for name, array in stacked.items():
        scratch[name + "_v"] = pltpu.VMEM(array.shape[1:], array.dtype)
    for name, array in copied.items():
        scratch[name + "_v"] = pltpu.VMEM(array.shape, array.dtype)
    scratch.update(
        g=pltpu.VMEM((2 * block_len, model), bf16),
        x_v=pltpu.VMEM((2, quarter, model), bf16),
        hg=pltpu.VMEM((2 * block_len, model), bf16),
        work=pltpu.VMEM((2 * hidden, model), bf16),
        dpre=pltpu.VMEM((2 * block_len, hidden), bf16),
        datt=pltpu.VMEM((2, block_len, width), bf16),
        dkv=pltpu.VMEM((2, block_len, 2 * width), f32),
        dqkv=pltpu.VMEM((2 * block_len, 3 * width), bf16),
        dbias=pltpu.VMEM((heads, min(128, block_len), 2 * block_len), f32),
        bias=pltpu.VMEM((heads, min(128, block_len), 2 * block_len), f32),
        part=pltpu.VMEM((slots, block_len, model), bf16),
        near=pltpu.VMEM((scatters, 2, quarter, model), bf16),
        out=pltpu.VMEM((slots, quarter, model), bf16),
        far=pltpu.VMEM((scatters, quarter, model), bf16),
        send_sems=pltpu.SemaphoreType.DMA((copies,)),
        recv_sems=pltpu.SemaphoreType.DMA((copies,)),
        local_sems=pltpu.SemaphoreType.DMA((len(far_ins) + 8,)),
    )
    if rec:
        scratch.update(
            ug=pltpu.VMEM((block_len, model), bf16),
            dsout=pltpu.VMEM((block_len, width), bf16),
            dskv=pltpu.VMEM((block_len, 2 * width), f32),
            state_v=pltpu.VMEM((quarter, model), bf16),
            dsqkv=pltpu.VMEM((2 * block_len, 3 * width), bf16),
        )
    else:
        scratch.update(mine=pltpu.VMEM((ring_rows, model), bf16))
    ring_names = []
    for flow_rows in (model, hidden) if rec else (ring_rows,):
        flow_scratch = ring_scratch(n, flow_rows, model, 2)
        flow_scratch = {name + str(len(ring_names)): kind for name, kind in flow_scratch.items()}
        scratch.update(flow_scratch)
        ring_names.append(list(flow_scratch))
    anywhere = pl.BlockSpec(memory_space=pl.ANY)
    inside = pl.BlockSpec(memory_space=pltpu.VMEM)
    results = pl.pallas_call(
        partial(backward_kernel, layer, n, ring_names, [*ins, *far_ins, *outs, *scratch]),
        out_shape=tuple(outs.values()),
        in_specs=[inside] * len(ins) + [anywhere] * len(far_ins),
        out_specs=[anywhere] * len(outs),
        scratch_shapes=list(scratch.values()),
        compiler_params=pltpu.CompilerParams(
            collective_id=3 + layer, has_side_effects=True, vmem_limit_bytes=VMEM_LIMIT
        ),
        name="backward_recurrent" if rec else "backward_local",
    )(*ins.values(), *far_ins.values())
    return SimpleNamespace(**dict(zip(outs, results)))


def place_kernel(
    width, hidden, feed_1, rest_1, full_0, acts_0, acts_1, igs_0, igs_1, state, sums, buckets,
    qkv, out, up, down, sqkv, sout, acts, igs, final, gain, shift, rel, up_bias, down_bias, sgain, sshift, gate,
    inward, outward, acts_v, igs_v, state_v, igs_tiles, state_tiles, in_sems, out_sems, row_sems,
):
    model = full_0.shape[2]
    layer = lax.axis_index("section")
    slots = inward.shape[0]

    rows_in = []
    for index, (first, second, target) in enumerate(((acts_0, acts_1, acts_v), (igs_0, igs_1, igs_v))):
        pl.when(layer == 0)(pltpu.make_async_copy(first, target, row_sems.at[index]).start)
        pl.when(layer == 1)(pltpu.make_async_copy(second, target, row_sems.at[index]).start)
        rows_in.append(pltpu.make_async_copy(first, target, row_sems.at[index]))
    rows_in.append(pltpu.make_async_copy(state, state_v, row_sems.at[2]))
    rows_in[2].start()
    at_rest = model + hidden
    jobs = []
    for half in range(2):
        columns = slice(half * width, (half + 1) * width)

        def projection(target):
            return [target.at[index : index + width, columns] for index in range(0, model, width)]

        for row in range(0, model, width):
            wide = slice(half * hidden, (half + 1) * hidden)
            jobs.append((half, (feed_1, row), row, [up.at[0, row : row + width, wide]]))
        for row in range(0, hidden, width):
            at = half * hidden + row
            jobs.append((half, (feed_1, model + row), model + row, [down.at[0, at : at + width]]))
        for part in range(3):
            row = part * width
            jobs.append((half, (rest_1, row), at_rest + row, projection(qkv.at[0, part])))
            jobs.append((half, (rest_1, 4 * width + row), None, projection(sqkv.at[part])))
        jobs.append((half, (rest_1, 3 * width), at_rest + 3 * width, [out.at[0, columns]]))
        jobs.append((half, (rest_1, 7 * width), None, [sout.at[columns]]))

    def load(index, start):
        half, (array, row), row_0, _ = jobs[index]
        slot = index % slots

        def made(source, at):
            return pltpu.make_async_copy(source.at[half, at : at + width], inward.at[slot], in_sems.at[slot])

        if not start:
            made(array, row).wait()
        elif row_0 is None:
            made(array, row).start()
        else:
            pl.when(layer == 1)(lambda: made(array, row).start())
            pl.when(layer == 0)(lambda: made(full_0, row_0).start())

    def stores(index):
        targets, slot = jobs[index][3], index % slots
        step = model // len(targets)
        return [
            pltpu.make_async_copy(
                outward.at[slot, :, k * step : (k + 1) * step], target, out_sems.at[slot, k]
            )
            for k, target in enumerate(targets)
        ]

    for index in range(slots):
        load(index, True)
    def place_sums():
        mine = [jnp.where(layer == 0, sums[index, :SMALL_ROWS], sums[index, SMALL_ROWS:]) for index in range(3)]
        gain[0] = mine[2][GAIN0 : GAIN1 + 1]
        shift[0] = mine[2][SHIFT0 : SHIFT1 + 1]
        down_bias[...] = mine[2][DOWN_BIAS : DOWN_BIAS + 1]
        for target, row in ((sgain, SGAIN), (sshift, SSHIFT), (gate, GATE)):
            target[...] = sums[2, SMALL_ROWS + row : SMALL_ROWS + row + 1]
        by_core = [jnp.where(layer == 0, mine[0], mine[1]), jnp.where(layer == 0, mine[1], mine[0])]
        heads, length = rel.shape[1] // 2, buckets.shape[1]
        hot = back_hot(buckets[...], rel.shape[2])
        for half in range(2):
            up_bias[:, half * hidden : (half + 1) * hidden] = by_core[half][UP_BIAS : UP_BIAS + 1, :hidden]
            for head in range(heads):
                row = by_core[half][BY_DISTANCE : BY_DISTANCE + 1, head * length : (head + 1) * length]
                at = half * heads + head
                row = jnp.broadcast_to(row, (16, length))
                rel[0, at : at + 1, :] = sum(dot_nt(part, hot) for part in in_parts(row))[:1]

    rows_out = []

    def place_rows():
        rows_in[0].wait()
        rows_out.append(pltpu.make_async_copy(acts_v, acts, row_sems.at[0]))
        rows_out[0].start()
        tiles = model // 128
        for index, source, target in ((1, igs_v, igs_tiles), (2, state_v, state_tiles)):
            rows_in[index].wait()
            for tile in range(tiles):
                target[..., tile, :] = source[..., tile * 128 : (tile + 1) * 128]
            rows_out.append(pltpu.make_async_copy(target, igs if index == 1 else final, row_sems.at[index]))
            rows_out[index].start()

    for index in range(len(jobs)):
        slot = index % slots
        if index == slots:
            place_rows()
        if index == 2 * slots:
            place_sums()
        load(index, False)
        if index >= slots:
            for made in stores(index - slots):
                made.wait()
        outward[slot] = inward[slot].astype(f32)
        for made in stores(index):
            made.start()
        if index + slots < len(jobs):
            load(index + slots, True)
    for index in range(len(jobs) - slots, len(jobs)):
        for made in stores(index):
            made.wait()
    for made in rows_out:
        made.wait()


def place_gradients(feed_1, rest_1, full_0, acts, igs, final, sums, buckets, bucket_count, chip_heads, width, hidden):
    model = full_0.shape[2]
    anywhere = pl.BlockSpec(memory_space=pl.ANY)
    inside = pl.BlockSpec(memory_space=pltpu.VMEM)
    slots, tiles = 8, model // 128
    blocks, rows = acts[0].shape[:2]
    far_shapes = (
        ((1, 3, model, 2 * width), f32),
        ((1, 2 * width, model), f32),
        ((1, model, 2 * hidden), f32),
        ((1, 2 * hidden, model), f32),
        ((3, model, 2 * width), f32),
        ((2 * width, model), f32),
        ((blocks, rows, model), bf16),
        ((blocks, rows, tiles, 128), f32),
        ((rows, tiles, 128), f32),
    )
    near_shapes = (
        (1, 2, model),
        (1, 2, model),
        (1, chip_heads, bucket_count),
        (1, 2 * hidden),
        (1, model),
        (1, model),
        (1, model),
        (1, model),
    )
    return pl.pallas_call(
        partial(place_kernel, width, hidden),
        out_shape=[jax.ShapeDtypeStruct(*kind) for kind in far_shapes]
        + [jax.ShapeDtypeStruct(shape, f32) for shape in near_shapes],
        in_specs=[anywhere] * 8 + [inside] * 2,
        out_specs=[anywhere] * len(far_shapes) + [inside] * len(near_shapes),
        scratch_shapes=[
            pltpu.VMEM((slots, width, model), bf16),
            pltpu.VMEM((slots, width, model), f32),
            pltpu.VMEM((blocks, rows, model), bf16),
            pltpu.VMEM((blocks, rows, model), f32),
            pltpu.VMEM((rows, model), f32),
            pltpu.VMEM((blocks, rows, tiles, 128), f32),
            pltpu.VMEM((rows, tiles, 128), f32),
            pltpu.SemaphoreType.DMA((slots,)),
            pltpu.SemaphoreType.DMA((slots, model // width)),
            pltpu.SemaphoreType.DMA((3,)),
        ],
        compiler_params=pltpu.CompilerParams(vmem_limit_bytes=VMEM_LIMIT),
        name="place_gradients",
    )(feed_1, rest_1, full_0, *acts, *igs, final, sums, buckets)


def local_part(
    tokens, valid_mask, buckets, state_init, norm_gain, norm_shift, w_qkv, w_out, rel_bias, w_up, up_bias,
    w_down, down_bias, state_gain, state_shift, w_state_qkv, w_state_out, gate_bias, cotangent,
):
    block_len = valid_mask.shape[1]
    model = tokens.shape[3]
    bucket_count, chip_heads = rel_bias.shape[1:]
    docs = lax.axis_size("dp")
    valid = valid_mask[:, :, 0].astype(f32)
    cot_rows = cotangent[:, :, 0, :]
    rows = tokens[:, :, 0, :]
    state = state_init[:, 0, :]
    small = SimpleNamespace(
        gain=norm_gain,
        shift=norm_shift,
        up_bias=up_bias[:, None, :],
        down_bias=down_bias[:, None, :],
        rel=jnp.swapaxes(rel_bias, 1, 2),
        buckets=buckets[None],
        sgain=state_gain[None],
        sshift=state_shift[None],
        gate=gate_bias[None],
    )
    own_weights = (w_qkv[0], w_out[0], w_up[0], w_down[0], w_state_qkv, w_state_out)
    kept0 = forward_layer(0, block_len, small, valid, own_weights, rows, state, cot_rows)
    small.gain, small.shift, small.rel = kept0.gain_both, kept0.shift_both, kept0.rel_both
    small.up_bias, small.down_bias = kept0.up_bias_both, kept0.down_bias_both
    weights = (kept0.wqkv, kept0.wout, kept0.wup, kept0.wdown, kept0.wsqkv, kept0.wsout)
    kept1 = forward_layer(1, block_len, small, valid, weights, kept0.acts, state)
    grad1 = backward_layer(1, docs, block_len, small, valid, weights, None, kept0.acts, state, kept1, kept0.cot_all)
    grad0 = backward_layer(0, docs, block_len, small, valid, weights, grad1.ig, rows, state, kept0, grad1.dw)
    full, sums = sum_gradients(docs, grad0.dw, grad0.small, grad1.small)
    (
        qkv_grad, out_grad, up_grad, down_grad, state_qkv_grad, state_out_grad, acts, input_grads, final,
        gain_grad, shift_grad, rel_grad, up_bias_grad, down_bias_grad, sgain_grad, sshift_grad, gate_grad,
    ) = place_gradients(
        grad1.full, grad0.full, full, (kept0.acts, kept1.acts), (grad0.ig, grad1.ig), grad1.final, sums,
        small.buckets, bucket_count, chip_heads, weights[0].shape[3], weights[2].shape[2],
    )
    return (
        acts[None, :, :, None, :],
        input_grads.reshape(1, 2, -1, 1, model),
        final.reshape(-1, 1, model),
        gain_grad,
        shift_grad,
        qkv_grad,
        out_grad,
        jnp.swapaxes(rel_grad, 1, 2),
        up_grad,
        up_bias_grad,
        down_grad,
        down_bias_grad,
        sgain_grad[0],
        sshift_grad[0],
        state_qkv_grad,
        state_out_grad,
        gate_grad[0],
    )


def solution(mesh):
    in_specs = (
        P(None, "mp", "dp", None),
        P(None, None, "dp"),
        P(),
        P("mp", "dp", None),
        P("section", None, None),
        P("section", None, None),
        P("section", None, None, "mp"),
        P("section", "mp", None),
        P("section", None, "mp"),
        P("section", None, "mp"),
        P("section", "mp"),
        P("section", "mp", None),
        P("section", None),
        P(),
        P(),
        P(None, None, "mp"),
        P("mp", None),
        P(),
        P(None, "mp", "dp", None),
    )
    out_specs = (
        P("section", None, "mp", "dp", None),
        P("section", None, "mp", "dp", None),
        P("mp", "dp", None),
        P("section", None, None),
        P("section", None, None),
        P("section", None, None, "mp"),
        P("section", "mp", None),
        P("section", None, "mp"),
        P("section", None, "mp"),
        P("section", "mp"),
        P("section", "mp", None),
        P("section", None),
        P(),
        P(),
        P(None, None, "mp"),
        P("mp", None),
        P(),
    )
    return jax.shard_map(local_part, mesh=mesh, in_specs=in_specs, out_specs=out_specs, check_vma=False)
```

```python
from functools import partial
from types import SimpleNamespace

import jax
import jax.numpy as jnp
from jax import lax
from jax.experimental import pallas as pl
from jax.experimental.pallas import tpu as pltpu
from jax.sharding import PartitionSpec as P

MESH = pl.DeviceIdType.MESH
f32, bf16 = jnp.float32, jnp.bfloat16
eps = 1e-05
negative = -1000000000.0
VMEM_LIMIT = 62 * 1024 * 1024


def dot(left, right):
    return lax.dot_general(left, right, (((1,), (0,)), ((), ())), preferred_element_type=f32)


def dot_nt(left, right):
    return lax.dot_general(left, right, (((1,), (1,)), ((), ())), preferred_element_type=f32)


def dot_tn(left, right):
    return lax.dot_general(left, right, (((0,), (0,)), ((), ())), preferred_element_type=f32)


def norm_parts(values):
    average = jnp.mean(values, axis=-1, keepdims=True)
    centered = values - average
    spread = jnp.mean(centered * centered, axis=-1, keepdims=True)
    scale = lax.rsqrt(spread + eps)
    return centered * scale, scale


def layer_norm(values, gain, shift):
    return norm_parts(values)[0] * gain + shift


class Place:
    def __init__(self, rows):
        self.c, self.x = lax.axis_index("section"), lax.axis_index("mp")
        self.core = {"section": 1 - self.c}
        self.chip = {"mp": 1 - self.x}
        self.quarter, self.half = rows // 4, rows // 2

    def rows(self, x_other=False, c_other=False):
        x = 1 - self.x if x_other else self.x
        c = 1 - self.c if c_other else self.c
        return pl.ds(pl.multiple_of(x * self.half + c * self.quarter, self.quarter), self.quarter)

    def chip_rows(self, x_other=False):
        x = 1 - self.x if x_other else self.x
        return pl.ds(pl.multiple_of(x * self.half, self.half), self.half)

    def core_rows(self, c_other=False):
        c = 1 - self.c if c_other else self.c
        return pl.ds(pl.multiple_of(c * self.quarter, self.quarter), self.quarter)

    def meet(self):
        barrier = pltpu.get_barrier_semaphore()
        for other in (self.core, self.chip):
            pl.semaphore_signal(barrier, inc=1, device_id=other, device_id_type=MESH)
        pl.semaphore_wait(barrier, 2)


class Net:
    def __init__(self, send_sems, recv_sems):
        self.send_sems, self.recv_sems, self.copies = send_sems, recv_sems, []

    def copy(self, source, target, device):
        index = len(self.copies)
        made = pltpu.make_async_remote_copy(
            src_ref=source,
            dst_ref=target,
            send_sem=self.send_sems.at[index],
            recv_sem=self.recv_sems.at[index],
            device_id=device,
            device_id_type=MESH,
        )
        made.start()
        self.copies.append(made)
        return made

    def sent(self, *copies):
        for made in copies:
            made.wait_send()
        self.copies = [None if any(held is made for made in copies) else held for held in self.copies]

    def drain(self):
        for made in self.copies:
            if made is not None:
                made.wait_send()


class Local:
    def __init__(self, sems):
        self.sems, self.copies, self.waited = sems, [], set()

    def copy(self, source, target):
        made = pltpu.make_async_copy(source, target, self.sems.at[len(self.copies)])
        made.start()
        self.copies.append(made)
        return len(self.copies) - 1

    def wait(self, *indices):
        for index in indices:
            if index not in self.waited:
                self.waited.add(index)
                self.copies[index].wait()

    def drain(self):
        self.wait(*range(len(self.copies)))


class Gather:
    def __init__(self, place, net, buffer):
        self.place, self.net, self.buffer = place, net, buffer

    def start(self):
        own = self.buffer.at[self.place.rows()]
        self.from_chip = self.net.copy(own, own, self.place.chip)
        self.from_core = self.net.copy(own, own, self.place.core)

    def forward(self):
        self.from_chip.wait_recv()
        passed = self.buffer.at[self.place.rows(x_other=True)]
        self.passed = self.net.copy(passed, passed, self.place.core)

    def finish(self):
        self.from_core.wait_recv()
        self.passed.wait_recv()


class Scatter:
    def __init__(self, place, net, part, near, out, far):
        self.place, self.net, self.part = place, net, part
        self.near, self.out, self.far = near, out, far

    def send(self, x_other):
        slot = 0 if x_other else 1
        rows = self.place.rows(x_other=x_other, c_other=True)
        made = self.net.copy(self.part.at[rows], self.near.at[slot], self.place.core)
        if x_other:
            self.first = made
        else:
            self.second = made

    def middle(self):
        self.first.wait_recv()
        mine = self.part[self.place.rows(x_other=True), :].astype(f32)
        self.out[...] = (mine + self.near[0].astype(f32)).astype(bf16)
        self.across = self.net.copy(self.out, self.far, self.place.chip)

    def finish(self):
        self.second.wait_recv()
        total = self.part[self.place.rows(), :].astype(f32) + self.near[1].astype(f32)
        self.across.wait_recv()
        return total + self.far[...].astype(f32)

    def release(self):
        self.net.sent(self.first, self.second, self.across)


def back_hot(buckets, count):
    length = buckets.shape[1]
    hot = lax.broadcasted_iota(jnp.int32, (count, length), 0) == buckets
    both = lax.broadcasted_iota(jnp.int32, (length, length), 0) + lax.broadcasted_iota(
        jnp.int32, (length, length), 1
    )
    turn = (both == 0) | (both == length)
    return dot(jnp.where(hot, 1.0, 0.0).astype(bf16), jnp.where(turn, 1.0, 0.0).astype(bf16)).astype(bf16)


def in_parts(values):
    high = values.astype(bf16)
    rest = values - high.astype(f32)
    middle = rest.astype(bf16)
    return high, middle, (rest - middle.astype(f32)).astype(bf16)


def bias_rows(rel, buckets, c):
    hot = back_hot(buckets, rel.shape[1])
    rows = sum(dot(part, hot) for part in in_parts(rel))
    heads = rel.shape[0] // 2
    return jnp.where(c == 0, rows[:heads], rows[heads:])


def fill_bias(bias, row0):
    head_count, length = row0.shape
    for head in range(head_count):
        start = jnp.broadcast_to(row0[head : head + 1], (bias.shape[1], length))
        rolled = pltpu.roll(start, 0, axis=1, stride=1, stride_axis=0)
        bias[head, :, :length] = rolled
        bias[head, :, length:] = rolled


def bias_columns(index, chunk, length):
    return pl.ds(pl.multiple_of(length - index * chunk, chunk), length)


def window_logits(query, key_cur, key_prev, bias, valid, block, first_row, scale):
    logits = dot_nt(query, key_cur)
    rows = first_row + lax.broadcasted_iota(jnp.int32, logits.shape, 0)
    here = lax.broadcasted_iota(jnp.int32, logits.shape, 1) <= rows
    usable = valid[block : block + 1, :] > 0.5
    if key_prev is None:
        keep = here & usable
    else:
        logits = jnp.where(here, logits, dot_nt(query, key_prev))
        keep = jnp.where(here, valid[block : block + 1, :], valid[block - 1 : block, :]) > 0.5
    return jnp.where(keep, logits * scale + bias, negative), here


def forward_stages(layer, r, place, net, local, scatter, slots):
    rec = layer == 1
    length = r.u_v.shape[1]
    heads = r.rel.shape[1] // 2
    head_size = r.att_v.shape[2] // heads
    width = heads * head_size
    scale = head_size ** (-0.5)
    chunk = min(128, length)

    gain = lambda index: r.gain[layer, index : index + 1, :]
    shift = lambda index: r.shift[layer, index : index + 1, :]

    def gather(buffer):
        return Gather(place, net, buffer)

    def own_rows(block):
        return r.x[block, place.core_rows(), :].astype(f32)

    def norm_state(rows, index):
        r.sn_v[index, place.rows(), :] = layer_norm(rows, r.sgain[...], r.sshift[...]).astype(bf16)

    def norm_first(block):
        rows = own_rows(block)
        r.u_v[block, place.rows(), :] = layer_norm(rows, gain(0), shift(0)).astype(bf16)

    def project(source, weights, target):
        for part in range(3):
            target[:, part * width : (part + 1) * width] = dot(source[...], weights[part]).astype(bf16)

    def reduce_from(values, weights, to):
        columns = weights.shape[1]
        step = min(512, columns)
        for x_other in (True, False):
            rows = place.chip_rows(x_other)

            @pl.loop(0, columns // step)
            def _(index):
                at = pl.ds(pl.multiple_of(index * step, step), step)
                to.part[rows, at] = dot(values[rows, :], weights[:, at]).astype(bf16)

            to.send(x_other)

    def head_columns(head):
        return [slice(part * width + head * head_size, part * width + (head + 1) * head_size) for part in range(3)]

    def pack(columns):
        lane = lax.broadcasted_iota(jnp.int32, (chunk, 128), 1)
        packed = jnp.zeros((chunk, 128), f32)
        for index, column in enumerate(columns):
            packed = jnp.where(lane == index, column, packed)
        return packed

    def attend_window(index, head, block):
        qkv = r.qkv_v.at[block]
        prev = r.qkv_v.at[block - 1] if block > 0 else None
        at = pl.ds(pl.multiple_of(index * chunk, chunk), chunk)
        q_at, k_at, v_at = head_columns(head)
        logits, here = window_logits(
            qkv[at, q_at],
            qkv[:, k_at],
            None if prev is None else prev[:, k_at],
            r.bias[head, :, bias_columns(index, chunk, length)],
            r.valid,
            block,
            index * chunk,
            scale,
        )
        peak = jnp.max(logits, axis=-1, keepdims=True)
        probs = jnp.exp(logits - peak)
        total = jnp.sum(probs, axis=-1, keepdims=True)
        if prev is None:
            result = dot(probs.astype(bf16), qkv[:, v_at])
        else:
            result = dot(jnp.where(here, probs, 0.0).astype(bf16), qkv[:, v_at])
            result += dot(jnp.where(here, 0.0, probs).astype(bf16), prev[:, v_at])
        return peak, total, result

    def attend_state(index, head, block, window):
        peak_window, total_window, result_window = window
        at = pl.ds(pl.multiple_of(index * chunk, chunk), chunk)
        q_at, k_at, v_at = head_columns(head)
        state = r.sqkv_v.at[block]
        logits = dot_nt(r.qkv_v[block, at, q_at], state[:, k_at]) * scale
        peak = jnp.maximum(peak_window, jnp.max(logits, axis=-1, keepdims=True))
        less = jnp.exp(peak_window - peak)
        probs = jnp.exp(logits - peak)
        total = total_window * less + jnp.sum(probs, axis=-1, keepdims=True)
        return peak, total, result_window * less + dot(probs.astype(bf16), state[:, v_at])

    def attend(block, window=True, state=rec):
        @pl.loop(0, length // chunk)
        def _(index):
            at = pl.ds(pl.multiple_of(index * chunk, chunk), chunk)
            kept = []
            for head in range(heads):
                q_at = head_columns(head)[0]
                if window:
                    found = attend_window(index, head, block)
                else:
                    found = (
                        r.lse_v[block, at, 2 * head : 2 * head + 1],
                        r.lse_v[block, at, 2 * head + 1 : 2 * head + 2],
                        r.early[at, q_at],
                    )
                if state:
                    found = attend_state(index, head, block, found)
                if state or not rec:
                    peak, total, result = found
                    r.att_v[block, at, q_at] = (result / total).astype(bf16)
                    kept.append(peak + jnp.log(total))
                else:
                    r.early[at, q_at] = found[2]
                    kept.extend(found[:2])
            r.lse_v[block, at, :] = pack(kept)

    def recur(block):
        qkv, state = r.qkv_v.at[block], r.sqkv_v.at[block]

        @pl.loop(0, length // chunk)
        def _(index):
            at = pl.ds(pl.multiple_of(index * chunk, chunk), chunk)
            lses = []
            for head in range(heads):
                q_at = slice(head * head_size, (head + 1) * head_size)
                k_at = slice(width + head * head_size, width + (head + 1) * head_size)
                v_at = slice(2 * width + head * head_size, 2 * width + (head + 1) * head_size)
                logits = dot_nt(state[at, q_at], qkv[:, k_at]) * scale
                logits = jnp.where(r.valid[block : block + 1, :] > 0.5, logits, negative)
                peak = jnp.max(logits, axis=-1, keepdims=True)
                probs = jnp.exp(logits - peak)
                total = jnp.sum(probs, axis=-1, keepdims=True)
                r.sout_v[block, at, q_at] = (dot(probs.astype(bf16), qkv[:, v_at]) / total).astype(bf16)
                lses.append(peak + jnp.log(total))
            if block == 0:
                r.rlse_v[at, :] = pack(lses)

    def take_branch(block, from_out):
        rows = own_rows(block) + from_out.finish()
        r.h_v[block] = rows
        r.wn_v[block, place.rows(), :] = layer_norm(rows, gain(1), shift(1)).astype(bf16)

    def feed_up(block):
        columns = r.wup_v.shape[1]
        step = 256

        @pl.loop(0, columns // step)
        def _(index):
            at = pl.ds(pl.multiple_of(index * step, step), step)
            bias_at = pl.ds(pl.multiple_of(place.c * columns + index * step, step), step)
            pre = dot(r.wn_v[block], r.wup_v[:, at]) + r.up_bias[layer, :, bias_at]
            r.pre_v[block, :, at] = pre.astype(bf16)
            r.act_v[block, :, at] = (0.5 * pre * (1.0 + lax.erf(pre * (0.5**0.5)))).astype(bf16)

    def take_result(block, from_down):
        rows = r.h_v[block] + from_down.finish() + r.down_bias[layer]
        own = r.acts_v.at[block, place.core_rows()]
        own[...] = rows.astype(bf16)
        return net.copy(own, own, place.core)

    branch = [scatter(slots[0]), scatter(slots[1])]
    result = [scatter(slots[2]), scatter(slots[3])]
    first = [gather(r.u_v.at[block]) for block in range(2)]
    second = [gather(r.wn_v.at[block]) for block in range(2)]
    return SimpleNamespace(**locals())


def forward_kernel(names, *refs):
    every = dict(zip(names, refs))
    r = SimpleNamespace(**every)
    own = [{name[:-2]: ref for name, ref in every.items() if name.endswith(mark)} for mark in ("_0", "_1")]
    r0, r1 = (SimpleNamespace(**{**every, **part}) for part in own)
    r1.x = r0.acts_v
    place = Place(r0.u_v.shape[1])
    net, local = Net(r.send_sems, r.recv_sems), Local(r.local_sems)
    gate = jax.nn.sigmoid(r.gate[...])
    scatter_count = [0]

    def scatter(slot):
        index = scatter_count[0]
        scatter_count[0] += 1
        return Scatter(place, net, r.part.at[slot], r.near.at[index], r.out.at[slot], r.far.at[index])

    def share(source, target, axis=None):
        def half(c):
            if axis is None:
                return source.at[0]
            size = source.shape[axis] // 2
            index = [slice(None)] * len(source.shape)
            index[axis] = pl.ds(pl.multiple_of(c * size, size), size)
            return source.at[tuple(index)]

        target = target.at[place.c]
        return net.copy(half(1 - place.c), target, place.core), local.copy(half(place.c), target)

    def shared(*pairs):
        for far, near in pairs:
            far.wait_recv()
            local.wait(near)

    class Cotangent:
        def __init__(self, block):
            source, target = r.cot.at[block, place.core_rows()], r.cot_all.at[block, place.rows()]
            self.block = block
            self.across, self.near = net.copy(source, target, place.chip), net.copy(source, target, place.core)
            self.staged = local.copy(source, r.cot_v.at[block])

        def forward(self):
            self.across.wait_recv()
            passed = r.cot_all.at[self.block, place.rows(x_other=True)]
            self.passed = net.copy(passed, passed, place.core)
            local.wait(self.staged)
            local.copy(r.cot_v.at[self.block], r.cot_all.at[self.block, place.rows()])

        def finish(self):
            self.near.wait_recv()
            self.passed.wait_recv()

    place.meet()
    smalls = [
        share(r.gain_own, r.gain),
        share(r.shift_own, r.shift),
        share(r.up_bias_own, r.up_bias),
        share(r.down_bias_own, r.down_bias),
        share(r.rel_own, r.rel),
    ]
    first_weights = [share(r.qkv_own, r.wqkv_s, 2), share(r.out_own, r.wout_s, 0)]
    later_weights = [share(r.up_own, r.wup_s, 1), share(r.down_own, r.wdown_s, 0)]
    state_weights = []
    for source, target, axis in ((r.sqkv_own, r.wsqkv_v, 2), (r.sout_own, r.wsout_v, 0)):
        size = source.shape[axis] // 2
        at = pl.ds(pl.multiple_of(place.c * size, size), size)
        part = source.at[:, :, at] if axis == 2 else source.at[at]
        state_weights.append(local.copy(part, target))
    for layer, one in enumerate((r0, r1)):
        one.wqkv_v, one.wout_v = r.wqkv_s.at[layer], r.wout_s.at[layer]
        one.wup_v, one.wdown_v = r.wup_s.at[layer], r.wdown_s.at[layer]
    zero = forward_stages(0, r0, place, net, local, scatter, (0, 1, 2, 3))
    one = forward_stages(1, r1, place, net, local, scatter, (1, 0, 2, 3))
    update = scatter(0)
    state = [one.gather(r1.sn_v.at[block]) for block in range(2)]
    kept = []

    def keep(source, target):
        kept.append(local.copy(source, target))

    one.norm_state(r.state[place.core_rows(), :].astype(f32), 0)
    state[0].start()
    shared(*smalls)
    for block in range(2):
        zero.norm_first(block)
        zero.first[block].start()
    fill_bias(r.bias, bias_rows(r.rel[0], r.buckets[...], place.c))
    state[0].forward()
    zero.first[0].forward()
    shared(*first_weights)
    zero.first[0].finish()
    zero.project(r0.u_v.at[0], r0.wqkv_v, r0.qkv_v.at[0])
    zero.attend(0)
    zero.reduce_from(r0.att_v.at[0], r0.wout_v, zero.branch[0])
    zero.first[1].forward()
    zero.branch[0].middle()
    state[0].finish()
    local.wait(*state_weights)
    one.project(r1.sn_v.at[0], r.wsqkv_v, r1.sqkv_v.at[0])
    zero.first[1].finish()
    zero.project(r0.u_v.at[1], r0.wqkv_v, r0.qkv_v.at[1])
    keep(r0.u_v, r0.u)
    keep(r0.qkv_v, r0.qkv)
    zero.attend(1)
    zero.reduce_from(r0.att_v.at[1], r0.wout_v, zero.branch[1])
    zero.take_branch(0, zero.branch[0])
    zero.second[0].start()
    keep(r0.att_v, r0.att)
    keep(r0.lse_v, r0.lse)
    zero.branch[1].middle()
    shared(*later_weights)
    for source, target in (
        (r.wqkv_s, r.wqkv),
        (r.wout_s, r.wout),
        (r.wup_s, r.wup),
        (r.wdown_s, r.wdown),
        (r.wsqkv_v, r.wsqkv),
        (r.wsout_v, r.wsout),
        (r.gain, r.gain_both),
        (r.shift, r.shift_both),
        (r.up_bias, r.up_bias_both),
        (r.down_bias, r.down_bias_both),
        (r.rel, r.rel_both),
    ):
        local.copy(source, target)
    zero.second[0].forward()
    zero.second[0].finish()
    zero.feed_up(0)
    zero.reduce_from(r0.act_v.at[0], r0.wdown_v, zero.result[0])
    zero.take_branch(1, zero.branch[1])
    zero.second[1].start()
    keep(r0.h_v, r0.h)
    zero.result[0].middle()
    zero.second[1].forward()
    zero.second[1].finish()
    keep(r0.wn_v, r0.wn)
    zero.feed_up(1)
    keep(r0.pre_v, r0.pre)
    keep(r0.act_v, r0.act)
    zero.reduce_from(r0.act_v.at[1], r0.wdown_v, zero.result[1])
    sent = [zero.take_result(0, zero.result[0])]
    one.norm_first(0)
    one.first[0].start()
    zero.result[1].middle()
    cotangents = [Cotangent(1)]
    fill_bias(r.bias, bias_rows(r.rel[1], r.buckets[...], place.c))
    for done in (*zero.branch, zero.result[0]):
        done.release()
    sent.append(zero.take_result(1, zero.result[1]))
    one.norm_first(1)
    one.first[1].start()
    zero.result[1].release()
    local.wait(*kept)
    one.first[0].forward()
    one.first[0].finish()
    one.project(r1.u_v.at[0], r1.wqkv_v, r1.qkv_v.at[0])
    one.recur(0)
    one.reduce_from(r1.sout_v.at[0], r.wsout_v, update)
    cotangents[0].forward()
    update.middle()
    one.attend(0)
    one.reduce_from(r1.att_v.at[0], r1.wout_v, one.branch[0])
    one.first[1].forward()
    one.first[1].finish()
    one.project(r1.u_v.at[1], r1.wqkv_v, r1.qkv_v.at[1])
    local.copy(r1.u_v, r1.u)
    local.copy(r1.qkv_v, r1.qkv)
    one.branch[0].middle()
    update_rows = update.finish()
    update.release()
    r1.z_v[...] = update_rows
    state_rows = gate * r.state[place.core_rows(), :].astype(f32) + (1.0 - gate) * update_rows
    r1.s1_v[...] = state_rows
    one.norm_state(state_rows, 1)
    state[1].start()
    local.copy(r1.z_v, r1.z)
    local.copy(r1.s1_v, r1.s1)
    one.attend(1, state=False)
    one.take_branch(0, one.branch[0])
    one.second[0].start()
    state[1].forward()
    state[1].finish()
    one.project(r1.sn_v.at[1], r.wsqkv_v, r1.sqkv_v.at[1])
    local.copy(r1.sn_v, r1.sn)
    local.copy(r1.sqkv_v, r1.sqkv)
    one.attend(1, window=False)
    one.reduce_from(r1.att_v.at[1], r1.wout_v, one.branch[1])
    local.copy(r1.att_v, r1.att)
    local.copy(r1.lse_v, r1.lse)
    one.second[0].forward()
    one.branch[1].middle()
    one.second[0].finish()
    one.feed_up(0)
    one.reduce_from(r1.act_v.at[0], r1.wdown_v, one.result[0])
    one.take_branch(1, one.branch[1])
    one.second[1].start()
    local.copy(r1.h_v, r1.h)
    one.result[0].middle()
    cotangents.append(Cotangent(0))
    one.recur(1)
    local.copy(r1.sout_v, r1.sout)
    local.copy(r1.rlse_v, r1.rlse)
    one.second[1].forward()
    one.second[1].finish()
    local.copy(r1.wn_v, r1.wn)
    one.feed_up(1)
    local.copy(r1.pre_v, r1.pre)
    local.copy(r1.act_v, r1.act)
    one.reduce_from(r1.act_v.at[1], r1.wdown_v, one.result[1])
    sent.append(one.take_result(0, one.result[0]))
    one.result[1].middle()
    cotangents[1].forward()
    sent.append(one.take_result(1, one.result[1]))
    for made in sent:
        made.wait_recv()
    local.copy(r0.acts_v, r0.acts)
    local.copy(r1.acts_v, r1.acts)
    for made in cotangents:
        made.finish()
    local.drain()
    net.drain()


def forward_layers(block_len, small, valid, weights, rows, state, cot):
    wqkv, wout, wup, wdown, wsqkv, wsout = weights
    model = rows.shape[2]
    width, hidden = wqkv.shape[2] // 2, wup.shape[1] // 2
    quarter = block_len // 4
    heads = small.rel.shape[1] // 2

    def held(shape, dtype):
        return jax.ShapeDtypeStruct(shape, dtype)

    local_kinds = dict(
        qkv=held((2, block_len, 3 * width), bf16),
        lse=held((2, block_len, 128), f32),
        att=held((2, block_len, width), bf16),
        pre=held((2, block_len, hidden), bf16),
        act=held((2, block_len, hidden), bf16),
        h=held((2, quarter, model), f32),
    )
    own_kinds = dict(
        u=held((2, block_len, model), bf16),
        wn=held((2, block_len, model), bf16),
        acts=held((2, 2 * quarter, model), bf16),
    )
    rec_kinds = dict(
        sn=held((2, block_len, model), bf16),
        sqkv=held((2, block_len, 3 * width), bf16),
        rlse=held((block_len, 128), f32),
        sout=held((2, block_len, width), bf16),
        s1=held((quarter, model), f32),
        z=held((quarter, model), f32),
    )
    outs, scratch = {}, {}
    for mark in ("_0", "_1"):
        outs.update({name + mark: kind for name, kind in {**local_kinds, **own_kinds}.items()})
        scratch.update({name + "_v" + mark: pltpu.VMEM(kind.shape, kind.dtype) for name, kind in own_kinds.items()})
    outs.update({name + "_1": kind for name, kind in rec_kinds.items()})
    scratch.update({name + "_v_1": pltpu.VMEM(kind.shape, kind.dtype) for name, kind in rec_kinds.items()})
    scratch.update({name + "_v": pltpu.VMEM(kind.shape, kind.dtype) for name, kind in local_kinds.items()})
    outs.update(cot_all=held((2, block_len, model), bf16))
    ins = dict(
        x=rows,
        buckets=small.buckets,
        valid=valid,
        state=state,
        sgain=small.sgain,
        sshift=small.sshift,
        gate=small.gate,
    )
    far_ins = dict(
        qkv_own=wqkv, out_own=wout, up_own=wup, down_own=wdown, sqkv_own=wsqkv, sout_own=wsout, cot=cot
    )
    for name in ("gain", "shift", "up_bias", "down_bias", "rel"):
        array = getattr(small, name)
        far_ins[name + "_own"] = array
        outs[name + "_both"] = held((2, *array.shape[1:]), f32)
        scratch[name] = pltpu.VMEM((2, *array.shape[1:]), f32)
    stacked = dict(wqkv=(3, model, width), wout=(width, model), wup=(model, hidden), wdown=(hidden, model))
    for name, shape in stacked.items():
        outs[name] = held((2, *shape), bf16)
        scratch[name + "_s"] = pltpu.VMEM((2, *shape), bf16)
    for name, shape in dict(wsqkv=(3, model, width), wsout=(width, model)).items():
        outs[name] = held(shape, bf16)
        scratch[name + "_v"] = pltpu.VMEM(shape, bf16)
    scatters, gathers = 9, 12
    copies = 3 * (scatters + gathers) + 4 + 9
    scratch.update(
        cot_v=pltpu.VMEM((2, quarter, model), bf16),
        early=pltpu.VMEM((block_len, width), f32),
        bias=pltpu.VMEM((heads, min(128, block_len), 2 * block_len), f32),
        part=pltpu.VMEM((4, block_len, model), bf16),
        near=pltpu.VMEM((scatters, 2, quarter, model), bf16),
        out=pltpu.VMEM((4, quarter, model), bf16),
        far=pltpu.VMEM((scatters, quarter, model), bf16),
        send_sems=pltpu.SemaphoreType.DMA((copies,)),
        recv_sems=pltpu.SemaphoreType.DMA((copies,)),
        local_sems=pltpu.SemaphoreType.DMA((len(far_ins) + len(outs) + 4,)),
    )
    anywhere = pl.BlockSpec(memory_space=pl.ANY)
    inside = pl.BlockSpec(memory_space=pltpu.VMEM)
    results = pl.pallas_call(
        partial(forward_kernel, [*ins, *far_ins, *outs, *scratch]),
        out_shape=tuple(outs.values()),
        in_specs=[inside] * len(ins) + [anywhere] * len(far_ins),
        out_specs=[anywhere] * len(outs),
        scratch_shapes=list(scratch.values()),
        compiler_params=pltpu.CompilerParams(
            collective_id=0, has_side_effects=True, vmem_limit_bytes=VMEM_LIMIT
        ),
        name="forward_layers",
    )(*ins.values(), *far_ins.values())
    given = dict(zip(outs, results))
    layers = [
        SimpleNamespace(**{name[:-2]: array for name, array in given.items() if name.endswith(mark)})
        for mark in ("_0", "_1")
    ]
    return (*layers, SimpleNamespace(**given))


def ring_place(n, c, d):
    if n % 2:
        at = d

        def index_at(p):
            return p

    else:
        a, b = d // 2, d % 2
        at = a + b * (n - 1 - 2 * a)

        def index_at(p):
            b = p // (n // 2)
            return 2 * (p + b * (n - 1 - 2 * p)) + b

    def flip(p):
        return p + c * (n - 1 - 2 * p)

    return flip(at), lambda p: index_at(flip(p))


class Ring:
    def __init__(self, n):
        self.n, self.c = n, lax.axis_index("section")
        self.q, index_at = ring_place(n, self.c, lax.axis_index("dp"))
        self.after = {"dp": index_at((self.q + 1) % n)}
        self.before = {"dp": index_at((self.q + n - 1) % n)}
        self.core, self.chip = {"section": 1 - self.c}, {"mp": 1 - lax.axis_index("mp")}

    def meet(self):
        barrier = pltpu.get_barrier_semaphore()
        for other in (self.after, self.before, self.core, self.chip):
            pl.semaphore_signal(barrier, inc=1, device_id=other, device_id_type=MESH)
        pl.semaphore_wait(barrier, 4)


def remote(source, target, send, recv, to):
    return pltpu.make_async_remote_copy(
        src_ref=source, dst_ref=target, send_sem=send, recv_sem=recv, device_id=to, device_id_type=MESH
    )


def ring_subs(n, rows, most):
    return max(k for k in range(1, most + 1) if rows // n % (16 * k) == 0)


def ring_scratch(n, rows, model, most):
    subs = ring_subs(n, rows, most)
    sems = pltpu.SemaphoreType.DMA
    return dict(
        held=pltpu.VMEM((n - 1, rows // n, model), bf16),
        rs_send=sems((n - 1, subs)),
        rs_recv=sems((n - 1, subs)),
        ag_send=sems((n - 1, subs)),
        ag_recv=sems((n - 1, subs)),
        core_send=sems((n, subs)),
        core_recv=sems((n, subs)),
        own_sems=sems((subs,)),
    )


class RingSum:
    def __init__(self, ring, mine, full, held, rs_send, rs_recv, ag_send, ag_recv, core_send, core_recv, own_sems):
        self.ring, self.mine, self.full, self.held = ring, mine, full, held
        self.rs_send, self.rs_recv, self.ag_send, self.ag_recv = rs_send, rs_recv, ag_send, ag_recv
        self.core_send, self.core_recv, self.own_sems = core_send, core_recv, own_sems
        self.chunk, self.subs = held.shape[1], own_sems.shape[0]
        self.sub = self.chunk // self.subs
        self.half = (ring.n - 1) * self.subs
        self.total = 2 * self.half
        self.done = 0

    def rows(self, owner, k):
        owner = (owner + 2 * self.ring.n) % self.ring.n
        return pl.ds(pl.multiple_of(owner * self.chunk + k * self.sub, self.sub), self.sub)

    def piece(self, k):
        return slice(k * self.sub, (k + 1) * self.sub) if isinstance(k, int) else pl.ds(
            pl.multiple_of(k * self.sub, self.sub), self.sub
        )

    def summed(self, s, k):
        return self.held.at[s, self.piece(k)]

    def gathered(self, s, k):
        return self.full.at[self.ring.c, self.rows(self.ring.q + 1 - s, k)]

    def reduce(self, s, k, source):
        return remote(source, self.summed(s, k), self.rs_send.at[s, k], self.rs_recv.at[s, k], self.ring.after)

    def gather(self, s, k, source):
        return remote(source, self.gathered(s, k), self.ag_send.at[s, k], self.ag_recv.at[s, k], self.ring.after)

    def to_core(self, s, k, source):
        return remote(source, self.gathered(s, k), self.core_send.at[s, k], self.core_recv.at[s, k], self.ring.core)

    def from_core(self, s, k):
        n, q = self.ring.n, self.ring.q
        target = self.full.at[1 - self.ring.c, self.rows(n - q - s, k)]
        return remote(target, target, self.core_send.at[s, k], self.core_recv.at[s, k], self.ring.core)

    def own(self, k):
        return pltpu.make_async_copy(self.summed(self.ring.n - 2, k), self.gathered(0, k), self.own_sems.at[k])

    def start(self):
        for k in range(self.subs):
            self.reduce(0, k, self.mine.at[self.rows(self.ring.q, k)]).start()

    def add(self, s, k):
        self.reduce(s, k, self.summed(s, k)).wait_recv()
        self.held[s, self.piece(k), :] = (
            self.held[s, self.piece(k), :].astype(f32)
            + self.mine[self.rows(self.ring.q - 1 - s, k), :].astype(f32)
        ).astype(bf16)

    def add_middle(self, s, k):
        self.add(s, k)
        self.reduce(s + 1, k, self.summed(s, k)).start()

    def add_last(self, s, k):
        self.add(s, k)
        self.gather(0, k, self.summed(s, k)).start()
        self.to_core(0, k, self.summed(s, k)).start()
        self.own(k).start()

    def pass_middle(self, s, k):
        at = self.gathered(s + 1, k)
        self.gather(s, k, at).wait_recv()
        self.gather(s + 1, k, at).start()
        self.to_core(s + 1, k, at).start()

    def pass_last(self, s, k):
        at = self.gathered(s + 1, k)
        self.gather(s, k, at).wait_recv()
        self.to_core(s + 1, k, at).start()

    def pump_one(self, t):
        last = self.ring.n - 2
        s, k = t // self.subs, t % self.subs
        kinds = (
            (s < last, self.add_middle, s),
            (s == last, self.add_last, s),
            ((s > last) & (s < 2 * last + 1), self.pass_middle, s - last - 1),
            (s == 2 * last + 1, self.pass_last, s - last - 1),
        )
        for here, act, step in kinds:
            if isinstance(t, int):
                if here:
                    act(step, k)
            else:
                pl.when(here)(partial(act, step, k))

    def pump(self, count=1):
        for _ in range(min(count, self.total - self.done)):
            self.pump_one(self.done)
            self.done += 1

    def pumps_in(self, loop_steps, each):
        each = min(each, (self.total - self.done) // loop_steps)
        base = self.done
        self.done += each * loop_steps

        def pump(index):
            for piece in range(each):
                self.pump_one(base + index * each + piece)

        return pump

    def run(self, until):
        last = self.ring.n - 2
        for first, end, act in (
            (0, last, self.add_middle),
            (last, last + 1, self.add_last),
            (last + 1, 2 * last + 1, self.pass_middle),
            (2 * last + 1, 2 * last + 2, self.pass_last),
        ):
            while self.done < min(end * self.subs, until) and self.done % self.subs:
                self.pump()
            step, stop = self.done // self.subs, min(end, until // self.subs)
            if first <= step < stop:
                base = last + 1 if first > last else 0

                @pl.loop(step - base, stop - base)
                def _(s):
                    for k in range(self.subs):
                        act(s, k)

                self.done = stop * self.subs

    def release_mine(self):
        for k in range(self.subs):
            self.reduce(0, k, self.mine.at[self.rows(self.ring.q, k)]).wait_send()

    def finish(self, released=False):
        self.run(self.total)
        if not released:
            self.release_mine()
        last = self.ring.n - 2

        @pl.loop(0, last + 2)
        def _(s):
            for k in range(self.subs):
                self.from_core(s, k).wait_recv()
                self.to_core(s, k, self.gathered(s, k)).wait_send()

        @pl.loop(0, last + 1)
        def _(s):
            for k in range(self.subs):
                self.gather(s, k, self.gathered(s, k)).wait_send()

        @pl.loop(0, last)
        def _(s):
            for k in range(self.subs):
                self.reduce(s + 1, k, self.summed(s, k)).wait_send()

        for k in range(self.subs):
            self.own(k).wait()


def sum_kernel(n, parts, small_0, small_1, full, small_out, mine, small_held, small_sum, small_far, small, *rest):
    ring_refs, (small_send, small_recv, local_sems) = rest[:-3], rest[-3:]
    ring = Ring(n)
    flow = RingSum(ring, mine, full, *ring_refs)

    def small_step(s, first):
        source = small if first else small_held.at[s - 1]
        return remote(source, small_held.at[s], small_send.at[s], small_recv.at[s], ring.after)

    load = pltpu.make_async_copy(parts, mine, local_sems.at[0])
    load.start()
    small[: small_0.shape[0]] = small_0[...]
    small[small_0.shape[0] :] = small_1[...]
    ring.meet()
    small_step(0, True).start()
    load.wait()
    flow.start()

    @pl.loop(0, n - 2)
    def _(s):
        for k in range(flow.subs):
            flow.add_middle(s, k)
        small_step(s, True).wait_recv()
        small_step(s + 1, False).start()

    flow.done = (n - 2) * flow.subs
    flow.run(flow.half)
    small_step(n - 2, True).wait_recv()
    small_out[0] = small[...]

    @pl.loop(0, n - 1)
    def _(s):
        small_out[0] += small_held[s]

    between = remote(small_out.at[0], small_out.at[1], small_send.at[n - 1], small_recv.at[n - 1], ring.core)
    between.start()
    between.wait_recv()
    small_sum[...] = small_out[0] + small_out[1]
    across = remote(small_sum, small_far, small_send.at[n], small_recv.at[n], ring.chip)
    across.start()
    across.wait_recv()
    small_out[2] = small_sum[...] + small_far[...]
    flow.finish()

    @pl.loop(0, n - 1)
    def _(s):
        small_step(s, True).wait_send()

    between.wait_send()
    across.wait_send()


def sum_gradients(n, parts, small_0, small_1):
    rows, model = parts.shape
    both = (small_0.shape[0] + small_1.shape[0], model)
    anywhere = pl.BlockSpec(memory_space=pl.ANY)
    inside = pl.BlockSpec(memory_space=pltpu.VMEM)
    sems = pltpu.SemaphoreType.DMA
    return pl.pallas_call(
        partial(sum_kernel, n),
        out_shape=(
            jax.ShapeDtypeStruct((2, rows, model), bf16),
            jax.ShapeDtypeStruct((3,) + both, f32),
        ),
        in_specs=[anywhere, inside, inside],
        out_specs=[anywhere, inside],
        scratch_shapes=[
            pltpu.VMEM((rows, model), bf16),
            pltpu.VMEM((n - 1,) + both, f32),
            pltpu.VMEM(both, f32),
            pltpu.VMEM(both, f32),
            pltpu.VMEM(both, f32),
            *ring_scratch(n, rows, model, 6).values(),
            sems((n + 1,)),
            sems((n + 1,)),
            sems((1,)),
        ],
        compiler_params=pltpu.CompilerParams(
            collective_id=5, has_side_effects=True, vmem_limit_bytes=VMEM_LIMIT
        ),
        name="sum_gradients",
    )(parts, small_0, small_1)


def norm_back(rows, gain, grad):
    normed, scale = norm_parts(rows)
    inner = grad * gain
    means = jnp.mean(inner, axis=-1, keepdims=True), jnp.mean(inner * normed, axis=-1, keepdims=True)
    by_rows = scale * (inner - means[0] - normed * means[1])
    return by_rows, jnp.sum(grad * normed, axis=0, keepdims=True), jnp.sum(grad, axis=0, keepdims=True)


GAIN0, GAIN1, SHIFT0, SHIFT1, DOWN_BIAS, SGAIN, SSHIFT, GATE, UP_BIAS, BY_DISTANCE = range(10)
SMALL_ROWS = 16


def backward_kernel(layer, n, ring_names, names, *refs):
    r = SimpleNamespace(**dict(zip(names, refs)))
    rec = layer == 1
    heads, length = r.rel.shape[1] // 2, r.valid.shape[1]
    head_size = r.att_v.shape[1] // heads
    width = heads * head_size
    hidden = r.wup_v.shape[1]
    model = r.wup_v.shape[0]
    scale = head_size ** (-0.5)
    place = Place(length)
    net, local = Net(r.send_sems, r.recv_sems), Local(r.local_sems)
    chunk = min(128, length)

    ring = Ring(n)
    r.act, r.by_down = r.work.at[:hidden], r.work.at[hidden:]
    ring_refs = [[getattr(r, name) for name in flow_names] for flow_names in ring_names]
    if rec:
        up_flow = RingSum(ring, r.act, r.full.at[:, :model], *ring_refs[0])
        down_flow = RingSum(ring, r.by_down, r.full.at[:, model:], *ring_refs[1])
        act = [local.copy(r.act_in, r.act), local.copy(r.g_in, r.g)]
    else:
        rest_flow = RingSum(ring, r.mine, r.full, *ring_refs[0])
        parts = local.copy(r.parts, r.mine)
        act = [local.copy(r.act_in, r.act)]
    flows = []

    def launch(flow):
        flow.start()
        flows.append(flow)

    def tick(count=1):
        for _ in range(count):
            for flow in flows:
                flow.pump()

    def tick_at(index, *steps):
        for step in steps:

            @pl.when(index == step)
            def _():
                tick()

    ring.meet()
    wdown = local.copy(r.wdown.at[layer], r.wdown_v)
    pre = local.copy(r.pre, r.pre_v)
    wup = local.copy(r.wup.at[layer], r.wup_v)
    hidden_rows = local.copy(r.h, r.h_v)
    wn = local.copy(r.wn, r.wn_v)
    attention = [
        local.copy(r.wout.at[layer], r.wout_v),
        local.copy(r.qkv, r.qkv_v),
        local.copy(r.att, r.att_v),
        local.copy(r.lse, r.lse_v),
    ]
    if rec:
        attention += [local.copy(r.sqkv, r.sqkv_v), local.copy(r.wsqkv, r.wsqkv_v)]
        chain = [
            local.copy(r.s1, r.s1_v),
            local.copy(r.z, r.z_v),
            local.copy(r.wsout, r.wsout_v),
            local.copy(r.sout, r.sout_v),
            local.copy(r.rlse, r.rlse_v),
        ]
    wqkv = [local.copy(r.wqkv.at[layer], r.wqkv_v)]
    wqkv += [local.copy(r.x.at[block, place.core_rows()], r.x_v.at[block]) for block in range(2)]
    if rec:
        chain.append(local.copy(r.state.at[place.core_rows()], r.state_v))

    gain = lambda index: r.gain[layer, index : index + 1, :]
    small = r.small_v
    small[...] = jnp.zeros(small.shape, f32)
    r.dkv[...] = jnp.zeros(r.dkv.shape, f32)
    r.dbias[...] = jnp.zeros(r.dbias.shape, f32)
    if rec:
        r.dskv[...] = jnp.zeros(r.dskv.shape, f32)

    def add_small(index, value):
        small[index : index + 1, :] += value

    def gather(buffer):
        return Gather(place, net, buffer)

    scatter_count = [0]

    def scatter(slot):
        index = scatter_count[0]
        scatter_count[0] += 1
        return Scatter(place, net, r.part.at[slot], r.near.at[index], r.out.at[slot], r.far.at[index])

    def block_rows(block):
        return slice(block * length, (block + 1) * length)

    def own_grad(block):
        if rec:
            return r.g[pl.ds(place_row(block), place.quarter), :].astype(f32)
        return r.gy[block, place.core_rows(), :].astype(bf16).astype(f32)

    def feed_back(block):
        step = 256
        rows = block_rows(block)

        @pl.loop(0, hidden // step)
        def _(index):
            at = pl.ds(pl.multiple_of(index * step, step), step)
            pre = r.pre_v[rows, at].astype(f32)
            by_act = dot_nt(r.g[rows, :], r.wdown_v[at, :])
            below = 0.5 * (1.0 + lax.erf(pre * (0.5**0.5)))
            by_pre = by_act * (below + pre * jnp.exp(-0.5 * pre * pre) * 0.3989422804014327)
            small[UP_BIAS : UP_BIAS + 1, at] += jnp.sum(by_pre, axis=0, keepdims=True)
            r.dpre[rows, at] = by_pre.astype(bf16)

    def reduce_back(terms, to):
        step = min(512, model)
        for x_other in (True, False):
            rows = place.chip_rows(x_other)

            @pl.loop(0, model // step)
            def _(index):
                at = pl.ds(pl.multiple_of(index * step, step), step)
                total = None
                for values, weights in terms:
                    term = dot_nt(values[rows, :], weights[at, :])
                    total = term if total is None else total + term
                to.part[rows, at] = total.astype(bf16)

            to.send(x_other)

    def update_last():
        step = min(512, model)
        for x_other in (True, False):
            rows = place.chip_rows(x_other)

            @pl.loop(0, model // step)
            def _(index):
                at = pl.ds(pl.multiple_of(index * step, step), step)
                last_update.part[rows, at] = dot(r.sout_v[1, rows, :], r.wsout_v[:, at]).astype(bf16)

            last_update.send(x_other)

    def take_feed(block, from_feed):
        by_norm = from_feed.finish()
        grad = own_grad(block)
        by_rows, by_gain, by_shift = norm_back(r.h_v[block], gain(1), by_norm)
        add_small(GAIN1, by_gain)
        add_small(SHIFT1, by_shift)
        add_small(DOWN_BIAS, jnp.sum(grad, axis=0, keepdims=True))
        total = grad + by_rows
        r.ig_v[block] = total
        r.hg[pl.ds(place_row(block), place.quarter), :] = total.astype(bf16)

    def place_row(block):
        return pl.multiple_of(block * length + place.x * place.half + place.c * place.quarter, place.quarter)

    def weight_grad(left, right, target, at_row=0):
        step = 256

        @pl.loop(0, left.shape[1] // step)
        def _(index):
            at = pl.ds(pl.multiple_of(index * step, step), step)
            to = pl.ds(pl.multiple_of(at_row + index * step, step), step)
            target[to, :] = dot_tn(left[:, at], right[...]).astype(bf16)

    def projection_grad(normed, grads, target):
        @pl.loop(0, model // width)
        def _(index):
            tick_at(index, 0, 1, 2)
            at = pl.ds(pl.multiple_of(index * width, width), width)
            found = dot_tn(normed[:, at], grads[...]).astype(bf16)
            for part in range(3):
                to = slice(part * width, (part + 1) * width)
                target[to, at] = found[:, to]

    def branch_back(block):
        r.datt[block] = dot_nt(r.hg[block_rows(block), :], r.wout_v[...]).astype(bf16)

    def columns(head, part):
        return slice(part * width + head * head_size, part * width + (head + 1) * head_size)

    def attend_back(block, window=True, state=rec):
        qkv = r.qkv_v.at[block]
        prev = r.qkv_v.at[block - 1] if block > 0 else None

        @pl.loop(0, length // chunk)
        def _(index):
            if window:
                tick_at(index, 1, 3)
            at = pl.ds(pl.multiple_of(index * chunk, chunk), chunk)
            block_at = pl.ds(pl.multiple_of(block * length + index * chunk, chunk), chunk)
            for head in range(heads):
                q_at, k_at, v_at = (columns(head, part) for part in range(3))
                early_at = pl.ds(pl.multiple_of(index * width + head * head_size, head_size), head_size)
                query = qkv[at, q_at]
                lse = r.lse_v[block, at, head : head + 1]
                grad = r.datt[block, at, q_at]
                delta = jnp.sum(
                    grad.astype(f32) * r.att_v[block_at, q_at].astype(f32), axis=-1, keepdims=True
                )
                by_query = None
                if state:
                    skv = r.sqkv_v.at[block]
                    state_probs = jnp.exp(dot_nt(query, skv[:, k_at]) * scale - lse)
                    by_state = state_probs * (dot_nt(grad, skv[:, v_at]) - delta) * scale
                    low_state = by_state.astype(bf16)
                    by_query = dot(low_state, skv[:, k_at])
                    r.dskv[:, q_at] += dot_tn(low_state, query)
                    r.dskv[:, k_at] += dot_tn(state_probs.astype(bf16), grad)
                    if not window:
                        r.h_v[0, :, early_at] = by_query
                elif rec:
                    by_query = r.h_v[0, :, early_at]
                if not window:
                    continue
                key, value = qkv[:, k_at], qkv[:, v_at]
                logits, here = window_logits(
                    query,
                    key,
                    None if prev is None else prev[:, k_at],
                    r.bias[head, :, bias_columns(index, chunk, length)],
                    r.valid,
                    block,
                    index * chunk,
                    scale,
                )
                probs = jnp.exp(logits - lse)
                by_probs = dot_nt(grad, value)
                if prev is not None:
                    by_probs = jnp.where(here, by_probs, dot_nt(grad, prev[:, v_at]))
                by_logits = probs * (by_probs - delta)
                r.dbias[head, :, bias_columns(index, chunk, length)] += by_logits
                by_logits = by_logits * scale
                if prev is None:
                    low = by_logits.astype(bf16)
                    low_probs = probs.astype(bf16)
                    by_window = dot(low, key)
                else:
                    low = jnp.where(here, by_logits, 0.0).astype(bf16)
                    low_probs = jnp.where(here, probs, 0.0).astype(bf16)
                    low_prev = jnp.where(here, 0.0, by_logits).astype(bf16)
                    low_probs_prev = jnp.where(here, 0.0, probs).astype(bf16)
                    by_window = dot(low, key) + dot(low_prev, prev[:, k_at])
                    r.dkv[block - 1, :, q_at] += dot_tn(low_prev, query)
                    r.dkv[block - 1, :, k_at] += dot_tn(low_probs_prev, grad)
                r.dkv[block, :, q_at] += dot_tn(low, query)
                r.dkv[block, :, k_at] += dot_tn(low_probs, grad)
                by_query = by_window if by_query is None else by_query + by_window
                r.dqkv[block_at, q_at] = by_query.astype(bf16)

    def recur_back():
        qkv, state = r.qkv_v.at[0], r.sqkv_v.at[0]

        @pl.loop(0, length // chunk)
        def _(index):
            tick_at(index, 2)
            at = pl.ds(pl.multiple_of(index * chunk, chunk), chunk)
            for head in range(heads):
                q_at, k_at, v_at = (columns(head, part) for part in range(3))
                query, key, value = state[at, q_at], qkv[:, k_at], qkv[:, v_at]
                logits = dot_nt(query, key) * scale
                logits = jnp.where(r.valid[0:1, :] > 0.5, logits, negative)
                probs = jnp.exp(logits - r.rlse_v[at, head : head + 1])
                grad = r.dsout[at, q_at]
                delta = jnp.sum(
                    grad.astype(f32) * r.sout_v[0, at, q_at].astype(f32), axis=-1, keepdims=True
                )
                low = (probs * (dot_nt(grad, value) - delta) * scale).astype(bf16)
                r.dsqkv[at, q_at] = dot(low, key).astype(bf16)
                r.dkv[0, :, q_at] += dot_tn(low, query)
                r.dkv[0, :, k_at] += dot_tn(probs.astype(bf16), grad)

    def close_keys(block):
        r.dqkv[block_rows(block), width:] = r.dkv[block].astype(bf16)

    def close_state(block):
        r.dsqkv[block_rows(block), width:] = r.dskv[...].astype(bf16)
        if block == 1:
            r.dskv[...] = jnp.zeros(r.dskv.shape, f32)

    def input_back(block, to):
        rows = block_rows(block)
        reduce_back(
            [
                (r.dqkv.at[rows, part * width : (part + 1) * width], r.wqkv_v.at[part])
                for part in range(3)
            ],
            to,
        )

    def state_back(block, to):
        rows = block_rows(block)
        reduce_back(
            [
                (r.dsqkv.at[rows, part * width : (part + 1) * width], r.wsqkv_v.at[part])
                for part in ((0, 1, 2) if block == 0 else (1, 2))
            ],
            to,
        )

    def give(rows, target):
        local.copy(rows, target)
        return net.copy(rows, target, place.core)

    def take_input(block, from_input):
        by_norm = from_input.finish()
        rows = r.x_v[block].astype(f32)
        by_rows, by_gain, by_shift = norm_back(rows, gain(0), by_norm)
        add_small(GAIN0, by_gain)
        add_small(SHIFT0, by_shift)
        r.ig_v[block] += by_rows
        return give(r.ig_v.at[block], r.ig.at[block, place.core_rows()])

    def take_state(rows, from_state):
        by_rows, by_gain, by_shift = norm_back(rows, r.sgain[...], from_state.finish())
        add_small(SGAIN, by_gain)
        add_small(SSHIFT, by_shift)
        return by_rows

    def close_bias():
        tile = r.dbias.shape[1]
        for head in range(heads):
            folded = r.dbias[head, :, :length] + r.dbias[head, :, length:]
            row = lax.broadcasted_iota(jnp.int32, folded.shape, 0)
            bit = 1
            while bit < tile:
                moved = pltpu.roll(folded, length - bit, axis=1)
                folded = jnp.where((row & bit) != 0, moved, folded)
                bit *= 2
            small[BY_DISTANCE : BY_DISTANCE + 1, head * length : (head + 1) * length] = jnp.sum(
                folded, axis=0, keepdims=True
            )

    if rec:
        at_qkv, at_sqkv = 0, 4 * width
    else:
        at_up, at_down, at_qkv = 0, model, model + hidden
    at_out = 3 * width

    feed = [scatter(0), scatter(1)]
    inputs = [scatter(2 if rec else 0), scatter(1)]
    if not rec:
        grads = [gather(r.g.at[block_rows(block)]) for block in range(2)]
    hiddens = [gather(r.hg.at[block_rows(block)]) for block in range(2)]
    if rec:
        states = [scatter(0), scatter(0)]
        last_update = scatter(2)
        updates = gather(r.ug)
    if not rec:
        for block in (1, 0):
            r.g[pl.ds(place_row(block), place.quarter), :] = own_grad(block).astype(bf16)
            grads[block].start()
        local.wait(parts)
        launch(rest_flow)
    fill_bias(r.bias, bias_rows(r.rel[layer], r.buckets[...], place.c))
    local.wait(*act)
    if rec:
        weight_grad(r.act, r.g, r.by_down)
        launch(down_flow)
    else:
        tick()
        grads[1].forward()
        tick()
        grads[1].finish()
    local.wait(wdown, pre, wup)
    feed_back(1)
    tick()
    reduce_back([(r.dpre.at[block_rows(1)], r.wup_v)], feed[1])
    if rec:
        tick()
    else:
        grads[0].forward()
        tick()
        grads[0].finish()
    feed_back(0)
    feed[1].middle()
    tick()
    reduce_back([(r.dpre.at[block_rows(0)], r.wup_v)], feed[0])
    tick()
    feed[0].middle()
    if not rec:
        weight_grad(r.act, r.g, r.by_down)
        down_out = local.copy(r.by_down, r.dw.at[at_down:at_qkv])
    tick()
    local.wait(wn)
    weight_grad(r.wn_v, r.dpre, r.act)
    if rec:
        launch(up_flow)
        sn_in = local.copy(r.sn, r.pre_v)
    else:
        local.copy(r.act, r.dw.at[at_up:at_down])
    tick()
    u_in = local.copy(r.u, r.wn_v)
    local.wait(hidden_rows)
    take_feed(1, feed[1])
    hiddens[1].start()
    tick(2)
    take_feed(0, feed[0])
    hiddens[0].start()
    tick()
    if rec:
        local.wait(*chain)
        update_last()
    tick()
    hiddens[1].forward()
    tick()
    hiddens[1].finish()
    local.wait(*attention)
    branch_back(1)
    if rec:
        last_update.middle()
    tick()
    feed[0].release()
    feed[1].release()
    if rec:
        attend_back(1, window=False)
        close_state(1)
        state_back(1, states[1])
        tick()
        hiddens[0].forward()
        states[1].middle()
        attend_back(1, state=False)
    else:
        attend_back(1)
        hiddens[0].forward()
    close_keys(1)
    local.wait(*wqkv)
    input_back(1, inputs[1])
    tick()
    hiddens[0].finish()
    branch_back(0)
    sent = []
    if rec:
        tick()
        gate = jax.nn.sigmoid(r.gate[...])
        by_state = take_state(r.s1_v[...], states[1])
        states[1].release()
        before = r.state_v[...].astype(f32)
        add_small(
            GATE,
            jnp.sum(by_state * (before - r.z_v[...]) * gate * (1.0 - gate), axis=0, keepdims=True),
        )
        r.ug[place.rows(), :] = ((1.0 - gate) * by_state).astype(bf16)
        updates.start()
        r.s1_v[...] = gate * r.s1_v[...] + (1.0 - gate) * last_update.finish()
        sent.append(give(r.s1_v, r.final.at[place.core_rows()]))
        last_update.release()
    inputs[1].middle()
    tick()
    attend_back(0)
    tick()
    if rec:
        updates.forward()
        tick()
        updates.finish()
        r.dsout[...] = dot_nt(r.ug[...], r.wsout_v[...]).astype(bf16)
        recur_back()
        tick()
    close_keys(0)
    input_back(0, inputs[0])
    tick()
    if rec:
        close_state(0)
        state_back(0, states[0])
        tick()
    sent.append(take_input(1, inputs[1]))
    inputs[0].middle()
    tick()
    if rec:
        states[0].middle()
    weight_grad(r.att_v, r.hg, r.dpre, at_out)
    close_bias()
    local.wait(u_in)
    projection_grad(r.wn_v, r.dqkv, r.dpre)
    local.copy(r.dpre, r.dw.at[at_qkv : at_qkv + 4 * width])
    tick()
    if rec:
        r.dsqkv[block_rows(1), 0:width] = jnp.zeros((length, width), bf16)
        local.wait(sn_in)
        projection_grad(r.pre_v, r.dsqkv, r.g)
        tick()
        weight_grad(r.sout_v.at[0], r.ug, r.g, at_out)
        local.copy(r.g, r.dw.at[at_sqkv:])
    sent.append(take_input(0, inputs[0]))
    if rec:
        take_state(r.state_v[...].astype(f32), states[0])
    local.copy(small, r.small)
    for made in sent:
        made.wait_recv()
    while any(flow.done < flow.total for flow in flows):
        tick()
    for flow in flows:
        flow.finish()
    local.drain()
    net.drain()


def backward_layer(layer, n, block_len, small, valid, weights, grad_rows, rows, state, kept, parts=None):
    rec = layer == 1
    wqkv, wout, wup, wdown = weights[:4]
    model = rows.shape[2]
    width, hidden = wqkv.shape[3], wup.shape[2]
    quarter = block_len // 4
    heads = small.rel.shape[1] // 2

    def held(shape, dtype):
        return jax.ShapeDtypeStruct(shape, dtype)

    dw_rows = 8 * width if rec else model + hidden + 4 * width
    ring_rows = model + hidden if rec else parts.shape[0]
    outs = dict(
        full=held((2, ring_rows, model), bf16),
        dw=held((dw_rows, model), bf16),
        small=held((SMALL_ROWS, model), f32),
        ig=held((2, 2 * quarter, model), f32),
    )
    ins = dict(
        gain=small.gain, rel=small.rel, buckets=small.buckets, valid=valid
    )

    def flat(array):
        return array.reshape((-1,) + array.shape[2:])

    stacked = dict(wqkv=wqkv, wout=wout, wup=wup, wdown=wdown)
    copied = dict(
        qkv=kept.qkv, lse=kept.lse, att=flat(kept.att), wn=flat(kept.wn), pre=flat(kept.pre), h=kept.h
    )
    late = dict(act_in=flat(kept.act), u=flat(kept.u), x=rows)
    if rec:
        late.update(state=state)
        ins.update(sgain=small.sgain, sshift=small.sshift, gate=small.gate)
        copied.update(wsqkv=weights[4], wsout=weights[5])
        copied.update(sqkv=kept.sqkv, rlse=kept.rlse, sout=kept.sout, s1=kept.s1, z=kept.z)
        late.update(sn=flat(kept.sn), g_in=flat(parts))
        outs.update(final=held((2 * quarter, model), f32))
    else:
        ins.update(gy=grad_rows)
        late.update(parts=parts)
    far_ins = {**stacked, **copied, **late}
    scatters = 7 if rec else 4
    slots = 3 if rec else 2
    copies = (3 * 7 + 3 * 3 + 3) if rec else (3 * 4 + 3 * 4 + 2)
    scratch = dict(small_v=pltpu.VMEM(outs["small"].shape, f32), ig_v=pltpu.VMEM((2, quarter, model), f32))
    for name, array in stacked.items():
        scratch[name + "_v"] = pltpu.VMEM(array.shape[1:], array.dtype)
    for name, array in copied.items():
        scratch[name + "_v"] = pltpu.VMEM(array.shape, array.dtype)
    scratch.update(
        g=pltpu.VMEM((2 * block_len, model), bf16),
        x_v=pltpu.VMEM((2, quarter, model), bf16),
        hg=pltpu.VMEM((2 * block_len, model), bf16),
        work=pltpu.VMEM((2 * hidden, model), bf16),
        dpre=pltpu.VMEM((2 * block_len, hidden), bf16),
        datt=pltpu.VMEM((2, block_len, width), bf16),
        dkv=pltpu.VMEM((2, block_len, 2 * width), f32),
        dqkv=pltpu.VMEM((2 * block_len, 3 * width), bf16),
        dbias=pltpu.VMEM((heads, min(128, block_len), 2 * block_len), f32),
        bias=pltpu.VMEM((heads, min(128, block_len), 2 * block_len), f32),
        part=pltpu.VMEM((slots, block_len, model), bf16),
        near=pltpu.VMEM((scatters, 2, quarter, model), bf16),
        out=pltpu.VMEM((slots, quarter, model), bf16),
        far=pltpu.VMEM((scatters, quarter, model), bf16),
        send_sems=pltpu.SemaphoreType.DMA((copies,)),
        recv_sems=pltpu.SemaphoreType.DMA((copies,)),
        local_sems=pltpu.SemaphoreType.DMA((len(far_ins) + 8,)),
    )
    if rec:
        scratch.update(
            ug=pltpu.VMEM((block_len, model), bf16),
            dsout=pltpu.VMEM((block_len, width), bf16),
            dskv=pltpu.VMEM((block_len, 2 * width), f32),
            state_v=pltpu.VMEM((quarter, model), bf16),
            dsqkv=pltpu.VMEM((2 * block_len, 3 * width), bf16),
        )
    else:
        scratch.update(mine=pltpu.VMEM((ring_rows, model), bf16))
    ring_names = []
    for flow_rows in (model, hidden) if rec else (ring_rows,):
        flow_scratch = ring_scratch(n, flow_rows, model, 2)
        flow_scratch = {name + str(len(ring_names)): kind for name, kind in flow_scratch.items()}
        scratch.update(flow_scratch)
        ring_names.append(list(flow_scratch))
    anywhere = pl.BlockSpec(memory_space=pl.ANY)
    inside = pl.BlockSpec(memory_space=pltpu.VMEM)
    results = pl.pallas_call(
        partial(backward_kernel, layer, n, ring_names, [*ins, *far_ins, *outs, *scratch]),
        out_shape=tuple(outs.values()),
        in_specs=[inside] * len(ins) + [anywhere] * len(far_ins),
        out_specs=[anywhere] * len(outs),
        scratch_shapes=list(scratch.values()),
        compiler_params=pltpu.CompilerParams(
            collective_id=3 + layer, has_side_effects=True, vmem_limit_bytes=VMEM_LIMIT
        ),
        name="backward_recurrent" if rec else "backward_local",
    )(*ins.values(), *far_ins.values())
    return SimpleNamespace(**dict(zip(outs, results)))


def place_kernel(
    width, hidden, feed_1, rest_1, full_0, acts_0, acts_1, igs_0, igs_1, state, sums, buckets,
    qkv, out, up, down, sqkv, sout, acts, igs, final, gain, shift, rel, up_bias, down_bias, sgain, sshift, gate,
    inward, outward, acts_v, igs_v, state_v, igs_tiles, state_tiles, in_sems, out_sems, row_sems,
):
    model = full_0.shape[2]
    layer = lax.axis_index("section")
    slots = inward.shape[0]

    rows_in = []
    for index, (first, second, target) in enumerate(((acts_0, acts_1, acts_v), (igs_0, igs_1, igs_v))):
        pl.when(layer == 0)(pltpu.make_async_copy(first, target, row_sems.at[index]).start)
        pl.when(layer == 1)(pltpu.make_async_copy(second, target, row_sems.at[index]).start)
        rows_in.append(pltpu.make_async_copy(first, target, row_sems.at[index]))
    rows_in.append(pltpu.make_async_copy(state, state_v, row_sems.at[2]))
    rows_in[2].start()
    at_rest = model + hidden
    jobs = []
    for half in range(2):
        columns = slice(half * width, (half + 1) * width)

        def projection(target):
            return [target.at[index : index + width, columns] for index in range(0, model, width)]

        for row in range(0, model, width):
            wide = slice(half * hidden, (half + 1) * hidden)
            jobs.append((half, (feed_1, row), row, [up.at[0, row : row + width, wide]]))
        for row in range(0, hidden, width):
            at = half * hidden + row
            jobs.append((half, (feed_1, model + row), model + row, [down.at[0, at : at + width]]))
        for part in range(3):
            row = part * width
            jobs.append((half, (rest_1, row), at_rest + row, projection(qkv.at[0, part])))
            jobs.append((half, (rest_1, 4 * width + row), None, projection(sqkv.at[part])))
        jobs.append((half, (rest_1, 3 * width), at_rest + 3 * width, [out.at[0, columns]]))
        jobs.append((half, (rest_1, 7 * width), None, [sout.at[columns]]))

    def load(index, start):
        half, (array, row), row_0, _ = jobs[index]
        slot = index % slots

        def made(source, at):
            return pltpu.make_async_copy(source.at[half, at : at + width], inward.at[slot], in_sems.at[slot])

        if not start:
            made(array, row).wait()
        elif row_0 is None:
            made(array, row).start()
        else:
            pl.when(layer == 1)(lambda: made(array, row).start())
            pl.when(layer == 0)(lambda: made(full_0, row_0).start())

    def stores(index):
        targets, slot = jobs[index][3], index % slots
        step = model // len(targets)
        return [
            pltpu.make_async_copy(
                outward.at[slot, :, k * step : (k + 1) * step], target, out_sems.at[slot, k]
            )
            for k, target in enumerate(targets)
        ]

    for index in range(slots):
        load(index, True)
    def place_sums():
        mine = [jnp.where(layer == 0, sums[index, :SMALL_ROWS], sums[index, SMALL_ROWS:]) for index in range(3)]
        gain[0] = mine[2][GAIN0 : GAIN1 + 1]
        shift[0] = mine[2][SHIFT0 : SHIFT1 + 1]
        down_bias[...] = mine[2][DOWN_BIAS : DOWN_BIAS + 1]
        for target, row in ((sgain, SGAIN), (sshift, SSHIFT), (gate, GATE)):
            target[...] = sums[2, SMALL_ROWS + row : SMALL_ROWS + row + 1]
        by_core = [jnp.where(layer == 0, mine[0], mine[1]), jnp.where(layer == 0, mine[1], mine[0])]
        heads, length = rel.shape[1] // 2, buckets.shape[1]
        hot = back_hot(buckets[...], rel.shape[2])
        for half in range(2):
            up_bias[:, half * hidden : (half + 1) * hidden] = by_core[half][UP_BIAS : UP_BIAS + 1, :hidden]
            for head in range(heads):
                row = by_core[half][BY_DISTANCE : BY_DISTANCE + 1, head * length : (head + 1) * length]
                at = half * heads + head
                row = jnp.broadcast_to(row, (16, length))
                rel[0, at : at + 1, :] = sum(dot_nt(part, hot) for part in in_parts(row))[:1]

    rows_out = []

    def place_rows():
        rows_in[0].wait()
        rows_out.append(pltpu.make_async_copy(acts_v, acts, row_sems.at[0]))
        rows_out[0].start()
        tiles = model // 128
        for index, source, target in ((1, igs_v, igs_tiles), (2, state_v, state_tiles)):
            rows_in[index].wait()
            for tile in range(tiles):
                target[..., tile, :] = source[..., tile * 128 : (tile + 1) * 128]
            rows_out.append(pltpu.make_async_copy(target, igs if index == 1 else final, row_sems.at[index]))
            rows_out[index].start()

    for index in range(len(jobs)):
        slot = index % slots
        if index == slots:
            place_rows()
        if index == 2 * slots:
            place_sums()
        load(index, False)
        if index >= slots:
            for made in stores(index - slots):
                made.wait()
        outward[slot] = inward[slot].astype(f32)
        for made in stores(index):
            made.start()
        if index + slots < len(jobs):
            load(index + slots, True)
    for index in range(len(jobs) - slots, len(jobs)):
        for made in stores(index):
            made.wait()
    for made in rows_out:
        made.wait()


def place_gradients(feed_1, rest_1, full_0, acts, igs, final, sums, buckets, bucket_count, chip_heads, width, hidden):
    model = full_0.shape[2]
    anywhere = pl.BlockSpec(memory_space=pl.ANY)
    inside = pl.BlockSpec(memory_space=pltpu.VMEM)
    slots, tiles = 8, model // 128
    blocks, rows = acts[0].shape[:2]
    far_shapes = (
        ((1, 3, model, 2 * width), f32),
        ((1, 2 * width, model), f32),
        ((1, model, 2 * hidden), f32),
        ((1, 2 * hidden, model), f32),
        ((3, model, 2 * width), f32),
        ((2 * width, model), f32),
        ((blocks, rows, model), bf16),
        ((blocks, rows, tiles, 128), f32),
        ((rows, tiles, 128), f32),
    )
    near_shapes = (
        (1, 2, model),
        (1, 2, model),
        (1, chip_heads, bucket_count),
        (1, 2 * hidden),
        (1, model),
        (1, model),
        (1, model),
        (1, model),
    )
    return pl.pallas_call(
        partial(place_kernel, width, hidden),
        out_shape=[jax.ShapeDtypeStruct(*kind) for kind in far_shapes]
        + [jax.ShapeDtypeStruct(shape, f32) for shape in near_shapes],
        in_specs=[anywhere] * 8 + [inside] * 2,
        out_specs=[anywhere] * len(far_shapes) + [inside] * len(near_shapes),
        scratch_shapes=[
            pltpu.VMEM((slots, width, model), bf16),
            pltpu.VMEM((slots, width, model), f32),
            pltpu.VMEM((blocks, rows, model), bf16),
            pltpu.VMEM((blocks, rows, model), f32),
            pltpu.VMEM((rows, model), f32),
            pltpu.VMEM((blocks, rows, tiles, 128), f32),
            pltpu.VMEM((rows, tiles, 128), f32),
            pltpu.SemaphoreType.DMA((slots,)),
            pltpu.SemaphoreType.DMA((slots, model // width)),
            pltpu.SemaphoreType.DMA((3,)),
        ],
        compiler_params=pltpu.CompilerParams(vmem_limit_bytes=VMEM_LIMIT),
        name="place_gradients",
    )(feed_1, rest_1, full_0, *acts, *igs, final, sums, buckets)


def local_part(
    tokens, valid_mask, buckets, state_init, norm_gain, norm_shift, w_qkv, w_out, rel_bias, w_up, up_bias,
    w_down, down_bias, state_gain, state_shift, w_state_qkv, w_state_out, gate_bias, cotangent,
):
    block_len = valid_mask.shape[1]
    model = tokens.shape[3]
    bucket_count, chip_heads = rel_bias.shape[1:]
    docs = lax.axis_size("dp")
    valid = valid_mask[:, :, 0].astype(f32)
    cot_rows = cotangent[:, :, 0, :]
    rows = tokens[:, :, 0, :]
    state = state_init[:, 0, :]
    small = SimpleNamespace(
        gain=norm_gain,
        shift=norm_shift,
        up_bias=up_bias[:, None, :],
        down_bias=down_bias[:, None, :],
        rel=jnp.swapaxes(rel_bias, 1, 2),
        buckets=buckets[None],
        sgain=state_gain[None],
        sshift=state_shift[None],
        gate=gate_bias[None],
    )
    own_weights = (w_qkv[0], w_out[0], w_up[0], w_down[0], w_state_qkv, w_state_out)
    kept0, kept1, both = forward_layers(block_len, small, valid, own_weights, rows, state, cot_rows)
    small.gain, small.shift, small.rel = both.gain_both, both.shift_both, both.rel_both
    small.up_bias, small.down_bias = both.up_bias_both, both.down_bias_both
    weights = (both.wqkv, both.wout, both.wup, both.wdown, both.wsqkv, both.wsout)
    grad1 = backward_layer(1, docs, block_len, small, valid, weights, None, kept0.acts, state, kept1, both.cot_all)
    grad0 = backward_layer(0, docs, block_len, small, valid, weights, grad1.ig, rows, state, kept0, grad1.dw)
    full, sums = sum_gradients(docs, grad0.dw, grad0.small, grad1.small)
    (
        qkv_grad, out_grad, up_grad, down_grad, state_qkv_grad, state_out_grad, acts, input_grads, final,
        gain_grad, shift_grad, rel_grad, up_bias_grad, down_bias_grad, sgain_grad, sshift_grad, gate_grad,
    ) = place_gradients(
        grad1.full, grad0.full, full, (kept0.acts, kept1.acts), (grad0.ig, grad1.ig), grad1.final, sums,
        small.buckets, bucket_count, chip_heads, weights[0].shape[3], weights[2].shape[2],
    )
    return (
        acts[None, :, :, None, :],
        input_grads.reshape(1, 2, -1, 1, model),
        final.reshape(-1, 1, model),
        gain_grad,
        shift_grad,
        qkv_grad,
        out_grad,
        jnp.swapaxes(rel_grad, 1, 2),
        up_grad,
        up_bias_grad,
        down_grad,
        down_bias_grad,
        sgain_grad[0],
        sshift_grad[0],
        state_qkv_grad,
        state_out_grad,
        gate_grad[0],
    )


def solution(mesh):
    in_specs = (
        P(None, "mp", "dp", None),
        P(None, None, "dp"),
        P(),
        P("mp", "dp", None),
        P("section", None, None),
        P("section", None, None),
        P("section", None, None, "mp"),
        P("section", "mp", None),
        P("section", None, "mp"),
        P("section", None, "mp"),
        P("section", "mp"),
        P("section", "mp", None),
        P("section", None),
        P(),
        P(),
        P(None, None, "mp"),
        P("mp", None),
        P(),
        P(None, "mp", "dp", None),
    )
    out_specs = (
        P("section", None, "mp", "dp", None),
        P("section", None, "mp", "dp", None),
        P("mp", "dp", None),
        P("section", None, None),
        P("section", None, None),
        P("section", None, None, "mp"),
        P("section", "mp", None),
        P("section", None, "mp"),
        P("section", None, "mp"),
        P("section", "mp"),
        P("section", "mp", None),
        P("section", None),
        P(),
        P(),
        P(None, None, "mp"),
        P("mp", None),
        P(),
    )
    return jax.shard_map(local_part, mesh=mesh, in_specs=in_specs, out_specs=out_specs, check_vma=False)
```
